256 devices in a mesh: gx: 32 (over x, z_lo, core), gy: 8 (over z_hi, y).
Axes of the slice: x: 4, y: 4, z: 8 (z_hi: 2, z_lo: 4; z = z_hi * 4 + z_lo), core: 2. Of those that a mesh axis runs over, the one named last changes fastest.
Arguments:
- tracers: float32 [2, 16, 384, 4096], P(None, None, 'gy', 'gx'), may hold values from -6 to 6
- east_speed: float32 [16, 384, 4096], P(None, 'gy', 'gx'), may hold values from -0.45 to 0.45
- north_speed: float32 [16, 384, 4096], P(None, 'gy', 'gx'), may hold values from -0.45 to 0.45
- bottom_level: int32 [384, 4096], P('gy', 'gx'), may hold values from 0 to 16
Outputs:
- stepped: float32 [2, 16, 384, 4096], P(None, None, 'gy', 'gx')
The draws below stay inside these ranges and needn't reach their ends.
Inputs may be any that keep to these rules, and one draw needn't show every extreme that they name: Level k of a column is water where k < bottom_level, land otherwise.
All inputs are finite; a program needn't handle non-finite values.
Results may differ from the reference program's by a relative error of at most 0.0003.
Values sent between devices are 32-bit elements; how exact they have to be, the bound alone decides.
A program may use at most 64 MiB of HBM per device.

```python
import jax
import jax.numpy as jnp
from jax import lax

CY = 48
NZ = 16
NXG = 4096
NYG = 384
N_GY = 8


def place_ends(values, key, least, high):
    longest = values.shape.index(max(values.shape))
    spots = []
    for shift in (0, 1):
        where = [jax.random.randint(jax.random.fold_in(key, axis), (), 0, length) for axis, length in enumerate(values.shape)]
        where[longest] = (where[longest] + shift) % values.shape[longest]
        spots.append(tuple(where))
    return values.at[spots[0]].set(least).at[spots[1]].set(high)


def block_levels(own_key, dims, split, smallest, top_value):
    loudness = 1.0
    for axis_at, parts in split:
        draws = jax.random.uniform(jax.random.fold_in(jax.random.fold_in(own_key, 6), axis_at), (parts,), jnp.float32, smallest / len(split), top_value / len(split))
        loudness = loudness * jnp.repeat(jnp.exp(draws), dims[axis_at] // parts).reshape((-1,) + (1,) * (len(dims) - 1 - axis_at))
    return loudness


def noise(key, extent, scale, most, split=(), kind=jnp.bfloat16):
    entries = jax.random.normal(key, extent, jnp.float32) * scale
    if len(split) > 0:
        entries = block_levels(key, extent, split, -0.22, 0.18) * entries
    return jnp.clip(entries, min=-most, max=most).astype(kind)


def setup_inputs(seed: int = 0) -> dict:
    keys = jax.random.split(jax.random.key(seed), 5)
    return {
        "tracers": noise(keys[0], (2, NZ, NYG, NXG), 1.0, 6.0, ((2, 8), (3, 32)), jnp.float32),
        "east_speed": jnp.clip(jax.random.uniform(keys[1], (NZ, NYG, NXG), jnp.float32, -0.45, 0.45) * block_levels(keys[1], (NZ, NYG, NXG), ((1, 8), (2, 32)), -0.4, 0.0), -0.45, 0.45),
        "north_speed": jnp.clip(jax.random.uniform(keys[2], (NZ, NYG, NXG), jnp.float32, -0.45, 0.45) * block_levels(keys[2], (NZ, NYG, NXG), ((1, 8), (2, 32)), -0.4, 0.0), -0.45, 0.45),
        "bottom_level": place_ends(jax.random.randint(keys[3], (NYG, NXG), 0, NZ + 1), jax.random.fold_in(keys[3], 1), 0, NZ).astype(jnp.int32),
    }


ALPHA_HEAT = 0.4
BETA_SALT = 0.6
RHO_FLOOR = 0.25
SLOPE_MAX = 1.0
DIFFUSIVITY = 0.1


def minmod_limit(first, second):
    return 0.5 * (jnp.sign(first) + jnp.sign(second)) * jnp.minimum(jnp.abs(first), jnp.abs(second))


def vertical_steps(field, wet_mask):
    interfaces = (field[..., 1:, :, :] - field[..., :-1, :, :]) * (wet_mask[1:] * wet_mask[:-1])
    zero_level = jnp.zeros_like(interfaces[..., :1, :, :])
    centred = 0.5 * (jnp.concatenate([zero_level, interfaces], axis=-3) + jnp.concatenate([interfaces, zero_level], axis=-3))
    return interfaces, centred


def directional(tracer, density, tracer_dz, density_dz, wet_mask, velocity, from_end, length):
    faces = length + 1

    def piece(array, offset, number=faces):
        return lax.slice_in_dim(array, offset, offset + number, axis=array.ndim - from_end)

    mask_back, mask_here, mask_next, mask_far = [piece(wet_mask, shift_by) for shift_by in range(4)]
    value_back, value_here, value_next, value_far = [piece(tracer, shift_by) for shift_by in range(4)]
    face_mask = mask_here * mask_next
    speed = piece(velocity, 1) * face_mask
    local_grad = (value_next - value_here) * face_mask
    forward = speed >= 0.0
    upstream = jnp.where(forward, (value_here - value_back) * (mask_here * mask_back), (value_far - value_next) * (mask_next * mask_far))
    upwind_value = jnp.where(forward, value_here, value_next)
    adv_flux = speed * upwind_value + 0.5 * jnp.abs(speed) * (1.0 - jnp.abs(speed)) * minmod_limit(local_grad, upstream)
    density_grad = (piece(density, 2) - piece(density, 1)) * face_mask
    stratified = jnp.maximum(0.5 * (piece(density_dz, 1) + piece(density_dz, 2)), RHO_FLOOR)
    slope = jnp.clip(-density_grad / stratified, -SLOPE_MAX, SLOPE_MAX)
    iso_flux = DIFFUSIVITY * face_mask * (local_grad + slope * 0.5 * (piece(tracer_dz, 1) + piece(tracer_dz, 2)))

    def difference(array):
        return piece(array, 1, length) - piece(array, 0, length)

    def centre(array):
        return 0.5 * (piece(array, 1, length) + piece(array, 0, length))

    return difference(adv_flux), difference(iso_flux), difference(speed), centre(local_grad), centre(density_grad)


def tracer_step(tracer_pad, bottom_pad, east_pad, north_pad):
    levels_count = tracer_pad.shape[1]
    rows_count = tracer_pad.shape[2] - 4
    cols_count = tracer_pad.shape[3] - 4
    level_ids = jnp.arange(levels_count).astype(tracer_pad.dtype)
    wet_mask = (level_ids[:, None, None] < bottom_pad[None]).astype(tracer_pad.dtype)
    density = BETA_SALT * tracer_pad[1] - ALPHA_HEAT * tracer_pad[0]
    tracer_inter, tracer_dz = vertical_steps(tracer_pad, wet_mask)
    density_inter, density_dz = vertical_steps(density, wet_mask)

    def inner_rows(array):
        return array[..., 2:rows_count + 2, :]

    def inner_cols(array):
        return array[..., 2:cols_count + 2]

    east_adv, east_iso, east_vel, grad_tx, grad_rx = directional(
        inner_rows(tracer_pad), inner_rows(density), inner_rows(tracer_dz), inner_rows(density_dz),
        inner_rows(wet_mask), inner_rows(east_pad), 1, cols_count)
    north_adv, north_iso, north_vel, grad_ty, grad_ry = directional(
        inner_cols(tracer_pad), inner_cols(density), inner_cols(tracer_dz), inner_cols(density_dz),
        inner_cols(wet_mask), inner_cols(north_pad), 2, rows_count)
    centre_mask = inner_cols(inner_rows(wet_mask))
    centre_tracer = inner_cols(inner_rows(tracer_pad))
    inter_tracer = inner_cols(inner_rows(tracer_inter))
    inter_density = inner_cols(inner_rows(density_inter))

    def level_mean(array):
        return 0.5 * (array[..., 1:, :, :] + array[..., :-1, :, :])

    stratified = jnp.maximum(inter_density, RHO_FLOOR)
    slope_x = jnp.clip(-level_mean(grad_rx) / stratified, -SLOPE_MAX, SLOPE_MAX)
    slope_y = jnp.clip(-level_mean(grad_ry) / stratified, -SLOPE_MAX, SLOPE_MAX)
    inter_mask = centre_mask[1:] * centre_mask[:-1]
    vertical_flux = DIFFUSIVITY * inter_mask * (slope_x * level_mean(grad_tx) + slope_y * level_mean(grad_ty)
                                                + (slope_x * slope_x + slope_y * slope_y) * inter_tracer)
    zero_level = jnp.zeros_like(vertical_flux[..., :1, :, :])
    vertical_div = jnp.concatenate([vertical_flux, zero_level], axis=-3) - jnp.concatenate([zero_level, vertical_flux], axis=-3)
    tendency = (-(east_adv + north_adv) + centre_tracer * (east_vel + north_vel)
                + east_iso + north_iso + vertical_div)
    return centre_mask * (centre_tracer + tendency)


def fold_pad(field, with_fold):
    rows_total = field.shape[-2]
    south = jnp.zeros_like(field[..., :2, :])
    if with_fold:
        north = jnp.flip(field[..., rows_total - 2:, :], axis=(-2, -1))
    else:
        north = jnp.zeros_like(south)
    tall = jnp.concatenate([south, field, north], axis=-2)
    return jnp.concatenate([tall[..., -2:], tall, tall[..., :2]], axis=-1)


def reference(tracers, east_speed, north_speed, bottom_level):
    tracer_pad = fold_pad(tracers, True)
    bottom_pad = fold_pad(bottom_level.astype(jnp.float32), True)
    east_pad = fold_pad(east_speed, False)
    north_pad = fold_pad(north_speed, False)

    def band(index):
        start = index * CY
        return tracer_step(lax.dynamic_slice_in_dim(tracer_pad, start, CY + 4, axis=2),
                           lax.dynamic_slice_in_dim(bottom_pad, start, CY + 4, axis=0),
                           lax.dynamic_slice_in_dim(east_pad, start, CY + 4, axis=1),
                           lax.dynamic_slice_in_dim(north_pad, start, CY + 4, axis=1))

    bands = lax.map(band, jnp.arange(N_GY, dtype=jnp.int32))
    return jnp.transpose(bands, (1, 2, 0, 3, 4)).reshape(2, NZ, NYG, NXG)
```

```python
import functools

import jax
import jax.numpy as jnp
from jax import lax
from jax.experimental import pallas as pl
from jax.experimental.pallas import tpu as pltpu
from jax.sharding import PartitionSpec as P

MESH = pl.DeviceIdType.MESH
NT, NZ, CY, CX = 2, 16, 48, 128
PAD = 8
TALL = CY + 2 * PAD
OCTETS = CY // 8
ROWS_FROM_NORTH = 72
ROWS_FROM_SOUTH = 88
PACKED = 13
HEAT = 0.4
SALT = 0.6


def reciprocal(value):
    guess = pl.reciprocal(value, approx=True)
    return guess * (2.0 - value * guess)


def minmod(first, second):
    return jnp.maximum(jnp.minimum(first, second), 0.0) + jnp.minimum(
        jnp.maximum(first, second), 0.0
    )


def density(pair):
    return SALT * pair[1] - HEAT * pair[0]


def face_fluxes(local, before, after, dz_sum, speed):
    slope = jnp.clip(
        (0.1 * density(local)) * reciprocal(jnp.maximum(density(dz_sum), 1.0)), -0.025, 0.025
    )
    size = jnp.abs(speed)
    limited = 0.5 * size * (1.0 - size)
    forward = speed >= 0.0
    linear = jnp.minimum(speed, 0.0) - 0.1
    low, high, second = [], [], []
    for t in range(NT):
        correction = limited * minmod(local[t], jnp.where(forward, before[t], after[t]))
        taken = correction + (linear * local[t] + slope * dz_sum[t])
        low.append(taken)
        high.append(taken - speed * local[t])
        second.append(correction)
    return low, high, second, forward


def lanes_left(value):
    return pltpu.roll(value, CX - 1, 1)


def lanes_right(value):
    return pltpu.roll(value, 1, 1)


def rows_up(value):
    return pltpu.roll(value, 7, 0)


def rows_down(value):
    return pltpu.roll(value, 1, 0)


def edge_terms(field, dz, bottom, speed, level, nxt, prv, low_at, high_at, low_second, high_second):
    wet = jnp.minimum(bottom, nxt(bottom)) > level
    local = [jnp.where(wet, nxt(f) - f, 0.0) for f in field]
    dz_sum = [z + nxt(z) for z in dz]
    masked = jnp.where(wet, speed, 0.0)
    low, high, second, forward = face_fluxes(
        local, [prv(d) for d in local], [nxt(d) for d in local], dz_sum, masked
    )
    zero = jnp.zeros_like(masked)
    terms, steps = [], []
    for t in range(NT):
        late = zero
        if low_second is not None:
            late = late + jnp.where(low_second & ~forward, second[t], 0.0)
        if high_second is not None:
            late = late + jnp.where(high_second & forward, second[t], 0.0)
        arriving, term, step = late, -late, zero
        if high_at is not None:
            arriving = arriving + jnp.where(high_at, high[t], 0.0)
            step = step + prv(jnp.where(high_at, local[t], 0.0))
        if low_at is not None:
            term = term - jnp.where(low_at, low[t], 0.0)
            step = step + jnp.where(low_at, local[t], 0.0)
        terms.append(term + prv(arriving))
        steps.append(step)
    return terms, steps


def kernel(
    n_gx, n_gy,
    tracers, east, north, bottom, out,
    T, U, V, bottom_int, bf, be, bn, TZ, XY, YB, GX, GY,
    packed, from_west, from_east, to_north, to_south, from_north, from_south,
    strip, strip_b, strip_v, edge_c, edge_g,
    load_sem, send_sem, recv_sem,
):
    gx, gy = lax.axis_index("gx"), lax.axis_index("gy")
    east_id = (lax.rem(gx + 1, n_gx), gy)
    west_id = (lax.rem(gx + n_gx - 1, n_gx), gy)
    north_id = (gx, gy + 1)
    south_id = (gx, gy - 1)
    mirror_id = (n_gx - 1 - gx, gy)
    top = gy == n_gy - 1
    base = gy == 0

    barrier = pltpu.get_barrier_semaphore()

    def greet(device):
        pl.semaphore_signal(barrier, inc=1, device_id=device, device_id_type=MESH)

    greet(east_id)
    greet(west_id)
    pl.when(top)(lambda: greet(mirror_id))
    pl.when(jnp.logical_not(top))(lambda: greet(north_id))
    pl.when(jnp.logical_not(base))(lambda: greet(south_id))

    loads = [
        pltpu.make_async_copy(tracers, T.at[:, :, pl.ds(PAD, CY), :], load_sem.at[0]),
        pltpu.make_async_copy(bottom, bottom_int, load_sem.at[1]),
        pltpu.make_async_copy(east, U, load_sem.at[2]),
        pltpu.make_async_copy(north, V, load_sem.at[3]),
    ]
    for load in loads:
        load.start()

    lane = lax.broadcasted_iota(jnp.int32, (8, CX), 1)
    row = lax.broadcasted_iota(jnp.int32, (8, CX), 0)
    zeros = jnp.zeros((8, CX), jnp.float32)

    def octet(o):
        return pl.ds(PAD + 8 * o, 8)

    def shifted(o, by):
        return pl.ds(PAD + 8 * o + by, 8)

    for pad in (pl.ds(0, PAD), pl.ds(PAD + CY, PAD)):
        bf[pad, :] = zeros
        bn[pad, :] = zeros

    def clear(k, carry):
        for t in range(NT):
            YB[t, k, pl.ds(0, PAD), :] = zeros
            TZ[t, k, pl.ds(PAD + CY, PAD), :] = zeros
        strip_v[k] = zeros
        return carry

    lax.fori_loop(0, NZ, clear, 0)

    @pl.when(base)
    def _():
        from_south[...] = jnp.zeros_like(from_south)

    for load in loads:
        load.wait()

    for o in range(OCTETS):
        bf[octet(o), :] = bottom_int[pl.ds(8 * o, 8), :].astype(jnp.float32)
    for o in range(OCTETS):
        here = bf[octet(o), :]
        be[octet(o), :] = jnp.where(lane == CX - 1, 0.0, jnp.minimum(here, lanes_left(here)))
        bn[octet(o), :] = jnp.minimum(here, bf[shifted(o, 1), :])

    def rows_out(k, carry):
        for t in range(NT):
            spot = pl.ds(2 * (NZ * t + k), 2)
            last = T[t, k, pl.ds(PAD + CY - 2, 2), :]
            first = T[t, k, pl.ds(PAD, 2), :]
            to_north[spot, :] = last
            to_south[spot, :] = first
            strip[t, k, pl.ds(0, 2), :] = last
            strip[t, k, pl.ds(6, 2), :] = first
        last_v = V[k, pl.ds(CY - 2, 2), :]
        to_north[pl.ds(72 + k, 1), :] = last_v[1:2]
        strip_v[k, pl.ds(0, 2), :] = last_v
        strip_v[k, pl.ds(6, 1), :] = V[k, pl.ds(0, 1), :]
        return carry

    lax.fori_loop(0, NZ, rows_out, 0)
    last_b = bf[pl.ds(PAD + CY - 2, 2), :]
    first_b = bf[pl.ds(PAD, 2), :]
    to_north[pl.ds(64, 8), :] = zeros
    to_south[pl.ds(64, 8), :] = zeros
    to_north[pl.ds(64, 2), :] = last_b
    to_south[pl.ds(64, 2), :] = first_b
    strip_b[pl.ds(0, 2), :] = last_b
    strip_b[pl.ds(6, 2), :] = first_b

    slot_of = lane // 4

    def pack(k_low, carry):
        t0, t1, speed = zeros, zeros, zeros
        for k_high in range(4):
            for o in range(OCTETS):
                slot = k_high * 8 + o
                here = slot_of == slot
                shift = (4 * slot + 2) % CX
                k = 4 * k_high + k_low
                t0 = jnp.where(here, pltpu.roll(T[0, k, octet(o), :], shift, 1), t0)
                t1 = jnp.where(here, pltpu.roll(T[1, k, octet(o), :], shift, 1), t1)
                speed = jnp.where(here, pltpu.roll(U[k, pl.ds(8 * o, 8), :], shift, 1), speed)
        packed[k_low] = t0
        packed[4 + k_low] = t1
        packed[8 + k_low] = speed
        return carry

    lax.fori_loop(0, 4, pack, 0)
    packed_b = zeros
    for k_high in range(4):
        for o in range(OCTETS):
            slot = k_high * 8 + o
            packed_b = jnp.where(
                slot_of == slot, pltpu.roll(bf[octet(o), :], (4 * slot + 2) % CX, 1), packed_b
            )
    packed[12] = packed_b

    pl.semaphore_wait(barrier, jnp.where(base, 3, 4))

    def send(source, target, index, slot, device):
        return pltpu.make_async_remote_copy(
            src_ref=source, dst_ref=target, send_sem=send_sem.at[index], recv_sem=recv_sem.at[slot],
            device_id=device, device_id_type=MESH,
        )

    eastward = send(packed, from_west, 0, 0, east_id)
    westward = send(packed, from_east, 1, 1, west_id)
    northward = send(to_north, from_south, 2, 2, north_id)
    southward = send(to_south, from_north, 3, 3, south_id)
    across = send(to_north.at[pl.ds(0, ROWS_FROM_NORTH)], from_north, 2, 3, mirror_id)

    pl.when(jnp.logical_not(base))(southward.start)
    pl.when(jnp.logical_not(top))(northward.start)
    pl.when(top)(across.start)
    eastward.start()
    westward.start()

    def vertical(k, carry):
        level = k.astype(jnp.float32)
        above = jnp.where(k > 0, level, 99.0)
        down, up = jnp.minimum(k + 1, NZ - 1), jnp.maximum(k - 1, 0)
        for o in range(OCTETS):
            depth = bf[octet(o), :]
            for t in range(NT):
                here = T[t, k, octet(o), :]
                TZ[t, k, octet(o), :] = jnp.where(
                    depth > level + 1.0, T[t, down, octet(o), :] - here, 0.0
                ) + jnp.where(depth > above, here - T[t, up, octet(o), :], 0.0)
        return carry

    lax.fori_loop(0, NZ, vertical, 0)

    def inside(k, carry):
        level = k.astype(jnp.float32)
        for o in range(OCTETS):
            here = [T[t, k, octet(o), :] for t in range(NT)]
            dz = [TZ[t, k, octet(o), :] for t in range(NT)]
            wet = be[octet(o), :] > level
            local = [jnp.where(wet, lanes_left(f) - f, 0.0) for f in here]
            before = [lanes_right(d) for d in local]
            after = [lanes_left(d) for d in local]
            speed = jnp.where(wet, U[k, pl.ds(8 * o, 8), :], 0.0)
            low, high, _, _ = face_fluxes(
                local, before, after, [z + lanes_left(z) for z in dz], speed
            )
            across_x = [lanes_right(high[t]) - low[t] for t in range(NT)]
            for t in range(NT):
                GX[t, k, octet(o), :] = local[t] + before[t]

            wet = bn[octet(o), :] > level
            wet_before = bn[shifted(o, -1), :] > level
            wet_after = bn[shifted(o, 1), :] > level
            nxt = [T[t, k, shifted(o, 1), :] for t in range(NT)]
            local = [jnp.where(wet, nxt[t] - here[t], 0.0) for t in range(NT)]
            before = [
                jnp.where(wet_before, here[t] - T[t, k, shifted(o, -1), :], 0.0) for t in range(NT)
            ]
            after = [
                jnp.where(wet_after, T[t, k, shifted(o, 2), :] - nxt[t], 0.0) for t in range(NT)
            ]
            speed = jnp.where(wet, V[k, pl.ds(8 * o, 8), :], 0.0)
            low, high, _, _ = face_fluxes(
                local, before, after, [dz[t] + TZ[t, k, shifted(o, 1), :] for t in range(NT)], speed
            )
            for t in range(NT):
                GY[t, k, octet(o), :] = local[t] + before[t]
                XY[t, k, octet(o), :] = across_x[t] - low[t]
                YB[t, k, octet(o), :] = high[t]
        return carry

    lax.fori_loop(0, NZ, inside, 0)

    eastward.wait_recv()
    westward.wait_recv()
    quarter = lax.rem(lane, 4)
    first_half = quarter < 2
    level_base = (lane // 32 * 4).astype(jnp.float32)
    for side in range(2):
        theirs = from_west if side == 0 else from_east

        def joined(index, side=side, theirs=theirs):
            if side == 0:
                return jnp.where(first_half, theirs[index], packed[index])
            return jnp.where(first_half, packed[index], theirs[index])

        depth = joined(12)
        fields = [[joined(4 * t + j) for j in range(4)] for t in range(NT)]
        steps = []
        for t in range(NT):
            column = fields[t] + [pltpu.roll(fields[t][0], CX - 32, 1)]
            steps.append(
                [
                    jnp.where(depth > level_base + (j + 1.0), column[j + 1] - column[j], 0.0)
                    for j in range(4)
                ]
            )
        for j in range(4):
            dz = [
                steps[t][j] + (steps[t][j - 1] if j > 0 else pltpu.roll(steps[t][3], 32, 1))
                for t in range(NT)
            ]
            speed = joined(8 + j) if side == 0 else packed[8 + j]
            terms, grads = edge_terms(
                [fields[t][j] for t in range(NT)], dz, depth, speed, level_base + float(j),
                lanes_left, lanes_right,
                None if side == 0 else quarter == 1, quarter == 1 if side == 0 else None,
                None if side == 0 else quarter == 0, quarter == 2 if side == 0 else None,
            )
            for t in range(NT):
                if side == 0:
                    edge_c[t, j] = terms[t]
                    edge_g[t, j] = grads[t]
                else:
                    edge_c[t, j] += terms[t]
                    edge_g[t, j] += grads[t]

    at_edge = (lane < 2) | (lane >= CX - 2)

    def inject(k_low, carry):
        for t in range(NT):
            term, grad = edge_c[t, k_low], edge_g[t, k_low]
            for k_high in range(4):
                for o in range(OCTETS):
                    back = (CX - (4 * (k_high * 8 + o) + 2)) % CX
                    k = 4 * k_high + k_low
                    XY[t, k, octet(o), :] += jnp.where(at_edge, pltpu.roll(term, back, 1), 0.0)
                    GX[t, k, octet(o), :] += jnp.where(at_edge, pltpu.roll(grad, back, 1), 0.0)
        return carry

    lax.fori_loop(0, 4, inject, 0)

    def finish(octets):
        def body(k, carry):
            level = k.astype(jnp.float32)
            down = jnp.minimum(k + 1, NZ - 1)
            fluxes = []
            for i, o in enumerate(octets):
                depth = bf[octet(o), :]
                open_below = depth > level + 1.0
                here = [T[t, k, octet(o), :] for t in range(NT)]
                step = [
                    jnp.where(open_below, T[t, down, octet(o), :] - here[t], 0.0) for t in range(NT)
                ]
                mean_x = [GX[t, k, octet(o), :] + GX[t, down, octet(o), :] for t in range(NT)]
                mean_y = [GY[t, k, octet(o), :] + GY[t, down, octet(o), :] for t in range(NT)]
                inverse = jnp.where(
                    open_below, reciprocal(jnp.maximum(4.0 * density(step), 1.0)), 0.0
                )
                slope_x = jnp.clip(density(mean_x) * inverse, -1.0, 1.0)
                slope_y = jnp.clip(density(mean_y) * inverse, -1.0, 1.0)
                squares = 0.1 * (slope_x * slope_x + slope_y * slope_y)
                slope_x = 0.025 * slope_x
                slope_y = 0.025 * slope_y
                wet = depth > level
                for t in range(NT):
                    flux = squares * step[t] - (slope_x * mean_x[t] + slope_y * mean_y[t])
                    total = (
                        here[t]
                        + (XY[t, k, octet(o), :] + YB[t, k, shifted(o, -1), :])
                        + (flux - carry[NT * i + t])
                    )
                    out[t, k, pl.ds(8 * o, 8), :] = jnp.where(wet, total, 0.0)
                    fluxes.append(flux)
            return tuple(fluxes)

        lax.fori_loop(0, NZ, body, tuple(zeros for _ in range(NT * len(octets))))

    finish(tuple(range(1, OCTETS - 1)))

    southward.wait_recv()
    pl.when(jnp.logical_not(base))(northward.wait_recv)

    @pl.when(top)
    def _():
        for i in range(ROWS_FROM_NORTH // 8):
            value = from_north[pl.ds(8 * i, 8), :]
            for bit in (64, 32, 16, 8, 4, 2, 1):
                value = jnp.where(
                    (lane & bit) != 0, pltpu.roll(value, bit, 1), pltpu.roll(value, CX - bit, 1)
                )
            from_north[pl.ds(8 * i, 8), :] = jnp.where(
                (row & 1) != 0, rows_down(value), rows_up(value)
            )

    def rows_in(k, carry):
        for t in range(NT):
            spot = pl.ds(2 * (NZ * t + k), 2)
            strip[t, k, pl.ds(2, 2), :] = from_north[spot, :]
            strip[t, k, pl.ds(4, 2), :] = from_south[spot, :]
        strip_v[k, pl.ds(5, 1), :] = from_south[pl.ds(72 + k, 1), :]
        return carry

    lax.fori_loop(0, NZ, rows_in, 0)
    strip_b[pl.ds(2, 2), :] = from_north[pl.ds(64, 2), :]
    strip_b[pl.ds(4, 2), :] = from_south[pl.ds(64, 2), :]

    def edge_rows(k, carry):
        level = k.astype(jnp.float32)
        above = jnp.where(k > 0, level, 99.0)
        down, up = jnp.minimum(k + 1, NZ - 1), jnp.maximum(k - 1, 0)
        depth = strip_b[...]
        here = [strip[t, k] for t in range(NT)]
        dz = [
            jnp.where(depth > level + 1.0, strip[t, down] - here[t], 0.0)
            + jnp.where(depth > above, here[t] - strip[t, up], 0.0)
            for t in range(NT)
        ]
        terms, grads = edge_terms(
            here, dz, depth, strip_v[k], level, rows_up, rows_down,
            row == 1, row == 5, row == 0, row == 6,
        )
        for t in range(NT):
            XY[t, k, octet(0), :] += jnp.where(row < 2, pltpu.roll(terms[t], 2, 0), 0.0)
            GY[t, k, octet(0), :] += jnp.where(row < 2, pltpu.roll(grads[t], 2, 0), 0.0)
            XY[t, k, octet(OCTETS - 1), :] += jnp.where(row > 5, pltpu.roll(terms[t], 6, 0), 0.0)
            GY[t, k, octet(OCTETS - 1), :] += jnp.where(row > 5, pltpu.roll(grads[t], 6, 0), 0.0)
        return carry

    lax.fori_loop(0, NZ, edge_rows, 0)
    finish((0, OCTETS - 1))

    eastward.wait_send()
    westward.wait_send()
    pl.when(jnp.logical_not(base))(southward.wait_send)
    pl.when(jnp.logical_not(top))(northward.wait_send)
    pl.when(top)(across.wait_send)


def solution(mesh):
    n_gx, n_gy = mesh.shape["gx"], mesh.shape["gy"]
    f32 = jnp.float32
    anywhere = pl.BlockSpec(memory_space=pl.ANY)
    field = pltpu.VMEM((NT, NZ, TALL, CX), f32)
    levels = pltpu.VMEM((NZ, CY, CX), f32)
    plane = pltpu.VMEM((TALL, CX), f32)
    packed = pltpu.VMEM((PACKED, 8, CX), f32)
    edge = pltpu.VMEM((NT, 4, 8, CX), f32)

    def on_device(tracers, east_speed, north_speed, bottom_level):
        return pl.pallas_call(
            functools.partial(kernel, n_gx, n_gy),
            out_shape=jax.ShapeDtypeStruct((NT, NZ, CY, CX), f32),
            in_specs=[anywhere] * 4,
            out_specs=pl.BlockSpec(memory_space=pltpu.VMEM),
            scratch_shapes=[
                field, levels, levels, pltpu.VMEM((CY, CX), jnp.int32), plane, plane, plane,
                field, field, field, field, field,
                packed, packed, packed,
                pltpu.VMEM((ROWS_FROM_SOUTH, CX), f32), pltpu.VMEM((ROWS_FROM_NORTH, CX), f32),
                pltpu.VMEM((ROWS_FROM_NORTH, CX), f32), pltpu.VMEM((ROWS_FROM_SOUTH, CX), f32),
                pltpu.VMEM((NT, NZ, 8, CX), f32), pltpu.VMEM((8, CX), f32),
                pltpu.VMEM((NZ, 8, CX), f32), edge, edge,
                pltpu.SemaphoreType.DMA((4,)), pltpu.SemaphoreType.DMA((4,)),
                pltpu.SemaphoreType.DMA((4,)),
            ],
            compiler_params=pltpu.CompilerParams(
                collective_id=0, has_side_effects=True, vmem_limit_bytes=40 * 1024 * 1024
            ),
        )(tracers, east_speed, north_speed, bottom_level)

    in_specs = (P(None, None, "gy", "gx"), P(None, "gy", "gx"), P(None, "gy", "gx"), P("gy", "gx"))
    return jax.shard_map(
        on_device, mesh=mesh, in_specs=in_specs, out_specs=P(None, None, "gy", "gx"), check_vma=False
    )
```

```python
import functools

import jax
import jax.numpy as jnp
from jax import lax
from jax.experimental import pallas as pl
from jax.experimental.pallas import tpu as pltpu
from jax.sharding import PartitionSpec as P

MESH = pl.DeviceIdType.MESH
NT, NZ, CY, CX = 2, 16, 48, 128
PAD = 8
TALL = CY + 2 * PAD
OCTETS = CY // 8
ROWS_FROM_NORTH = 72
ROWS_FROM_SOUTH = 88
PACKED = 13
HEAT = 0.4
SALT = 0.6


def reciprocal(value):
    guess = pl.reciprocal(value, approx=True)
    return guess * (2.0 - value * guess)


def minmod(first, second):
    return jnp.maximum(jnp.minimum(first, second), 0.0) + jnp.minimum(
        jnp.maximum(first, second), 0.0
    )


def density(pair):
    return SALT * pair[1] - HEAT * pair[0]


def face_fluxes(local, before, after, dz_sum, speed):
    slope = jnp.clip(
        (0.1 * density(local)) * reciprocal(jnp.maximum(density(dz_sum), 1.0)), -0.025, 0.025
    )
    size = jnp.abs(speed)
    limited = 0.5 * size * (1.0 - size)
    forward = speed >= 0.0
    linear = jnp.minimum(speed, 0.0) - 0.1
    low, high, second = [], [], []
    for t in range(NT):
        correction = limited * minmod(local[t], jnp.where(forward, before[t], after[t]))
        taken = correction + (linear * local[t] + slope * dz_sum[t])
        low.append(taken)
        high.append(taken - speed * local[t])
        second.append(correction)
    return low, high, second, forward


def lanes_left(value):
    return pltpu.roll(value, CX - 1, 1)


def lanes_right(value):
    return pltpu.roll(value, 1, 1)


def rows_up(value):
    return pltpu.roll(value, 7, 0)


def rows_down(value):
    return pltpu.roll(value, 1, 0)


def edge_terms(field, dz, bottom, speed, level, nxt, prv, low_at, high_at, low_second, high_second):
    wet = jnp.minimum(bottom, nxt(bottom)) > level
    local = [jnp.where(wet, nxt(f) - f, 0.0) for f in field]
    dz_sum = [z + nxt(z) for z in dz]
    masked = jnp.where(wet, speed, 0.0)
    low, high, second, forward = face_fluxes(
        local, [prv(d) for d in local], [nxt(d) for d in local], dz_sum, masked
    )
    zero = jnp.zeros_like(masked)
    terms, steps = [], []
    for t in range(NT):
        late = zero
        if low_second is not None:
            late = late + jnp.where(low_second & ~forward, second[t], 0.0)
        if high_second is not None:
            late = late + jnp.where(high_second & forward, second[t], 0.0)
        arriving, term, step = late, -late, zero
        if high_at is not None:
            arriving = arriving + jnp.where(high_at, high[t], 0.0)
            step = step + prv(jnp.where(high_at, local[t], 0.0))
        if low_at is not None:
            term = term - jnp.where(low_at, low[t], 0.0)
            step = step + jnp.where(low_at, local[t], 0.0)
        terms.append(term + prv(arriving))
        steps.append(step)
    return terms, steps


def kernel(
    n_gx, n_gy,
    tracers, east, north, bottom, out,
    T, U, V, bottom_int, bf, be, bn, TZ, XY, YB, GX, GY,
    packed, from_west, from_east, to_north, to_south, from_north, from_south,
    strip, strip_b, strip_v, edge_c, edge_g,
    load_sem, send_sem, recv_sem,
):
    gx, gy = lax.axis_index("gx"), lax.axis_index("gy")
    east_id = (lax.rem(gx + 1, n_gx), gy)
    west_id = (lax.rem(gx + n_gx - 1, n_gx), gy)
    north_id = (gx, gy + 1)
    south_id = (gx, gy - 1)
    mirror_id = (n_gx - 1 - gx, gy)
    top = gy == n_gy - 1
    base = gy == 0

    barrier = pltpu.get_barrier_semaphore()

    def greet(device):
        pl.semaphore_signal(barrier, inc=1, device_id=device, device_id_type=MESH)

    greet(east_id)
    greet(west_id)
    pl.when(top)(lambda: greet(mirror_id))
    pl.when(jnp.logical_not(top))(lambda: greet(north_id))
    pl.when(jnp.logical_not(base))(lambda: greet(south_id))

    loads = [
        pltpu.make_async_copy(tracers, T.at[:, :, pl.ds(PAD, CY), :], load_sem.at[0]),
        pltpu.make_async_copy(bottom, bottom_int, load_sem.at[1]),
        pltpu.make_async_copy(east, U, load_sem.at[2]),
        pltpu.make_async_copy(north, V, load_sem.at[3]),
    ]
    for load in loads:
        load.start()

    lane = lax.broadcasted_iota(jnp.int32, (8, CX), 1)
    row = lax.broadcasted_iota(jnp.int32, (8, CX), 0)
    zeros = jnp.zeros((8, CX), jnp.float32)

    def octet(o):
        return pl.ds(PAD + 8 * o, 8)

    def shifted(o, by):
        return pl.ds(PAD + 8 * o + by, 8)

    for pad in (pl.ds(0, PAD), pl.ds(PAD + CY, PAD)):
        bf[pad, :] = zeros
        bn[pad, :] = zeros

    def clear(k, carry):
        for t in range(NT):
            YB[t, k, pl.ds(0, PAD), :] = zeros
            TZ[t, k, pl.ds(PAD + CY, PAD), :] = zeros
        strip_v[k] = zeros
        return carry

    lax.fori_loop(0, NZ, clear, 0)

    @pl.when(base)
    def _():
        from_south[...] = jnp.zeros_like(from_south)

    for load in loads:
        load.wait()

    for o in range(OCTETS):
        bf[octet(o), :] = bottom_int[pl.ds(8 * o, 8), :].astype(jnp.float32)
    for o in range(OCTETS):
        here = bf[octet(o), :]
        be[octet(o), :] = jnp.where(lane == CX - 1, 0.0, jnp.minimum(here, lanes_left(here)))
        bn[octet(o), :] = jnp.minimum(here, bf[shifted(o, 1), :])

    def rows_out(k, carry):
        for t in range(NT):
            spot = pl.ds(2 * (NZ * t + k), 2)
            last = T[t, k, pl.ds(PAD + CY - 2, 2), :]
            first = T[t, k, pl.ds(PAD, 2), :]
            to_north[spot, :] = last
            to_south[spot, :] = first
            strip[t, k, pl.ds(0, 2), :] = last
            strip[t, k, pl.ds(6, 2), :] = first
        last_v = V[k, pl.ds(CY - 2, 2), :]
        to_north[pl.ds(72 + k, 1), :] = last_v[1:2]
        strip_v[k, pl.ds(0, 2), :] = last_v
        strip_v[k, pl.ds(6, 1), :] = V[k, pl.ds(0, 1), :]
        return carry

    lax.fori_loop(0, NZ, rows_out, 0)
    last_b = bf[pl.ds(PAD + CY - 2, 2), :]
    first_b = bf[pl.ds(PAD, 2), :]
    to_north[pl.ds(64, 8), :] = zeros
    to_south[pl.ds(64, 8), :] = zeros
    to_north[pl.ds(64, 2), :] = last_b
    to_south[pl.ds(64, 2), :] = first_b
    strip_b[pl.ds(0, 2), :] = last_b
    strip_b[pl.ds(6, 2), :] = first_b

    slot_of = lane // 4

    def pack(k_low, carry):
        t0, t1, speed = zeros, zeros, zeros
        for k_high in range(4):
            for o in range(OCTETS):
                slot = k_high * 8 + o
                here = slot_of == slot
                shift = (4 * slot + 2) % CX
                k = 4 * k_high + k_low
                t0 = jnp.where(here, pltpu.roll(T[0, k, octet(o), :], shift, 1), t0)
                t1 = jnp.where(here, pltpu.roll(T[1, k, octet(o), :], shift, 1), t1)
                speed = jnp.where(here, pltpu.roll(U[k, pl.ds(8 * o, 8), :], shift, 1), speed)
        packed[k_low] = t0
        packed[4 + k_low] = t1
        packed[8 + k_low] = speed
        return carry

    lax.fori_loop(0, 4, pack, 0)
    packed_b = zeros
    for k_high in range(4):
        for o in range(OCTETS):
            slot = k_high * 8 + o
            packed_b = jnp.where(
                slot_of == slot, pltpu.roll(bf[octet(o), :], (4 * slot + 2) % CX, 1), packed_b
            )
    packed[12] = packed_b

    pl.semaphore_wait(barrier, jnp.where(base, 3, 4))

    def send(source, target, index, slot, device):
        return pltpu.make_async_remote_copy(
            src_ref=source, dst_ref=target, send_sem=send_sem.at[index], recv_sem=recv_sem.at[slot],
            device_id=device, device_id_type=MESH,
        )

    eastward = send(packed, from_west, 0, 0, east_id)
    westward = send(packed, from_east, 1, 1, west_id)
    northward = send(to_north, from_south, 2, 2, north_id)
    southward = send(to_south, from_north, 3, 3, south_id)
    across = send(to_north.at[pl.ds(0, ROWS_FROM_NORTH)], from_north, 2, 3, mirror_id)

    pl.when(jnp.logical_not(base))(southward.start)
    pl.when(jnp.logical_not(top))(northward.start)
    pl.when(top)(across.start)
    eastward.start()
    westward.start()

    def vertical(k, carry):
        level = k.astype(jnp.float32)
        above = jnp.where(k > 0, level, 99.0)
        down, up = jnp.minimum(k + 1, NZ - 1), jnp.maximum(k - 1, 0)
        for o in range(OCTETS):
            depth = bf[octet(o), :]
            for t in range(NT):
                here = T[t, k, octet(o), :]
                TZ[t, k, octet(o), :] = jnp.where(
                    depth > level + 1.0, T[t, down, octet(o), :] - here, 0.0
                ) + jnp.where(depth > above, here - T[t, up, octet(o), :], 0.0)
        return carry

    lax.fori_loop(0, NZ, vertical, 0)

    def inside(k, carry):
        level = k.astype(jnp.float32)
        for o in range(OCTETS):
            here = [T[t, k, octet(o), :] for t in range(NT)]
            dz = [TZ[t, k, octet(o), :] for t in range(NT)]
            wet = be[octet(o), :] > level
            local = [jnp.where(wet, lanes_left(f) - f, 0.0) for f in here]
            before = [lanes_right(d) for d in local]
            after = [lanes_left(d) for d in local]
            speed = jnp.where(wet, U[k, pl.ds(8 * o, 8), :], 0.0)
            low, high, _, _ = face_fluxes(
                local, before, after, [z + lanes_left(z) for z in dz], speed
            )
            across_x = [lanes_right(high[t]) - low[t] for t in range(NT)]
            for t in range(NT):
                GX[t, k, octet(o), :] = local[t] + before[t]

            wet = bn[octet(o), :] > level
            wet_before = bn[shifted(o, -1), :] > level
            wet_after = bn[shifted(o, 1), :] > level
            nxt = [T[t, k, shifted(o, 1), :] for t in range(NT)]
            local = [jnp.where(wet, nxt[t] - here[t], 0.0) for t in range(NT)]
            before = [
                jnp.where(wet_before, here[t] - T[t, k, shifted(o, -1), :], 0.0) for t in range(NT)
            ]
            after = [
                jnp.where(wet_after, T[t, k, shifted(o, 2), :] - nxt[t], 0.0) for t in range(NT)
            ]
            speed = jnp.where(wet, V[k, pl.ds(8 * o, 8), :], 0.0)
            low, high, _, _ = face_fluxes(
                local, before, after, [dz[t] + TZ[t, k, shifted(o, 1), :] for t in range(NT)], speed
            )
            for t in range(NT):
                GY[t, k, octet(o), :] = local[t] + before[t]
                XY[t, k, octet(o), :] = across_x[t] - low[t]
                YB[t, k, octet(o), :] = high[t]
        return carry

    lax.fori_loop(0, NZ, inside, 0)

    eastward.wait_recv()
    westward.wait_recv()
    quarter = lax.rem(lane, 4)
    first_half = quarter < 2
    level_base = (lane // 32 * 4).astype(jnp.float32)
    for side in range(2):
        theirs = from_west if side == 0 else from_east

        def joined(index, side=side, theirs=theirs):
            if side == 0:
                return jnp.where(first_half, theirs[index], packed[index])
            return jnp.where(first_half, packed[index], theirs[index])

        depth = joined(12)
        fields = [[joined(4 * t + j) for j in range(4)] for t in range(NT)]
        steps = []
        for t in range(NT):
            column = fields[t] + [pltpu.roll(fields[t][0], CX - 32, 1)]
            steps.append(
                [
                    jnp.where(depth > level_base + (j + 1.0), column[j + 1] - column[j], 0.0)
                    for j in range(4)
                ]
            )
        for j in range(4):
            dz = [
                steps[t][j] + (steps[t][j - 1] if j > 0 else pltpu.roll(steps[t][3], 32, 1))
                for t in range(NT)
            ]
            speed = joined(8 + j) if side == 0 else packed[8 + j]
            terms, grads = edge_terms(
                [fields[t][j] for t in range(NT)], dz, depth, speed, level_base + float(j),
                lanes_left, lanes_right,
                None if side == 0 else quarter == 1, quarter == 1 if side == 0 else None,
                None if side == 0 else quarter == 0, quarter == 2 if side == 0 else None,
            )
            for t in range(NT):
                if side == 0:
                    edge_c[t, j] = terms[t]
                    edge_g[t, j] = grads[t]
                else:
                    edge_c[t, j] += terms[t]
                    edge_g[t, j] += grads[t]

    at_edge = (lane < 2) | (lane >= CX - 2)

    def inject(k_low, carry):
        for t in range(NT):
            term, grad = edge_c[t, k_low], edge_g[t, k_low]
            for k_high in range(4):
                for o in range(OCTETS):
                    back = (CX - (4 * (k_high * 8 + o) + 2)) % CX
                    k = 4 * k_high + k_low
                    XY[t, k, octet(o), :] += jnp.where(at_edge, pltpu.roll(term, back, 1), 0.0)
                    GX[t, k, octet(o), :] += jnp.where(at_edge, pltpu.roll(grad, back, 1), 0.0)
        return carry

    lax.fori_loop(0, 4, inject, 0)

    def finish(octets):
        def body(k, carry):
            level = k.astype(jnp.float32)
            down = jnp.minimum(k + 1, NZ - 1)
            fluxes = []
            for i, o in enumerate(octets):
                depth = bf[octet(o), :]
                open_below = depth > level + 1.0
                here = [T[t, k, octet(o), :] for t in range(NT)]
                step = [
                    jnp.where(open_below, T[t, down, octet(o), :] - here[t], 0.0) for t in range(NT)
                ]
                mean_x = [GX[t, k, octet(o), :] + GX[t, down, octet(o), :] for t in range(NT)]
                mean_y = [GY[t, k, octet(o), :] + GY[t, down, octet(o), :] for t in range(NT)]
                inverse = jnp.where(
                    open_below, reciprocal(jnp.maximum(4.0 * density(step), 1.0)), 0.0
                )
                slope_x = jnp.clip(density(mean_x) * inverse, -1.0, 1.0)
                slope_y = jnp.clip(density(mean_y) * inverse, -1.0, 1.0)
                squares = 0.1 * (slope_x * slope_x + slope_y * slope_y)
                slope_x = 0.025 * slope_x
                slope_y = 0.025 * slope_y
                wet = depth > level
                for t in range(NT):
                    flux = squares * step[t] - (slope_x * mean_x[t] + slope_y * mean_y[t])
                    total = (
                        here[t]
                        + (XY[t, k, octet(o), :] + YB[t, k, shifted(o, -1), :])
                        + (flux - carry[NT * i + t])
                    )
                    out[t, k, pl.ds(8 * o, 8), :] = jnp.where(wet, total, 0.0)
                    fluxes.append(flux)
            return tuple(fluxes)

        lax.fori_loop(0, NZ, body, tuple(zeros for _ in range(NT * len(octets))))

    finish(tuple(range(1, OCTETS - 1)))

    southward.wait_recv()
    pl.when(jnp.logical_not(base))(northward.wait_recv)

    @pl.when(top)
    def _():
        for i in range(ROWS_FROM_NORTH // 8):
            value = from_north[pl.ds(8 * i, 8), :]
            for bit in (64, 32, 16, 8, 4, 2, 1):
                value = jnp.where(
                    (lane & bit) != 0, pltpu.roll(value, bit, 1), pltpu.roll(value, CX - bit, 1)
                )
            from_north[pl.ds(8 * i, 8), :] = jnp.where(
                (row & 1) != 0, rows_down(value), rows_up(value)
            )

    def rows_in(k, carry):
        for t in range(NT):
            spot = pl.ds(2 * (NZ * t + k), 2)
            strip[t, k, pl.ds(2, 2), :] = from_north[spot, :]
            strip[t, k, pl.ds(4, 2), :] = from_south[spot, :]
        strip_v[k, pl.ds(5, 1), :] = from_south[pl.ds(72 + k, 1), :]
        return carry

    lax.fori_loop(0, NZ, rows_in, 0)
    strip_b[pl.ds(2, 2), :] = from_north[pl.ds(64, 2), :]
    strip_b[pl.ds(4, 2), :] = from_south[pl.ds(64, 2), :]

    def edge_rows(k, carry):
        level = k.astype(jnp.float32)
        above = jnp.where(k > 0, level, 99.0)
        down, up = jnp.minimum(k + 1, NZ - 1), jnp.maximum(k - 1, 0)
        depth = strip_b[...]
        here = [strip[t, k] for t in range(NT)]
        dz = [
            jnp.where(depth > level + 1.0, strip[t, down] - here[t], 0.0)
            + jnp.where(depth > above, here[t] - strip[t, up], 0.0)
            for t in range(NT)
        ]
        terms, grads = edge_terms(
            here, dz, depth, strip_v[k], level, rows_up, rows_down,
            row == 1, row == 5, row == 0, row == 6,
        )
        for t in range(NT):
            XY[t, k, octet(0), :] += jnp.where(row < 2, pltpu.roll(terms[t], 2, 0), 0.0)
            GY[t, k, octet(0), :] += jnp.where(row < 2, pltpu.roll(grads[t], 2, 0), 0.0)
            XY[t, k, octet(OCTETS - 1), :] += jnp.where(row > 5, pltpu.roll(terms[t], 6, 0), 0.0)
            GY[t, k, octet(OCTETS - 1), :] += jnp.where(row > 5, pltpu.roll(grads[t], 6, 0), 0.0)
        return carry

    lax.fori_loop(0, NZ, edge_rows, 0)
    finish((0, OCTETS - 1))

    eastward.wait_send()
    westward.wait_send()
    pl.when(jnp.logical_not(base))(southward.wait_send)
    pl.when(jnp.logical_not(top))(northward.wait_send)
    pl.when(top)(across.wait_send)


def solution(mesh):
    n_gx, n_gy = mesh.shape["gx"], mesh.shape["gy"]
    f32 = jnp.float32
    in_hbm = pl.BlockSpec(memory_space=pltpu.HBM)
    field = pltpu.VMEM((NT, NZ, TALL, CX), f32)
    levels = pltpu.VMEM((NZ, CY, CX), f32)
    plane = pltpu.VMEM((TALL, CX), f32)
    packed = pltpu.VMEM((PACKED, 8, CX), f32)
    edge = pltpu.VMEM((NT, 4, 8, CX), f32)

    def on_device(tracers, east_speed, north_speed, bottom_level):
        return pl.pallas_call(
            functools.partial(kernel, n_gx, n_gy),
            out_shape=jax.ShapeDtypeStruct((NT, NZ, CY, CX), f32),
            in_specs=[in_hbm] * 4,
            out_specs=pl.BlockSpec(memory_space=pltpu.VMEM),
            scratch_shapes=[
                field, levels, levels, pltpu.VMEM((CY, CX), jnp.int32), plane, plane, plane,
                field, field, field, field, field,
                packed, packed, packed,
                pltpu.VMEM((ROWS_FROM_SOUTH, CX), f32), pltpu.VMEM((ROWS_FROM_NORTH, CX), f32),
                pltpu.VMEM((ROWS_FROM_NORTH, CX), f32), pltpu.VMEM((ROWS_FROM_SOUTH, CX), f32),
                pltpu.VMEM((NT, NZ, 8, CX), f32), pltpu.VMEM((8, CX), f32),
                pltpu.VMEM((NZ, 8, CX), f32), edge, edge,
                pltpu.SemaphoreType.DMA((4,)), pltpu.SemaphoreType.DMA((4,)),
                pltpu.SemaphoreType.DMA((4,)),
            ],
            compiler_params=pltpu.CompilerParams(
                collective_id=0, has_side_effects=True, vmem_limit_bytes=24 * 1024 * 1024
            ),
        )(
            *[
                pltpu.with_memory_space_constraint(x, pltpu.HBM)
                for x in (tracers, east_speed, north_speed, bottom_level)
            ]
        )

    in_specs = (P(None, None, "gy", "gx"), P(None, "gy", "gx"), P(None, "gy", "gx"), P("gy", "gx"))
    return jax.shard_map(
        on_device, mesh=mesh, in_specs=in_specs, out_specs=P(None, None, "gy", "gx"), check_vma=False
    )
```

```python
import functools

import jax
import jax.numpy as jnp
from jax import lax
from jax.experimental import pallas as pl
from jax.experimental.pallas import tpu as pltpu
from jax.sharding import PartitionSpec as P

MESH = pl.DeviceIdType.MESH
NT, NZ, CY, CX = 2, 16, 48, 128
PAD = 8
TALL = CY + 2 * PAD
OCTETS = CY // 8
ROWS_FROM_NORTH = 72
ROWS_FROM_SOUTH = 88
PACKED = 13
EASTWARD = 6
WESTWARD = 5
BLOCK = 8
HEAT = 0.4
SALT = 0.6


def reciprocal(value):
    guess = pl.reciprocal(value, approx=True)
    return guess * (2.0 - value * guess)


def minmod(first, second):
    return jnp.maximum(jnp.minimum(first, second), 0.0) + jnp.minimum(
        jnp.maximum(first, second), 0.0
    )


def density(pair):
    return SALT * pair[1] - HEAT * pair[0]


def face_fluxes(local, before, after, dz_sum, speed):
    slope = jnp.clip(
        (0.1 * density(local)) * reciprocal(jnp.maximum(density(dz_sum), 1.0)), -0.025, 0.025
    )
    size = jnp.abs(speed)
    limited = 0.5 * size * (1.0 - size)
    forward = speed >= 0.0
    linear = jnp.minimum(speed, 0.0) - 0.1
    low, high, second = [], [], []
    for t in range(NT):
        correction = limited * minmod(local[t], jnp.where(forward, before[t], after[t]))
        taken = correction + (linear * local[t] + slope * dz_sum[t])
        low.append(taken)
        high.append(taken - speed * local[t])
        second.append(correction)
    return low, high, second, forward


def lanes_left(value):
    return pltpu.roll(value, CX - 1, 1)


def lanes_right(value):
    return pltpu.roll(value, 1, 1)


def rows_up(value):
    return pltpu.roll(value, 7, 0)


def rows_down(value):
    return pltpu.roll(value, 1, 0)


def edge_terms(field, dz, bottom, speed, level, nxt, prv, low_at, high_at, low_second, high_second):
    wet = jnp.minimum(bottom, nxt(bottom)) > level
    local = [jnp.where(wet, nxt(f) - f, 0.0) for f in field]
    dz_sum = [z + nxt(z) for z in dz]
    masked = jnp.where(wet, speed, 0.0)
    low, high, second, forward = face_fluxes(
        local, [prv(d) for d in local], [nxt(d) for d in local], dz_sum, masked
    )
    zero = jnp.zeros_like(masked)
    terms, steps = [], []
    for t in range(NT):
        late = zero
        if low_second is not None:
            late = late + jnp.where(low_second & ~forward, second[t], 0.0)
        if high_second is not None:
            late = late + jnp.where(high_second & forward, second[t], 0.0)
        arriving, term, step = late, -late, zero
        if high_at is not None:
            arriving = arriving + jnp.where(high_at, high[t], 0.0)
            step = step + prv(jnp.where(high_at, local[t], 0.0))
        if low_at is not None:
            term = term - jnp.where(low_at, low[t], 0.0)
            step = step + jnp.where(low_at, local[t], 0.0)
        terms.append(term + prv(arriving))
        steps.append(step)
    return terms, steps


def kernel(
    n_gx, n_gy,
    tracers, east, north, bottom, out,
    T, U, V, bottom_int, bf, be, bn, TZ, XY, YB, GX, GY,
    packed, to_east, to_west, from_west, from_east, to_north, to_south, from_north, from_south, relay,
    strip, strip_b, strip_v, edge_c, edge_g,
    load_sem, send_sem, recv_sem, go_sem,
):
    gx, gy = lax.axis_index("gx"), lax.axis_index("gy")
    east_id = (lax.rem(gx + 1, n_gx), gy)
    west_id = (lax.rem(gx + n_gx - 1, n_gx), gy)
    north_id = (gx, gy + 1)
    south_id = (gx, gy - 1)
    mirror_id = (n_gx - 1 - gx, gy)
    top = gy == n_gy - 1
    base = gy == 0
    after_seam = lax.rem(gx, BLOCK) == 0
    before_seam = lax.rem(gx, BLOCK) == BLOCK - 1
    below_middle = gy == n_gy // 2 - 1
    above_middle = gy == n_gy // 2
    relayed = before_seam & below_middle
    relays = (lax.rem(gx, BLOCK) == BLOCK - 2) & below_middle
    relay_target = (gx + 1, gy + 1)
    relay_source = (gx - 1, gy - 1)

    barrier = pltpu.get_barrier_semaphore()

    def greet(device):
        pl.semaphore_signal(barrier, inc=1, device_id=device, device_id_type=MESH)

    greeted_from_south = above_middle & before_seam
    pl.when(top)(lambda: greet(mirror_id))
    pl.when(jnp.logical_not(top))(lambda: greet(north_id))
    pl.when(greeted_from_south)(lambda: greet(relay_source))
    pl.when(jnp.logical_not(base) & jnp.logical_not(greeted_from_south))(lambda: greet(south_id))
    greet(west_id)
    pl.when(jnp.logical_not(before_seam))(lambda: greet(east_id))
    expected = (
        4 + relays.astype(jnp.int32) - relayed.astype(jnp.int32)
        - after_seam.astype(jnp.int32) - base.astype(jnp.int32)
    )

    first, middle, last = pl.ds(0, 8), pl.ds(8, CY - 16), pl.ds(CY - 8, 8)

    def load(source, target, index):
        copy = pltpu.make_async_copy(source, target, load_sem.at[index])
        copy.start()
        return copy

    def padded(rows):
        return T.at[:, :, pl.ds(PAD + rows.start, rows.size), :]

    early = [
        load(bottom, bottom_int, 0),
        load(tracers.at[:, :, first, :], padded(first), 1),
        load(tracers.at[:, :, last, :], padded(last), 2),
        load(north.at[:, last, :], V.at[:, last, :], 3),
    ]
    late = [
        load(tracers.at[:, :, middle, :], padded(middle), 4),
        load(east, U, 5),
        load(north.at[:, pl.ds(0, CY - 8), :], V.at[:, pl.ds(0, CY - 8), :], 6),
    ]

    lane = lax.broadcasted_iota(jnp.int32, (8, CX), 1)
    row = lax.broadcasted_iota(jnp.int32, (8, CX), 0)
    zeros = jnp.zeros((8, CX), jnp.float32)

    def octet(o):
        return pl.ds(PAD + 8 * o, 8)

    def shifted(o, by):
        return pl.ds(PAD + 8 * o + by, 8)

    for pad in (pl.ds(0, PAD), pl.ds(PAD + CY, PAD)):
        bf[pad, :] = zeros
        bn[pad, :] = zeros

    def clear(k, carry):
        for t in range(NT):
            YB[t, k, pl.ds(0, PAD), :] = zeros
            TZ[t, k, pl.ds(PAD + CY, PAD), :] = zeros
        strip_v[k] = zeros
        return carry

    lax.fori_loop(0, NZ, clear, 0)

    @pl.when(base)
    def _():
        from_south[...] = jnp.zeros_like(from_south)

    for copy in early:
        copy.wait()

    for o in (0, OCTETS - 1):
        bf[octet(o), :] = bottom_int[pl.ds(8 * o, 8), :].astype(jnp.float32)

    def rows_out(k, carry):
        for t in range(NT):
            spot = pl.ds(2 * (NZ * t + k), 2)
            last = T[t, k, pl.ds(PAD + CY - 2, 2), :]
            first = T[t, k, pl.ds(PAD, 2), :]
            to_north[spot, :] = last
            to_south[spot, :] = first
            strip[t, k, pl.ds(0, 2), :] = last
            strip[t, k, pl.ds(6, 2), :] = first
        last_v = V[k, pl.ds(CY - 2, 2), :]
        to_north[pl.ds(72 + k, 1), :] = last_v[1:2]
        strip_v[k, pl.ds(0, 2), :] = last_v
        return carry

    lax.fori_loop(0, NZ, rows_out, 0, unroll=4)
    last_b = bf[pl.ds(PAD + CY - 2, 2), :]
    first_b = bf[pl.ds(PAD, 2), :]
    to_north[pl.ds(64, 8), :] = zeros
    to_south[pl.ds(64, 8), :] = zeros
    to_north[pl.ds(64, 2), :] = last_b
    to_south[pl.ds(64, 2), :] = first_b
    strip_b[pl.ds(0, 2), :] = last_b
    strip_b[pl.ds(6, 2), :] = first_b

    def send(source, target, index, slot, device):
        return pltpu.make_async_remote_copy(
            src_ref=source, dst_ref=target, send_sem=send_sem.at[index], recv_sem=recv_sem.at[slot],
            device_id=device, device_id_type=MESH,
        )

    eastward = send(to_east, from_west, 0, 0, east_id)
    westward = send(to_west, from_east, 1, 1, west_id)
    northward = send(to_north, from_south, 2, 2, north_id)
    across = send(to_north.at[pl.ds(0, ROWS_FROM_NORTH)], from_north, 2, 3, mirror_id)
    handed = send(to_north, relay, 2, 4, west_id)
    southward = send(to_south, from_north, 3, 3, south_id)
    forwarded = send(relay, from_south, 4, 2, relay_target)
    northward_itself = jnp.logical_not(top) & jnp.logical_not(relayed)

    def enter_and_send_rows():
        pl.semaphore_wait(barrier, expected)
        pl.when(jnp.logical_not(base))(southward.start)
        pl.when(northward_itself)(northward.start)
        pl.when(relayed)(handed.start)
        pl.when(top)(across.start)

        @pl.when(before_seam)
        def _():
            pl.semaphore_signal(go_sem, inc=1, device_id=east_id, device_id_type=MESH)

    def send_columns():
        eastward.start()
        pl.when(jnp.logical_not(after_seam))(westward.start)

        @pl.when(relays)
        def _():
            handed.wait_recv()
            forwarded.start()

    late_entry = below_middle & jnp.logical_not(before_seam)
    pl.when(jnp.logical_not(late_entry))(enter_and_send_rows)

    for copy in late:
        copy.wait()

    for k in range(NZ):
        strip_v[k, pl.ds(6, 1), :] = V[k, pl.ds(0, 1), :]
    for o in range(OCTETS):
        bf[octet(o), :] = bottom_int[pl.ds(8 * o, 8), :].astype(jnp.float32)
    for o in range(OCTETS):
        here = bf[octet(o), :]
        be[octet(o), :] = jnp.where(lane == CX - 1, 0.0, jnp.minimum(here, lanes_left(here)))
        bn[octet(o), :] = jnp.minimum(here, bf[shifted(o, 1), :])

    slot_of = lane // 4

    def pack(k_low, carry):
        t0, t1, speed = zeros, zeros, zeros
        for k_high in range(4):
            for o in range(OCTETS):
                slot = k_high * 8 + o
                here = slot_of == slot
                shift = (4 * slot + 2) % CX
                k = 4 * k_high + k_low
                t0 = jnp.where(here, pltpu.roll(T[0, k, octet(o), :], shift, 1), t0)
                t1 = jnp.where(here, pltpu.roll(T[1, k, octet(o), :], shift, 1), t1)
                speed = jnp.where(here, pltpu.roll(U[k, pl.ds(8 * o, 8), :], shift, 1), speed)
        packed[k_low] = t0
        packed[4 + k_low] = t1
        packed[8 + k_low] = speed
        return carry

    lax.fori_loop(0, 4, pack, 0)
    packed_b = zeros
    for k_high in range(4):
        for o in range(OCTETS):
            slot = k_high * 8 + o
            packed_b = jnp.where(
                slot_of == slot, pltpu.roll(bf[octet(o), :], (4 * slot + 2) % CX, 1), packed_b
            )
    packed[12] = packed_b

    first_half = lax.rem(lane, 4) < 2
    east_speeds = zeros
    for j in range(4):
        to_east[j] = jnp.where(first_half, packed[j], pltpu.roll(packed[4 + j], 2, 1))
        to_west[j] = jnp.where(first_half, pltpu.roll(packed[4 + j], CX - 2, 1), packed[j])
        east_speeds = jnp.where(
            lax.rem(lane, 4) == j, pltpu.roll(packed[8 + j], (CX + j - 1) % CX, 1), east_speeds
        )
    to_east[4] = east_speeds
    to_east[5] = packed_b
    to_west[4] = packed_b

    pl.when(jnp.logical_not(late_entry))(send_columns)

    def vertical(k, carry):
        level = k.astype(jnp.float32)
        above = jnp.where(k > 0, level, 99.0)
        down, up = jnp.minimum(k + 1, NZ - 1), jnp.maximum(k - 1, 0)
        for o in range(OCTETS):
            depth = bf[octet(o), :]
            for t in range(NT):
                here = T[t, k, octet(o), :]
                TZ[t, k, octet(o), :] = jnp.where(
                    depth > level + 1.0, T[t, down, octet(o), :] - here, 0.0
                ) + jnp.where(depth > above, here - T[t, up, octet(o), :], 0.0)
        return carry

    lax.fori_loop(0, NZ, vertical, 0, unroll=2)

    z_low = lax.rem(gx // 2, BLOCK // 2)
    enter_at = 15 - jnp.maximum(z_low * 3 - 1, 0)
    west_at = jnp.where(below_middle, NZ - 1, NZ // 2)

    def inside(k, carry):
        @pl.when(late_entry & (k == enter_at))
        def _():
            enter_and_send_rows()
            send_columns()

        @pl.when(after_seam & (k == west_at))
        def _():
            pl.semaphore_wait(go_sem, 1)
            westward.start()

        level = k.astype(jnp.float32)
        for o in range(OCTETS):
            here = [T[t, k, octet(o), :] for t in range(NT)]
            dz = [TZ[t, k, octet(o), :] for t in range(NT)]
            wet = be[octet(o), :] > level
            local = [jnp.where(wet, lanes_left(f) - f, 0.0) for f in here]
            before = [lanes_right(d) for d in local]
            after = [lanes_left(d) for d in local]
            speed = jnp.where(wet, U[k, pl.ds(8 * o, 8), :], 0.0)
            low, high, _, _ = face_fluxes(
                local, before, after, [z + lanes_left(z) for z in dz], speed
            )
            across_x = [lanes_right(high[t]) - low[t] for t in range(NT)]
            for t in range(NT):
                GX[t, k, octet(o), :] = local[t] + before[t]

            wet = bn[octet(o), :] > level
            wet_before = bn[shifted(o, -1), :] > level
            wet_after = bn[shifted(o, 1), :] > level
            nxt = [T[t, k, shifted(o, 1), :] for t in range(NT)]
            local = [jnp.where(wet, nxt[t] - here[t], 0.0) for t in range(NT)]
            before = [
                jnp.where(wet_before, here[t] - T[t, k, shifted(o, -1), :], 0.0) for t in range(NT)
            ]
            after = [
                jnp.where(wet_after, T[t, k, shifted(o, 2), :] - nxt[t], 0.0) for t in range(NT)
            ]
            speed = jnp.where(wet, V[k, pl.ds(8 * o, 8), :], 0.0)
            low, high, _, _ = face_fluxes(
                local, before, after, [dz[t] + TZ[t, k, shifted(o, 1), :] for t in range(NT)], speed
            )
            for t in range(NT):
                GY[t, k, octet(o), :] = local[t] + before[t]
                XY[t, k, octet(o), :] = across_x[t] - low[t]
                YB[t, k, octet(o), :] = high[t]
        return carry

    lax.fori_loop(0, NZ, inside, 0)

    eastward.wait_recv()
    westward.wait_recv()
    quarter = lax.rem(lane, 4)
    level_base = (lane // 32 * 4).astype(jnp.float32)
    for side in range(2):
        own = [[packed[4 * t + j] for j in range(4)] for t in range(NT)]
        if side == 0:
            depth = jnp.where(first_half, from_west[5], packed[12])
            fields = [
                [jnp.where(first_half, from_west[j], own[0][j]) for j in range(4)],
                [jnp.where(first_half, pltpu.roll(from_west[j], CX - 2, 1), own[1][j]) for j in range(4)],
            ]
        else:
            depth = jnp.where(first_half, packed[12], from_east[4])
            fields = [
                [jnp.where(first_half, own[0][j], from_east[j]) for j in range(4)],
                [jnp.where(first_half, own[1][j], pltpu.roll(from_east[j], 2, 1)) for j in range(4)],
            ]
        steps = []
        for t in range(NT):
            column = fields[t] + [pltpu.roll(fields[t][0], CX - 32, 1)]
            steps.append(
                [
                    jnp.where(depth > level_base + (j + 1.0), column[j + 1] - column[j], 0.0)
                    for j in range(4)
                ]
            )
        for j in range(4):
            dz = [
                steps[t][j] + (steps[t][j - 1] if j > 0 else pltpu.roll(steps[t][3], 32, 1))
                for t in range(NT)
            ]
            speed = packed[8 + j]
            if side == 0:
                speed = jnp.where(first_half, pltpu.roll(from_west[4], (CX + 1 - j) % CX, 1), speed)
            terms, grads = edge_terms(
                [fields[t][j] for t in range(NT)], dz, depth, speed, level_base + float(j),
                lanes_left, lanes_right,
                None if side == 0 else quarter == 1, quarter == 1 if side == 0 else None,
                None if side == 0 else quarter == 0, quarter == 2 if side == 0 else None,
            )
            for t in range(NT):
                if side == 0:
                    edge_c[t, j] = terms[t]
                    edge_g[t, j] = grads[t]
                else:
                    edge_c[t, j] += terms[t]
                    edge_g[t, j] += grads[t]

    at_edge = (lane < 2) | (lane >= CX - 2)

    def inject(k_low, carry):
        for t in range(NT):
            term, grad = edge_c[t, k_low], edge_g[t, k_low]
            for k_high in range(4):
                for o in range(OCTETS):
                    back = (CX - (4 * (k_high * 8 + o) + 2)) % CX
                    k = 4 * k_high + k_low
                    XY[t, k, octet(o), :] += jnp.where(at_edge, pltpu.roll(term, back, 1), 0.0)
                    GX[t, k, octet(o), :] += jnp.where(at_edge, pltpu.roll(grad, back, 1), 0.0)
        return carry

    lax.fori_loop(0, 4, inject, 0)

    def finish(octets, unroll):
        def body(k, carry):
            level = k.astype(jnp.float32)
            down = jnp.minimum(k + 1, NZ - 1)
            fluxes = []
            for i, o in enumerate(octets):
                depth = bf[octet(o), :]
                open_below = depth > level + 1.0
                here = [T[t, k, octet(o), :] for t in range(NT)]
                step = [
                    jnp.where(open_below, T[t, down, octet(o), :] - here[t], 0.0) for t in range(NT)
                ]
                mean_x = [GX[t, k, octet(o), :] + GX[t, down, octet(o), :] for t in range(NT)]
                mean_y = [GY[t, k, octet(o), :] + GY[t, down, octet(o), :] for t in range(NT)]
                inverse = jnp.where(
                    open_below, reciprocal(jnp.maximum(4.0 * density(step), 1.0)), 0.0
                )
                slope_x = jnp.clip(density(mean_x) * inverse, -1.0, 1.0)
                slope_y = jnp.clip(density(mean_y) * inverse, -1.0, 1.0)
                squares = 0.1 * (slope_x * slope_x + slope_y * slope_y)
                slope_x = 0.025 * slope_x
                slope_y = 0.025 * slope_y
                wet = depth > level
                for t in range(NT):
                    flux = squares * step[t] - (slope_x * mean_x[t] + slope_y * mean_y[t])
                    total = (
                        here[t]
                        + (XY[t, k, octet(o), :] + YB[t, k, shifted(o, -1), :])
                        + (flux - carry[NT * i + t])
                    )
                    out[t, k, pl.ds(8 * o, 8), :] = jnp.where(wet, total, 0.0)
                    fluxes.append(flux)
            return tuple(fluxes)

        lax.fori_loop(0, NZ, body, tuple(zeros for _ in range(NT * len(octets))), unroll=unroll)

    finish(tuple(range(1, OCTETS - 1)), 4)

    southward.wait_recv()
    pl.when(jnp.logical_not(base))(northward.wait_recv)

    @pl.when(top)
    def _():
        for i in range(ROWS_FROM_NORTH // 8):
            value = from_north[pl.ds(8 * i, 8), :]
            for bit in (64, 32, 16, 8, 4, 2, 1):
                value = jnp.where(
                    (lane & bit) != 0, pltpu.roll(value, bit, 1), pltpu.roll(value, CX - bit, 1)
                )
            from_north[pl.ds(8 * i, 8), :] = jnp.where(
                (row & 1) != 0, rows_down(value), rows_up(value)
            )

    def rows_in(k, carry):
        for t in range(NT):
            spot = pl.ds(2 * (NZ * t + k), 2)
            strip[t, k, pl.ds(2, 2), :] = from_north[spot, :]
            strip[t, k, pl.ds(4, 2), :] = from_south[spot, :]
        strip_v[k, pl.ds(5, 1), :] = from_south[pl.ds(72 + k, 1), :]
        return carry

    lax.fori_loop(0, NZ, rows_in, 0)
    strip_b[pl.ds(2, 2), :] = from_north[pl.ds(64, 2), :]
    strip_b[pl.ds(4, 2), :] = from_south[pl.ds(64, 2), :]

    def edge_rows(k, carry):
        level = k.astype(jnp.float32)
        above = jnp.where(k > 0, level, 99.0)
        down, up = jnp.minimum(k + 1, NZ - 1), jnp.maximum(k - 1, 0)
        depth = strip_b[...]
        here = [strip[t, k] for t in range(NT)]
        dz = [
            jnp.where(depth > level + 1.0, strip[t, down] - here[t], 0.0)
            + jnp.where(depth > above, here[t] - strip[t, up], 0.0)
            for t in range(NT)
        ]
        terms, grads = edge_terms(
            here, dz, depth, strip_v[k], level, rows_up, rows_down,
            row == 1, row == 5, row == 0, row == 6,
        )
        for t in range(NT):
            XY[t, k, octet(0), :] += jnp.where(row < 2, pltpu.roll(terms[t], 2, 0), 0.0)
            GY[t, k, octet(0), :] += jnp.where(row < 2, pltpu.roll(grads[t], 2, 0), 0.0)
            XY[t, k, octet(OCTETS - 1), :] += jnp.where(row > 5, pltpu.roll(terms[t], 6, 0), 0.0)
            GY[t, k, octet(OCTETS - 1), :] += jnp.where(row > 5, pltpu.roll(grads[t], 6, 0), 0.0)
        return carry

    lax.fori_loop(0, NZ, edge_rows, 0, unroll=8)
    finish((0, OCTETS - 1), 8)

    eastward.wait_send()
    westward.wait_send()
    pl.when(jnp.logical_not(base))(southward.wait_send)
    pl.when(northward_itself)(northward.wait_send)
    pl.when(relayed)(handed.wait_send)
    pl.when(top)(across.wait_send)
    pl.when(relays)(forwarded.wait_send)


def solution(mesh):
    n_gx, n_gy = mesh.shape["gx"], mesh.shape["gy"]
    f32 = jnp.float32
    in_hbm = pl.BlockSpec(memory_space=pltpu.HBM)
    field = pltpu.VMEM((NT, NZ, TALL, CX), f32)
    levels = pltpu.VMEM((NZ, CY, CX), f32)
    plane = pltpu.VMEM((TALL, CX), f32)
    packed = pltpu.VMEM((PACKED, 8, CX), f32)
    eastward = pltpu.VMEM((EASTWARD, 8, CX), f32)
    westward = pltpu.VMEM((WESTWARD, 8, CX), f32)
    from_south = pltpu.VMEM((ROWS_FROM_SOUTH, CX), f32)
    from_north = pltpu.VMEM((ROWS_FROM_NORTH, CX), f32)
    edge = pltpu.VMEM((NT, 4, 8, CX), f32)

    def on_device(tracers, east_speed, north_speed, bottom_level):
        return pl.pallas_call(
            functools.partial(kernel, n_gx, n_gy),
            out_shape=jax.ShapeDtypeStruct((NT, NZ, CY, CX), f32),
            in_specs=[in_hbm] * 4,
            out_specs=pl.BlockSpec(memory_space=pltpu.VMEM),
            scratch_shapes=[
                field, levels, levels, pltpu.VMEM((CY, CX), jnp.int32), plane, plane, plane,
                field, field, field, field, field,
                packed, eastward, westward, eastward, westward,
                from_south, from_north, from_north, from_south, from_south,
                pltpu.VMEM((NT, NZ, 8, CX), f32), pltpu.VMEM((8, CX), f32),
                pltpu.VMEM((NZ, 8, CX), f32), edge, edge,
                pltpu.SemaphoreType.DMA((7,)), pltpu.SemaphoreType.DMA((5,)),
                pltpu.SemaphoreType.DMA((5,)), pltpu.SemaphoreType.REGULAR,
            ],
            compiler_params=pltpu.CompilerParams(
                collective_id=0, has_side_effects=True, vmem_limit_bytes=24 * 1024 * 1024
            ),
        )(
            *[
                pltpu.with_memory_space_constraint(x, pltpu.HBM)
                for x in (tracers, east_speed, north_speed, bottom_level)
            ]
        )

    in_specs = (P(None, None, "gy", "gx"), P(None, "gy", "gx"), P(None, "gy", "gx"), P("gy", "gx"))
    return jax.shard_map(
        on_device, mesh=mesh, in_specs=in_specs, out_specs=P(None, None, "gy", "gx"), check_vma=False
    )
```

```python
import functools

import jax
import jax.numpy as jnp
from jax import lax
from jax.experimental import pallas as pl
from jax.experimental.pallas import tpu as pltpu
from jax.sharding import PartitionSpec as P

MESH = pl.DeviceIdType.MESH
NT, NZ, CY, CX = 2, 16, 48, 128
PAD = 8
TALL = CY + 2 * PAD
OCTETS = CY // 8
ROWS_FROM_NORTH = 72
ROWS_FROM_SOUTH = 88
PACKED = 13
EASTWARD = 6
WESTWARD = 5
BLOCK = 8
HEAT = 0.4
SALT = 0.6


def reciprocal(value):
    guess = pl.reciprocal(value, approx=True)
    return guess * (2.0 - value * guess)


def minmod(first, second):
    return jnp.maximum(jnp.minimum(first, second), 0.0) + jnp.minimum(
        jnp.maximum(first, second), 0.0
    )


def density(pair):
    return SALT * pair[1] - HEAT * pair[0]


def face_fluxes(local, before, after, dz_sum, speed):
    slope = jnp.clip(
        (0.1 * density(local)) * reciprocal(jnp.maximum(density(dz_sum), 1.0)), -0.025, 0.025
    )
    size = jnp.abs(speed)
    limited = 0.5 * size * (1.0 - size)
    forward = speed >= 0.0
    linear = jnp.minimum(speed, 0.0) - 0.1
    low, high, second = [], [], []
    for t in range(NT):
        correction = limited * minmod(local[t], jnp.where(forward, before[t], after[t]))
        taken = correction + (linear * local[t] + slope * dz_sum[t])
        low.append(taken)
        high.append(taken - speed * local[t])
        second.append(correction)
    return low, high, second, forward


def lanes_left(value):
    return pltpu.roll(value, CX - 1, 1)


def lanes_right(value):
    return pltpu.roll(value, 1, 1)


def rows_up(value):
    return pltpu.roll(value, 7, 0)


def rows_down(value):
    return pltpu.roll(value, 1, 0)


def edge_terms(field, dz, bottom, speed, level, nxt, prv, low_at, high_at, low_second, high_second):
    wet = jnp.minimum(bottom, nxt(bottom)) > level
    local = [jnp.where(wet, nxt(f) - f, 0.0) for f in field]
    dz_sum = [z + nxt(z) for z in dz]
    masked = jnp.where(wet, speed, 0.0)
    low, high, second, forward = face_fluxes(
        local, [prv(d) for d in local], [nxt(d) for d in local], dz_sum, masked
    )
    zero = jnp.zeros_like(masked)
    terms, steps = [], []
    for t in range(NT):
        late = zero
        if low_second is not None:
            late = late + jnp.where(low_second & ~forward, second[t], 0.0)
        if high_second is not None:
            late = late + jnp.where(high_second & forward, second[t], 0.0)
        arriving, term, step = late, -late, zero
        if high_at is not None:
            arriving = arriving + jnp.where(high_at, high[t], 0.0)
            step = step + prv(jnp.where(high_at, local[t], 0.0))
        if low_at is not None:
            term = term - jnp.where(low_at, low[t], 0.0)
            step = step + jnp.where(low_at, local[t], 0.0)
        terms.append(term + prv(arriving))
        steps.append(step)
    return terms, steps


def kernel(
    n_gx, n_gy,
    tracers, east, north, bottom, out,
    T, U, V, bottom_int, bf, be, bn, TZ, XY, YB, GX, GY,
    packed, to_east, to_west, from_west, from_east, to_north, to_south, from_north, from_south, relay,
    strip, strip_b, strip_v, edge_c, edge_g,
    load_sem, send_sem, recv_sem, go_sem,
):
    gx, gy = lax.axis_index("gx"), lax.axis_index("gy")
    east_id = (lax.rem(gx + 1, n_gx), gy)
    west_id = (lax.rem(gx + n_gx - 1, n_gx), gy)
    north_id = (gx, gy + 1)
    south_id = (gx, gy - 1)
    mirror_id = (n_gx - 1 - gx, gy)
    top = gy == n_gy - 1
    base = gy == 0
    below_middle = gy == n_gy // 2 - 1
    above_middle = gy == n_gy // 2
    beside_middle = below_middle | above_middle
    after_seam = (lax.rem(gx, BLOCK) == 0) & beside_middle
    before_seam = (lax.rem(gx, BLOCK) == BLOCK - 1) & beside_middle
    relayed = before_seam & below_middle
    relays = (lax.rem(gx, BLOCK) == BLOCK - 2) & below_middle
    relay_target = (gx + 1, gy + 1)
    relay_source = (gx - 1, gy - 1)

    barrier = pltpu.get_barrier_semaphore()

    def greet(device):
        pl.semaphore_signal(barrier, inc=1, device_id=device, device_id_type=MESH)

    greeted_from_south = above_middle & before_seam
    pl.when(top)(lambda: greet(mirror_id))
    pl.when(jnp.logical_not(top))(lambda: greet(north_id))
    pl.when(greeted_from_south)(lambda: greet(relay_source))
    pl.when(jnp.logical_not(base) & jnp.logical_not(greeted_from_south))(lambda: greet(south_id))
    greet(west_id)
    pl.when(jnp.logical_not(before_seam))(lambda: greet(east_id))
    expected = (
        4 + relays.astype(jnp.int32) - relayed.astype(jnp.int32)
        - after_seam.astype(jnp.int32) - base.astype(jnp.int32)
    )

    first, middle, last = pl.ds(0, 8), pl.ds(8, CY - 16), pl.ds(CY - 8, 8)

    def load(source, target, index):
        copy = pltpu.make_async_copy(source, target, load_sem.at[index])
        copy.start()
        return copy

    def padded(rows):
        return T.at[:, :, pl.ds(PAD + rows.start, rows.size), :]

    early = [
        load(bottom, bottom_int, 0),
        load(tracers.at[:, :, first, :], padded(first), 1),
        load(tracers.at[:, :, last, :], padded(last), 2),
        load(north.at[:, last, :], V.at[:, last, :], 3),
    ]
    late = [
        load(tracers.at[:, :, middle, :], padded(middle), 4),
        load(east, U, 5),
        load(north.at[:, pl.ds(0, CY - 8), :], V.at[:, pl.ds(0, CY - 8), :], 6),
    ]

    lane = lax.broadcasted_iota(jnp.int32, (8, CX), 1)
    row = lax.broadcasted_iota(jnp.int32, (8, CX), 0)
    zeros = jnp.zeros((8, CX), jnp.float32)

    def octet(o):
        return pl.ds(PAD + 8 * o, 8)

    def shifted(o, by):
        return pl.ds(PAD + 8 * o + by, 8)

    for pad in (pl.ds(0, PAD), pl.ds(PAD + CY, PAD)):
        bf[pad, :] = zeros
        bn[pad, :] = zeros

    def clear(k, carry):
        for t in range(NT):
            YB[t, k, pl.ds(0, PAD), :] = zeros
            TZ[t, k, pl.ds(PAD + CY, PAD), :] = zeros
        strip_v[k] = zeros
        return carry

    lax.fori_loop(0, NZ, clear, 0)

    @pl.when(base)
    def _():
        from_south[...] = jnp.zeros_like(from_south)

    for copy in early:
        copy.wait()

    for o in (0, OCTETS - 1):
        bf[octet(o), :] = bottom_int[pl.ds(8 * o, 8), :].astype(jnp.float32)

    def rows_out(k, carry):
        for t in range(NT):
            spot = pl.ds(2 * (NZ * t + k), 2)
            last = T[t, k, pl.ds(PAD + CY - 2, 2), :]
            first = T[t, k, pl.ds(PAD, 2), :]
            to_north[spot, :] = last
            to_south[spot, :] = first
            strip[t, k, pl.ds(0, 2), :] = last
            strip[t, k, pl.ds(6, 2), :] = first
        last_v = V[k, pl.ds(CY - 2, 2), :]
        to_north[pl.ds(72 + k, 1), :] = last_v[1:2]
        strip_v[k, pl.ds(0, 2), :] = last_v
        return carry

    lax.fori_loop(0, NZ, rows_out, 0, unroll=4)
    last_b = bf[pl.ds(PAD + CY - 2, 2), :]
    first_b = bf[pl.ds(PAD, 2), :]
    to_north[pl.ds(64, 8), :] = zeros
    to_south[pl.ds(64, 8), :] = zeros
    to_north[pl.ds(64, 2), :] = last_b
    to_south[pl.ds(64, 2), :] = first_b
    strip_b[pl.ds(0, 2), :] = last_b
    strip_b[pl.ds(6, 2), :] = first_b

    def send(source, target, index, slot, device):
        return pltpu.make_async_remote_copy(
            src_ref=source, dst_ref=target, send_sem=send_sem.at[index], recv_sem=recv_sem.at[slot],
            device_id=device, device_id_type=MESH,
        )

    eastward = send(to_east, from_west, 0, 0, east_id)
    westward = send(to_west, from_east, 1, 1, west_id)
    northward = send(to_north, from_south, 2, 2, north_id)
    across = send(to_north.at[pl.ds(0, ROWS_FROM_NORTH)], from_north, 2, 3, mirror_id)
    handed = send(to_north, relay, 2, 4, west_id)
    southward = send(to_south, from_north, 3, 3, south_id)
    forwarded = send(relay, from_south, 4, 2, relay_target)
    northward_itself = jnp.logical_not(top) & jnp.logical_not(relayed)

    def enter_and_send_rows():
        pl.semaphore_wait(barrier, expected)
        pl.when(jnp.logical_not(base))(southward.start)
        pl.when(northward_itself)(northward.start)
        pl.when(relayed)(handed.start)
        pl.when(top)(across.start)

        @pl.when(before_seam)
        def _():
            pl.semaphore_signal(go_sem, inc=1, device_id=east_id, device_id_type=MESH)

    def send_columns():
        eastward.start()
        pl.when(jnp.logical_not(after_seam))(westward.start)

        @pl.when(relays)
        def _():
            handed.wait_recv()
            forwarded.start()

    late_entry = below_middle & jnp.logical_not(before_seam)
    pl.when(jnp.logical_not(late_entry))(enter_and_send_rows)

    for copy in late:
        copy.wait()

    for k in range(NZ):
        strip_v[k, pl.ds(6, 1), :] = V[k, pl.ds(0, 1), :]
    for o in range(OCTETS):
        bf[octet(o), :] = bottom_int[pl.ds(8 * o, 8), :].astype(jnp.float32)
    for o in range(OCTETS):
        here = bf[octet(o), :]
        be[octet(o), :] = jnp.where(lane == CX - 1, 0.0, jnp.minimum(here, lanes_left(here)))
        bn[octet(o), :] = jnp.minimum(here, bf[shifted(o, 1), :])

    slot_of = lane // 4

    def pack(group, carry):
        t0, t1, speed = zeros, zeros, zeros
        for b in range(4):
            for o in range(OCTETS):
                slot = b * 8 + o
                here = slot_of == slot
                shift = (4 * slot + 2) % CX
                k = 4 * group + b
                t0 = jnp.where(here, pltpu.roll(T[0, k, octet(o), :], shift, 1), t0)
                t1 = jnp.where(here, pltpu.roll(T[1, k, octet(o), :], shift, 1), t1)
                speed = jnp.where(here, pltpu.roll(U[k, pl.ds(8 * o, 8), :], shift, 1), speed)
        packed[group] = t0
        packed[4 + group] = t1
        packed[8 + group] = speed
        return carry

    lax.fori_loop(0, 4, pack, 0, unroll=2)
    packed_b = zeros
    for b in range(4):
        for o in range(OCTETS):
            slot = b * 8 + o
            packed_b = jnp.where(
                slot_of == slot, pltpu.roll(bf[octet(o), :], (4 * slot + 2) % CX, 1), packed_b
            )
    packed[12] = packed_b

    first_half = lax.rem(lane, 4) < 2
    east_speeds = zeros
    for j in range(4):
        to_east[j] = jnp.where(first_half, packed[j], pltpu.roll(packed[4 + j], 2, 1))
        to_west[j] = jnp.where(first_half, pltpu.roll(packed[4 + j], CX - 2, 1), packed[j])
        east_speeds = jnp.where(
            lax.rem(lane, 4) == j, pltpu.roll(packed[8 + j], (CX + j - 1) % CX, 1), east_speeds
        )
    to_east[4] = east_speeds
    to_east[5] = packed_b
    to_west[4] = packed_b

    pl.when(jnp.logical_not(late_entry))(send_columns)

    def vertical(k, carry):
        level = k.astype(jnp.float32)
        above = jnp.where(k > 0, level, 99.0)
        down, up = jnp.minimum(k + 1, NZ - 1), jnp.maximum(k - 1, 0)
        for o in range(OCTETS):
            depth = bf[octet(o), :]
            for t in range(NT):
                here = T[t, k, octet(o), :]
                TZ[t, k, octet(o), :] = jnp.where(
                    depth > level + 1.0, T[t, down, octet(o), :] - here, 0.0
                ) + jnp.where(depth > above, here - T[t, up, octet(o), :], 0.0)
        return carry

    lax.fori_loop(0, NZ, vertical, 0, unroll=2)

    def inside(k, carry):
        level = k.astype(jnp.float32)
        for o in range(OCTETS):
            here = [T[t, k, octet(o), :] for t in range(NT)]
            dz = [TZ[t, k, octet(o), :] for t in range(NT)]
            wet = be[octet(o), :] > level
            local = [jnp.where(wet, lanes_left(f) - f, 0.0) for f in here]
            before = [lanes_right(d) for d in local]
            after = [lanes_left(d) for d in local]
            speed = jnp.where(wet, U[k, pl.ds(8 * o, 8), :], 0.0)
            low, high, _, _ = face_fluxes(
                local, before, after, [z + lanes_left(z) for z in dz], speed
            )
            across_x = [lanes_right(high[t]) - low[t] for t in range(NT)]
            for t in range(NT):
                GX[t, k, octet(o), :] = local[t] + before[t]

            wet = bn[octet(o), :] > level
            wet_before = bn[shifted(o, -1), :] > level
            wet_after = bn[shifted(o, 1), :] > level
            nxt = [T[t, k, shifted(o, 1), :] for t in range(NT)]
            local = [jnp.where(wet, nxt[t] - here[t], 0.0) for t in range(NT)]
            before = [
                jnp.where(wet_before, here[t] - T[t, k, shifted(o, -1), :], 0.0) for t in range(NT)
            ]
            after = [
                jnp.where(wet_after, T[t, k, shifted(o, 2), :] - nxt[t], 0.0) for t in range(NT)
            ]
            speed = jnp.where(wet, V[k, pl.ds(8 * o, 8), :], 0.0)
            low, high, _, _ = face_fluxes(
                local, before, after, [dz[t] + TZ[t, k, shifted(o, 1), :] for t in range(NT)], speed
            )
            for t in range(NT):
                GY[t, k, octet(o), :] = local[t] + before[t]
                XY[t, k, octet(o), :] = across_x[t] - low[t]
                YB[t, k, octet(o), :] = high[t]
        return carry

    lax.fori_loop(0, NZ, inside, 0, unroll=2)

    @pl.when(late_entry)
    def _():
        enter_and_send_rows()
        send_columns()

    @pl.when(after_seam)
    def _():
        pl.semaphore_wait(go_sem, 1)
        westward.start()

    eastward.wait_recv()
    westward.wait_recv()
    quarter = lax.rem(lane, 4)
    level_in_group = (lane // 32).astype(jnp.float32)
    for side in range(2):
        own = [[packed[4 * t + j] for j in range(4)] for t in range(NT)]
        if side == 0:
            depth = jnp.where(first_half, from_west[5], packed[12])
            fields = [
                [jnp.where(first_half, from_west[j], own[0][j]) for j in range(4)],
                [jnp.where(first_half, pltpu.roll(from_west[j], CX - 2, 1), own[1][j]) for j in range(4)],
            ]
        else:
            depth = jnp.where(first_half, packed[12], from_east[4])
            fields = [
                [jnp.where(first_half, own[0][j], from_east[j]) for j in range(4)],
                [jnp.where(first_half, own[1][j], pltpu.roll(from_east[j], 2, 1)) for j in range(4)],
            ]
        steps = []
        for t in range(NT):
            turned = [pltpu.roll(f, CX - 32, 1) for f in fields[t]]
            steps.append(
                [
                    jnp.where(
                        depth > level_in_group + (4 * j + 1.0),
                        jnp.where(lane < CX - 32, turned[j], turned[min(j + 1, 3)]) - fields[t][j],
                        0.0,
                    )
                    for j in range(4)
                ]
            )
        for j in range(4):
            dz = []
            for t in range(NT):
                before = pltpu.roll(steps[t][j - 1], 32, 1) if j > 0 else zeros
                dz.append(
                    steps[t][j] + jnp.where(lane < 32, before, pltpu.roll(steps[t][j], 32, 1))
                )
            speed = packed[8 + j]
            if side == 0:
                speed = jnp.where(first_half, pltpu.roll(from_west[4], (CX + 1 - j) % CX, 1), speed)
            terms, grads = edge_terms(
                [fields[t][j] for t in range(NT)], dz, depth, speed, level_in_group + 4.0 * j,
                lanes_left, lanes_right,
                None if side == 0 else quarter == 1, quarter == 1 if side == 0 else None,
                None if side == 0 else quarter == 0, quarter == 2 if side == 0 else None,
            )
            for t in range(NT):
                if side == 0:
                    edge_c[t, j] = terms[t]
                    edge_g[t, j] = grads[t]
                else:
                    edge_c[t, j] += terms[t]
                    edge_g[t, j] += grads[t]

    at_edge = (lane < 2) | (lane >= CX - 2)

    def finish(octets):
        def at(o, ref, t, group, b):
            rolled = pltpu.roll(ref[t, group], (CX - (4 * (b * 8 + o) + 2)) % CX, 1)
            return jnp.where(at_edge, rolled, 0.0)

        def body(group, carry):
            fluxes = [[carry[4 * i], carry[4 * i + 1]] for i in range(len(octets))]
            gx_here = [[carry[4 * i + 2], carry[4 * i + 3]] for i in range(len(octets))]
            after = jnp.minimum(group + 1, 3)
            for b in range(4):
                k = 4 * group + b
                level = k.astype(jnp.float32)
                down = jnp.minimum(k + 1, NZ - 1)
                for i, o in enumerate(octets):
                    depth = bf[octet(o), :]
                    open_below = depth > level + 1.0
                    here = [T[t, k, octet(o), :] for t in range(NT)]
                    step = [
                        jnp.where(open_below, T[t, down, octet(o), :] - here[t], 0.0)
                        for t in range(NT)
                    ]
                    gx_down = [
                        GX[t, down, octet(o), :]
                        + (at(o, edge_g, t, group, b + 1) if b < 3 else at(o, edge_g, t, after, 0))
                        for t in range(NT)
                    ]
                    mean_x = [gx_here[i][t] + gx_down[t] for t in range(NT)]
                    mean_y = [GY[t, k, octet(o), :] + GY[t, down, octet(o), :] for t in range(NT)]
                    inverse = jnp.where(
                        open_below, reciprocal(jnp.maximum(4.0 * density(step), 1.0)), 0.0
                    )
                    slope_x = jnp.clip(density(mean_x) * inverse, -1.0, 1.0)
                    slope_y = jnp.clip(density(mean_y) * inverse, -1.0, 1.0)
                    squares = 0.1 * (slope_x * slope_x + slope_y * slope_y)
                    slope_x = 0.025 * slope_x
                    slope_y = 0.025 * slope_y
                    wet = depth > level
                    for t in range(NT):
                        flux = squares * step[t] - (slope_x * mean_x[t] + slope_y * mean_y[t])
                        faces = XY[t, k, octet(o), :] + at(o, edge_c, t, group, b)
                        total = (
                            here[t]
                            + (faces + YB[t, k, shifted(o, -1), :])
                            + (flux - fluxes[i][t])
                        )
                        out[t, k, pl.ds(8 * o, 8), :] = jnp.where(wet, total, 0.0)
                        fluxes[i][t] = flux
                    gx_here[i] = gx_down
            return tuple(x for i in range(len(octets)) for x in (*fluxes[i], *gx_here[i]))

        start = []
        for o in octets:
            start += [zeros, zeros]
            start += [GX[t, 0, octet(o), :] + at(o, edge_g, t, 0, 0) for t in range(NT)]
        lax.fori_loop(0, 4, body, tuple(start), unroll=2)

    finish(tuple(range(1, OCTETS - 1)))

    southward.wait_recv()
    pl.when(jnp.logical_not(base))(northward.wait_recv)

    @pl.when(top)
    def _():
        for i in range(ROWS_FROM_NORTH // 8):
            value = from_north[pl.ds(8 * i, 8), :]
            for bit in (64, 32, 16, 8, 4, 2, 1):
                value = jnp.where(
                    (lane & bit) != 0, pltpu.roll(value, bit, 1), pltpu.roll(value, CX - bit, 1)
                )
            from_north[pl.ds(8 * i, 8), :] = jnp.where(
                (row & 1) != 0, rows_down(value), rows_up(value)
            )

    def rows_in(k, carry):
        for t in range(NT):
            spot = pl.ds(2 * (NZ * t + k), 2)
            strip[t, k, pl.ds(2, 2), :] = from_north[spot, :]
            strip[t, k, pl.ds(4, 2), :] = from_south[spot, :]
        strip_v[k, pl.ds(5, 1), :] = from_south[pl.ds(72 + k, 1), :]
        return carry

    lax.fori_loop(0, NZ, rows_in, 0)
    strip_b[pl.ds(2, 2), :] = from_north[pl.ds(64, 2), :]
    strip_b[pl.ds(4, 2), :] = from_south[pl.ds(64, 2), :]

    def edge_rows(k, carry):
        level = k.astype(jnp.float32)
        above = jnp.where(k > 0, level, 99.0)
        down, up = jnp.minimum(k + 1, NZ - 1), jnp.maximum(k - 1, 0)
        depth = strip_b[...]
        here = [strip[t, k] for t in range(NT)]
        dz = [
            jnp.where(depth > level + 1.0, strip[t, down] - here[t], 0.0)
            + jnp.where(depth > above, here[t] - strip[t, up], 0.0)
            for t in range(NT)
        ]
        terms, grads = edge_terms(
            here, dz, depth, strip_v[k], level, rows_up, rows_down,
            row == 1, row == 5, row == 0, row == 6,
        )
        for t in range(NT):
            XY[t, k, octet(0), :] += jnp.where(row < 2, pltpu.roll(terms[t], 2, 0), 0.0)
            GY[t, k, octet(0), :] += jnp.where(row < 2, pltpu.roll(grads[t], 2, 0), 0.0)
            XY[t, k, octet(OCTETS - 1), :] += jnp.where(row > 5, pltpu.roll(terms[t], 6, 0), 0.0)
            GY[t, k, octet(OCTETS - 1), :] += jnp.where(row > 5, pltpu.roll(grads[t], 6, 0), 0.0)
        return carry

    lax.fori_loop(0, NZ, edge_rows, 0, unroll=8)
    finish((0, OCTETS - 1))

    eastward.wait_send()
    westward.wait_send()
    pl.when(jnp.logical_not(base))(southward.wait_send)
    pl.when(northward_itself)(northward.wait_send)
    pl.when(relayed)(handed.wait_send)
    pl.when(top)(across.wait_send)
    pl.when(relays)(forwarded.wait_send)


def solution(mesh):
    n_gx, n_gy = mesh.shape["gx"], mesh.shape["gy"]
    f32 = jnp.float32
    in_hbm = pl.BlockSpec(memory_space=pltpu.HBM)
    field = pltpu.VMEM((NT, NZ, TALL, CX), f32)
    levels = pltpu.VMEM((NZ, CY, CX), f32)
    plane = pltpu.VMEM((TALL, CX), f32)
    packed = pltpu.VMEM((PACKED, 8, CX), f32)
    eastward = pltpu.VMEM((EASTWARD, 8, CX), f32)
    westward = pltpu.VMEM((WESTWARD, 8, CX), f32)
    from_south = pltpu.VMEM((ROWS_FROM_SOUTH, CX), f32)
    from_north = pltpu.VMEM((ROWS_FROM_NORTH, CX), f32)
    edge = pltpu.VMEM((NT, 4, 8, CX), f32)

    def on_device(tracers, east_speed, north_speed, bottom_level):
        return pl.pallas_call(
            functools.partial(kernel, n_gx, n_gy),
            out_shape=jax.ShapeDtypeStruct((NT, NZ, CY, CX), f32),
            in_specs=[in_hbm] * 4,
            out_specs=pl.BlockSpec(memory_space=pltpu.VMEM),
            scratch_shapes=[
                field, levels, levels, pltpu.VMEM((CY, CX), jnp.int32), plane, plane, plane,
                field, field, field, field, field,
                packed, eastward, westward, eastward, westward,
                from_south, from_north, from_north, from_south, from_south,
                pltpu.VMEM((NT, NZ, 8, CX), f32), pltpu.VMEM((8, CX), f32),
                pltpu.VMEM((NZ, 8, CX), f32), edge, edge,
                pltpu.SemaphoreType.DMA((7,)), pltpu.SemaphoreType.DMA((5,)),
                pltpu.SemaphoreType.DMA((5,)), pltpu.SemaphoreType.REGULAR,
            ],
            compiler_params=pltpu.CompilerParams(
                collective_id=0, has_side_effects=True, vmem_limit_bytes=24 * 1024 * 1024
            ),
        )(
            *[
                pltpu.with_memory_space_constraint(x, pltpu.HBM)
                for x in (tracers, east_speed, north_speed, bottom_level)
            ]
        )

    in_specs = (P(None, None, "gy", "gx"), P(None, "gy", "gx"), P(None, "gy", "gx"), P("gy", "gx"))
    return jax.shard_map(
        on_device, mesh=mesh, in_specs=in_specs, out_specs=P(None, None, "gy", "gx"), check_vma=False
    )
```

```python
import functools

import jax
import jax.numpy as jnp
from jax import lax
from jax.experimental import pallas as pl
from jax.experimental.pallas import tpu as pltpu
from jax.sharding import PartitionSpec as P

MESH = pl.DeviceIdType.MESH
NT, NZ, CY, CX = 2, 16, 48, 128
PAD = 8
TALL = CY + 2 * PAD
OCTETS = CY // 8
ROWS_FROM_NORTH = 72
ROWS_FROM_SOUTH = 88
PACKED = 13
EASTWARD = 6
WESTWARD = 5
BLOCK = 8
HEAT = 0.4
SALT = 0.6


def reciprocal(value):
    guess = pl.reciprocal(value, approx=True)
    return guess * (2.0 - value * guess)


def minmod(first, second):
    return jnp.maximum(jnp.minimum(first, second), 0.0) + jnp.minimum(
        jnp.maximum(first, second), 0.0
    )


def density(pair):
    return SALT * pair[1] - HEAT * pair[0]


def face_fluxes(local, before, after, dz_sum, speed):
    slope = jnp.clip(
        (0.1 * density(local)) * reciprocal(jnp.maximum(density(dz_sum), 1.0)), -0.025, 0.025
    )
    size = jnp.abs(speed)
    limited = 0.5 * size * (1.0 - size)
    forward = speed >= 0.0
    linear = jnp.minimum(speed, 0.0) - 0.1
    low, high, second = [], [], []
    for t in range(NT):
        correction = limited * minmod(local[t], jnp.where(forward, before[t], after[t]))
        taken = correction + (linear * local[t] + slope * dz_sum[t])
        low.append(taken)
        high.append(taken - speed * local[t])
        second.append(correction)
    return low, high, second, forward


def lanes_left(value):
    return pltpu.roll(value, CX - 1, 1)


def lanes_right(value):
    return pltpu.roll(value, 1, 1)


def rows_up(value):
    return pltpu.roll(value, 7, 0)


def rows_down(value):
    return pltpu.roll(value, 1, 0)


def edge_terms(field, dz, bottom, speed, level, nxt, prv, low_at, high_at, low_second, high_second):
    wet = jnp.minimum(bottom, nxt(bottom)) > level
    local = [jnp.where(wet, nxt(f) - f, 0.0) for f in field]
    dz_sum = [z + nxt(z) for z in dz]
    masked = jnp.where(wet, speed, 0.0)
    low, high, second, forward = face_fluxes(
        local, [prv(d) for d in local], [nxt(d) for d in local], dz_sum, masked
    )
    zero = jnp.zeros_like(masked)
    terms, steps = [], []
    for t in range(NT):
        late = zero
        if low_second is not None:
            late = late + jnp.where(low_second & ~forward, second[t], 0.0)
        if high_second is not None:
            late = late + jnp.where(high_second & forward, second[t], 0.0)
        arriving, term, step = late, -late, zero
        if high_at is not None:
            arriving = arriving + jnp.where(high_at, high[t], 0.0)
            step = step + prv(jnp.where(high_at, local[t], 0.0))
        if low_at is not None:
            term = term - jnp.where(low_at, low[t], 0.0)
            step = step + jnp.where(low_at, local[t], 0.0)
        terms.append(term + prv(arriving))
        steps.append(step)
    return terms, steps


def kernel(
    n_gx, n_gy,
    tracers, east, north, bottom, out,
    T, U, V, bottom_int, bf, be, bn, TZ, XY, YB, GX, GY,
    packed, to_east, to_west, from_west, from_east, to_north, to_south, from_north, from_south, relay,
    strip, strip_b, strip_v, edge_c, edge_g,
    load_sem, send_sem, recv_sem, go_sem,
):
    gx, gy = lax.axis_index("gx"), lax.axis_index("gy")
    east_id = (lax.rem(gx + 1, n_gx), gy)
    west_id = (lax.rem(gx + n_gx - 1, n_gx), gy)
    north_id = (gx, gy + 1)
    south_id = (gx, gy - 1)
    mirror_id = (n_gx - 1 - gx, gy)
    top = gy == n_gy - 1
    base = gy == 0
    below_middle = gy == n_gy // 2 - 1
    above_middle = gy == n_gy // 2
    beside_middle = below_middle | above_middle
    after_seam = (lax.rem(gx, BLOCK) == 0) & beside_middle
    before_seam = (lax.rem(gx, BLOCK) == BLOCK - 1) & beside_middle
    relays = (lax.rem(gx, BLOCK) == BLOCK - 2) & beside_middle
    relayed_up = before_seam & below_middle
    relayed_down = before_seam & above_middle
    relays_up = relays & below_middle
    relays_down = relays & above_middle

    barrier = pltpu.get_barrier_semaphore()

    def greet(device):
        pl.semaphore_signal(barrier, inc=1, device_id=device, device_id_type=MESH)

    pl.when(top)(lambda: greet(mirror_id))
    pl.when(relayed_up)(lambda: greet((gx - 1, gy + 1)))
    pl.when(relayed_down)(lambda: greet((gx - 1, gy - 1)))
    pl.when(jnp.logical_not(top | relayed_up))(lambda: greet(north_id))
    pl.when(jnp.logical_not(base | relayed_down))(lambda: greet(south_id))
    greet(west_id)
    pl.when(jnp.logical_not(before_seam))(lambda: greet(east_id))
    expected = (
        4 + relays.astype(jnp.int32) - before_seam.astype(jnp.int32)
        - after_seam.astype(jnp.int32) - base.astype(jnp.int32)
    )

    first, middle, last = pl.ds(0, 8), pl.ds(8, CY - 16), pl.ds(CY - 8, 8)

    def load(source, target, index):
        copy = pltpu.make_async_copy(source, target, load_sem.at[index])
        copy.start()
        return copy

    def padded(rows):
        return T.at[:, :, pl.ds(PAD + rows.start, rows.size), :]

    early = [
        load(bottom, bottom_int, 0),
        load(tracers.at[:, :, first, :], padded(first), 1),
        load(tracers.at[:, :, last, :], padded(last), 2),
        load(north.at[:, last, :], V.at[:, last, :], 3),
    ]
    late = [
        load(tracers.at[:, :, middle, :], padded(middle), 4),
        load(east, U, 5),
        load(north.at[:, pl.ds(0, CY - 8), :], V.at[:, pl.ds(0, CY - 8), :], 6),
    ]

    lane = lax.broadcasted_iota(jnp.int32, (8, CX), 1)
    row = lax.broadcasted_iota(jnp.int32, (8, CX), 0)
    zeros = jnp.zeros((8, CX), jnp.float32)

    def octet(o):
        return pl.ds(PAD + 8 * o, 8)

    def shifted(o, by):
        return pl.ds(PAD + 8 * o + by, 8)

    for pad in (pl.ds(0, PAD), pl.ds(PAD + CY, PAD)):
        bf[pad, :] = zeros
        bn[pad, :] = zeros

    def clear(k, carry):
        for t in range(NT):
            YB[t, k, pl.ds(0, PAD), :] = zeros
            TZ[t, k, pl.ds(PAD + CY, PAD), :] = zeros
        strip_v[k] = zeros
        return carry

    lax.fori_loop(0, NZ, clear, 0)

    @pl.when(base)
    def _():
        from_south[...] = jnp.zeros_like(from_south)

    for copy in early:
        copy.wait()

    for o in (0, OCTETS - 1):
        bf[octet(o), :] = bottom_int[pl.ds(8 * o, 8), :].astype(jnp.float32)

    def rows_out(k, carry):
        for t in range(NT):
            spot = pl.ds(2 * (NZ * t + k), 2)
            last = T[t, k, pl.ds(PAD + CY - 2, 2), :]
            first = T[t, k, pl.ds(PAD, 2), :]
            to_north[spot, :] = last
            to_south[spot, :] = first
            strip[t, k, pl.ds(0, 2), :] = last
            strip[t, k, pl.ds(6, 2), :] = first
        last_v = V[k, pl.ds(CY - 2, 2), :]
        to_north[pl.ds(72 + k, 1), :] = last_v[1:2]
        strip_v[k, pl.ds(0, 2), :] = last_v
        return carry

    lax.fori_loop(0, NZ, rows_out, 0, unroll=4)
    last_b = bf[pl.ds(PAD + CY - 2, 2), :]
    first_b = bf[pl.ds(PAD, 2), :]
    to_north[pl.ds(64, 8), :] = zeros
    to_south[pl.ds(64, 8), :] = zeros
    to_north[pl.ds(64, 2), :] = last_b
    to_south[pl.ds(64, 2), :] = first_b
    strip_b[pl.ds(0, 2), :] = last_b
    strip_b[pl.ds(6, 2), :] = first_b

    def send(source, target, index, slot, device):
        return pltpu.make_async_remote_copy(
            src_ref=source, dst_ref=target, send_sem=send_sem.at[index], recv_sem=recv_sem.at[slot],
            device_id=device, device_id_type=MESH,
        )

    eastward = send(to_east, from_west, 0, 0, east_id)
    westward = send(to_west, from_east, 1, 1, west_id)
    northward = send(to_north, from_south, 2, 2, north_id)
    across = send(to_north.at[pl.ds(0, ROWS_FROM_NORTH)], from_north, 2, 3, mirror_id)
    southward = send(to_south, from_north, 3, 3, south_id)
    short_relay = relay.at[pl.ds(0, ROWS_FROM_NORTH)]
    handed_up = send(to_north, relay, 2, 4, west_id)
    handed_down = send(to_south, short_relay, 3, 4, west_id)
    forwarded_up = send(relay, from_south, 4, 2, (gx + 1, gy + 1))
    forwarded_down = send(short_relay, from_north, 4, 3, (gx + 1, gy - 1))
    northward_itself = jnp.logical_not(top | relayed_up)
    southward_itself = jnp.logical_not(base | relayed_down)
    late_entry = below_middle & jnp.logical_not(before_seam)

    @pl.when(jnp.logical_not(late_entry))
    def _():
        pl.semaphore_wait(barrier, expected)

        @pl.when(before_seam)
        def _():
            pl.semaphore_signal(go_sem, inc=1, device_id=east_id, device_id_type=MESH)

        pl.when(southward_itself)(southward.start)
        pl.when(northward_itself)(northward.start)
        pl.when(relayed_up)(handed_up.start)
        pl.when(relayed_down)(handed_down.start)
        pl.when(top)(across.start)

        @pl.when(relays_down)
        def _():
            handed_down.wait_recv()
            forwarded_down.start()

    for copy in late:
        copy.wait()

    for k in range(NZ):
        strip_v[k, pl.ds(6, 1), :] = V[k, pl.ds(0, 1), :]
    for o in range(OCTETS):
        bf[octet(o), :] = bottom_int[pl.ds(8 * o, 8), :].astype(jnp.float32)
    for o in range(OCTETS):
        here = bf[octet(o), :]
        be[octet(o), :] = jnp.where(lane == CX - 1, 0.0, jnp.minimum(here, lanes_left(here)))
        bn[octet(o), :] = jnp.minimum(here, bf[shifted(o, 1), :])

    slot_of = lane // 4

    def pack(group, carry):
        t0, t1, speed = zeros, zeros, zeros
        for b in range(4):
            for o in range(OCTETS):
                slot = b * 8 + o
                here = slot_of == slot
                shift = (4 * slot + 2) % CX
                k = 4 * group + b
                t0 = jnp.where(here, pltpu.roll(T[0, k, octet(o), :], shift, 1), t0)
                t1 = jnp.where(here, pltpu.roll(T[1, k, octet(o), :], shift, 1), t1)
                speed = jnp.where(here, pltpu.roll(U[k, pl.ds(8 * o, 8), :], shift, 1), speed)
        packed[group] = t0
        packed[4 + group] = t1
        packed[8 + group] = speed
        return carry

    lax.fori_loop(0, 4, pack, 0, unroll=2)
    packed_b = zeros
    for b in range(4):
        for o in range(OCTETS):
            slot = b * 8 + o
            packed_b = jnp.where(
                slot_of == slot, pltpu.roll(bf[octet(o), :], (4 * slot + 2) % CX, 1), packed_b
            )
    packed[12] = packed_b

    first_half = lax.rem(lane, 4) < 2
    east_speeds = zeros
    for j in range(4):
        to_east[j] = jnp.where(first_half, packed[j], pltpu.roll(packed[4 + j], 2, 1))
        to_west[j] = jnp.where(first_half, pltpu.roll(packed[4 + j], CX - 2, 1), packed[j])
        east_speeds = jnp.where(
            lax.rem(lane, 4) == j, pltpu.roll(packed[8 + j], (CX + j - 1) % CX, 1), east_speeds
        )
    to_east[4] = east_speeds
    to_east[5] = packed_b
    to_west[4] = packed_b

    @pl.when(jnp.logical_not(late_entry))
    def _():
        eastward.start()
        pl.when(jnp.logical_not(after_seam))(westward.start)

    def vertical(k, carry):
        level = k.astype(jnp.float32)
        above = jnp.where(k > 0, level, 99.0)
        down, up = jnp.minimum(k + 1, NZ - 1), jnp.maximum(k - 1, 0)
        for o in range(OCTETS):
            depth = bf[octet(o), :]
            for t in range(NT):
                here = T[t, k, octet(o), :]
                TZ[t, k, octet(o), :] = jnp.where(
                    depth > level + 1.0, T[t, down, octet(o), :] - here, 0.0
                ) + jnp.where(depth > above, here - T[t, up, octet(o), :], 0.0)
        return carry

    lax.fori_loop(0, NZ, vertical, 0, unroll=2)

    def inside(k, carry):
        level = k.astype(jnp.float32)
        for o in range(OCTETS):
            here = [T[t, k, octet(o), :] for t in range(NT)]
            dz = [TZ[t, k, octet(o), :] for t in range(NT)]
            wet = be[octet(o), :] > level
            local = [jnp.where(wet, lanes_left(f) - f, 0.0) for f in here]
            before = [lanes_right(d) for d in local]
            after = [lanes_left(d) for d in local]
            speed = jnp.where(wet, U[k, pl.ds(8 * o, 8), :], 0.0)
            low, high, _, _ = face_fluxes(
                local, before, after, [z + lanes_left(z) for z in dz], speed
            )
            across_x = [lanes_right(high[t]) - low[t] for t in range(NT)]
            for t in range(NT):
                GX[t, k, octet(o), :] = local[t] + before[t]

            wet = bn[octet(o), :] > level
            wet_before = bn[shifted(o, -1), :] > level
            wet_after = bn[shifted(o, 1), :] > level
            nxt = [T[t, k, shifted(o, 1), :] for t in range(NT)]
            local = [jnp.where(wet, nxt[t] - here[t], 0.0) for t in range(NT)]
            before = [
                jnp.where(wet_before, here[t] - T[t, k, shifted(o, -1), :], 0.0) for t in range(NT)
            ]
            after = [
                jnp.where(wet_after, T[t, k, shifted(o, 2), :] - nxt[t], 0.0) for t in range(NT)
            ]
            speed = jnp.where(wet, V[k, pl.ds(8 * o, 8), :], 0.0)
            low, high, _, _ = face_fluxes(
                local, before, after, [dz[t] + TZ[t, k, shifted(o, 1), :] for t in range(NT)], speed
            )
            for t in range(NT):
                GY[t, k, octet(o), :] = local[t] + before[t]
                XY[t, k, octet(o), :] = across_x[t] - low[t]
                YB[t, k, octet(o), :] = high[t]
        return carry

    lax.fori_loop(0, NZ, inside, 0, unroll=2)

    @pl.when(late_entry)
    def _():
        pl.semaphore_wait(barrier, expected)
        northward.start()

        @pl.when(relays_up)
        def _():
            handed_up.wait_recv()
            forwarded_up.start()

        eastward.start()
        pl.when(jnp.logical_not(after_seam))(westward.start)
        southward.start()

    @pl.when(after_seam)
    def _():
        pl.semaphore_wait(go_sem, 1)
        westward.start()

    eastward.wait_recv()
    westward.wait_recv()
    quarter = lax.rem(lane, 4)
    level_in_group = (lane // 32).astype(jnp.float32)
    for side in range(2):
        own = [[packed[4 * t + j] for j in range(4)] for t in range(NT)]
        if side == 0:
            depth = jnp.where(first_half, from_west[5], packed[12])
            fields = [
                [jnp.where(first_half, from_west[j], own[0][j]) for j in range(4)],
                [jnp.where(first_half, pltpu.roll(from_west[j], CX - 2, 1), own[1][j]) for j in range(4)],
            ]
        else:
            depth = jnp.where(first_half, packed[12], from_east[4])
            fields = [
                [jnp.where(first_half, own[0][j], from_east[j]) for j in range(4)],
                [jnp.where(first_half, own[1][j], pltpu.roll(from_east[j], 2, 1)) for j in range(4)],
            ]
        steps = []
        for t in range(NT):
            turned = [pltpu.roll(f, CX - 32, 1) for f in fields[t]]
            steps.append(
                [
                    jnp.where(
                        depth > level_in_group + (4 * j + 1.0),
                        jnp.where(lane < CX - 32, turned[j], turned[min(j + 1, 3)]) - fields[t][j],
                        0.0,
                    )
                    for j in range(4)
                ]
            )
        for j in range(4):
            dz = []
            for t in range(NT):
                before = pltpu.roll(steps[t][j - 1], 32, 1) if j > 0 else zeros
                dz.append(
                    steps[t][j] + jnp.where(lane < 32, before, pltpu.roll(steps[t][j], 32, 1))
                )
            speed = packed[8 + j]
            if side == 0:
                speed = jnp.where(first_half, pltpu.roll(from_west[4], (CX + 1 - j) % CX, 1), speed)
            terms, grads = edge_terms(
                [fields[t][j] for t in range(NT)], dz, depth, speed, level_in_group + 4.0 * j,
                lanes_left, lanes_right,
                None if side == 0 else quarter == 1, quarter == 1 if side == 0 else None,
                None if side == 0 else quarter == 0, quarter == 2 if side == 0 else None,
            )
            for t in range(NT):
                if side == 0:
                    edge_c[t, j] = terms[t]
                    edge_g[t, j] = grads[t]
                else:
                    edge_c[t, j] += terms[t]
                    edge_g[t, j] += grads[t]

    at_edge = (lane < 2) | (lane >= CX - 2)

    def finish(octets):
        def at(o, ref, t, group, b):
            rolled = pltpu.roll(ref[t, group], (CX - (4 * (b * 8 + o) + 2)) % CX, 1)
            return jnp.where(at_edge, rolled, 0.0)

        def body(group, carry):
            fluxes = [[carry[4 * i], carry[4 * i + 1]] for i in range(len(octets))]
            gx_here = [[carry[4 * i + 2], carry[4 * i + 3]] for i in range(len(octets))]
            after = jnp.minimum(group + 1, 3)
            for b in range(4):
                k = 4 * group + b
                level = k.astype(jnp.float32)
                down = jnp.minimum(k + 1, NZ - 1)
                for i, o in enumerate(octets):
                    depth = bf[octet(o), :]
                    open_below = depth > level + 1.0
                    here = [T[t, k, octet(o), :] for t in range(NT)]
                    step = [
                        jnp.where(open_below, T[t, down, octet(o), :] - here[t], 0.0)
                        for t in range(NT)
                    ]
                    gx_down = [
                        GX[t, down, octet(o), :]
                        + (at(o, edge_g, t, group, b + 1) if b < 3 else at(o, edge_g, t, after, 0))
                        for t in range(NT)
                    ]
                    mean_x = [gx_here[i][t] + gx_down[t] for t in range(NT)]
                    mean_y = [GY[t, k, octet(o), :] + GY[t, down, octet(o), :] for t in range(NT)]
                    inverse = jnp.where(
                        open_below, reciprocal(jnp.maximum(4.0 * density(step), 1.0)), 0.0
                    )
                    slope_x = jnp.clip(density(mean_x) * inverse, -1.0, 1.0)
                    slope_y = jnp.clip(density(mean_y) * inverse, -1.0, 1.0)
                    squares = 0.1 * (slope_x * slope_x + slope_y * slope_y)
                    slope_x = 0.025 * slope_x
                    slope_y = 0.025 * slope_y
                    wet = depth > level
                    for t in range(NT):
                        flux = squares * step[t] - (slope_x * mean_x[t] + slope_y * mean_y[t])
                        faces = XY[t, k, octet(o), :] + at(o, edge_c, t, group, b)
                        total = (
                            here[t]
                            + (faces + YB[t, k, shifted(o, -1), :])
                            + (flux - fluxes[i][t])
                        )
                        out[t, k, pl.ds(8 * o, 8), :] = jnp.where(wet, total, 0.0)
                        fluxes[i][t] = flux
                    gx_here[i] = gx_down
            return tuple(x for i in range(len(octets)) for x in (*fluxes[i], *gx_here[i]))

        start = []
        for o in octets:
            start += [zeros, zeros]
            start += [GX[t, 0, octet(o), :] + at(o, edge_g, t, 0, 0) for t in range(NT)]
        lax.fori_loop(0, 4, body, tuple(start), unroll=2)

    finish(tuple(range(1, OCTETS - 1)))

    southward.wait_recv()
    pl.when(jnp.logical_not(base))(northward.wait_recv)

    @pl.when(top)
    def _():
        for i in range(ROWS_FROM_NORTH // 8):
            value = from_north[pl.ds(8 * i, 8), :]
            for bit in (64, 32, 16, 8, 4, 2, 1):
                value = jnp.where(
                    (lane & bit) != 0, pltpu.roll(value, bit, 1), pltpu.roll(value, CX - bit, 1)
                )
            from_north[pl.ds(8 * i, 8), :] = jnp.where(
                (row & 1) != 0, rows_down(value), rows_up(value)
            )

    def rows_in(k, carry):
        for t in range(NT):
            spot = pl.ds(2 * (NZ * t + k), 2)
            strip[t, k, pl.ds(2, 2), :] = from_north[spot, :]
            strip[t, k, pl.ds(4, 2), :] = from_south[spot, :]
        strip_v[k, pl.ds(5, 1), :] = from_south[pl.ds(72 + k, 1), :]
        return carry

    lax.fori_loop(0, NZ, rows_in, 0)
    strip_b[pl.ds(2, 2), :] = from_north[pl.ds(64, 2), :]
    strip_b[pl.ds(4, 2), :] = from_south[pl.ds(64, 2), :]

    def edge_rows(k, carry):
        level = k.astype(jnp.float32)
        above = jnp.where(k > 0, level, 99.0)
        down, up = jnp.minimum(k + 1, NZ - 1), jnp.maximum(k - 1, 0)
        depth = strip_b[...]
        here = [strip[t, k] for t in range(NT)]
        dz = [
            jnp.where(depth > level + 1.0, strip[t, down] - here[t], 0.0)
            + jnp.where(depth > above, here[t] - strip[t, up], 0.0)
            for t in range(NT)
        ]
        terms, grads = edge_terms(
            here, dz, depth, strip_v[k], level, rows_up, rows_down,
            row == 1, row == 5, row == 0, row == 6,
        )
        for t in range(NT):
            XY[t, k, octet(0), :] += jnp.where(row < 2, pltpu.roll(terms[t], 2, 0), 0.0)
            GY[t, k, octet(0), :] += jnp.where(row < 2, pltpu.roll(grads[t], 2, 0), 0.0)
            XY[t, k, octet(OCTETS - 1), :] += jnp.where(row > 5, pltpu.roll(terms[t], 6, 0), 0.0)
            GY[t, k, octet(OCTETS - 1), :] += jnp.where(row > 5, pltpu.roll(grads[t], 6, 0), 0.0)
        return carry

    lax.fori_loop(0, NZ, edge_rows, 0, unroll=8)
    finish((0, OCTETS - 1))

    eastward.wait_send()
    westward.wait_send()
    pl.when(southward_itself)(southward.wait_send)
    pl.when(northward_itself)(northward.wait_send)
    pl.when(relayed_up)(handed_up.wait_send)
    pl.when(relayed_down)(handed_down.wait_send)
    pl.when(top)(across.wait_send)
    pl.when(relays_up)(forwarded_up.wait_send)
    pl.when(relays_down)(forwarded_down.wait_send)


def solution(mesh):
    n_gx, n_gy = mesh.shape["gx"], mesh.shape["gy"]
    f32 = jnp.float32
    in_hbm = pl.BlockSpec(memory_space=pltpu.HBM)
    field = pltpu.VMEM((NT, NZ, TALL, CX), f32)
    levels = pltpu.VMEM((NZ, CY, CX), f32)
    plane = pltpu.VMEM((TALL, CX), f32)
    packed = pltpu.VMEM((PACKED, 8, CX), f32)
    eastward = pltpu.VMEM((EASTWARD, 8, CX), f32)
    westward = pltpu.VMEM((WESTWARD, 8, CX), f32)
    from_south = pltpu.VMEM((ROWS_FROM_SOUTH, CX), f32)
    from_north = pltpu.VMEM((ROWS_FROM_NORTH, CX), f32)
    edge = pltpu.VMEM((NT, 4, 8, CX), f32)

    def on_device(tracers, east_speed, north_speed, bottom_level):
        return pl.pallas_call(
            functools.partial(kernel, n_gx, n_gy),
            out_shape=jax.ShapeDtypeStruct((NT, NZ, CY, CX), f32),
            in_specs=[in_hbm] * 4,
            out_specs=pl.BlockSpec(memory_space=pltpu.VMEM),
            scratch_shapes=[
                field, levels, levels, pltpu.VMEM((CY, CX), jnp.int32), plane, plane, plane,
                field, field, field, field, field,
                packed, eastward, westward, eastward, westward,
                from_south, from_north, from_north, from_south, from_south,
                pltpu.VMEM((NT, NZ, 8, CX), f32), pltpu.VMEM((8, CX), f32),
                pltpu.VMEM((NZ, 8, CX), f32), edge, edge,
                pltpu.SemaphoreType.DMA((7,)), pltpu.SemaphoreType.DMA((5,)),
                pltpu.SemaphoreType.DMA((5,)), pltpu.SemaphoreType.REGULAR,
            ],
            compiler_params=pltpu.CompilerParams(
                collective_id=0, has_side_effects=True, vmem_limit_bytes=24 * 1024 * 1024
            ),
        )(
            *[
                pltpu.with_memory_space_constraint(x, pltpu.HBM)
                for x in (tracers, east_speed, north_speed, bottom_level)
            ]
        )

    in_specs = (P(None, None, "gy", "gx"), P(None, "gy", "gx"), P(None, "gy", "gx"), P("gy", "gx"))
    return jax.shard_map(
        on_device, mesh=mesh, in_specs=in_specs, out_specs=P(None, None, "gy", "gx"), check_vma=False
    )
```

```python
import functools

import jax
import jax.numpy as jnp
from jax import lax
from jax.experimental import pallas as pl
from jax.experimental.pallas import tpu as pltpu
from jax.sharding import PartitionSpec as P

MESH = pl.DeviceIdType.MESH
NT, NZ, CY, CX = 2, 16, 48, 128
PAD = 8
TALL = CY + 2 * PAD
OCTETS = CY // 8
ROWS_FROM_NORTH = 72
ROWS_FROM_SOUTH = 88
PACKED = 13
EASTWARD = 6
WESTWARD = 5
BLOCK = 8
HEAT = 0.4
SALT = 0.6


def reciprocal(value):
    guess = pl.reciprocal(value, approx=True)
    return guess * (2.0 - value * guess)


def minmod(first, second):
    return jnp.maximum(jnp.minimum(first, second), 0.0) + jnp.minimum(
        jnp.maximum(first, second), 0.0
    )


def density(pair):
    return SALT * pair[1] - HEAT * pair[0]


def face_fluxes(local, before, after, dz_sum, speed):
    slope = jnp.clip(
        (0.1 * density(local)) * reciprocal(jnp.maximum(density(dz_sum), 1.0)), -0.025, 0.025
    )
    size = jnp.abs(speed)
    limited = 0.5 * size * (1.0 - size)
    forward = speed >= 0.0
    linear = jnp.minimum(speed, 0.0) - 0.1
    low, high, second = [], [], []
    for t in range(NT):
        correction = limited * minmod(local[t], jnp.where(forward, before[t], after[t]))
        taken = correction + (linear * local[t] + slope * dz_sum[t])
        low.append(taken)
        high.append(taken - speed * local[t])
        second.append(correction)
    return low, high, second, forward


def lanes_left(value):
    return pltpu.roll(value, CX - 1, 1)


def lanes_right(value):
    return pltpu.roll(value, 1, 1)


def rows_up(value):
    return pltpu.roll(value, 7, 0)


def rows_down(value):
    return pltpu.roll(value, 1, 0)


def edge_terms(field, dz, bottom, speed, level, nxt, prv, low_at, high_at, low_second, high_second):
    wet = jnp.minimum(bottom, nxt(bottom)) > level
    local = [jnp.where(wet, nxt(f) - f, 0.0) for f in field]
    dz_sum = [z + nxt(z) for z in dz]
    masked = jnp.where(wet, speed, 0.0)
    low, high, second, forward = face_fluxes(
        local, [prv(d) for d in local], [nxt(d) for d in local], dz_sum, masked
    )
    zero = jnp.zeros_like(masked)
    terms, steps = [], []
    for t in range(NT):
        late = zero
        if low_second is not None:
            late = late + jnp.where(low_second & ~forward, second[t], 0.0)
        if high_second is not None:
            late = late + jnp.where(high_second & forward, second[t], 0.0)
        arriving, term, step = late, -late, zero
        if high_at is not None:
            arriving = arriving + jnp.where(high_at, high[t], 0.0)
            step = step + prv(jnp.where(high_at, local[t], 0.0))
        if low_at is not None:
            term = term - jnp.where(low_at, low[t], 0.0)
            step = step + jnp.where(low_at, local[t], 0.0)
        terms.append(term + prv(arriving))
        steps.append(step)
    return terms, steps


def kernel(
    n_gx, n_gy,
    tracers, east, north, bottom, out,
    T, U, V, bottom_int, bf, be, bn, TZ, XY, YB, GX, GY,
    packed, to_east, to_west, from_west, from_east, to_north, to_south, from_north, from_south, relay,
    strip, strip_b, strip_v, edge_c, edge_g,
    load_sem, send_sem, recv_sem, go_sem,
):
    gx, gy = lax.axis_index("gx"), lax.axis_index("gy")
    east_id = (lax.rem(gx + 1, n_gx), gy)
    west_id = (lax.rem(gx + n_gx - 1, n_gx), gy)
    north_id = (gx, gy + 1)
    south_id = (gx, gy - 1)
    mirror_id = (n_gx - 1 - gx, gy)
    top = gy == n_gy - 1
    base = gy == 0
    below_middle = gy == n_gy // 2 - 1
    above_middle = gy == n_gy // 2
    beside_middle = below_middle | above_middle
    after_seam = (lax.rem(gx, BLOCK) == 0) & beside_middle
    before_seam = (lax.rem(gx, BLOCK) == BLOCK - 1) & beside_middle
    relays = (lax.rem(gx, BLOCK) == BLOCK - 2) & beside_middle
    relayed_up = before_seam & below_middle
    relayed_down = before_seam & above_middle
    relays_up = relays & below_middle
    relays_down = relays & above_middle

    barrier = pltpu.get_barrier_semaphore()

    def greet(device):
        pl.semaphore_signal(barrier, inc=1, device_id=device, device_id_type=MESH)

    pl.when(top)(lambda: greet(mirror_id))
    pl.when(relayed_up)(lambda: greet((gx - 1, gy + 1)))
    pl.when(relayed_down)(lambda: greet((gx - 1, gy - 1)))
    pl.when(jnp.logical_not(top | relayed_up))(lambda: greet(north_id))
    pl.when(jnp.logical_not(base | relayed_down))(lambda: greet(south_id))
    greet(west_id)
    pl.when(jnp.logical_not(before_seam))(lambda: greet(east_id))
    expected = (
        4 + relays.astype(jnp.int32) - before_seam.astype(jnp.int32)
        - after_seam.astype(jnp.int32) - base.astype(jnp.int32)
    )

    first, middle, last = pl.ds(0, 8), pl.ds(8, CY - 16), pl.ds(CY - 8, 8)

    def load(source, target, index):
        copy = pltpu.make_async_copy(source, target, load_sem.at[index])
        copy.start()
        return copy

    def padded(rows):
        return T.at[:, :, pl.ds(PAD + rows.start, rows.size), :]

    early = [
        load(bottom, bottom_int, 0),
        load(tracers.at[:, :, first, :], padded(first), 1),
        load(tracers.at[:, :, last, :], padded(last), 2),
        load(north.at[:, last, :], V.at[:, last, :], 3),
    ]
    late = [
        load(tracers.at[:, :, middle, :], padded(middle), 4),
        load(east, U, 5),
        load(north.at[:, pl.ds(0, CY - 8), :], V.at[:, pl.ds(0, CY - 8), :], 6),
    ]

    lane = lax.broadcasted_iota(jnp.int32, (8, CX), 1)
    row = lax.broadcasted_iota(jnp.int32, (8, CX), 0)
    zeros = jnp.zeros((8, CX), jnp.float32)

    def octet(o):
        return pl.ds(PAD + 8 * o, 8)

    def shifted(o, by):
        return pl.ds(PAD + 8 * o + by, 8)

    for pad in (pl.ds(0, PAD), pl.ds(PAD + CY, PAD)):
        bf[pad, :] = zeros
        bn[pad, :] = zeros

    def clear(k, carry):
        for t in range(NT):
            YB[t, k, pl.ds(0, PAD), :] = zeros
            TZ[t, k, pl.ds(PAD + CY, PAD), :] = zeros
        strip_v[k] = zeros
        return carry

    lax.fori_loop(0, NZ, clear, 0)

    @pl.when(base)
    def _():
        from_south[...] = jnp.zeros_like(from_south)

    for copy in early:
        copy.wait()

    for o in (0, OCTETS - 1):
        bf[octet(o), :] = bottom_int[pl.ds(8 * o, 8), :].astype(jnp.float32)

    def rows_out(k, carry):
        for t in range(NT):
            spot = pl.ds(2 * (NZ * t + k), 2)
            last = T[t, k, pl.ds(PAD + CY - 2, 2), :]
            first = T[t, k, pl.ds(PAD, 2), :]
            to_north[spot, :] = last
            to_south[spot, :] = first
            strip[t, k, pl.ds(0, 2), :] = last
            strip[t, k, pl.ds(6, 2), :] = first
        last_v = V[k, pl.ds(CY - 2, 2), :]
        to_north[pl.ds(72 + k, 1), :] = last_v[1:2]
        strip_v[k, pl.ds(0, 2), :] = last_v
        return carry

    lax.fori_loop(0, NZ, rows_out, 0, unroll=4)
    last_b = bf[pl.ds(PAD + CY - 2, 2), :]
    first_b = bf[pl.ds(PAD, 2), :]
    to_north[pl.ds(64, 8), :] = zeros
    to_south[pl.ds(64, 8), :] = zeros
    to_north[pl.ds(64, 2), :] = last_b
    to_south[pl.ds(64, 2), :] = first_b
    strip_b[pl.ds(0, 2), :] = last_b
    strip_b[pl.ds(6, 2), :] = first_b

    def send(source, target, index, slot, device):
        return pltpu.make_async_remote_copy(
            src_ref=source, dst_ref=target, send_sem=send_sem.at[index], recv_sem=recv_sem.at[slot],
            device_id=device, device_id_type=MESH,
        )

    eastward = send(to_east, from_west, 0, 0, east_id)
    westward = send(to_west, from_east, 1, 1, west_id)
    northward = send(to_north, from_south, 2, 2, north_id)
    across = send(to_north.at[pl.ds(0, ROWS_FROM_NORTH)], from_north, 2, 3, mirror_id)
    southward = send(to_south, from_north, 3, 3, south_id)
    short_relay = relay.at[pl.ds(0, ROWS_FROM_NORTH)]
    handed_up = send(to_north, relay, 2, 4, west_id)
    handed_down = send(to_south, short_relay, 3, 4, west_id)
    forwarded_up = send(relay, from_south, 4, 2, (gx + 1, gy + 1))
    forwarded_down = send(short_relay, from_north, 4, 3, (gx + 1, gy - 1))
    northward_itself = jnp.logical_not(top | relayed_up)
    southward_itself = jnp.logical_not(base | relayed_down)
    late_entry = below_middle & jnp.logical_not(before_seam)

    @pl.when(jnp.logical_not(late_entry))
    def _():
        pl.semaphore_wait(barrier, expected)

        @pl.when(before_seam)
        def _():
            pl.semaphore_signal(go_sem, inc=1, device_id=east_id, device_id_type=MESH)

        pl.when(southward_itself)(southward.start)
        pl.when(northward_itself)(northward.start)
        pl.when(relayed_up)(handed_up.start)
        pl.when(relayed_down)(handed_down.start)
        pl.when(top)(across.start)

        @pl.when(relays_down)
        def _():
            handed_down.wait_recv()
            forwarded_down.start()

    for copy in late:
        copy.wait()

    for k in range(NZ):
        strip_v[k, pl.ds(6, 1), :] = V[k, pl.ds(0, 1), :]
    for o in range(OCTETS):
        bf[octet(o), :] = bottom_int[pl.ds(8 * o, 8), :].astype(jnp.float32)
    for o in range(OCTETS):
        here = bf[octet(o), :]
        be[octet(o), :] = jnp.where(lane == CX - 1, 0.0, jnp.minimum(here, lanes_left(here)))
        bn[octet(o), :] = jnp.minimum(here, bf[shifted(o, 1), :])

    slot_of = lane // 4

    def pack(group, carry):
        t0, t1, speed = zeros, zeros, zeros
        for b in range(4):
            for o in range(OCTETS):
                slot = b * 8 + o
                here = slot_of == slot
                shift = (4 * slot + 2) % CX
                k = 4 * group + b
                t0 = jnp.where(here, pltpu.roll(T[0, k, octet(o), :], shift, 1), t0)
                t1 = jnp.where(here, pltpu.roll(T[1, k, octet(o), :], shift, 1), t1)
                speed = jnp.where(here, pltpu.roll(U[k, pl.ds(8 * o, 8), :], shift, 1), speed)
        packed[group] = t0
        packed[4 + group] = t1
        packed[8 + group] = speed
        return carry

    lax.fori_loop(0, 4, pack, 0, unroll=2)
    packed_b = zeros
    for b in range(4):
        for o in range(OCTETS):
            slot = b * 8 + o
            packed_b = jnp.where(
                slot_of == slot, pltpu.roll(bf[octet(o), :], (4 * slot + 2) % CX, 1), packed_b
            )
    packed[12] = packed_b

    first_half = lax.rem(lane, 4) < 2
    east_speeds = zeros
    for j in range(4):
        to_east[j] = jnp.where(first_half, packed[j], pltpu.roll(packed[4 + j], 2, 1))
        to_west[j] = jnp.where(first_half, pltpu.roll(packed[4 + j], CX - 2, 1), packed[j])
        east_speeds = jnp.where(
            lax.rem(lane, 4) == j, pltpu.roll(packed[8 + j], (CX + j - 1) % CX, 1), east_speeds
        )
    to_east[4] = east_speeds
    to_east[5] = packed_b
    to_west[4] = packed_b

    @pl.when(jnp.logical_not(late_entry))
    def _():
        eastward.start()
        pl.when(jnp.logical_not(after_seam))(westward.start)

    def vertical(k, carry):
        level = k.astype(jnp.float32)
        above = jnp.where(k > 0, level, 99.0)
        down, up = jnp.minimum(k + 1, NZ - 1), jnp.maximum(k - 1, 0)
        for o in range(OCTETS):
            depth = bf[octet(o), :]
            for t in range(NT):
                here = T[t, k, octet(o), :]
                TZ[t, k, octet(o), :] = jnp.where(
                    depth > level + 1.0, T[t, down, octet(o), :] - here, 0.0
                ) + jnp.where(depth > above, here - T[t, up, octet(o), :], 0.0)
        return carry

    lax.fori_loop(0, NZ, vertical, 0, unroll=2)

    def inside(k, carry):
        level = k.astype(jnp.float32)
        for o in range(OCTETS):
            here = [T[t, k, octet(o), :] for t in range(NT)]
            dz = [TZ[t, k, octet(o), :] for t in range(NT)]
            wet = be[octet(o), :] > level
            local = [jnp.where(wet, lanes_left(f) - f, 0.0) for f in here]
            before = [lanes_right(d) for d in local]
            after = [lanes_left(d) for d in local]
            speed = jnp.where(wet, U[k, pl.ds(8 * o, 8), :], 0.0)
            low, high, _, _ = face_fluxes(
                local, before, after, [z + lanes_left(z) for z in dz], speed
            )
            across_x = [lanes_right(high[t]) - low[t] for t in range(NT)]
            for t in range(NT):
                GX[t, k, octet(o), :] = local[t] + before[t]

            wet = bn[octet(o), :] > level
            wet_before = bn[shifted(o, -1), :] > level
            wet_after = bn[shifted(o, 1), :] > level
            nxt = [T[t, k, shifted(o, 1), :] for t in range(NT)]
            local = [jnp.where(wet, nxt[t] - here[t], 0.0) for t in range(NT)]
            before = [
                jnp.where(wet_before, here[t] - T[t, k, shifted(o, -1), :], 0.0) for t in range(NT)
            ]
            after = [
                jnp.where(wet_after, T[t, k, shifted(o, 2), :] - nxt[t], 0.0) for t in range(NT)
            ]
            speed = jnp.where(wet, V[k, pl.ds(8 * o, 8), :], 0.0)
            low, high, _, _ = face_fluxes(
                local, before, after, [dz[t] + TZ[t, k, shifted(o, 1), :] for t in range(NT)], speed
            )
            for t in range(NT):
                GY[t, k, octet(o), :] = local[t] + before[t]
                XY[t, k, octet(o), :] = across_x[t] - low[t]
                YB[t, k, octet(o), :] = high[t]
        return carry

    lax.fori_loop(0, NZ, inside, 0, unroll=2)

    @pl.when(late_entry)
    def _():
        pl.semaphore_wait(barrier, expected)
        northward.start()

        @pl.when(relays_up)
        def _():
            handed_up.wait_recv()
            forwarded_up.start()

        eastward.start()
        pl.when(jnp.logical_not(after_seam))(westward.start)
        southward.start()

    @pl.when(after_seam)
    def _():
        pl.semaphore_wait(go_sem, 1)
        westward.start()

    def edge_rows_in():
        southward.wait_recv()
        pl.when(jnp.logical_not(base))(northward.wait_recv)

        @pl.when(top)
        def _():
            for i in range(ROWS_FROM_NORTH // 8):
                value = from_north[pl.ds(8 * i, 8), :]
                for bit in (64, 32, 16, 8, 4, 2, 1):
                    value = jnp.where(
                        (lane & bit) != 0, pltpu.roll(value, bit, 1), pltpu.roll(value, CX - bit, 1)
                    )
                from_north[pl.ds(8 * i, 8), :] = jnp.where(
                    (row & 1) != 0, rows_down(value), rows_up(value)
                )

        def rows_in(k, carry):
            for t in range(NT):
                spot = pl.ds(2 * (NZ * t + k), 2)
                strip[t, k, pl.ds(2, 2), :] = from_north[spot, :]
                strip[t, k, pl.ds(4, 2), :] = from_south[spot, :]
            strip_v[k, pl.ds(5, 1), :] = from_south[pl.ds(72 + k, 1), :]
            return carry

        lax.fori_loop(0, NZ, rows_in, 0)
        strip_b[pl.ds(2, 2), :] = from_north[pl.ds(64, 2), :]
        strip_b[pl.ds(4, 2), :] = from_south[pl.ds(64, 2), :]

        def edge_rows(k, carry):
            level = k.astype(jnp.float32)
            above = jnp.where(k > 0, level, 99.0)
            down, up = jnp.minimum(k + 1, NZ - 1), jnp.maximum(k - 1, 0)
            depth = strip_b[...]
            here = [strip[t, k] for t in range(NT)]
            dz = [
                jnp.where(depth > level + 1.0, strip[t, down] - here[t], 0.0)
                + jnp.where(depth > above, here[t] - strip[t, up], 0.0)
                for t in range(NT)
            ]
            terms, grads = edge_terms(
                here, dz, depth, strip_v[k], level, rows_up, rows_down,
                row == 1, row == 5, row == 0, row == 6,
            )
            for t in range(NT):
                XY[t, k, octet(0), :] += jnp.where(row < 2, pltpu.roll(terms[t], 2, 0), 0.0)
                GY[t, k, octet(0), :] += jnp.where(row < 2, pltpu.roll(grads[t], 2, 0), 0.0)
                XY[t, k, octet(OCTETS - 1), :] += jnp.where(row > 5, pltpu.roll(terms[t], 6, 0), 0.0)
                GY[t, k, octet(OCTETS - 1), :] += jnp.where(row > 5, pltpu.roll(grads[t], 6, 0), 0.0)
            return carry

        lax.fori_loop(0, NZ, edge_rows, 0, unroll=8)

    rows_late = beside_middle & jnp.logical_not(below_middle & (lax.rem(gx, BLOCK) == 1))
    pl.when(jnp.logical_not(rows_late))(edge_rows_in)

    eastward.wait_recv()
    westward.wait_recv()
    quarter = lax.rem(lane, 4)
    level_in_group = (lane // 32).astype(jnp.float32)
    for side in range(2):
        own = [[packed[4 * t + j] for j in range(4)] for t in range(NT)]
        if side == 0:
            depth = jnp.where(first_half, from_west[5], packed[12])
            fields = [
                [jnp.where(first_half, from_west[j], own[0][j]) for j in range(4)],
                [jnp.where(first_half, pltpu.roll(from_west[j], CX - 2, 1), own[1][j]) for j in range(4)],
            ]
        else:
            depth = jnp.where(first_half, packed[12], from_east[4])
            fields = [
                [jnp.where(first_half, own[0][j], from_east[j]) for j in range(4)],
                [jnp.where(first_half, own[1][j], pltpu.roll(from_east[j], 2, 1)) for j in range(4)],
            ]
        steps = []
        for t in range(NT):
            turned = [pltpu.roll(f, CX - 32, 1) for f in fields[t]]
            steps.append(
                [
                    jnp.where(
                        depth > level_in_group + (4 * j + 1.0),
                        jnp.where(lane < CX - 32, turned[j], turned[min(j + 1, 3)]) - fields[t][j],
                        0.0,
                    )
                    for j in range(4)
                ]
            )
        for j in range(4):
            dz = []
            for t in range(NT):
                before = pltpu.roll(steps[t][j - 1], 32, 1) if j > 0 else zeros
                dz.append(
                    steps[t][j] + jnp.where(lane < 32, before, pltpu.roll(steps[t][j], 32, 1))
                )
            speed = packed[8 + j]
            if side == 0:
                speed = jnp.where(first_half, pltpu.roll(from_west[4], (CX + 1 - j) % CX, 1), speed)
            terms, grads = edge_terms(
                [fields[t][j] for t in range(NT)], dz, depth, speed, level_in_group + 4.0 * j,
                lanes_left, lanes_right,
                None if side == 0 else quarter == 1, quarter == 1 if side == 0 else None,
                None if side == 0 else quarter == 0, quarter == 2 if side == 0 else None,
            )
            for t in range(NT):
                if side == 0:
                    edge_c[t, j] = terms[t]
                    edge_g[t, j] = grads[t]
                else:
                    edge_c[t, j] += terms[t]
                    edge_g[t, j] += grads[t]

    at_edge = (lane < 2) | (lane >= CX - 2)

    def finish(octets):
        def at(o, ref, t, group, b):
            rolled = pltpu.roll(ref[t, group], (CX - (4 * (b * 8 + o) + 2)) % CX, 1)
            return jnp.where(at_edge, rolled, 0.0)

        def body(group, carry):
            fluxes = [[carry[4 * i], carry[4 * i + 1]] for i in range(len(octets))]
            gx_here = [[carry[4 * i + 2], carry[4 * i + 3]] for i in range(len(octets))]
            after = jnp.minimum(group + 1, 3)
            for b in range(4):
                k = 4 * group + b
                level = k.astype(jnp.float32)
                down = jnp.minimum(k + 1, NZ - 1)
                for i, o in enumerate(octets):
                    depth = bf[octet(o), :]
                    open_below = depth > level + 1.0
                    here = [T[t, k, octet(o), :] for t in range(NT)]
                    step = [
                        jnp.where(open_below, T[t, down, octet(o), :] - here[t], 0.0)
                        for t in range(NT)
                    ]
                    gx_down = [
                        GX[t, down, octet(o), :]
                        + (at(o, edge_g, t, group, b + 1) if b < 3 else at(o, edge_g, t, after, 0))
                        for t in range(NT)
                    ]
                    mean_x = [gx_here[i][t] + gx_down[t] for t in range(NT)]
                    mean_y = [GY[t, k, octet(o), :] + GY[t, down, octet(o), :] for t in range(NT)]
                    inverse = jnp.where(
                        open_below, reciprocal(jnp.maximum(4.0 * density(step), 1.0)), 0.0
                    )
                    slope_x = jnp.clip(density(mean_x) * inverse, -1.0, 1.0)
                    slope_y = jnp.clip(density(mean_y) * inverse, -1.0, 1.0)
                    squares = 0.1 * (slope_x * slope_x + slope_y * slope_y)
                    slope_x = 0.025 * slope_x
                    slope_y = 0.025 * slope_y
                    wet = depth > level
                    for t in range(NT):
                        flux = squares * step[t] - (slope_x * mean_x[t] + slope_y * mean_y[t])
                        faces = XY[t, k, octet(o), :] + at(o, edge_c, t, group, b)
                        total = (
                            here[t]
                            + (faces + YB[t, k, shifted(o, -1), :])
                            + (flux - fluxes[i][t])
                        )
                        out[t, k, pl.ds(8 * o, 8), :] = jnp.where(wet, total, 0.0)
                        fluxes[i][t] = flux
                    gx_here[i] = gx_down
            return tuple(x for i in range(len(octets)) for x in (*fluxes[i], *gx_here[i]))

        start = []
        for o in octets:
            start += [zeros, zeros]
            start += [GX[t, 0, octet(o), :] + at(o, edge_g, t, 0, 0) for t in range(NT)]
        lax.fori_loop(0, 4, body, tuple(start), unroll=2)

    finish(tuple(range(1, OCTETS - 1)))

    pl.when(rows_late)(edge_rows_in)
    finish((0, OCTETS - 1))

    eastward.wait_send()
    westward.wait_send()
    pl.when(southward_itself)(southward.wait_send)
    pl.when(northward_itself)(northward.wait_send)
    pl.when(relayed_up)(handed_up.wait_send)
    pl.when(relayed_down)(handed_down.wait_send)
    pl.when(top)(across.wait_send)
    pl.when(relays_up)(forwarded_up.wait_send)
    pl.when(relays_down)(forwarded_down.wait_send)


def solution(mesh):
    n_gx, n_gy = mesh.shape["gx"], mesh.shape["gy"]
    f32 = jnp.float32
    in_hbm = pl.BlockSpec(memory_space=pltpu.HBM)
    field = pltpu.VMEM((NT, NZ, TALL, CX), f32)
    levels = pltpu.VMEM((NZ, CY, CX), f32)
    plane = pltpu.VMEM((TALL, CX), f32)
    packed = pltpu.VMEM((PACKED, 8, CX), f32)
    eastward = pltpu.VMEM((EASTWARD, 8, CX), f32)
    westward = pltpu.VMEM((WESTWARD, 8, CX), f32)
    from_south = pltpu.VMEM((ROWS_FROM_SOUTH, CX), f32)
    from_north = pltpu.VMEM((ROWS_FROM_NORTH, CX), f32)
    edge = pltpu.VMEM((NT, 4, 8, CX), f32)

    def on_device(tracers, east_speed, north_speed, bottom_level):
        return pl.pallas_call(
            functools.partial(kernel, n_gx, n_gy),
            out_shape=jax.ShapeDtypeStruct((NT, NZ, CY, CX), f32),
            in_specs=[in_hbm] * 4,
            out_specs=pl.BlockSpec(memory_space=pltpu.VMEM),
            scratch_shapes=[
                field, levels, levels, pltpu.VMEM((CY, CX), jnp.int32), plane, plane, plane,
                field, field, field, field, field,
                packed, eastward, westward, eastward, westward,
                from_south, from_north, from_north, from_south, from_south,
                pltpu.VMEM((NT, NZ, 8, CX), f32), pltpu.VMEM((8, CX), f32),
                pltpu.VMEM((NZ, 8, CX), f32), edge, edge,
                pltpu.SemaphoreType.DMA((7,)), pltpu.SemaphoreType.DMA((5,)),
                pltpu.SemaphoreType.DMA((5,)), pltpu.SemaphoreType.REGULAR,
            ],
            compiler_params=pltpu.CompilerParams(
                collective_id=0, has_side_effects=True, vmem_limit_bytes=24 * 1024 * 1024
            ),
        )(
            *[
                pltpu.with_memory_space_constraint(x, pltpu.HBM)
                for x in (tracers, east_speed, north_speed, bottom_level)
            ]
        )

    in_specs = (P(None, None, "gy", "gx"), P(None, "gy", "gx"), P(None, "gy", "gx"), P("gy", "gx"))
    return jax.shard_map(
        on_device, mesh=mesh, in_specs=in_specs, out_specs=P(None, None, "gy", "gx"), check_vma=False
    )
```

```python
import functools

import jax
import jax.numpy as jnp
from jax import lax
from jax.experimental import pallas as pl
from jax.experimental.pallas import tpu as pltpu
from jax.sharding import PartitionSpec as P

MESH = pl.DeviceIdType.MESH
NT, NZ, CY, CX = 2, 16, 48, 128
PAD = 8
TALL = CY + 2 * PAD
OCTETS = CY // 8
ROWS_FROM_NORTH = 72
ROWS_FROM_SOUTH = 88
PACKED = 13
EASTWARD = 6
WESTWARD = 5
BLOCK = 8
HEAT = 0.4
SALT = 0.6


def reciprocal(value):
    guess = pl.reciprocal(value, approx=True)
    return guess * (2.0 - value * guess)


def minmod(first, second):
    return jnp.maximum(jnp.minimum(first, second), 0.0) + jnp.minimum(
        jnp.maximum(first, second), 0.0
    )


def density(pair):
    return SALT * pair[1] - HEAT * pair[0]


def face_fluxes(local, before, after, dz_sum, speed):
    slope = jnp.clip(
        (0.1 * density(local)) * reciprocal(jnp.maximum(density(dz_sum), 1.0)), -0.025, 0.025
    )
    size = jnp.abs(speed)
    limited = 0.5 * size * (1.0 - size)
    forward = speed >= 0.0
    linear = jnp.minimum(speed, 0.0) - 0.1
    low, high, second = [], [], []
    for t in range(NT):
        correction = limited * minmod(local[t], jnp.where(forward, before[t], after[t]))
        taken = correction + (linear * local[t] + slope * dz_sum[t])
        low.append(taken)
        high.append(taken - speed * local[t])
        second.append(correction)
    return low, high, second, forward


def lanes_left(value):
    return pltpu.roll(value, CX - 1, 1)


def lanes_right(value):
    return pltpu.roll(value, 1, 1)


def rows_up(value):
    return pltpu.roll(value, 7, 0)


def rows_down(value):
    return pltpu.roll(value, 1, 0)


def edge_terms(field, dz, bottom, speed, level, nxt, prv, low_at, high_at, low_second, high_second):
    wet = jnp.minimum(bottom, nxt(bottom)) > level
    local = [jnp.where(wet, nxt(f) - f, 0.0) for f in field]
    dz_sum = [z + nxt(z) for z in dz]
    masked = jnp.where(wet, speed, 0.0)
    low, high, second, forward = face_fluxes(
        local, [prv(d) for d in local], [nxt(d) for d in local], dz_sum, masked
    )
    zero = jnp.zeros_like(masked)
    terms, steps = [], []
    for t in range(NT):
        late = zero
        if low_second is not None:
            late = late + jnp.where(low_second & ~forward, second[t], 0.0)
        if high_second is not None:
            late = late + jnp.where(high_second & forward, second[t], 0.0)
        arriving, term, step = late, -late, zero
        if high_at is not None:
            arriving = arriving + jnp.where(high_at, high[t], 0.0)
            step = step + prv(jnp.where(high_at, local[t], 0.0))
        if low_at is not None:
            term = term - jnp.where(low_at, low[t], 0.0)
            step = step + jnp.where(low_at, local[t], 0.0)
        terms.append(term + prv(arriving))
        steps.append(step)
    return terms, steps


def kernel(
    n_gx, n_gy,
    tracers, east, north, bottom, out,
    T, U, V, bottom_int, bf, be, bn, TZ, XY, YB, GX, GY, FY, Q,
    packed, to_east, to_west, from_west, from_east, to_north, to_south, from_north, from_south, relay,
    strip, strip_b, strip_v, edge_c, edge_g,
    load_sem, send_sem, recv_sem, go_sem,
):
    gx, gy = lax.axis_index("gx"), lax.axis_index("gy")
    east_id = (lax.rem(gx + 1, n_gx), gy)
    west_id = (lax.rem(gx + n_gx - 1, n_gx), gy)
    north_id = (gx, gy + 1)
    south_id = (gx, gy - 1)
    mirror_id = (n_gx - 1 - gx, gy)
    top = gy == n_gy - 1
    base = gy == 0
    below_middle = gy == n_gy // 2 - 1
    above_middle = gy == n_gy // 2
    beside_middle = below_middle | above_middle
    after_seam = (lax.rem(gx, BLOCK) == 0) & beside_middle
    before_seam = (lax.rem(gx, BLOCK) == BLOCK - 1) & beside_middle
    relays = (lax.rem(gx, BLOCK) == BLOCK - 2) & beside_middle
    relayed_up = before_seam & below_middle
    relayed_down = before_seam & above_middle
    relays_up = relays & below_middle
    relays_down = relays & above_middle

    barrier = pltpu.get_barrier_semaphore()

    def greet(device):
        pl.semaphore_signal(barrier, inc=1, device_id=device, device_id_type=MESH)

    pl.when(top)(lambda: greet(mirror_id))
    pl.when(relayed_up)(lambda: greet((gx - 1, gy + 1)))
    pl.when(relayed_down)(lambda: greet((gx - 1, gy - 1)))
    pl.when(jnp.logical_not(top | relayed_up))(lambda: greet(north_id))
    pl.when(jnp.logical_not(base | relayed_down))(lambda: greet(south_id))
    greet(west_id)
    pl.when(jnp.logical_not(before_seam))(lambda: greet(east_id))
    expected = (
        4 + relays.astype(jnp.int32) - before_seam.astype(jnp.int32)
        - after_seam.astype(jnp.int32) - base.astype(jnp.int32)
    )

    first, middle, last = pl.ds(0, 8), pl.ds(8, CY - 16), pl.ds(CY - 8, 8)

    def load(source, target, index):
        copy = pltpu.make_async_copy(source, target, load_sem.at[index])
        copy.start()
        return copy

    def padded(rows):
        return T.at[:, :, pl.ds(PAD + rows.start, rows.size), :]

    early = [
        load(bottom, bottom_int, 0),
        load(tracers.at[:, :, first, :], padded(first), 1),
        load(tracers.at[:, :, last, :], padded(last), 2),
        load(north.at[:, last, :], V.at[:, last, :], 3),
    ]
    late = [
        load(tracers.at[:, :, middle, :], padded(middle), 4),
        load(east, U, 5),
        load(north.at[:, pl.ds(0, CY - 8), :], V.at[:, pl.ds(0, CY - 8), :], 6),
    ]

    lane = lax.broadcasted_iota(jnp.int32, (8, CX), 1)
    row = lax.broadcasted_iota(jnp.int32, (8, CX), 0)
    zeros = jnp.zeros((8, CX), jnp.float32)

    def octet(o):
        return pl.ds(PAD + 8 * o, 8)

    def shifted(o, by):
        return pl.ds(PAD + 8 * o + by, 8)

    for pad in (pl.ds(0, PAD), pl.ds(PAD + CY, PAD)):
        bf[pad, :] = zeros
        bn[pad, :] = zeros

    def clear(k, carry):
        for t in range(NT):
            YB[t, k, pl.ds(0, PAD), :] = zeros
            TZ[t, k, pl.ds(PAD + CY, PAD), :] = zeros
        strip_v[k] = zeros
        return carry

    lax.fori_loop(0, NZ, clear, 0)

    @pl.when(base)
    def _():
        from_south[...] = jnp.zeros_like(from_south)

    for copy in early:
        copy.wait()

    for o in (0, OCTETS - 1):
        bf[octet(o), :] = bottom_int[pl.ds(8 * o, 8), :].astype(jnp.float32)

    def rows_out(k, carry):
        for t in range(NT):
            spot = pl.ds(2 * (NZ * t + k), 2)
            last = T[t, k, pl.ds(PAD + CY - 2, 2), :]
            first = T[t, k, pl.ds(PAD, 2), :]
            to_north[spot, :] = last
            to_south[spot, :] = first
            strip[t, k, pl.ds(0, 2), :] = last
            strip[t, k, pl.ds(6, 2), :] = first
        last_v = V[k, pl.ds(CY - 2, 2), :]
        to_north[pl.ds(72 + k, 1), :] = last_v[1:2]
        strip_v[k, pl.ds(0, 2), :] = last_v
        return carry

    lax.fori_loop(0, NZ, rows_out, 0, unroll=4)
    last_b = bf[pl.ds(PAD + CY - 2, 2), :]
    first_b = bf[pl.ds(PAD, 2), :]
    to_north[pl.ds(64, 8), :] = zeros
    to_south[pl.ds(64, 8), :] = zeros
    to_north[pl.ds(64, 2), :] = last_b
    to_south[pl.ds(64, 2), :] = first_b
    strip_b[pl.ds(0, 2), :] = last_b
    strip_b[pl.ds(6, 2), :] = first_b

    def send(source, target, index, slot, device):
        return pltpu.make_async_remote_copy(
            src_ref=source, dst_ref=target, send_sem=send_sem.at[index], recv_sem=recv_sem.at[slot],
            device_id=device, device_id_type=MESH,
        )

    eastward = send(to_east, from_west, 0, 0, east_id)
    westward = send(to_west, from_east, 1, 1, west_id)
    northward = send(to_north, from_south, 2, 2, north_id)
    across = send(to_north.at[pl.ds(0, ROWS_FROM_NORTH)], from_north, 2, 3, mirror_id)
    southward = send(to_south, from_north, 3, 3, south_id)
    short_relay = relay.at[pl.ds(0, ROWS_FROM_NORTH)]
    handed_up = send(to_north, relay, 2, 4, west_id)
    handed_down = send(to_south, short_relay, 3, 4, west_id)
    forwarded_up = send(relay, from_south, 4, 2, (gx + 1, gy + 1))
    forwarded_down = send(short_relay, from_north, 4, 3, (gx + 1, gy - 1))
    northward_itself = jnp.logical_not(top | relayed_up)
    southward_itself = jnp.logical_not(base | relayed_down)
    late_entry = below_middle & jnp.logical_not(before_seam)

    @pl.when(jnp.logical_not(late_entry))
    def _():
        pl.semaphore_wait(barrier, expected)

        @pl.when(before_seam)
        def _():
            pl.semaphore_signal(go_sem, inc=1, device_id=east_id, device_id_type=MESH)

        pl.when(southward_itself)(southward.start)
        pl.when(northward_itself)(northward.start)
        pl.when(relayed_up)(handed_up.start)
        pl.when(relayed_down)(handed_down.start)
        pl.when(top)(across.start)

        @pl.when(relays_down)
        def _():
            handed_down.wait_recv()
            forwarded_down.start()

    for copy in late:
        copy.wait()

    for k in range(NZ):
        strip_v[k, pl.ds(6, 1), :] = V[k, pl.ds(0, 1), :]
    for o in range(OCTETS):
        bf[octet(o), :] = bottom_int[pl.ds(8 * o, 8), :].astype(jnp.float32)
    for o in range(OCTETS):
        here = bf[octet(o), :]
        be[octet(o), :] = jnp.where(lane == CX - 1, 0.0, jnp.minimum(here, lanes_left(here)))
        bn[octet(o), :] = jnp.minimum(here, bf[shifted(o, 1), :])

    slot_of = lane // 4

    def pack(group, carry):
        t0, t1, speed = zeros, zeros, zeros
        for b in range(4):
            for o in range(OCTETS):
                slot = b * 8 + o
                here = slot_of == slot
                shift = (4 * slot + 2) % CX
                k = 4 * group + b
                t0 = jnp.where(here, pltpu.roll(T[0, k, octet(o), :], shift, 1), t0)
                t1 = jnp.where(here, pltpu.roll(T[1, k, octet(o), :], shift, 1), t1)
                speed = jnp.where(here, pltpu.roll(U[k, pl.ds(8 * o, 8), :], shift, 1), speed)
        packed[group] = t0
        packed[4 + group] = t1
        packed[8 + group] = speed
        return carry

    lax.fori_loop(0, 4, pack, 0, unroll=2)
    packed_b = zeros
    for b in range(4):
        for o in range(OCTETS):
            slot = b * 8 + o
            packed_b = jnp.where(
                slot_of == slot, pltpu.roll(bf[octet(o), :], (4 * slot + 2) % CX, 1), packed_b
            )
    packed[12] = packed_b

    first_half = lax.rem(lane, 4) < 2
    east_speeds = zeros
    for j in range(4):
        to_east[j] = jnp.where(first_half, packed[j], pltpu.roll(packed[4 + j], 2, 1))
        to_west[j] = jnp.where(first_half, pltpu.roll(packed[4 + j], CX - 2, 1), packed[j])
        east_speeds = jnp.where(
            lax.rem(lane, 4) == j, pltpu.roll(packed[8 + j], (CX + j - 1) % CX, 1), east_speeds
        )
    to_east[4] = east_speeds
    to_east[5] = packed_b
    to_west[4] = packed_b

    @pl.when(jnp.logical_not(late_entry))
    def _():
        eastward.start()
        pl.when(jnp.logical_not(after_seam))(westward.start)

    def vertical(k, carry):
        level = k.astype(jnp.float32)
        above = jnp.where(k > 0, level, 99.0)
        down, up = jnp.minimum(k + 1, NZ - 1), jnp.maximum(k - 1, 0)
        for o in range(OCTETS):
            depth = bf[octet(o), :]
            for t in range(NT):
                here = T[t, k, octet(o), :]
                TZ[t, k, octet(o), :] = jnp.where(
                    depth > level + 1.0, T[t, down, octet(o), :] - here, 0.0
                ) + jnp.where(depth > above, here - T[t, up, octet(o), :], 0.0)
        return carry

    lax.fori_loop(0, NZ, vertical, 0, unroll=2)

    def inside(k, carry):
        level = k.astype(jnp.float32)
        for o in range(OCTETS):
            here = [T[t, k, octet(o), :] for t in range(NT)]
            dz = [TZ[t, k, octet(o), :] for t in range(NT)]
            wet = be[octet(o), :] > level
            local = [jnp.where(wet, lanes_left(f) - f, 0.0) for f in here]
            before = [lanes_right(d) for d in local]
            after = [lanes_left(d) for d in local]
            speed = jnp.where(wet, U[k, pl.ds(8 * o, 8), :], 0.0)
            low, high, _, _ = face_fluxes(
                local, before, after, [z + lanes_left(z) for z in dz], speed
            )
            across_x = [lanes_right(high[t]) - low[t] for t in range(NT)]
            for t in range(NT):
                GX[t, k, octet(o), :] = local[t] + before[t]

            wet = bn[octet(o), :] > level
            wet_before = bn[shifted(o, -1), :] > level
            wet_after = bn[shifted(o, 1), :] > level
            nxt = [T[t, k, shifted(o, 1), :] for t in range(NT)]
            local = [jnp.where(wet, nxt[t] - here[t], 0.0) for t in range(NT)]
            before = [
                jnp.where(wet_before, here[t] - T[t, k, shifted(o, -1), :], 0.0) for t in range(NT)
            ]
            after = [
                jnp.where(wet_after, T[t, k, shifted(o, 2), :] - nxt[t], 0.0) for t in range(NT)
            ]
            speed = jnp.where(wet, V[k, pl.ds(8 * o, 8), :], 0.0)
            low, high, _, _ = face_fluxes(
                local, before, after, [dz[t] + TZ[t, k, shifted(o, 1), :] for t in range(NT)], speed
            )
            for t in range(NT):
                GY[t, k, octet(o), :] = local[t] + before[t]
                XY[t, k, octet(o), :] = across_x[t] - low[t]
                YB[t, k, octet(o), :] = high[t]
        return carry

    lax.fori_loop(0, NZ, inside, 0, unroll=2)

    @pl.when(late_entry)
    def _():
        pl.semaphore_wait(barrier, expected)
        northward.start()

        @pl.when(relays_up)
        def _():
            handed_up.wait_recv()
            forwarded_up.start()

        eastward.start()
        pl.when(jnp.logical_not(after_seam))(westward.start)
        southward.start()

    @pl.when(after_seam)
    def _():
        pl.semaphore_wait(go_sem, 1)
        westward.start()

    def prepare(octets):
        def body(k, carry):
            level = k.astype(jnp.float32)
            down = jnp.minimum(k + 1, NZ - 1)
            for o in octets:
                open_below = bf[octet(o), :] > level + 1.0
                here = [T[t, k, octet(o), :] for t in range(NT)]
                step = [T[t, down, octet(o), :] - here[t] for t in range(NT)]
                mean_y = [GY[t, k, octet(o), :] + GY[t, down, octet(o), :] for t in range(NT)]
                inverse = jnp.where(
                    open_below, reciprocal(jnp.maximum(4.0 * density(step), 1.0)), 0.0
                )
                slope = jnp.clip(density(mean_y) * inverse, -1.0, 1.0)
                square = 0.1 * (slope * slope)
                slope = 0.025 * slope
                Q[k, octet(o), :] = inverse
                for t in range(NT):
                    FY[t, k, octet(o), :] = square * step[t] - slope * mean_y[t]
                    XY[t, k, octet(o), :] += here[t] + YB[t, k, shifted(o, -1), :]
            return carry

        lax.fori_loop(0, NZ, body, 0, unroll=2)

    inner, outer = tuple(range(1, OCTETS - 1)), (0, OCTETS - 1)
    prepare(inner)

    def edge_rows_in():
        southward.wait_recv()
        pl.when(jnp.logical_not(base))(northward.wait_recv)

        @pl.when(top)
        def _():
            for i in range(ROWS_FROM_NORTH // 8):
                value = from_north[pl.ds(8 * i, 8), :]
                for bit in (64, 32, 16, 8, 4, 2, 1):
                    value = jnp.where(
                        (lane & bit) != 0, pltpu.roll(value, bit, 1), pltpu.roll(value, CX - bit, 1)
                    )
                from_north[pl.ds(8 * i, 8), :] = jnp.where(
                    (row & 1) != 0, rows_down(value), rows_up(value)
                )

        def rows_in(k, carry):
            for t in range(NT):
                spot = pl.ds(2 * (NZ * t + k), 2)
                strip[t, k, pl.ds(2, 2), :] = from_north[spot, :]
                strip[t, k, pl.ds(4, 2), :] = from_south[spot, :]
            strip_v[k, pl.ds(5, 1), :] = from_south[pl.ds(72 + k, 1), :]
            return carry

        lax.fori_loop(0, NZ, rows_in, 0)
        strip_b[pl.ds(2, 2), :] = from_north[pl.ds(64, 2), :]
        strip_b[pl.ds(4, 2), :] = from_south[pl.ds(64, 2), :]

        def edge_rows(k, carry):
            level = k.astype(jnp.float32)
            above = jnp.where(k > 0, level, 99.0)
            down, up = jnp.minimum(k + 1, NZ - 1), jnp.maximum(k - 1, 0)
            depth = strip_b[...]
            here = [strip[t, k] for t in range(NT)]
            dz = [
                jnp.where(depth > level + 1.0, strip[t, down] - here[t], 0.0)
                + jnp.where(depth > above, here[t] - strip[t, up], 0.0)
                for t in range(NT)
            ]
            terms, grads = edge_terms(
                here, dz, depth, strip_v[k], level, rows_up, rows_down,
                row == 1, row == 5, row == 0, row == 6,
            )
            for t in range(NT):
                XY[t, k, octet(0), :] += jnp.where(row < 2, pltpu.roll(terms[t], 2, 0), 0.0)
                GY[t, k, octet(0), :] += jnp.where(row < 2, pltpu.roll(grads[t], 2, 0), 0.0)
                XY[t, k, octet(OCTETS - 1), :] += jnp.where(row > 5, pltpu.roll(terms[t], 6, 0), 0.0)
                GY[t, k, octet(OCTETS - 1), :] += jnp.where(row > 5, pltpu.roll(grads[t], 6, 0), 0.0)
            return carry

        lax.fori_loop(0, NZ, edge_rows, 0, unroll=8)

    rows_late = (below_middle | above_middle | (gy == n_gy // 2 - 2)) & jnp.logical_not(
        below_middle & (lax.rem(gx, BLOCK) == 1)
    )

    @pl.when(jnp.logical_not(rows_late))
    def _():
        edge_rows_in()
        prepare(outer)

    quarter = lax.rem(lane, 4)
    level_in_group = (lane // 32).astype(jnp.float32)
    def edge_columns_in(side, first):
        (eastward if side == 0 else westward).wait_recv()
        own = [[packed[4 * t + j] for j in range(4)] for t in range(NT)]
        if side == 0:
            depth = jnp.where(first_half, from_west[5], packed[12])
            fields = [
                [jnp.where(first_half, from_west[j], own[0][j]) for j in range(4)],
                [jnp.where(first_half, pltpu.roll(from_west[j], CX - 2, 1), own[1][j]) for j in range(4)],
            ]
        else:
            depth = jnp.where(first_half, packed[12], from_east[4])
            fields = [
                [jnp.where(first_half, own[0][j], from_east[j]) for j in range(4)],
                [jnp.where(first_half, own[1][j], pltpu.roll(from_east[j], 2, 1)) for j in range(4)],
            ]
        steps = []
        for t in range(NT):
            turned = [pltpu.roll(f, CX - 32, 1) for f in fields[t]]
            steps.append(
                [
                    jnp.where(
                        depth > level_in_group + (4 * j + 1.0),
                        jnp.where(lane < CX - 32, turned[j], turned[min(j + 1, 3)]) - fields[t][j],
                        0.0,
                    )
                    for j in range(4)
                ]
            )
        for j in range(4):
            dz = []
            for t in range(NT):
                before = pltpu.roll(steps[t][j - 1], 32, 1) if j > 0 else zeros
                dz.append(
                    steps[t][j] + jnp.where(lane < 32, before, pltpu.roll(steps[t][j], 32, 1))
                )
            speed = packed[8 + j]
            if side == 0:
                speed = jnp.where(first_half, pltpu.roll(from_west[4], (CX + 1 - j) % CX, 1), speed)
            terms, grads = edge_terms(
                [fields[t][j] for t in range(NT)], dz, depth, speed, level_in_group + 4.0 * j,
                lanes_left, lanes_right,
                None if side == 0 else quarter == 1, quarter == 1 if side == 0 else None,
                None if side == 0 else quarter == 0, quarter == 2 if side == 0 else None,
            )
            for t in range(NT):
                if first:
                    edge_c[t, j] = terms[t]
                    edge_g[t, j] = grads[t]
                else:
                    edge_c[t, j] += terms[t]
                    edge_g[t, j] += grads[t]

    even = lax.rem(gx, 2) == 0

    @pl.when(even)
    def _():
        edge_columns_in(1, True)
        edge_columns_in(0, False)

    @pl.when(jnp.logical_not(even))
    def _():
        edge_columns_in(0, True)
        edge_columns_in(1, False)

    at_edge = (lane < 2) | (lane >= CX - 2)

    def finish(octets, prepared):
        def at(o, ref, t, group, b):
            rolled = pltpu.roll(ref[t, group], (CX - (4 * (b * 8 + o) + 2)) % CX, 1)
            return jnp.where(at_edge, rolled, 0.0)

        def body(group, carry):
            fluxes = [[carry[4 * i], carry[4 * i + 1]] for i in range(len(octets))]
            gx_here = [[carry[4 * i + 2], carry[4 * i + 3]] for i in range(len(octets))]
            after = jnp.minimum(group + 1, 3)
            for b in range(4):
                k = 4 * group + b
                level = k.astype(jnp.float32)
                down = jnp.minimum(k + 1, NZ - 1)
                for i, o in enumerate(octets):
                    depth = bf[octet(o), :]
                    here = [T[t, k, octet(o), :] for t in range(NT)]
                    step = [T[t, down, octet(o), :] - here[t] for t in range(NT)]
                    gx_down = [
                        GX[t, down, octet(o), :]
                        + (at(o, edge_g, t, group, b + 1) if b < 3 else at(o, edge_g, t, after, 0))
                        for t in range(NT)
                    ]
                    mean_x = [gx_here[i][t] + gx_down[t] for t in range(NT)]
                    wet = depth > level
                    if prepared:
                        inverse = Q[k, octet(o), :]
                        other = [FY[t, k, octet(o), :] for t in range(NT)]
                        rest = [XY[t, k, octet(o), :] for t in range(NT)]
                    else:
                        mean_y = [
                            GY[t, k, octet(o), :] + GY[t, down, octet(o), :] for t in range(NT)
                        ]
                        inverse = jnp.where(
                            depth > level + 1.0, reciprocal(jnp.maximum(4.0 * density(step), 1.0)), 0.0
                        )
                        slope = jnp.clip(density(mean_y) * inverse, -1.0, 1.0)
                        square = 0.1 * (slope * slope)
                        slope = 0.025 * slope
                        other = [square * step[t] - slope * mean_y[t] for t in range(NT)]
                        rest = [
                            here[t] + (XY[t, k, octet(o), :] + YB[t, k, shifted(o, -1), :])
                            for t in range(NT)
                        ]
                    slope = jnp.clip(density(mean_x) * inverse, -1.0, 1.0)
                    square = 0.1 * (slope * slope)
                    slope = 0.025 * slope
                    for t in range(NT):
                        flux = other[t] + (square * step[t] - slope * mean_x[t])
                        total = (rest[t] + at(o, edge_c, t, group, b)) + (flux - fluxes[i][t])
                        out[t, k, pl.ds(8 * o, 8), :] = jnp.where(wet, total, 0.0)
                        fluxes[i][t] = flux
                    gx_here[i] = gx_down
            return tuple(x for i in range(len(octets)) for x in (*fluxes[i], *gx_here[i]))

        start = []
        for o in octets:
            start += [zeros, zeros]
            start += [GX[t, 0, octet(o), :] + at(o, edge_g, t, 0, 0) for t in range(NT)]
        lax.fori_loop(0, 4, body, tuple(start), unroll=2)

    finish(inner, True)

    @pl.when(rows_late)
    def _():
        edge_rows_in()
        finish(outer, False)

    @pl.when(jnp.logical_not(rows_late))
    def _():
        finish(outer, True)

    eastward.wait_send()
    westward.wait_send()
    pl.when(southward_itself)(southward.wait_send)
    pl.when(northward_itself)(northward.wait_send)
    pl.when(relayed_up)(handed_up.wait_send)
    pl.when(relayed_down)(handed_down.wait_send)
    pl.when(top)(across.wait_send)
    pl.when(relays_up)(forwarded_up.wait_send)
    pl.when(relays_down)(forwarded_down.wait_send)


def solution(mesh):
    n_gx, n_gy = mesh.shape["gx"], mesh.shape["gy"]
    f32 = jnp.float32
    in_hbm = pl.BlockSpec(memory_space=pltpu.HBM)
    field = pltpu.VMEM((NT, NZ, TALL, CX), f32)
    levels = pltpu.VMEM((NZ, CY, CX), f32)
    plane = pltpu.VMEM((TALL, CX), f32)
    packed = pltpu.VMEM((PACKED, 8, CX), f32)
    eastward = pltpu.VMEM((EASTWARD, 8, CX), f32)
    westward = pltpu.VMEM((WESTWARD, 8, CX), f32)
    from_south = pltpu.VMEM((ROWS_FROM_SOUTH, CX), f32)
    from_north = pltpu.VMEM((ROWS_FROM_NORTH, CX), f32)
    edge = pltpu.VMEM((NT, 4, 8, CX), f32)

    def on_device(tracers, east_speed, north_speed, bottom_level):
        return pl.pallas_call(
            functools.partial(kernel, n_gx, n_gy),
            out_shape=jax.ShapeDtypeStruct((NT, NZ, CY, CX), f32),
            in_specs=[in_hbm] * 4,
            out_specs=pl.BlockSpec(memory_space=pltpu.VMEM),
            scratch_shapes=[
                field, levels, levels, pltpu.VMEM((CY, CX), jnp.int32), plane, plane, plane,
                field, field, field, field, field, field, pltpu.VMEM((NZ, TALL, CX), f32),
                packed, eastward, westward, eastward, westward,
                from_south, from_north, from_north, from_south, from_south,
                pltpu.VMEM((NT, NZ, 8, CX), f32), pltpu.VMEM((8, CX), f32),
                pltpu.VMEM((NZ, 8, CX), f32), edge, edge,
                pltpu.SemaphoreType.DMA((7,)), pltpu.SemaphoreType.DMA((5,)),
                pltpu.SemaphoreType.DMA((5,)), pltpu.SemaphoreType.REGULAR,
            ],
            compiler_params=pltpu.CompilerParams(
                collective_id=0, has_side_effects=True, vmem_limit_bytes=24 * 1024 * 1024
            ),
        )(
            *[
                pltpu.with_memory_space_constraint(x, pltpu.HBM)
                for x in (tracers, east_speed, north_speed, bottom_level)
            ]
        )

    in_specs = (P(None, None, "gy", "gx"), P(None, "gy", "gx"), P(None, "gy", "gx"), P("gy", "gx"))
    return jax.shard_map(
        on_device, mesh=mesh, in_specs=in_specs, out_specs=P(None, None, "gy", "gx"), check_vma=False
    )
```

```python
import functools

import jax
import jax.numpy as jnp
from jax import lax
from jax.experimental import pallas as pl
from jax.experimental.pallas import tpu as pltpu
from jax.sharding import PartitionSpec as P

MESH = pl.DeviceIdType.MESH
NT, NZ, CY, CX = 2, 16, 48, 128
PAD = 8
TALL = CY + 2 * PAD
OCTETS = CY // 8
FOLD_ROWS = 72
OWN_LAST, FROM_NORTH, FROM_SOUTH, OWN_FIRST = (pl.ds(i, 2) for i in (0, 2, 4, 6))
PACKED = 13
EASTWARD = 6
WESTWARD = 5
BLOCK = 8
HEAT = 0.4
SALT = 0.6


def reciprocal(value):
    guess = pl.reciprocal(value, approx=True)
    return guess * (2.0 - value * guess)


def minmod(first, second):
    return jnp.maximum(jnp.minimum(first, second), 0.0) + jnp.minimum(
        jnp.maximum(first, second), 0.0
    )


def density(pair):
    return SALT * pair[1] - HEAT * pair[0]


def face_fluxes(local, before, after, dz_sum, speed):
    slope = jnp.clip(
        (0.1 * density(local)) * reciprocal(jnp.maximum(density(dz_sum), 1.0)), -0.025, 0.025
    )
    size = jnp.abs(speed)
    limited = 0.5 * size * (1.0 - size)
    forward = speed >= 0.0
    linear = jnp.minimum(speed, 0.0) - 0.1
    low, high, second = [], [], []
    for t in range(NT):
        correction = limited * minmod(local[t], jnp.where(forward, before[t], after[t]))
        taken = correction + (linear * local[t] + slope * dz_sum[t])
        low.append(taken)
        high.append(taken - speed * local[t])
        second.append(correction)
    return low, high, second, forward


def lanes_left(value):
    return pltpu.roll(value, CX - 1, 1)


def lanes_right(value):
    return pltpu.roll(value, 1, 1)


def rows_up(value):
    return pltpu.roll(value, 7, 0)


def rows_down(value):
    return pltpu.roll(value, 1, 0)


def edge_terms(field, dz, bottom, speed, level, nxt, prv, low_at, high_at, low_second, high_second):
    wet = jnp.minimum(bottom, nxt(bottom)) > level
    local = [jnp.where(wet, nxt(f) - f, 0.0) for f in field]
    dz_sum = [z + nxt(z) for z in dz]
    masked = jnp.where(wet, speed, 0.0)
    low, high, second, forward = face_fluxes(
        local, [prv(d) for d in local], [nxt(d) for d in local], dz_sum, masked
    )
    zero = jnp.zeros_like(masked)
    terms, steps = [], []
    for t in range(NT):
        late = zero
        if low_second is not None:
            late = late + jnp.where(low_second & ~forward, second[t], 0.0)
        if high_second is not None:
            late = late + jnp.where(high_second & forward, second[t], 0.0)
        arriving, term, step = late, -late, zero
        if high_at is not None:
            arriving = arriving + jnp.where(high_at, high[t], 0.0)
            step = step + prv(jnp.where(high_at, local[t], 0.0))
        if low_at is not None:
            term = term - jnp.where(low_at, low[t], 0.0)
            step = step + jnp.where(low_at, local[t], 0.0)
        terms.append(term + prv(arriving))
        steps.append(step)
    return terms, steps


def kernel(
    n_gx, n_gy,
    tracers, east, north, bottom, out,
    T, U, V, bottom_int, bf, be, bn, TZ, XY, YB, GX, GY, FY, Q,
    packed, to_east, to_west, from_west, from_east, relay, relay_b, relay_v, folded,
    strip, strip_b, strip_v, edge_c, edge_g,
    load_sem, send_sem, recv_sem, go_sem,
):
    gx, gy = lax.axis_index("gx"), lax.axis_index("gy")
    east_id = (lax.rem(gx + 1, n_gx), gy)
    west_id = (lax.rem(gx + n_gx - 1, n_gx), gy)
    north_id = (gx, gy + 1)
    south_id = (gx, gy - 1)
    mirror_id = (n_gx - 1 - gx, gy)
    top = gy == n_gy - 1
    base = gy == 0
    below_middle = gy == n_gy // 2 - 1
    above_middle = gy == n_gy // 2
    beside_middle = below_middle | above_middle
    after_seam = (lax.rem(gx, BLOCK) == 0) & beside_middle
    before_seam = (lax.rem(gx, BLOCK) == BLOCK - 1) & beside_middle
    relays = (lax.rem(gx, BLOCK) == BLOCK - 2) & beside_middle
    relayed_up = before_seam & below_middle
    relayed_down = before_seam & above_middle
    relays_up = relays & below_middle
    relays_down = relays & above_middle

    barrier = pltpu.get_barrier_semaphore()

    def greet(device):
        pl.semaphore_signal(barrier, inc=1, device_id=device, device_id_type=MESH)

    pl.when(top)(lambda: greet(mirror_id))
    pl.when(relayed_up)(lambda: greet((gx - 1, gy + 1)))
    pl.when(relayed_down)(lambda: greet((gx - 1, gy - 1)))
    pl.when(jnp.logical_not(top | relayed_up))(lambda: greet(north_id))
    pl.when(jnp.logical_not(base | relayed_down))(lambda: greet(south_id))
    greet(west_id)
    pl.when(jnp.logical_not(before_seam))(lambda: greet(east_id))
    expected = (
        4 + relays.astype(jnp.int32) - before_seam.astype(jnp.int32)
        - after_seam.astype(jnp.int32) - base.astype(jnp.int32)
    )

    def load(source, target, index):
        copy = pltpu.make_async_copy(source, target, load_sem.at[index])
        copy.start()
        return copy

    last_rows, first_rows = pl.ds(CY - 2, 2), pl.ds(0, 2)
    early = [
        load(tracers.at[:, :, last_rows, :], strip.at[:, :, OWN_LAST, :], 0),
        load(tracers.at[:, :, first_rows, :], strip.at[:, :, OWN_FIRST, :], 1),
        load(bottom.at[last_rows, :], strip_b.at[OWN_LAST, :], 2),
        load(bottom.at[first_rows, :], strip_b.at[OWN_FIRST, :], 3),
        load(north.at[:, last_rows, :], strip_v.at[:, OWN_LAST, :], 4),
        load(north.at[:, first_rows, :], strip_v.at[:, OWN_FIRST, :], 5),
    ]
    late = [
        load(tracers, T.at[:, :, pl.ds(PAD, CY), :], 6),
        load(bottom, bottom_int, 7),
        load(east, U, 8),
        load(north, V, 9),
    ]

    lane = lax.broadcasted_iota(jnp.int32, (8, CX), 1)
    row = lax.broadcasted_iota(jnp.int32, (8, CX), 0)
    zeros = jnp.zeros((8, CX), jnp.float32)

    def octet(o):
        return pl.ds(PAD + 8 * o, 8)

    def shifted(o, by):
        return pl.ds(PAD + 8 * o + by, 8)

    for pad in (pl.ds(0, PAD), pl.ds(PAD + CY, PAD)):
        bf[pad, :] = zeros
        bn[pad, :] = zeros

    def clear(k, carry):
        for t in range(NT):
            YB[t, k, pl.ds(0, PAD), :] = zeros
            TZ[t, k, pl.ds(PAD + CY, PAD), :] = zeros
        return carry

    lax.fori_loop(0, NZ, clear, 0)

    @pl.when(base)
    def _():
        strip_b[FROM_SOUTH, :] = jnp.zeros((2, CX), jnp.int32)
        for t in range(NT):
            for k in range(NZ):
                strip[t, k, FROM_SOUTH, :] = jnp.zeros((2, CX), jnp.float32)

    for copy in early:
        copy.wait()

    def send(source, target, index, slot, device):
        return pltpu.make_async_remote_copy(
            src_ref=source, dst_ref=target, send_sem=send_sem.at[index], recv_sem=recv_sem.at[slot],
            device_id=device, device_id_type=MESH,
        )

    def bundle(sources, targets, index, slot, device):
        pairs = enumerate(zip(sources, targets, strict=True))
        return [send(source, target, index + i, slot + i, device) for i, (source, target) in pairs]

    def start(copies):
        for copy in copies:
            copy.start()

    def wait_recv(copies):
        for copy in copies:
            copy.wait_recv()

    def wait_send(copies):
        for copy in copies:
            copy.wait_send()

    eastward = send(to_east, from_west, 0, 0, east_id)
    westward = send(to_west, from_east, 1, 1, west_id)
    last = [strip.at[:, :, OWN_LAST, :], strip_b.at[OWN_LAST, :], strip_v.at[:, pl.ds(1, 1), :]]
    first = [strip.at[:, :, OWN_FIRST, :], strip_b.at[OWN_FIRST, :]]
    from_south = [strip.at[:, :, FROM_SOUTH, :], strip_b.at[FROM_SOUTH, :], strip_v.at[:, pl.ds(5, 1), :]]
    from_north = [strip.at[:, :, FROM_NORTH, :], strip_b.at[FROM_NORTH, :]]
    between = [relay, relay_b, relay_v]
    northward = bundle(last, from_south, 2, 2, north_id)
    southward = bundle(first, from_north, 5, 5, south_id)
    across = bundle(last[:2], from_north, 2, 5, mirror_id)
    handed_up = bundle(last, between, 2, 7, west_id)
    handed_down = bundle(first, between[:2], 5, 7, west_id)
    forwarded_up = bundle(between, from_south, 7, 2, (gx + 1, gy + 1))
    forwarded_down = bundle(between[:2], from_north, 7, 5, (gx + 1, gy - 1))
    northward_itself = jnp.logical_not(top | relayed_up)
    southward_itself = jnp.logical_not(base | relayed_down)
    even = lax.rem(gx, 2) == 0
    late_entry = (below_middle & (lax.rem(gx, BLOCK) < BLOCK - 2)) | (
        (lax.rem(gx, BLOCK) == 0) & (gy < n_gy // 2 - 1)
    )

    @pl.when(jnp.logical_not(late_entry))
    def _():
        pl.semaphore_wait(barrier, expected)

        @pl.when(before_seam)
        def _():
            pl.semaphore_signal(go_sem, inc=1, device_id=east_id, device_id_type=MESH)

        pl.when(northward_itself & below_middle)(lambda: start(northward))
        pl.when(relayed_up)(lambda: start(handed_up))

        @pl.when(relays_up)
        def _():
            wait_recv(handed_up)
            start(forwarded_up)

        pl.when(southward_itself)(lambda: start(southward))
        pl.when(relayed_down)(lambda: start(handed_down))
        pl.when(northward_itself & jnp.logical_not(below_middle))(lambda: start(northward))
        pl.when(top)(lambda: start(across))

        @pl.when(relays_down)
        def _():
            wait_recv(handed_down)
            start(forwarded_down)

    def send_columns():
        pl.when(jnp.logical_not(even))(eastward.start)
        pl.when(jnp.logical_not(after_seam))(westward.start)
        pl.when(even)(eastward.start)

    for copy in late:
        copy.wait()

    for o in range(OCTETS):
        bf[octet(o), :] = bottom_int[pl.ds(8 * o, 8), :].astype(jnp.float32)
    for o in range(OCTETS):
        here = bf[octet(o), :]
        be[octet(o), :] = jnp.where(lane == CX - 1, 0.0, jnp.minimum(here, lanes_left(here)))
        bn[octet(o), :] = jnp.minimum(here, bf[shifted(o, 1), :])

    slot_of = lane // 4

    def pack(group, carry):
        t0, t1, speed = zeros, zeros, zeros
        for b in range(4):
            for o in range(OCTETS):
                slot = b * 8 + o
                here = slot_of == slot
                shift = (4 * slot + 2) % CX
                k = 4 * group + b
                t0 = jnp.where(here, pltpu.roll(T[0, k, octet(o), :], shift, 1), t0)
                t1 = jnp.where(here, pltpu.roll(T[1, k, octet(o), :], shift, 1), t1)
                speed = jnp.where(here, pltpu.roll(U[k, pl.ds(8 * o, 8), :], shift, 1), speed)
        packed[group] = t0
        packed[4 + group] = t1
        packed[8 + group] = speed
        return carry

    lax.fori_loop(0, 4, pack, 0, unroll=2)
    packed_b = zeros
    for b in range(4):
        for o in range(OCTETS):
            slot = b * 8 + o
            packed_b = jnp.where(
                slot_of == slot, pltpu.roll(bf[octet(o), :], (4 * slot + 2) % CX, 1), packed_b
            )
    packed[12] = packed_b

    first_half = lax.rem(lane, 4) < 2
    east_speeds = zeros
    for j in range(4):
        to_east[j] = jnp.where(first_half, packed[j], pltpu.roll(packed[4 + j], 2, 1))
        to_west[j] = jnp.where(first_half, pltpu.roll(packed[4 + j], CX - 2, 1), packed[j])
        east_speeds = jnp.where(
            lax.rem(lane, 4) == j, pltpu.roll(packed[8 + j], (CX + j - 1) % CX, 1), east_speeds
        )
    to_east[4] = east_speeds
    to_east[5] = packed_b
    to_west[4] = packed_b

    pl.when(jnp.logical_not(late_entry))(send_columns)

    def vertical(k, carry):
        level = k.astype(jnp.float32)
        above = jnp.where(k > 0, level, 99.0)
        down, up = jnp.minimum(k + 1, NZ - 1), jnp.maximum(k - 1, 0)
        for o in range(OCTETS):
            depth = bf[octet(o), :]
            for t in range(NT):
                here = T[t, k, octet(o), :]
                TZ[t, k, octet(o), :] = jnp.where(
                    depth > level + 1.0, T[t, down, octet(o), :] - here, 0.0
                ) + jnp.where(depth > above, here - T[t, up, octet(o), :], 0.0)
        return carry

    lax.fori_loop(0, NZ, vertical, 0, unroll=2)

    def inside(k, carry):
        level = k.astype(jnp.float32)
        for o in range(OCTETS):
            here = [T[t, k, octet(o), :] for t in range(NT)]
            dz = [TZ[t, k, octet(o), :] for t in range(NT)]
            wet = be[octet(o), :] > level
            local = [jnp.where(wet, lanes_left(f) - f, 0.0) for f in here]
            before = [lanes_right(d) for d in local]
            after = [lanes_left(d) for d in local]
            speed = jnp.where(wet, U[k, pl.ds(8 * o, 8), :], 0.0)
            low, high, _, _ = face_fluxes(
                local, before, after, [z + lanes_left(z) for z in dz], speed
            )
            across_x = [lanes_right(high[t]) - low[t] for t in range(NT)]
            for t in range(NT):
                GX[t, k, octet(o), :] = local[t] + before[t]

            wet = bn[octet(o), :] > level
            wet_before = bn[shifted(o, -1), :] > level
            wet_after = bn[shifted(o, 1), :] > level
            nxt = [T[t, k, shifted(o, 1), :] for t in range(NT)]
            local = [jnp.where(wet, nxt[t] - here[t], 0.0) for t in range(NT)]
            before = [
                jnp.where(wet_before, here[t] - T[t, k, shifted(o, -1), :], 0.0) for t in range(NT)
            ]
            after = [
                jnp.where(wet_after, T[t, k, shifted(o, 2), :] - nxt[t], 0.0) for t in range(NT)
            ]
            speed = jnp.where(wet, V[k, pl.ds(8 * o, 8), :], 0.0)
            low, high, _, _ = face_fluxes(
                local, before, after, [dz[t] + TZ[t, k, shifted(o, 1), :] for t in range(NT)], speed
            )
            for t in range(NT):
                GY[t, k, octet(o), :] = local[t] + before[t]
                XY[t, k, octet(o), :] = across_x[t] - low[t]
                YB[t, k, octet(o), :] = high[t]
        return carry

    lax.fori_loop(0, NZ, inside, 0, unroll=2)

    @pl.when(late_entry)
    def _():
        pl.semaphore_wait(barrier, expected)
        start(northward)
        send_columns()
        pl.when(jnp.logical_not(base))(lambda: start(southward))

    @pl.when(after_seam)
    def _():
        pl.semaphore_wait(go_sem, 1)
        westward.start()

    def prepare(octets):
        def body(k, carry):
            level = k.astype(jnp.float32)
            down = jnp.minimum(k + 1, NZ - 1)
            for o in octets:
                open_below = bf[octet(o), :] > level + 1.0
                here = [T[t, k, octet(o), :] for t in range(NT)]
                step = [T[t, down, octet(o), :] - here[t] for t in range(NT)]
                mean_y = [GY[t, k, octet(o), :] + GY[t, down, octet(o), :] for t in range(NT)]
                inverse = jnp.where(
                    open_below, reciprocal(jnp.maximum(4.0 * density(step), 1.0)), 0.0
                )
                slope = jnp.clip(density(mean_y) * inverse, -1.0, 1.0)
                square = 0.1 * (slope * slope)
                slope = 0.025 * slope
                Q[k, octet(o), :] = inverse
                for t in range(NT):
                    FY[t, k, octet(o), :] = square * step[t] - slope * mean_y[t]
                    XY[t, k, octet(o), :] += here[t] + YB[t, k, shifted(o, -1), :]
            return carry

        lax.fori_loop(0, NZ, body, 0, unroll=2)

    inner, outer = tuple(range(1, OCTETS - 1)), (0, OCTETS - 1)
    prepare(inner)

    def edge_rows_in():
        wait_recv(southward)
        pl.when(jnp.logical_not(base))(lambda: wait_recv(northward))

        @pl.when(top)
        def _():
            def gather(k, carry):
                for t in range(NT):
                    folded[pl.ds(2 * (NZ * t + k), 2), :] = strip[t, k, FROM_NORTH, :]
                return carry

            def scatter(k, carry):
                for t in range(NT):
                    strip[t, k, FROM_NORTH, :] = folded[pl.ds(2 * (NZ * t + k), 2), :]
                return carry

            lax.fori_loop(0, NZ, gather, 0, unroll=4)
            folded[pl.ds(64, 8), :] = strip_b[...].astype(jnp.float32)
            for i in range(FOLD_ROWS // 8):
                value = folded[pl.ds(8 * i, 8), :]
                for bit in (64, 32, 16, 8, 4, 2, 1):
                    value = jnp.where(
                        (lane & bit) != 0, pltpu.roll(value, bit, 1), pltpu.roll(value, CX - bit, 1)
                    )
                folded[pl.ds(8 * i, 8), :] = jnp.where(
                    (row & 1) != 0, rows_down(value), rows_up(value)
                )
            lax.fori_loop(0, NZ, scatter, 0, unroll=4)
            strip_b[FROM_NORTH, :] = folded[pl.ds(66, 2), :].astype(jnp.int32)

        def edge_rows(k, carry):
            level = k.astype(jnp.float32)
            above = jnp.where(k > 0, level, 99.0)
            down, up = jnp.minimum(k + 1, NZ - 1), jnp.maximum(k - 1, 0)
            depth = strip_b[...].astype(jnp.float32)
            here = [strip[t, k] for t in range(NT)]
            dz = [
                jnp.where(depth > level + 1.0, strip[t, down] - here[t], 0.0)
                + jnp.where(depth > above, here[t] - strip[t, up], 0.0)
                for t in range(NT)
            ]
            terms, grads = edge_terms(
                here, dz, depth, strip_v[k], level, rows_up, rows_down,
                row == 1, row == 5, row == 0, row == 6,
            )
            for t in range(NT):
                XY[t, k, octet(0), :] += jnp.where(row < 2, pltpu.roll(terms[t], 2, 0), 0.0)
                GY[t, k, octet(0), :] += jnp.where(row < 2, pltpu.roll(grads[t], 2, 0), 0.0)
                XY[t, k, octet(OCTETS - 1), :] += jnp.where(row > 5, pltpu.roll(terms[t], 6, 0), 0.0)
                GY[t, k, octet(OCTETS - 1), :] += jnp.where(row > 5, pltpu.roll(grads[t], 6, 0), 0.0)
            return carry

        lax.fori_loop(0, NZ, edge_rows, 0, unroll=8)

    rows_late = (below_middle | above_middle | (gy == n_gy // 2 - 2)) & jnp.logical_not(
        below_middle & (lax.rem(gx, BLOCK) == 1)
    )

    @pl.when(jnp.logical_not(rows_late))
    def _():
        edge_rows_in()
        prepare(outer)

    quarter = lax.rem(lane, 4)
    level_in_group = (lane // 32).astype(jnp.float32)
    def edge_columns_in(side, first):
        (eastward if side == 0 else westward).wait_recv()
        own = [[packed[4 * t + j] for j in range(4)] for t in range(NT)]
        if side == 0:
            depth = jnp.where(first_half, from_west[5], packed[12])
            fields = [
                [jnp.where(first_half, from_west[j], own[0][j]) for j in range(4)],
                [jnp.where(first_half, pltpu.roll(from_west[j], CX - 2, 1), own[1][j]) for j in range(4)],
            ]
        else:
            depth = jnp.where(first_half, packed[12], from_east[4])
            fields = [
                [jnp.where(first_half, own[0][j], from_east[j]) for j in range(4)],
                [jnp.where(first_half, own[1][j], pltpu.roll(from_east[j], 2, 1)) for j in range(4)],
            ]
        steps = []
        for t in range(NT):
            turned = [pltpu.roll(f, CX - 32, 1) for f in fields[t]]
            steps.append(
                [
                    jnp.where(
                        depth > level_in_group + (4 * j + 1.0),
                        jnp.where(lane < CX - 32, turned[j], turned[min(j + 1, 3)]) - fields[t][j],
                        0.0,
                    )
                    for j in range(4)
                ]
            )
        for j in range(4):
            dz = []
            for t in range(NT):
                before = pltpu.roll(steps[t][j - 1], 32, 1) if j > 0 else zeros
                dz.append(
                    steps[t][j] + jnp.where(lane < 32, before, pltpu.roll(steps[t][j], 32, 1))
                )
            speed = packed[8 + j]
            if side == 0:
                speed = jnp.where(first_half, pltpu.roll(from_west[4], (CX + 1 - j) % CX, 1), speed)
            terms, grads = edge_terms(
                [fields[t][j] for t in range(NT)], dz, depth, speed, level_in_group + 4.0 * j,
                lanes_left, lanes_right,
                None if side == 0 else quarter == 1, quarter == 1 if side == 0 else None,
                None if side == 0 else quarter == 0, quarter == 2 if side == 0 else None,
            )
            for t in range(NT):
                if first:
                    edge_c[t, j] = terms[t]
                    edge_g[t, j] = grads[t]
                else:
                    edge_c[t, j] += terms[t]
                    edge_g[t, j] += grads[t]

    @pl.when(even)
    def _():
        edge_columns_in(1, True)
        edge_columns_in(0, False)

    @pl.when(jnp.logical_not(even))
    def _():
        edge_columns_in(0, True)
        edge_columns_in(1, False)

    at_edge = (lane < 2) | (lane >= CX - 2)

    def finish(octets, prepared):
        def at(o, ref, t, group, b):
            rolled = pltpu.roll(ref[t, group], (CX - (4 * (b * 8 + o) + 2)) % CX, 1)
            return jnp.where(at_edge, rolled, 0.0)

        def body(group, carry):
            fluxes = [[carry[4 * i], carry[4 * i + 1]] for i in range(len(octets))]
            gx_here = [[carry[4 * i + 2], carry[4 * i + 3]] for i in range(len(octets))]
            after = jnp.minimum(group + 1, 3)
            for b in range(4):
                k = 4 * group + b
                level = k.astype(jnp.float32)
                down = jnp.minimum(k + 1, NZ - 1)
                for i, o in enumerate(octets):
                    depth = bf[octet(o), :]
                    here = [T[t, k, octet(o), :] for t in range(NT)]
                    step = [T[t, down, octet(o), :] - here[t] for t in range(NT)]
                    gx_down = [
                        GX[t, down, octet(o), :]
                        + (at(o, edge_g, t, group, b + 1) if b < 3 else at(o, edge_g, t, after, 0))
                        for t in range(NT)
                    ]
                    mean_x = [gx_here[i][t] + gx_down[t] for t in range(NT)]
                    wet = depth > level
                    if prepared:
                        inverse = Q[k, octet(o), :]
                        other = [FY[t, k, octet(o), :] for t in range(NT)]
                        rest = [XY[t, k, octet(o), :] for t in range(NT)]
                    else:
                        mean_y = [
                            GY[t, k, octet(o), :] + GY[t, down, octet(o), :] for t in range(NT)
                        ]
                        inverse = jnp.where(
                            depth > level + 1.0, reciprocal(jnp.maximum(4.0 * density(step), 1.0)), 0.0
                        )
                        slope = jnp.clip(density(mean_y) * inverse, -1.0, 1.0)
                        square = 0.1 * (slope * slope)
                        slope = 0.025 * slope
                        other = [square * step[t] - slope * mean_y[t] for t in range(NT)]
                        rest = [
                            here[t] + (XY[t, k, octet(o), :] + YB[t, k, shifted(o, -1), :])
                            for t in range(NT)
                        ]
                    slope = jnp.clip(density(mean_x) * inverse, -1.0, 1.0)
                    square = 0.1 * (slope * slope)
                    slope = 0.025 * slope
                    for t in range(NT):
                        flux = other[t] + (square * step[t] - slope * mean_x[t])
                        total = (rest[t] + at(o, edge_c, t, group, b)) + (flux - fluxes[i][t])
                        out[t, k, pl.ds(8 * o, 8), :] = jnp.where(wet, total, 0.0)
                        fluxes[i][t] = flux
                    gx_here[i] = gx_down
            return tuple(x for i in range(len(octets)) for x in (*fluxes[i], *gx_here[i]))

        start = []
        for o in octets:
            start += [zeros, zeros]
            start += [GX[t, 0, octet(o), :] + at(o, edge_g, t, 0, 0) for t in range(NT)]
        lax.fori_loop(0, 4, body, tuple(start), unroll=2)

    finish(inner, True)

    @pl.when(rows_late)
    def _():
        edge_rows_in()
        finish(outer, False)

    @pl.when(jnp.logical_not(rows_late))
    def _():
        finish(outer, True)

    eastward.wait_send()
    westward.wait_send()
    pl.when(southward_itself)(lambda: wait_send(southward))
    pl.when(northward_itself)(lambda: wait_send(northward))
    pl.when(relayed_up)(lambda: wait_send(handed_up))
    pl.when(relayed_down)(lambda: wait_send(handed_down))
    pl.when(top)(lambda: wait_send(across))
    pl.when(relays_up)(lambda: wait_send(forwarded_up))
    pl.when(relays_down)(lambda: wait_send(forwarded_down))


def solution(mesh):
    n_gx, n_gy = mesh.shape["gx"], mesh.shape["gy"]
    f32 = jnp.float32
    in_hbm = pl.BlockSpec(memory_space=pltpu.HBM)
    field = pltpu.VMEM((NT, NZ, TALL, CX), f32)
    levels = pltpu.VMEM((NZ, CY, CX), f32)
    plane = pltpu.VMEM((TALL, CX), f32)
    packed = pltpu.VMEM((PACKED, 8, CX), f32)
    eastward = pltpu.VMEM((EASTWARD, 8, CX), f32)
    westward = pltpu.VMEM((WESTWARD, 8, CX), f32)
    edge = pltpu.VMEM((NT, 4, 8, CX), f32)

    def on_device(tracers, east_speed, north_speed, bottom_level):
        return pl.pallas_call(
            functools.partial(kernel, n_gx, n_gy),
            out_shape=jax.ShapeDtypeStruct((NT, NZ, CY, CX), f32),
            in_specs=[in_hbm] * 4,
            out_specs=pl.BlockSpec(memory_space=pltpu.VMEM),
            scratch_shapes=[
                field, levels, levels, pltpu.VMEM((CY, CX), jnp.int32), plane, plane, plane,
                field, field, field, field, field, field, pltpu.VMEM((NZ, TALL, CX), f32),
                packed, eastward, westward, eastward, westward,
                pltpu.VMEM((NT, NZ, 2, CX), f32), pltpu.VMEM((2, CX), jnp.int32),
                pltpu.VMEM((NZ, 1, CX), f32), pltpu.VMEM((FOLD_ROWS, CX), f32),
                pltpu.VMEM((NT, NZ, 8, CX), f32), pltpu.VMEM((8, CX), jnp.int32),
                pltpu.VMEM((NZ, 8, CX), f32), edge, edge,
                pltpu.SemaphoreType.DMA((10,)), pltpu.SemaphoreType.DMA((10,)),
                pltpu.SemaphoreType.DMA((10,)), pltpu.SemaphoreType.REGULAR,
            ],
            compiler_params=pltpu.CompilerParams(
                collective_id=0, has_side_effects=True, vmem_limit_bytes=24 * 1024 * 1024
            ),
        )(
            *[
                pltpu.with_memory_space_constraint(x, pltpu.HBM)
                for x in (tracers, east_speed, north_speed, bottom_level)
            ]
        )

    in_specs = (P(None, None, "gy", "gx"), P(None, "gy", "gx"), P(None, "gy", "gx"), P("gy", "gx"))
    return jax.shard_map(
        on_device, mesh=mesh, in_specs=in_specs, out_specs=P(None, None, "gy", "gx"), check_vma=False
    )
```

```python
import functools

import jax
import jax.numpy as jnp
from jax import lax
from jax.experimental import pallas as pl
from jax.experimental.pallas import tpu as pltpu
from jax.sharding import PartitionSpec as P

MESH = pl.DeviceIdType.MESH
NT, NZ, CY, CX = 2, 16, 48, 128
PAD = 8
TALL = CY + 2 * PAD
OCTETS = CY // 8
FOLD_ROWS = 72
OWN_LAST, FROM_NORTH, FROM_SOUTH, OWN_FIRST = (pl.ds(i, 2) for i in (0, 2, 4, 6))
PACKED = 13
EASTWARD = 6
WESTWARD = 5
BLOCK = 8
HEAT = 0.4
SALT = 0.6


def reciprocal(value):
    guess = pl.reciprocal(value, approx=True)
    return guess * (2.0 - value * guess)


def minmod(first, second):
    return jnp.maximum(jnp.minimum(first, second), 0.0) + jnp.minimum(
        jnp.maximum(first, second), 0.0
    )


def density(pair):
    return SALT * pair[1] - HEAT * pair[0]


def face_fluxes(local, before, after, dz_sum, speed):
    slope = jnp.clip(
        (0.1 * density(local)) * reciprocal(jnp.maximum(density(dz_sum), 1.0)), -0.025, 0.025
    )
    size = jnp.abs(speed)
    limited = 0.5 * size * (1.0 - size)
    forward = speed >= 0.0
    linear = jnp.minimum(speed, 0.0) - 0.1
    low, high, second = [], [], []
    for t in range(NT):
        correction = limited * minmod(local[t], jnp.where(forward, before[t], after[t]))
        taken = correction + (linear * local[t] + slope * dz_sum[t])
        low.append(taken)
        high.append(taken - speed * local[t])
        second.append(correction)
    return low, high, second, forward


def lanes_left(value):
    return pltpu.roll(value, CX - 1, 1)


def lanes_right(value):
    return pltpu.roll(value, 1, 1)


def rows_up(value):
    return pltpu.roll(value, 7, 0)


def rows_down(value):
    return pltpu.roll(value, 1, 0)


def edge_terms(field, dz, bottom, speed, level, nxt, prv, low_at, high_at, low_second, high_second):
    wet = jnp.minimum(bottom, nxt(bottom)) > level
    local = [jnp.where(wet, nxt(f) - f, 0.0) for f in field]
    dz_sum = [z + nxt(z) for z in dz]
    masked = jnp.where(wet, speed, 0.0)
    low, high, second, forward = face_fluxes(
        local, [prv(d) for d in local], [nxt(d) for d in local], dz_sum, masked
    )
    zero = jnp.zeros_like(masked)
    terms, steps = [], []
    for t in range(NT):
        late = zero
        if low_second is not None:
            late = late + jnp.where(low_second & ~forward, second[t], 0.0)
        if high_second is not None:
            late = late + jnp.where(high_second & forward, second[t], 0.0)
        arriving, term, step = late, -late, zero
        if high_at is not None:
            arriving = arriving + jnp.where(high_at, high[t], 0.0)
            step = step + prv(jnp.where(high_at, local[t], 0.0))
        if low_at is not None:
            term = term - jnp.where(low_at, low[t], 0.0)
            step = step + jnp.where(low_at, local[t], 0.0)
        terms.append(term + prv(arriving))
        steps.append(step)
    return terms, steps


def kernel(
    n_gx, n_gy,
    tracers, east, north, bottom, out,
    T, U, V, bottom_int, bf, be, bn, TZ, XY, YB, GX, GY, FY, Q,
    packed, to_east, to_west, from_west, from_east, relay, relay_b, relay_v, folded,
    strip, strip_b, strip_v, edge_c, edge_g,
    load_sem, send_sem, recv_sem, go_sem,
):
    gx, gy = lax.axis_index("gx"), lax.axis_index("gy")
    east_id = (lax.rem(gx + 1, n_gx), gy)
    west_id = (lax.rem(gx + n_gx - 1, n_gx), gy)
    north_id = (gx, gy + 1)
    south_id = (gx, gy - 1)
    mirror_id = (n_gx - 1 - gx, gy)
    top = gy == n_gy - 1
    base = gy == 0
    below_middle = gy == n_gy // 2 - 1
    above_middle = gy == n_gy // 2
    place = lax.rem(gx, BLOCK)
    by_go = gy <= n_gy // 2
    after_seam = (place == 0) & by_go
    before_seam = (place == BLOCK - 1) & by_go
    crosses_down = place == BLOCK - 1
    crosses_up = crosses_down | (place == 2)
    relayed_up = crosses_up & below_middle
    relayed_down = crosses_down & above_middle
    relays_up = ((place == BLOCK - 2) | (place == 3)) & below_middle
    relays_down = (place == BLOCK - 2) & above_middle
    chip_mate = gx + 1 - 2 * lax.rem(gx, 2)

    barrier = pltpu.get_barrier_semaphore()

    def greet(device):
        pl.semaphore_signal(barrier, inc=1, device_id=device, device_id_type=MESH)

    pl.when(top)(lambda: greet(mirror_id))
    mate_sends_down = crosses_down & below_middle
    mate_sends_up = crosses_up & above_middle
    pl.when(mate_sends_down)(lambda: greet((chip_mate, gy + 1)))
    pl.when(mate_sends_up)(lambda: greet((chip_mate, gy - 1)))
    pl.when(jnp.logical_not(top | mate_sends_down))(lambda: greet(north_id))
    pl.when(jnp.logical_not(base | mate_sends_up))(lambda: greet(south_id))
    greet(west_id)
    pl.when(jnp.logical_not(before_seam))(lambda: greet(east_id))
    expected = (
        4 + (relays_up | relays_down).astype(jnp.int32) - (relayed_up | relayed_down).astype(jnp.int32)
        - after_seam.astype(jnp.int32) - base.astype(jnp.int32)
    )

    def load(source, target, index):
        copy = pltpu.make_async_copy(source, target, load_sem.at[index])
        copy.start()
        return copy

    last_rows, first_rows = pl.ds(CY - 2, 2), pl.ds(0, 2)
    early = [
        load(tracers.at[:, :, last_rows, :], strip.at[:, :, OWN_LAST, :], 0),
        load(tracers.at[:, :, first_rows, :], strip.at[:, :, OWN_FIRST, :], 1),
        load(bottom.at[last_rows, :], strip_b.at[OWN_LAST, :], 2),
        load(bottom.at[first_rows, :], strip_b.at[OWN_FIRST, :], 3),
        load(north.at[:, last_rows, :], strip_v.at[:, OWN_LAST, :], 4),
        load(north.at[:, first_rows, :], strip_v.at[:, OWN_FIRST, :], 5),
    ]
    late = [
        load(tracers, T.at[:, :, pl.ds(PAD, CY), :], 6),
        load(bottom, bottom_int, 7),
        load(east, U, 8),
        load(north, V, 9),
    ]

    lane = lax.broadcasted_iota(jnp.int32, (8, CX), 1)
    row = lax.broadcasted_iota(jnp.int32, (8, CX), 0)
    zeros = jnp.zeros((8, CX), jnp.float32)

    def octet(o):
        return pl.ds(PAD + 8 * o, 8)

    def shifted(o, by):
        return pl.ds(PAD + 8 * o + by, 8)

    for pad in (pl.ds(0, PAD), pl.ds(PAD + CY, PAD)):
        bf[pad, :] = zeros
        bn[pad, :] = zeros

    def clear(k, carry):
        for t in range(NT):
            YB[t, k, pl.ds(0, PAD), :] = zeros
            TZ[t, k, pl.ds(PAD + CY, PAD), :] = zeros
        return carry

    lax.fori_loop(0, NZ, clear, 0)

    @pl.when(base)
    def _():
        strip_b[FROM_SOUTH, :] = jnp.zeros((2, CX), jnp.int32)
        for t in range(NT):
            for k in range(NZ):
                strip[t, k, FROM_SOUTH, :] = jnp.zeros((2, CX), jnp.float32)

    for copy in early:
        copy.wait()

    def send(source, target, index, slot, device):
        return pltpu.make_async_remote_copy(
            src_ref=source, dst_ref=target, send_sem=send_sem.at[index], recv_sem=recv_sem.at[slot],
            device_id=device, device_id_type=MESH,
        )

    def bundle(sources, targets, index, slot, device):
        pairs = enumerate(zip(sources, targets, strict=True))
        return [send(source, target, index + i, slot + i, device) for i, (source, target) in pairs]

    def start(copies):
        for copy in copies:
            copy.start()

    def wait_recv(copies):
        for copy in copies:
            copy.wait_recv()

    def wait_send(copies):
        for copy in copies:
            copy.wait_send()

    eastward = send(to_east, from_west, 0, 0, east_id)
    westward = send(to_west, from_east, 1, 1, west_id)
    last = [strip.at[:, :, OWN_LAST, :], strip_b.at[OWN_LAST, :], strip_v.at[:, pl.ds(1, 1), :]]
    first = [strip.at[:, :, OWN_FIRST, :], strip_b.at[OWN_FIRST, :]]
    from_south = [strip.at[:, :, FROM_SOUTH, :], strip_b.at[FROM_SOUTH, :], strip_v.at[:, pl.ds(5, 1), :]]
    from_north = [strip.at[:, :, FROM_NORTH, :], strip_b.at[FROM_NORTH, :]]
    between = [relay, relay_b, relay_v]
    northward = bundle(last, from_south, 2, 2, north_id)
    southward = bundle(first, from_north, 5, 5, south_id)
    across = bundle(last[:2], from_north, 2, 5, mirror_id)
    handed_up = bundle(last, between, 2, 7, (chip_mate, gy))
    handed_down = bundle(first, between[:2], 5, 7, (chip_mate, gy))
    forwarded_up = bundle(between, from_south, 7, 2, (chip_mate, gy + 1))
    forwarded_down = bundle(between[:2], from_north, 7, 5, (chip_mate, gy - 1))
    northward_itself = jnp.logical_not(top | relayed_up)
    southward_itself = jnp.logical_not(base | relayed_down)
    even = lax.rem(gx, 2) == 0
    late_entry = below_middle & jnp.logical_not(relayed_up) & (place < BLOCK - 2)

    @pl.when(jnp.logical_not(late_entry))
    def _():
        pl.semaphore_wait(barrier, expected)

        @pl.when(before_seam)
        def _():
            pl.semaphore_signal(go_sem, inc=1, device_id=east_id, device_id_type=MESH)

        pl.when(northward_itself & below_middle)(lambda: start(northward))
        pl.when(relayed_up)(lambda: start(handed_up))

        @pl.when(relays_up)
        def _():
            wait_recv(handed_up)
            start(forwarded_up)

        pl.when(southward_itself)(lambda: start(southward))
        pl.when(relayed_down)(lambda: start(handed_down))
        pl.when(northward_itself & jnp.logical_not(below_middle))(lambda: start(northward))
        pl.when(top)(lambda: start(across))

        @pl.when(relays_down)
        def _():
            wait_recv(handed_down)
            start(forwarded_down)

    def send_columns():
        pl.when(jnp.logical_not(even))(eastward.start)
        pl.when(jnp.logical_not(after_seam))(westward.start)
        pl.when(even)(eastward.start)

    for copy in late:
        copy.wait()

    for o in range(OCTETS):
        bf[octet(o), :] = bottom_int[pl.ds(8 * o, 8), :].astype(jnp.float32)
    for o in range(OCTETS):
        here = bf[octet(o), :]
        be[octet(o), :] = jnp.where(lane == CX - 1, 0.0, jnp.minimum(here, lanes_left(here)))
        bn[octet(o), :] = jnp.minimum(here, bf[shifted(o, 1), :])

    slot_of = lane // 4

    def pack(group, carry):
        t0, t1, speed = zeros, zeros, zeros
        for b in range(4):
            for o in range(OCTETS):
                slot = b * 8 + o
                here = slot_of == slot
                shift = (4 * slot + 2) % CX
                k = 4 * group + b
                t0 = jnp.where(here, pltpu.roll(T[0, k, octet(o), :], shift, 1), t0)
                t1 = jnp.where(here, pltpu.roll(T[1, k, octet(o), :], shift, 1), t1)
                speed = jnp.where(here, pltpu.roll(U[k, pl.ds(8 * o, 8), :], shift, 1), speed)
        packed[group] = t0
        packed[4 + group] = t1
        packed[8 + group] = speed
        return carry

    lax.fori_loop(0, 4, pack, 0, unroll=2)
    packed_b = zeros
    for b in range(4):
        for o in range(OCTETS):
            slot = b * 8 + o
            packed_b = jnp.where(
                slot_of == slot, pltpu.roll(bf[octet(o), :], (4 * slot + 2) % CX, 1), packed_b
            )
    packed[12] = packed_b

    first_half = lax.rem(lane, 4) < 2
    east_speeds = zeros
    for j in range(4):
        to_east[j] = jnp.where(first_half, packed[j], pltpu.roll(packed[4 + j], 2, 1))
        to_west[j] = jnp.where(first_half, pltpu.roll(packed[4 + j], CX - 2, 1), packed[j])
        east_speeds = jnp.where(
            lax.rem(lane, 4) == j, pltpu.roll(packed[8 + j], (CX + j - 1) % CX, 1), east_speeds
        )
    to_east[4] = east_speeds
    to_east[5] = packed_b
    to_west[4] = packed_b

    pl.when(jnp.logical_not(late_entry))(send_columns)

    def vertical(k, carry):
        level = k.astype(jnp.float32)
        above = jnp.where(k > 0, level, 99.0)
        down, up = jnp.minimum(k + 1, NZ - 1), jnp.maximum(k - 1, 0)
        for o in range(OCTETS):
            depth = bf[octet(o), :]
            for t in range(NT):
                here = T[t, k, octet(o), :]
                TZ[t, k, octet(o), :] = jnp.where(
                    depth > level + 1.0, T[t, down, octet(o), :] - here, 0.0
                ) + jnp.where(depth > above, here - T[t, up, octet(o), :], 0.0)
        return carry

    lax.fori_loop(0, NZ, vertical, 0, unroll=2)

    def inside(k, carry):
        level = k.astype(jnp.float32)
        for o in range(OCTETS):
            here = [T[t, k, octet(o), :] for t in range(NT)]
            dz = [TZ[t, k, octet(o), :] for t in range(NT)]
            wet = be[octet(o), :] > level
            local = [jnp.where(wet, lanes_left(f) - f, 0.0) for f in here]
            before = [lanes_right(d) for d in local]
            after = [lanes_left(d) for d in local]
            speed = jnp.where(wet, U[k, pl.ds(8 * o, 8), :], 0.0)
            low, high, _, _ = face_fluxes(
                local, before, after, [z + lanes_left(z) for z in dz], speed
            )
            across_x = [lanes_right(high[t]) - low[t] for t in range(NT)]
            for t in range(NT):
                GX[t, k, octet(o), :] = local[t] + before[t]

            wet = bn[octet(o), :] > level
            wet_before = bn[shifted(o, -1), :] > level
            wet_after = bn[shifted(o, 1), :] > level
            nxt = [T[t, k, shifted(o, 1), :] for t in range(NT)]
            local = [jnp.where(wet, nxt[t] - here[t], 0.0) for t in range(NT)]
            before = [
                jnp.where(wet_before, here[t] - T[t, k, shifted(o, -1), :], 0.0) for t in range(NT)
            ]
            after = [
                jnp.where(wet_after, T[t, k, shifted(o, 2), :] - nxt[t], 0.0) for t in range(NT)
            ]
            speed = jnp.where(wet, V[k, pl.ds(8 * o, 8), :], 0.0)
            low, high, _, _ = face_fluxes(
                local, before, after, [dz[t] + TZ[t, k, shifted(o, 1), :] for t in range(NT)], speed
            )
            for t in range(NT):
                GY[t, k, octet(o), :] = local[t] + before[t]
                XY[t, k, octet(o), :] = across_x[t] - low[t]
                YB[t, k, octet(o), :] = high[t]
        return carry

    lax.fori_loop(0, NZ, inside, 0, unroll=2)

    @pl.when(late_entry)
    def _():
        pl.semaphore_wait(barrier, expected)
        start(northward)

        @pl.when(relays_up)
        def _():
            wait_recv(handed_up)
            start(forwarded_up)

        send_columns()
        start(southward)

    @pl.when(after_seam)
    def _():
        pl.semaphore_wait(go_sem, 1)
        westward.start()

    def prepare(octets):
        def body(k, carry):
            level = k.astype(jnp.float32)
            down = jnp.minimum(k + 1, NZ - 1)
            for o in octets:
                open_below = bf[octet(o), :] > level + 1.0
                here = [T[t, k, octet(o), :] for t in range(NT)]
                step = [T[t, down, octet(o), :] - here[t] for t in range(NT)]
                mean_y = [GY[t, k, octet(o), :] + GY[t, down, octet(o), :] for t in range(NT)]
                inverse = jnp.where(
                    open_below, reciprocal(jnp.maximum(4.0 * density(step), 1.0)), 0.0
                )
                slope = jnp.clip(density(mean_y) * inverse, -1.0, 1.0)
                square = 0.1 * (slope * slope)
                slope = 0.025 * slope
                Q[k, octet(o), :] = inverse
                for t in range(NT):
                    FY[t, k, octet(o), :] = square * step[t] - slope * mean_y[t]
                    XY[t, k, octet(o), :] += here[t] + YB[t, k, shifted(o, -1), :]
            return carry

        lax.fori_loop(0, NZ, body, 0, unroll=2)

    inner, outer = tuple(range(1, OCTETS - 1)), (0, OCTETS - 1)
    prepare(inner)

    def edge_rows_in():
        wait_recv(southward)
        pl.when(jnp.logical_not(base))(lambda: wait_recv(northward))

        @pl.when(top)
        def _():
            def gather(k, carry):
                for t in range(NT):
                    folded[pl.ds(2 * (NZ * t + k), 2), :] = strip[t, k, FROM_NORTH, :]
                return carry

            def scatter(k, carry):
                for t in range(NT):
                    strip[t, k, FROM_NORTH, :] = folded[pl.ds(2 * (NZ * t + k), 2), :]
                return carry

            lax.fori_loop(0, NZ, gather, 0, unroll=4)
            folded[pl.ds(64, 8), :] = strip_b[...].astype(jnp.float32)
            for i in range(FOLD_ROWS // 8):
                value = folded[pl.ds(8 * i, 8), :]
                for bit in (64, 32, 16, 8, 4, 2, 1):
                    value = jnp.where(
                        (lane & bit) != 0, pltpu.roll(value, bit, 1), pltpu.roll(value, CX - bit, 1)
                    )
                folded[pl.ds(8 * i, 8), :] = jnp.where(
                    (row & 1) != 0, rows_down(value), rows_up(value)
                )
            lax.fori_loop(0, NZ, scatter, 0, unroll=4)
            strip_b[FROM_NORTH, :] = folded[pl.ds(66, 2), :].astype(jnp.int32)

        def edge_rows(k, carry):
            level = k.astype(jnp.float32)
            above = jnp.where(k > 0, level, 99.0)
            down, up = jnp.minimum(k + 1, NZ - 1), jnp.maximum(k - 1, 0)
            depth = strip_b[...].astype(jnp.float32)
            here = [strip[t, k] for t in range(NT)]
            dz = [
                jnp.where(depth > level + 1.0, strip[t, down] - here[t], 0.0)
                + jnp.where(depth > above, here[t] - strip[t, up], 0.0)
                for t in range(NT)
            ]
            terms, grads = edge_terms(
                here, dz, depth, strip_v[k], level, rows_up, rows_down,
                row == 1, row == 5, row == 0, row == 6,
            )
            for t in range(NT):
                XY[t, k, octet(0), :] += jnp.where(row < 2, pltpu.roll(terms[t], 2, 0), 0.0)
                GY[t, k, octet(0), :] += jnp.where(row < 2, pltpu.roll(grads[t], 2, 0), 0.0)
                XY[t, k, octet(OCTETS - 1), :] += jnp.where(row > 5, pltpu.roll(terms[t], 6, 0), 0.0)
                GY[t, k, octet(OCTETS - 1), :] += jnp.where(row > 5, pltpu.roll(grads[t], 6, 0), 0.0)
            return carry

        lax.fori_loop(0, NZ, edge_rows, 0, unroll=8)

    rows_late = below_middle | above_middle | (gy == n_gy // 2 - 2)

    @pl.when(jnp.logical_not(rows_late))
    def _():
        edge_rows_in()
        prepare(outer)

    quarter = lax.rem(lane, 4)
    level_in_group = (lane // 32).astype(jnp.float32)
    def edge_columns_in(side, first):
        (eastward if side == 0 else westward).wait_recv()
        own = [[packed[4 * t + j] for j in range(4)] for t in range(NT)]
        if side == 0:
            depth = jnp.where(first_half, from_west[5], packed[12])
            fields = [
                [jnp.where(first_half, from_west[j], own[0][j]) for j in range(4)],
                [jnp.where(first_half, pltpu.roll(from_west[j], CX - 2, 1), own[1][j]) for j in range(4)],
            ]
        else:
            depth = jnp.where(first_half, packed[12], from_east[4])
            fields = [
                [jnp.where(first_half, own[0][j], from_east[j]) for j in range(4)],
                [jnp.where(first_half, own[1][j], pltpu.roll(from_east[j], 2, 1)) for j in range(4)],
            ]
        steps = []
        for t in range(NT):
            turned = [pltpu.roll(f, CX - 32, 1) for f in fields[t]]
            steps.append(
                [
                    jnp.where(
                        depth > level_in_group + (4 * j + 1.0),
                        jnp.where(lane < CX - 32, turned[j], turned[min(j + 1, 3)]) - fields[t][j],
                        0.0,
                    )
                    for j in range(4)
                ]
            )
        for j in range(4):
            dz = []
            for t in range(NT):
                before = pltpu.roll(steps[t][j - 1], 32, 1) if j > 0 else zeros
                dz.append(
                    steps[t][j] + jnp.where(lane < 32, before, pltpu.roll(steps[t][j], 32, 1))
                )
            speed = packed[8 + j]
            if side == 0:
                speed = jnp.where(first_half, pltpu.roll(from_west[4], (CX + 1 - j) % CX, 1), speed)
            terms, grads = edge_terms(
                [fields[t][j] for t in range(NT)], dz, depth, speed, level_in_group + 4.0 * j,
                lanes_left, lanes_right,
                None if side == 0 else quarter == 1, quarter == 1 if side == 0 else None,
                None if side == 0 else quarter == 0, quarter == 2 if side == 0 else None,
            )
            for t in range(NT):
                if first:
                    edge_c[t, j] = terms[t]
                    edge_g[t, j] = grads[t]
                else:
                    edge_c[t, j] += terms[t]
                    edge_g[t, j] += grads[t]

    @pl.when(even)
    def _():
        edge_columns_in(1, True)
        edge_columns_in(0, False)

    @pl.when(jnp.logical_not(even))
    def _():
        edge_columns_in(0, True)
        edge_columns_in(1, False)

    at_edge = (lane < 2) | (lane >= CX - 2)

    def finish(octets, prepared):
        def at(o, ref, t, group, b):
            rolled = pltpu.roll(ref[t, group], (CX - (4 * (b * 8 + o) + 2)) % CX, 1)
            return jnp.where(at_edge, rolled, 0.0)

        def body(group, carry):
            fluxes = [[carry[4 * i], carry[4 * i + 1]] for i in range(len(octets))]
            gx_here = [[carry[4 * i + 2], carry[4 * i + 3]] for i in range(len(octets))]
            after = jnp.minimum(group + 1, 3)
            for b in range(4):
                k = 4 * group + b
                level = k.astype(jnp.float32)
                down = jnp.minimum(k + 1, NZ - 1)
                for i, o in enumerate(octets):
                    depth = bf[octet(o), :]
                    here = [T[t, k, octet(o), :] for t in range(NT)]
                    step = [T[t, down, octet(o), :] - here[t] for t in range(NT)]
                    gx_down = [
                        GX[t, down, octet(o), :]
                        + (at(o, edge_g, t, group, b + 1) if b < 3 else at(o, edge_g, t, after, 0))
                        for t in range(NT)
                    ]
                    mean_x = [gx_here[i][t] + gx_down[t] for t in range(NT)]
                    wet = depth > level
                    if prepared:
                        inverse = Q[k, octet(o), :]
                        other = [FY[t, k, octet(o), :] for t in range(NT)]
                        rest = [XY[t, k, octet(o), :] for t in range(NT)]
                    else:
                        mean_y = [
                            GY[t, k, octet(o), :] + GY[t, down, octet(o), :] for t in range(NT)
                        ]
                        inverse = jnp.where(
                            depth > level + 1.0, reciprocal(jnp.maximum(4.0 * density(step), 1.0)), 0.0
                        )
                        slope = jnp.clip(density(mean_y) * inverse, -1.0, 1.0)
                        square = 0.1 * (slope * slope)
                        slope = 0.025 * slope
                        other = [square * step[t] - slope * mean_y[t] for t in range(NT)]
                        rest = [
                            here[t] + (XY[t, k, octet(o), :] + YB[t, k, shifted(o, -1), :])
                            for t in range(NT)
                        ]
                    slope = jnp.clip(density(mean_x) * inverse, -1.0, 1.0)
                    square = 0.1 * (slope * slope)
                    slope = 0.025 * slope
                    for t in range(NT):
                        flux = other[t] + (square * step[t] - slope * mean_x[t])
                        total = (rest[t] + at(o, edge_c, t, group, b)) + (flux - fluxes[i][t])
                        out[t, k, pl.ds(8 * o, 8), :] = jnp.where(wet, total, 0.0)
                        fluxes[i][t] = flux
                    gx_here[i] = gx_down
            return tuple(x for i in range(len(octets)) for x in (*fluxes[i], *gx_here[i]))

        start = []
        for o in octets:
            start += [zeros, zeros]
            start += [GX[t, 0, octet(o), :] + at(o, edge_g, t, 0, 0) for t in range(NT)]
        lax.fori_loop(0, 4, body, tuple(start), unroll=2)

    finish(inner, True)

    @pl.when(rows_late)
    def _():
        edge_rows_in()
        finish(outer, False)

    @pl.when(jnp.logical_not(rows_late))
    def _():
        finish(outer, True)

    eastward.wait_send()
    westward.wait_send()
    pl.when(southward_itself)(lambda: wait_send(southward))
    pl.when(northward_itself)(lambda: wait_send(northward))
    pl.when(relayed_up)(lambda: wait_send(handed_up))
    pl.when(relayed_down)(lambda: wait_send(handed_down))
    pl.when(top)(lambda: wait_send(across))
    pl.when(relays_up)(lambda: wait_send(forwarded_up))
    pl.when(relays_down)(lambda: wait_send(forwarded_down))


def solution(mesh):
    n_gx, n_gy = mesh.shape["gx"], mesh.shape["gy"]
    f32 = jnp.float32
    in_hbm = pl.BlockSpec(memory_space=pltpu.HBM)
    field = pltpu.VMEM((NT, NZ, TALL, CX), f32)
    levels = pltpu.VMEM((NZ, CY, CX), f32)
    plane = pltpu.VMEM((TALL, CX), f32)
    packed = pltpu.VMEM((PACKED, 8, CX), f32)
    eastward = pltpu.VMEM((EASTWARD, 8, CX), f32)
    westward = pltpu.VMEM((WESTWARD, 8, CX), f32)
    edge = pltpu.VMEM((NT, 4, 8, CX), f32)

    def on_device(tracers, east_speed, north_speed, bottom_level):
        return pl.pallas_call(
            functools.partial(kernel, n_gx, n_gy),
            out_shape=jax.ShapeDtypeStruct((NT, NZ, CY, CX), f32),
            in_specs=[in_hbm] * 4,
            out_specs=pl.BlockSpec(memory_space=pltpu.VMEM),
            scratch_shapes=[
                field, levels, levels, pltpu.VMEM((CY, CX), jnp.int32), plane, plane, plane,
                field, field, field, field, field, field, pltpu.VMEM((NZ, TALL, CX), f32),
                packed, eastward, westward, eastward, westward,
                pltpu.VMEM((NT, NZ, 2, CX), f32), pltpu.VMEM((2, CX), jnp.int32),
                pltpu.VMEM((NZ, 1, CX), f32), pltpu.VMEM((FOLD_ROWS, CX), f32),
                pltpu.VMEM((NT, NZ, 8, CX), f32), pltpu.VMEM((8, CX), jnp.int32),
                pltpu.VMEM((NZ, 8, CX), f32), edge, edge,
                pltpu.SemaphoreType.DMA((10,)), pltpu.SemaphoreType.DMA((10,)),
                pltpu.SemaphoreType.DMA((10,)), pltpu.SemaphoreType.REGULAR,
            ],
            compiler_params=pltpu.CompilerParams(
                collective_id=0, has_side_effects=True, vmem_limit_bytes=24 * 1024 * 1024
            ),
        )(
            *[
                pltpu.with_memory_space_constraint(x, pltpu.HBM)
                for x in (tracers, east_speed, north_speed, bottom_level)
            ]
        )

    in_specs = (P(None, None, "gy", "gx"), P(None, "gy", "gx"), P(None, "gy", "gx"), P("gy", "gx"))
    return jax.shard_map(
        on_device, mesh=mesh, in_specs=in_specs, out_specs=P(None, None, "gy", "gx"), check_vma=False
    )
```

```python
import functools

import jax
import jax.numpy as jnp
from jax import lax
from jax.experimental import pallas as pl
from jax.experimental.pallas import tpu as pltpu
from jax.sharding import PartitionSpec as P

MESH = pl.DeviceIdType.MESH
NT, NZ, CY, CX = 2, 16, 48, 128
PAD = 8
TALL = CY + 2 * PAD
OCTETS = CY // 8
FOLD_ROWS = 72
OWN_LAST, FROM_NORTH, FROM_SOUTH, OWN_FIRST = (pl.ds(i, 2) for i in (0, 2, 4, 6))
PACKED = 13
EASTWARD = 6
WESTWARD = 5
BLOCK = 8
HEAT = 0.4
SALT = 0.6


def reciprocal(value):
    guess = pl.reciprocal(value, approx=True)
    return guess * (2.0 - value * guess)


def minmod(first, second):
    return jnp.maximum(jnp.minimum(first, second), 0.0) + jnp.minimum(
        jnp.maximum(first, second), 0.0
    )


def density(pair):
    return SALT * pair[1] - HEAT * pair[0]


def face_fluxes(local, before, after, dz_sum, speed):
    slope = jnp.clip(
        (0.1 * density(local)) * reciprocal(jnp.maximum(density(dz_sum), 1.0)), -0.025, 0.025
    )
    size = jnp.abs(speed)
    limited = 0.5 * size * (1.0 - size)
    forward = speed >= 0.0
    linear = jnp.minimum(speed, 0.0) - 0.1
    low, high, second = [], [], []
    for t in range(NT):
        correction = limited * minmod(local[t], jnp.where(forward, before[t], after[t]))
        taken = correction + (linear * local[t] + slope * dz_sum[t])
        low.append(taken)
        high.append(taken - speed * local[t])
        second.append(correction)
    return low, high, second, forward


def lanes_left(value):
    return pltpu.roll(value, CX - 1, 1)


def lanes_right(value):
    return pltpu.roll(value, 1, 1)


def rows_up(value):
    return pltpu.roll(value, 7, 0)


def rows_down(value):
    return pltpu.roll(value, 1, 0)


def edge_terms(field, dz, bottom, speed, level, nxt, prv, low_at, high_at, low_second, high_second):
    wet = jnp.minimum(bottom, nxt(bottom)) > level
    local = [jnp.where(wet, nxt(f) - f, 0.0) for f in field]
    dz_sum = [z + nxt(z) for z in dz]
    masked = jnp.where(wet, speed, 0.0)
    low, high, second, forward = face_fluxes(
        local, [prv(d) for d in local], [nxt(d) for d in local], dz_sum, masked
    )
    zero = jnp.zeros_like(masked)
    terms, steps = [], []
    for t in range(NT):
        late = zero
        if low_second is not None:
            late = late + jnp.where(low_second & ~forward, second[t], 0.0)
        if high_second is not None:
            late = late + jnp.where(high_second & forward, second[t], 0.0)
        arriving, term, step = late, -late, zero
        if high_at is not None:
            arriving = arriving + jnp.where(high_at, high[t], 0.0)
            step = step + prv(jnp.where(high_at, local[t], 0.0))
        if low_at is not None:
            term = term - jnp.where(low_at, low[t], 0.0)
            step = step + jnp.where(low_at, local[t], 0.0)
        terms.append(term + prv(arriving))
        steps.append(step)
    return terms, steps


def kernel(
    n_gx, n_gy,
    tracers, east, north, bottom, out,
    T, U, V, bottom_int, bf, be, bn, TZ, XY, YB, GX, GY, FY, Q,
    packed, to_east, to_west, from_west, from_east, relay, relay_b, relay_v, folded,
    strip, strip_b, strip_v, edge_c, edge_g,
    load_sem, send_sem, recv_sem, go_sem, go_north_sem,
):
    gx, gy = lax.axis_index("gx"), lax.axis_index("gy")
    east_id = (lax.rem(gx + 1, n_gx), gy)
    west_id = (lax.rem(gx + n_gx - 1, n_gx), gy)
    north_id = (gx, gy + 1)
    south_id = (gx, gy - 1)
    mirror_id = (n_gx - 1 - gx, gy)
    top = gy == n_gy - 1
    base = gy == 0
    below_middle = gy == n_gy // 2 - 1
    above_middle = gy == n_gy // 2
    place = lax.rem(gx, BLOCK)
    by_go = gy <= n_gy // 2
    after_seam = (place == 0) & by_go
    before_seam = (place == BLOCK - 1) & by_go
    crosses_down = place == BLOCK - 1
    crosses_up = crosses_down | (place == 2)
    relayed_up = crosses_up & below_middle
    relayed_down = crosses_down & above_middle
    relays_up = ((place == BLOCK - 2) | (place == 3)) & below_middle
    relays_down = (place == BLOCK - 2) & above_middle
    chip_mate = gx + 1 - 2 * lax.rem(gx, 2)

    barrier = pltpu.get_barrier_semaphore()

    def greet(device):
        pl.semaphore_signal(barrier, inc=1, device_id=device, device_id_type=MESH)

    pl.when(top)(lambda: greet(mirror_id))
    above_go = gy == n_gy // 2 + 1
    mate_sends_down = crosses_down & below_middle
    mate_sends_up = crosses_up & above_middle
    pl.when(mate_sends_down)(lambda: greet((chip_mate, gy + 1)))
    pl.when(mate_sends_up)(lambda: greet((chip_mate, gy - 1)))
    pl.when(jnp.logical_not(top | mate_sends_down))(lambda: greet(north_id))
    pl.when(jnp.logical_not(base | mate_sends_up | above_go))(lambda: greet(south_id))
    greet(west_id)
    pl.when(jnp.logical_not(before_seam))(lambda: greet(east_id))
    expected = (
        4 + (relays_up | relays_down).astype(jnp.int32) - (relayed_up | relayed_down).astype(jnp.int32)
        - after_seam.astype(jnp.int32) - base.astype(jnp.int32) - above_middle.astype(jnp.int32)
    )

    def load(source, target, index):
        copy = pltpu.make_async_copy(source, target, load_sem.at[index])
        copy.start()
        return copy

    last_rows, first_rows = pl.ds(CY - 2, 2), pl.ds(0, 2)
    early = [
        load(tracers.at[:, :, last_rows, :], strip.at[:, :, OWN_LAST, :], 0),
        load(tracers.at[:, :, first_rows, :], strip.at[:, :, OWN_FIRST, :], 1),
        load(bottom.at[last_rows, :], strip_b.at[OWN_LAST, :], 2),
        load(bottom.at[first_rows, :], strip_b.at[OWN_FIRST, :], 3),
        load(north.at[:, last_rows, :], strip_v.at[:, OWN_LAST, :], 4),
        load(north.at[:, first_rows, :], strip_v.at[:, OWN_FIRST, :], 5),
    ]
    late = [
        load(tracers, T.at[:, :, pl.ds(PAD, CY), :], 6),
        load(bottom, bottom_int, 7),
        load(east, U, 8),
        load(north, V, 9),
    ]

    lane = lax.broadcasted_iota(jnp.int32, (8, CX), 1)
    row = lax.broadcasted_iota(jnp.int32, (8, CX), 0)
    zeros = jnp.zeros((8, CX), jnp.float32)

    def octet(o):
        return pl.ds(PAD + 8 * o, 8)

    def shifted(o, by):
        return pl.ds(PAD + 8 * o + by, 8)

    for pad in (pl.ds(0, PAD), pl.ds(PAD + CY, PAD)):
        bf[pad, :] = zeros
        bn[pad, :] = zeros

    def clear(k, carry):
        for t in range(NT):
            YB[t, k, pl.ds(0, PAD), :] = zeros
            TZ[t, k, pl.ds(PAD + CY, PAD), :] = zeros
        return carry

    lax.fori_loop(0, NZ, clear, 0)

    @pl.when(base)
    def _():
        strip_b[FROM_SOUTH, :] = jnp.zeros((2, CX), jnp.int32)
        for t in range(NT):
            for k in range(NZ):
                strip[t, k, FROM_SOUTH, :] = jnp.zeros((2, CX), jnp.float32)

    for copy in early:
        copy.wait()

    def send(source, target, index, slot, device):
        return pltpu.make_async_remote_copy(
            src_ref=source, dst_ref=target, send_sem=send_sem.at[index], recv_sem=recv_sem.at[slot],
            device_id=device, device_id_type=MESH,
        )

    def bundle(sources, targets, index, slot, device):
        pairs = enumerate(zip(sources, targets, strict=True))
        return [send(source, target, index + i, slot + i, device) for i, (source, target) in pairs]

    def start(copies):
        for copy in copies:
            copy.start()

    def wait_recv(copies):
        for copy in copies:
            copy.wait_recv()

    def wait_send(copies):
        for copy in copies:
            copy.wait_send()

    eastward = send(to_east, from_west, 0, 0, east_id)
    westward = send(to_west, from_east, 1, 1, west_id)
    last = [strip.at[:, :, OWN_LAST, :], strip_b.at[OWN_LAST, :], strip_v.at[:, pl.ds(1, 1), :]]
    first = [strip.at[:, :, OWN_FIRST, :], strip_b.at[OWN_FIRST, :]]
    from_south = [strip.at[:, :, FROM_SOUTH, :], strip_b.at[FROM_SOUTH, :], strip_v.at[:, pl.ds(5, 1), :]]
    from_north = [strip.at[:, :, FROM_NORTH, :], strip_b.at[FROM_NORTH, :]]
    between = [relay, relay_b, relay_v]
    northward = bundle(last, from_south, 2, 2, north_id)
    southward = bundle(first, from_north, 5, 5, south_id)
    across = bundle(last[:2], from_north, 2, 5, mirror_id)
    handed_up = bundle(last, between, 2, 7, (chip_mate, gy))
    handed_down = bundle(first, between[:2], 5, 7, (chip_mate, gy))
    forwarded_up = bundle(between, from_south, 7, 2, (chip_mate, gy + 1))
    forwarded_down = bundle(between[:2], from_north, 7, 5, (chip_mate, gy - 1))
    northward_itself = jnp.logical_not(top | relayed_up)
    southward_itself = jnp.logical_not(base | relayed_down)
    even = lax.rem(gx, 2) == 0
    late_entry = below_middle & jnp.logical_not(relayed_up) & (place < BLOCK - 2)

    @pl.when(jnp.logical_not(late_entry))
    def _():
        pl.semaphore_wait(barrier, expected)

        @pl.when(before_seam)
        def _():
            pl.semaphore_signal(go_sem, inc=1, device_id=east_id, device_id_type=MESH)

        @pl.when(above_go)
        def _():
            pl.semaphore_signal(go_north_sem, inc=1, device_id=south_id, device_id_type=MESH)

        pl.when(northward_itself & below_middle)(lambda: start(northward))
        pl.when(relayed_up)(lambda: start(handed_up))

        @pl.when(relays_up)
        def _():
            wait_recv(handed_up)
            start(forwarded_up)

        pl.when(southward_itself)(lambda: start(southward))
        pl.when(relayed_down)(lambda: start(handed_down))
        pl.when(northward_itself & jnp.logical_not(below_middle | above_middle))(lambda: start(northward))
        pl.when(top)(lambda: start(across))

        @pl.when(relays_down)
        def _():
            wait_recv(handed_down)
            start(forwarded_down)

    def send_columns():
        pl.when(jnp.logical_not(even))(eastward.start)
        pl.when(jnp.logical_not(after_seam))(westward.start)
        pl.when(even)(eastward.start)

    for copy in late[:3]:
        copy.wait()

    for o in range(OCTETS):
        bf[octet(o), :] = bottom_int[pl.ds(8 * o, 8), :].astype(jnp.float32)
    for o in range(OCTETS):
        here = bf[octet(o), :]
        be[octet(o), :] = jnp.where(lane == CX - 1, 0.0, jnp.minimum(here, lanes_left(here)))
        bn[octet(o), :] = jnp.minimum(here, bf[shifted(o, 1), :])

    slot_of = lane // 4

    def pack(group, carry):
        t0, t1, speed = zeros, zeros, zeros
        for b in range(4):
            for o in range(OCTETS):
                slot = b * 8 + o
                here = slot_of == slot
                shift = (4 * slot + 2) % CX
                k = 4 * group + b
                t0 = jnp.where(here, pltpu.roll(T[0, k, octet(o), :], shift, 1), t0)
                t1 = jnp.where(here, pltpu.roll(T[1, k, octet(o), :], shift, 1), t1)
                speed = jnp.where(here, pltpu.roll(U[k, pl.ds(8 * o, 8), :], shift, 1), speed)
        packed[group] = t0
        packed[4 + group] = t1
        packed[8 + group] = speed
        return carry

    lax.fori_loop(0, 4, pack, 0, unroll=4)
    packed_b = zeros
    for b in range(4):
        for o in range(OCTETS):
            slot = b * 8 + o
            packed_b = jnp.where(
                slot_of == slot, pltpu.roll(bf[octet(o), :], (4 * slot + 2) % CX, 1), packed_b
            )
    packed[12] = packed_b

    first_half = lax.rem(lane, 4) < 2
    east_speeds = zeros
    for j in range(4):
        to_east[j] = jnp.where(first_half, packed[j], pltpu.roll(packed[4 + j], 2, 1))
        to_west[j] = jnp.where(first_half, pltpu.roll(packed[4 + j], CX - 2, 1), packed[j])
        east_speeds = jnp.where(
            lax.rem(lane, 4) == j, pltpu.roll(packed[8 + j], (CX + j - 1) % CX, 1), east_speeds
        )
    to_east[4] = east_speeds
    to_east[5] = packed_b
    to_west[4] = packed_b

    pl.when(jnp.logical_not(late_entry))(send_columns)

    @pl.when(above_middle)
    def _():
        pl.semaphore_wait(go_north_sem, 1)
        start(northward)


    late[3].wait()

    def vertical(k, carry):
        level = k.astype(jnp.float32)
        above = jnp.where(k > 0, level, 99.0)
        down, up = jnp.minimum(k + 1, NZ - 1), jnp.maximum(k - 1, 0)
        for o in range(OCTETS):
            depth = bf[octet(o), :]
            for t in range(NT):
                here = T[t, k, octet(o), :]
                TZ[t, k, octet(o), :] = jnp.where(
                    depth > level + 1.0, T[t, down, octet(o), :] - here, 0.0
                ) + jnp.where(depth > above, here - T[t, up, octet(o), :], 0.0)
        return carry

    lax.fori_loop(0, NZ, vertical, 0, unroll=2)

    def inside(k, carry):
        level = k.astype(jnp.float32)
        for o in range(OCTETS):
            here = [T[t, k, octet(o), :] for t in range(NT)]
            dz = [TZ[t, k, octet(o), :] for t in range(NT)]
            wet = be[octet(o), :] > level
            local = [jnp.where(wet, lanes_left(f) - f, 0.0) for f in here]
            before = [lanes_right(d) for d in local]
            after = [lanes_left(d) for d in local]
            speed = jnp.where(wet, U[k, pl.ds(8 * o, 8), :], 0.0)
            low, high, _, _ = face_fluxes(
                local, before, after, [z + lanes_left(z) for z in dz], speed
            )
            across_x = [lanes_right(high[t]) - low[t] for t in range(NT)]
            for t in range(NT):
                GX[t, k, octet(o), :] = local[t] + before[t]

            wet = bn[octet(o), :] > level
            wet_before = bn[shifted(o, -1), :] > level
            wet_after = bn[shifted(o, 1), :] > level
            nxt = [T[t, k, shifted(o, 1), :] for t in range(NT)]
            local = [jnp.where(wet, nxt[t] - here[t], 0.0) for t in range(NT)]
            before = [
                jnp.where(wet_before, here[t] - T[t, k, shifted(o, -1), :], 0.0) for t in range(NT)
            ]
            after = [
                jnp.where(wet_after, T[t, k, shifted(o, 2), :] - nxt[t], 0.0) for t in range(NT)
            ]
            speed = jnp.where(wet, V[k, pl.ds(8 * o, 8), :], 0.0)
            low, high, _, _ = face_fluxes(
                local, before, after, [dz[t] + TZ[t, k, shifted(o, 1), :] for t in range(NT)], speed
            )
            for t in range(NT):
                GY[t, k, octet(o), :] = local[t] + before[t]
                XY[t, k, octet(o), :] = across_x[t] - low[t]
                YB[t, k, octet(o), :] = high[t]
        return carry

    lax.fori_loop(0, NZ, inside, 0, unroll=2)

    @pl.when(late_entry)
    def _():
        pl.semaphore_wait(barrier, expected)
        start(northward)

        @pl.when(relays_up)
        def _():
            wait_recv(handed_up)
            start(forwarded_up)

        send_columns()
        start(southward)

    @pl.when(after_seam)
    def _():
        pl.semaphore_wait(go_sem, 1)
        westward.start()

    def prepare(octets):
        def body(k, carry):
            level = k.astype(jnp.float32)
            down = jnp.minimum(k + 1, NZ - 1)
            for o in octets:
                open_below = bf[octet(o), :] > level + 1.0
                here = [T[t, k, octet(o), :] for t in range(NT)]
                step = [T[t, down, octet(o), :] - here[t] for t in range(NT)]
                mean_y = [GY[t, k, octet(o), :] + GY[t, down, octet(o), :] for t in range(NT)]
                inverse = jnp.where(
                    open_below, reciprocal(jnp.maximum(4.0 * density(step), 1.0)), 0.0
                )
                slope = jnp.clip(density(mean_y) * inverse, -1.0, 1.0)
                square = 0.1 * (slope * slope)
                slope = 0.025 * slope
                Q[k, octet(o), :] = inverse
                for t in range(NT):
                    FY[t, k, octet(o), :] = square * step[t] - slope * mean_y[t]
                    XY[t, k, octet(o), :] += here[t] + YB[t, k, shifted(o, -1), :]
            return carry

        lax.fori_loop(0, NZ, body, 0, unroll=2)

    inner, outer = tuple(range(1, OCTETS - 1)), (0, OCTETS - 1)
    prepare(inner)

    def edge_rows_in():
        wait_recv(southward)
        pl.when(jnp.logical_not(base))(lambda: wait_recv(northward))

        @pl.when(top)
        def _():
            def gather(k, carry):
                for t in range(NT):
                    folded[pl.ds(2 * (NZ * t + k), 2), :] = strip[t, k, FROM_NORTH, :]
                return carry

            def scatter(k, carry):
                for t in range(NT):
                    strip[t, k, FROM_NORTH, :] = folded[pl.ds(2 * (NZ * t + k), 2), :]
                return carry

            lax.fori_loop(0, NZ, gather, 0, unroll=4)
            folded[pl.ds(64, 8), :] = strip_b[...].astype(jnp.float32)
            for i in range(FOLD_ROWS // 8):
                value = folded[pl.ds(8 * i, 8), :]
                for bit in (64, 32, 16, 8, 4, 2, 1):
                    value = jnp.where(
                        (lane & bit) != 0, pltpu.roll(value, bit, 1), pltpu.roll(value, CX - bit, 1)
                    )
                folded[pl.ds(8 * i, 8), :] = jnp.where(
                    (row & 1) != 0, rows_down(value), rows_up(value)
                )
            lax.fori_loop(0, NZ, scatter, 0, unroll=4)
            strip_b[FROM_NORTH, :] = folded[pl.ds(66, 2), :].astype(jnp.int32)

        def edge_rows(k, carry):
            level = k.astype(jnp.float32)
            above = jnp.where(k > 0, level, 99.0)
            down, up = jnp.minimum(k + 1, NZ - 1), jnp.maximum(k - 1, 0)
            depth = strip_b[...].astype(jnp.float32)
            here = [strip[t, k] for t in range(NT)]
            dz = [
                jnp.where(depth > level + 1.0, strip[t, down] - here[t], 0.0)
                + jnp.where(depth > above, here[t] - strip[t, up], 0.0)
                for t in range(NT)
            ]
            terms, grads = edge_terms(
                here, dz, depth, strip_v[k], level, rows_up, rows_down,
                row == 1, row == 5, row == 0, row == 6,
            )
            for t in range(NT):
                XY[t, k, octet(0), :] += jnp.where(row < 2, pltpu.roll(terms[t], 2, 0), 0.0)
                GY[t, k, octet(0), :] += jnp.where(row < 2, pltpu.roll(grads[t], 2, 0), 0.0)
                XY[t, k, octet(OCTETS - 1), :] += jnp.where(row > 5, pltpu.roll(terms[t], 6, 0), 0.0)
                GY[t, k, octet(OCTETS - 1), :] += jnp.where(row > 5, pltpu.roll(grads[t], 6, 0), 0.0)
            return carry

        lax.fori_loop(0, NZ, edge_rows, 0, unroll=16)

    rows_late = below_middle | above_middle | (gy == n_gy // 2 - 2) | top

    @pl.when(jnp.logical_not(rows_late))
    def _():
        edge_rows_in()
        prepare(outer)

    quarter = lax.rem(lane, 4)
    level_in_group = (lane // 32).astype(jnp.float32)
    def edge_columns_in(side, first):
        (eastward if side == 0 else westward).wait_recv()
        own = [[packed[4 * t + j] for j in range(4)] for t in range(NT)]
        if side == 0:
            depth = jnp.where(first_half, from_west[5], packed[12])
            fields = [
                [jnp.where(first_half, from_west[j], own[0][j]) for j in range(4)],
                [jnp.where(first_half, pltpu.roll(from_west[j], CX - 2, 1), own[1][j]) for j in range(4)],
            ]
        else:
            depth = jnp.where(first_half, packed[12], from_east[4])
            fields = [
                [jnp.where(first_half, own[0][j], from_east[j]) for j in range(4)],
                [jnp.where(first_half, own[1][j], pltpu.roll(from_east[j], 2, 1)) for j in range(4)],
            ]
        steps = []
        for t in range(NT):
            turned = [pltpu.roll(f, CX - 32, 1) for f in fields[t]]
            steps.append(
                [
                    jnp.where(
                        depth > level_in_group + (4 * j + 1.0),
                        jnp.where(lane < CX - 32, turned[j], turned[min(j + 1, 3)]) - fields[t][j],
                        0.0,
                    )
                    for j in range(4)
                ]
            )
        for j in range(4):
            dz = []
            for t in range(NT):
                before = pltpu.roll(steps[t][j - 1], 32, 1) if j > 0 else zeros
                dz.append(
                    steps[t][j] + jnp.where(lane < 32, before, pltpu.roll(steps[t][j], 32, 1))
                )
            speed = packed[8 + j]
            if side == 0:
                speed = jnp.where(first_half, pltpu.roll(from_west[4], (CX + 1 - j) % CX, 1), speed)
            terms, grads = edge_terms(
                [fields[t][j] for t in range(NT)], dz, depth, speed, level_in_group + 4.0 * j,
                lanes_left, lanes_right,
                None if side == 0 else quarter == 1, quarter == 1 if side == 0 else None,
                None if side == 0 else quarter == 0, quarter == 2 if side == 0 else None,
            )
            for t in range(NT):
                if first:
                    edge_c[t, j] = terms[t]
                    edge_g[t, j] = grads[t]
                else:
                    edge_c[t, j] += terms[t]
                    edge_g[t, j] += grads[t]

    @pl.when(even)
    def _():
        edge_columns_in(1, True)
        edge_columns_in(0, False)

    @pl.when(jnp.logical_not(even))
    def _():
        edge_columns_in(0, True)
        edge_columns_in(1, False)

    at_edge = (lane < 2) | (lane >= CX - 2)

    def finish(octets, prepared):
        def at(o, ref, t, group, b):
            rolled = pltpu.roll(ref[t, group], (CX - (4 * (b * 8 + o) + 2)) % CX, 1)
            return jnp.where(at_edge, rolled, 0.0)

        def body(group, carry):
            fluxes = [[carry[4 * i], carry[4 * i + 1]] for i in range(len(octets))]
            gx_here = [[carry[4 * i + 2], carry[4 * i + 3]] for i in range(len(octets))]
            after = jnp.minimum(group + 1, 3)
            for b in range(4):
                k = 4 * group + b
                level = k.astype(jnp.float32)
                down = jnp.minimum(k + 1, NZ - 1)
                for i, o in enumerate(octets):
                    depth = bf[octet(o), :]
                    here = [T[t, k, octet(o), :] for t in range(NT)]
                    step = [T[t, down, octet(o), :] - here[t] for t in range(NT)]
                    gx_down = [
                        GX[t, down, octet(o), :]
                        + (at(o, edge_g, t, group, b + 1) if b < 3 else at(o, edge_g, t, after, 0))
                        for t in range(NT)
                    ]
                    mean_x = [gx_here[i][t] + gx_down[t] for t in range(NT)]
                    wet = depth > level
                    if prepared:
                        inverse = Q[k, octet(o), :]
                        other = [FY[t, k, octet(o), :] for t in range(NT)]
                        rest = [XY[t, k, octet(o), :] for t in range(NT)]
                    else:
                        mean_y = [
                            GY[t, k, octet(o), :] + GY[t, down, octet(o), :] for t in range(NT)
                        ]
                        inverse = jnp.where(
                            depth > level + 1.0, reciprocal(jnp.maximum(4.0 * density(step), 1.0)), 0.0
                        )
                        slope = jnp.clip(density(mean_y) * inverse, -1.0, 1.0)
                        square = 0.1 * (slope * slope)
                        slope = 0.025 * slope
                        other = [square * step[t] - slope * mean_y[t] for t in range(NT)]
                        rest = [
                            here[t] + (XY[t, k, octet(o), :] + YB[t, k, shifted(o, -1), :])
                            for t in range(NT)
                        ]
                    slope = jnp.clip(density(mean_x) * inverse, -1.0, 1.0)
                    square = 0.1 * (slope * slope)
                    slope = 0.025 * slope
                    for t in range(NT):
                        flux = other[t] + (square * step[t] - slope * mean_x[t])
                        total = (rest[t] + at(o, edge_c, t, group, b)) + (flux - fluxes[i][t])
                        out[t, k, pl.ds(8 * o, 8), :] = jnp.where(wet, total, 0.0)
                        fluxes[i][t] = flux
                    gx_here[i] = gx_down
            return tuple(x for i in range(len(octets)) for x in (*fluxes[i], *gx_here[i]))

        start = []
        for o in octets:
            start += [zeros, zeros]
            start += [GX[t, 0, octet(o), :] + at(o, edge_g, t, 0, 0) for t in range(NT)]
        lax.fori_loop(0, 4, body, tuple(start), unroll=4)

    finish(inner, True)

    @pl.when(rows_late)
    def _():
        edge_rows_in()
        finish(outer, False)

    @pl.when(jnp.logical_not(rows_late))
    def _():
        finish(outer, True)

    eastward.wait_send()
    westward.wait_send()
    pl.when(southward_itself)(lambda: wait_send(southward))
    pl.when(northward_itself)(lambda: wait_send(northward))
    pl.when(relayed_up)(lambda: wait_send(handed_up))
    pl.when(relayed_down)(lambda: wait_send(handed_down))
    pl.when(top)(lambda: wait_send(across))
    pl.when(relays_up)(lambda: wait_send(forwarded_up))
    pl.when(relays_down)(lambda: wait_send(forwarded_down))


def solution(mesh):
    n_gx, n_gy = mesh.shape["gx"], mesh.shape["gy"]
    f32 = jnp.float32
    in_hbm = pl.BlockSpec(memory_space=pltpu.HBM)
    field = pltpu.VMEM((NT, NZ, TALL, CX), f32)
    levels = pltpu.VMEM((NZ, CY, CX), f32)
    plane = pltpu.VMEM((TALL, CX), f32)
    packed = pltpu.VMEM((PACKED, 8, CX), f32)
    eastward = pltpu.VMEM((EASTWARD, 8, CX), f32)
    westward = pltpu.VMEM((WESTWARD, 8, CX), f32)
    edge = pltpu.VMEM((NT, 4, 8, CX), f32)

    def on_device(tracers, east_speed, north_speed, bottom_level):
        return pl.pallas_call(
            functools.partial(kernel, n_gx, n_gy),
            out_shape=jax.ShapeDtypeStruct((NT, NZ, CY, CX), f32),
            in_specs=[in_hbm] * 4,
            out_specs=pl.BlockSpec(memory_space=pltpu.VMEM),
            scratch_shapes=[
                field, levels, levels, pltpu.VMEM((CY, CX), jnp.int32), plane, plane, plane,
                field, field, field, field, field, field, pltpu.VMEM((NZ, TALL, CX), f32),
                packed, eastward, westward, eastward, westward,
                pltpu.VMEM((NT, NZ, 2, CX), f32), pltpu.VMEM((2, CX), jnp.int32),
                pltpu.VMEM((NZ, 1, CX), f32), pltpu.VMEM((FOLD_ROWS, CX), f32),
                pltpu.VMEM((NT, NZ, 8, CX), f32), pltpu.VMEM((8, CX), jnp.int32),
                pltpu.VMEM((NZ, 8, CX), f32), edge, edge,
                pltpu.SemaphoreType.DMA((10,)), pltpu.SemaphoreType.DMA((10,)),
                pltpu.SemaphoreType.DMA((10,)), pltpu.SemaphoreType.REGULAR, pltpu.SemaphoreType.REGULAR,
            ],
            compiler_params=pltpu.CompilerParams(
                collective_id=0, has_side_effects=True, vmem_limit_bytes=24 * 1024 * 1024
            ),
        )(
            *[
                pltpu.with_memory_space_constraint(x, pltpu.HBM)
                for x in (tracers, east_speed, north_speed, bottom_level)
            ]
        )

    in_specs = (P(None, None, "gy", "gx"), P(None, "gy", "gx"), P(None, "gy", "gx"), P("gy", "gx"))
    return jax.shard_map(
        on_device, mesh=mesh, in_specs=in_specs, out_specs=P(None, None, "gy", "gx"), check_vma=False
    )
```

```python
import functools

import jax
import jax.numpy as jnp
from jax import lax
from jax.experimental import pallas as pl
from jax.experimental.pallas import tpu as pltpu
from jax.sharding import PartitionSpec as P

MESH = pl.DeviceIdType.MESH
NT, NZ, CY, CX = 2, 16, 48, 128
PAD = 8
TALL = CY + 2 * PAD
OCTETS = CY // 8
FOLD_ROWS = 72
OWN_LAST, FROM_NORTH, FROM_SOUTH, OWN_FIRST = (pl.ds(i, 2) for i in (0, 2, 4, 6))
PACKED = 13
EASTWARD = 6
WESTWARD = 5
BLOCK = 8
HEAT = 0.4
SALT = 0.6


def reciprocal(value):
    guess = pl.reciprocal(value, approx=True)
    return guess * (2.0 - value * guess)


def minmod(first, second):
    return jnp.maximum(jnp.minimum(first, second), 0.0) + jnp.minimum(
        jnp.maximum(first, second), 0.0
    )


def density(pair):
    return SALT * pair[1] - HEAT * pair[0]


def face_fluxes(local, before, after, dz_sum, speed):
    slope = jnp.clip(
        (0.1 * density(local)) * reciprocal(jnp.maximum(density(dz_sum), 1.0)), -0.025, 0.025
    )
    size = jnp.abs(speed)
    limited = 0.5 * size * (1.0 - size)
    forward = speed >= 0.0
    linear = jnp.minimum(speed, 0.0) - 0.1
    low, high, second = [], [], []
    for t in range(NT):
        correction = limited * minmod(local[t], jnp.where(forward, before[t], after[t]))
        taken = correction + (linear * local[t] + slope * dz_sum[t])
        low.append(taken)
        high.append(taken - speed * local[t])
        second.append(correction)
    return low, high, second, forward


def lanes_left(value):
    return pltpu.roll(value, CX - 1, 1)


def lanes_right(value):
    return pltpu.roll(value, 1, 1)


def rows_up(value):
    return pltpu.roll(value, 7, 0)


def rows_down(value):
    return pltpu.roll(value, 1, 0)


def edge_terms(field, dz, bottom, speed, level, nxt, prv, low_at, high_at, low_second, high_second):
    wet = jnp.minimum(bottom, nxt(bottom)) > level
    local = [jnp.where(wet, nxt(f) - f, 0.0) for f in field]
    dz_sum = [z + nxt(z) for z in dz]
    masked = jnp.where(wet, speed, 0.0)
    low, high, second, forward = face_fluxes(
        local, [prv(d) for d in local], [nxt(d) for d in local], dz_sum, masked
    )
    zero = jnp.zeros_like(masked)
    terms, steps = [], []
    for t in range(NT):
        late = zero
        if low_second is not None:
            late = late + jnp.where(low_second & ~forward, second[t], 0.0)
        if high_second is not None:
            late = late + jnp.where(high_second & forward, second[t], 0.0)
        arriving, term, step = late, -late, zero
        if high_at is not None:
            arriving = arriving + jnp.where(high_at, high[t], 0.0)
            step = step + prv(jnp.where(high_at, local[t], 0.0))
        if low_at is not None:
            term = term - jnp.where(low_at, low[t], 0.0)
            step = step + jnp.where(low_at, local[t], 0.0)
        terms.append(term + prv(arriving))
        steps.append(step)
    return terms, steps


def kernel(
    n_gx, n_gy,
    tracers, east, north, bottom, out,
    T, U, V, bottom_int, bf, be, bn, TZ, XY, YB, GX, GY, FY, Q,
    packed, to_east, to_west, from_west, from_east, relay, relay_b, relay_v, folded,
    strip, strip_b, strip_v, edge_c, edge_g,
    load_sem, send_sem, recv_sem, go_sem, go_north_sem,
):
    gx, gy = lax.axis_index("gx"), lax.axis_index("gy")
    east_id = (lax.rem(gx + 1, n_gx), gy)
    west_id = (lax.rem(gx + n_gx - 1, n_gx), gy)
    north_id = (gx, gy + 1)
    south_id = (gx, gy - 1)
    mirror_id = (n_gx - 1 - gx, gy)
    top = gy == n_gy - 1
    base = gy == 0
    below_middle = gy == n_gy // 2 - 1
    above_middle = gy == n_gy // 2
    place = lax.rem(gx, BLOCK)
    by_go = gy <= n_gy // 2
    after_seam = (place == 0) & by_go
    before_seam = (place == BLOCK - 1) & by_go
    crosses_down = place == BLOCK - 1
    crosses_up = crosses_down | (place == 2)
    relayed_up = crosses_up & below_middle
    relayed_down = crosses_down & above_middle
    relays_up = ((place == BLOCK - 2) | (place == 3)) & below_middle
    relays_down = (place == BLOCK - 2) & above_middle
    chip_mate = gx + 1 - 2 * lax.rem(gx, 2)

    barrier = pltpu.get_barrier_semaphore()

    def greet(device):
        pl.semaphore_signal(barrier, inc=1, device_id=device, device_id_type=MESH)

    pl.when(top)(lambda: greet(mirror_id))
    above_go = gy == n_gy // 2 + 1
    mate_sends_down = crosses_down & below_middle
    mate_sends_up = crosses_up & above_middle
    pl.when(mate_sends_down)(lambda: greet((chip_mate, gy + 1)))
    pl.when(mate_sends_up)(lambda: greet((chip_mate, gy - 1)))
    pl.when(jnp.logical_not(top | mate_sends_down))(lambda: greet(north_id))
    pl.when(jnp.logical_not(base | mate_sends_up | above_go))(lambda: greet(south_id))
    greet(west_id)
    pl.when(jnp.logical_not(before_seam))(lambda: greet(east_id))
    expected = (
        4 + (relays_up | relays_down).astype(jnp.int32) - (relayed_up | relayed_down).astype(jnp.int32)
        - after_seam.astype(jnp.int32) - base.astype(jnp.int32) - above_middle.astype(jnp.int32)
    )

    def load(source, target, index):
        copy = pltpu.make_async_copy(source, target, load_sem.at[index])
        copy.start()
        return copy

    last_rows, first_rows = pl.ds(CY - 2, 2), pl.ds(0, 2)
    early = [
        load(tracers.at[:, :, last_rows, :], strip.at[:, :, OWN_LAST, :], 0),
        load(tracers.at[:, :, first_rows, :], strip.at[:, :, OWN_FIRST, :], 1),
        load(bottom.at[last_rows, :], strip_b.at[OWN_LAST, :], 2),
        load(bottom.at[first_rows, :], strip_b.at[OWN_FIRST, :], 3),
        load(north.at[:, last_rows, :], strip_v.at[:, OWN_LAST, :], 4),
        load(north.at[:, first_rows, :], strip_v.at[:, OWN_FIRST, :], 5),
    ]
    late = [
        load(tracers, T.at[:, :, pl.ds(PAD, CY), :], 6),
        load(bottom, bottom_int, 7),
        load(east, U, 8),
        load(north, V, 9),
    ]

    lane = lax.broadcasted_iota(jnp.int32, (8, CX), 1)
    row = lax.broadcasted_iota(jnp.int32, (8, CX), 0)
    zeros = jnp.zeros((8, CX), jnp.float32)

    def octet(o):
        return pl.ds(PAD + 8 * o, 8)

    def shifted(o, by):
        return pl.ds(PAD + 8 * o + by, 8)

    for pad in (pl.ds(0, PAD), pl.ds(PAD + CY, PAD)):
        bf[pad, :] = zeros
        bn[pad, :] = zeros

    def clear(k, carry):
        for t in range(NT):
            YB[t, k, pl.ds(0, PAD), :] = zeros
            TZ[t, k, pl.ds(PAD + CY, PAD), :] = zeros
        return carry

    lax.fori_loop(0, NZ, clear, 0)

    @pl.when(base)
    def _():
        strip_b[FROM_SOUTH, :] = jnp.zeros((2, CX), jnp.int32)
        for t in range(NT):
            for k in range(NZ):
                strip[t, k, FROM_SOUTH, :] = jnp.zeros((2, CX), jnp.float32)

    for copy in early:
        copy.wait()

    def send(source, target, index, slot, device):
        return pltpu.make_async_remote_copy(
            src_ref=source, dst_ref=target, send_sem=send_sem.at[index], recv_sem=recv_sem.at[slot],
            device_id=device, device_id_type=MESH,
        )

    def bundle(sources, targets, index, slot, device):
        pairs = enumerate(zip(sources, targets, strict=True))
        return [send(source, target, index + i, slot + i, device) for i, (source, target) in pairs]

    def start(copies):
        for copy in copies:
            copy.start()

    def wait_recv(copies):
        for copy in copies:
            copy.wait_recv()

    def wait_send(copies):
        for copy in copies:
            copy.wait_send()

    eastward = send(to_east, from_west, 0, 0, east_id)
    westward = send(to_west, from_east, 1, 1, west_id)
    last = [strip.at[:, :, OWN_LAST, :], strip_b.at[OWN_LAST, :], strip_v.at[:, pl.ds(1, 1), :]]
    first = [strip.at[:, :, OWN_FIRST, :], strip_b.at[OWN_FIRST, :]]
    from_south = [strip.at[:, :, FROM_SOUTH, :], strip_b.at[FROM_SOUTH, :], strip_v.at[:, pl.ds(5, 1), :]]
    from_north = [strip.at[:, :, FROM_NORTH, :], strip_b.at[FROM_NORTH, :]]
    between = [relay, relay_b, relay_v]
    northward = bundle(last, from_south, 2, 2, north_id)
    southward = bundle(first, from_north, 5, 5, south_id)
    across = bundle(last[:2], from_north, 2, 5, mirror_id)
    handed_up = bundle(last, between, 2, 7, (chip_mate, gy))
    handed_down = bundle(first, between[:2], 5, 7, (chip_mate, gy))
    forwarded_up = bundle(between, from_south, 7, 2, (chip_mate, gy + 1))
    forwarded_down = bundle(between[:2], from_north, 7, 5, (chip_mate, gy - 1))
    northward_itself = jnp.logical_not(top | relayed_up)
    southward_itself = jnp.logical_not(base | relayed_down)
    even = lax.rem(gx, 2) == 0
    late_entry = below_middle & jnp.logical_not(relayed_up) & (place < BLOCK - 2)

    @pl.when(jnp.logical_not(late_entry))
    def _():
        pl.semaphore_wait(barrier, expected)

        @pl.when(before_seam)
        def _():
            pl.semaphore_signal(go_sem, inc=1, device_id=east_id, device_id_type=MESH)

        @pl.when(above_go)
        def _():
            pl.semaphore_signal(go_north_sem, inc=1, device_id=south_id, device_id_type=MESH)

        pl.when(northward_itself & below_middle)(lambda: start(northward))
        pl.when(relayed_up)(lambda: start(handed_up))

        @pl.when(relays_up)
        def _():
            wait_recv(handed_up)
            start(forwarded_up)

        pl.when(southward_itself)(lambda: start(southward))
        pl.when(relayed_down)(lambda: start(handed_down))
        pl.when(northward_itself & jnp.logical_not(below_middle | above_middle))(lambda: start(northward))
        pl.when(top)(lambda: start(across))

        @pl.when(relays_down)
        def _():
            wait_recv(handed_down)
            start(forwarded_down)

    def send_columns():
        pl.when(jnp.logical_not(even))(eastward.start)
        pl.when(jnp.logical_not(after_seam))(westward.start)
        pl.when(even)(eastward.start)

    for copy in late[:3]:
        copy.wait()

    for o in range(OCTETS):
        bf[octet(o), :] = bottom_int[pl.ds(8 * o, 8), :].astype(jnp.float32)
    for o in range(OCTETS):
        here = bf[octet(o), :]
        be[octet(o), :] = jnp.where(lane == CX - 1, 0.0, jnp.minimum(here, lanes_left(here)))
        bn[octet(o), :] = jnp.minimum(here, bf[shifted(o, 1), :])

    slot_of = lane // 4

    def pack(group, carry):
        t0, t1, speed = zeros, zeros, zeros
        for b in range(4):
            for o in range(OCTETS):
                slot = b * 8 + o
                here = slot_of == slot
                shift = (4 * slot + 2) % CX
                k = 4 * group + b
                t0 = jnp.where(here, pltpu.roll(T[0, k, octet(o), :], shift, 1), t0)
                t1 = jnp.where(here, pltpu.roll(T[1, k, octet(o), :], shift, 1), t1)
                speed = jnp.where(here, pltpu.roll(U[k, pl.ds(8 * o, 8), :], shift, 1), speed)
        packed[group] = t0
        packed[4 + group] = t1
        packed[8 + group] = speed
        return carry

    lax.fori_loop(0, 4, pack, 0, unroll=4)
    packed_b = zeros
    for b in range(4):
        for o in range(OCTETS):
            slot = b * 8 + o
            packed_b = jnp.where(
                slot_of == slot, pltpu.roll(bf[octet(o), :], (4 * slot + 2) % CX, 1), packed_b
            )
    packed[12] = packed_b

    first_half = lax.rem(lane, 4) < 2
    east_speeds = zeros
    for j in range(4):
        to_east[j] = jnp.where(first_half, packed[j], pltpu.roll(packed[4 + j], 2, 1))
        to_west[j] = jnp.where(first_half, pltpu.roll(packed[4 + j], CX - 2, 1), packed[j])
        east_speeds = jnp.where(
            lax.rem(lane, 4) == j, pltpu.roll(packed[8 + j], (CX + j - 1) % CX, 1), east_speeds
        )
    to_east[4] = east_speeds
    to_east[5] = packed_b
    to_west[4] = packed_b

    pl.when(jnp.logical_not(late_entry))(send_columns)


    late[3].wait()

    def vertical(k, carry):
        level = k.astype(jnp.float32)
        above = jnp.where(k > 0, level, 99.0)
        down, up = jnp.minimum(k + 1, NZ - 1), jnp.maximum(k - 1, 0)
        for o in range(OCTETS):
            depth = bf[octet(o), :]
            for t in range(NT):
                here = T[t, k, octet(o), :]
                TZ[t, k, octet(o), :] = jnp.where(
                    depth > level + 1.0, T[t, down, octet(o), :] - here, 0.0
                ) + jnp.where(depth > above, here - T[t, up, octet(o), :], 0.0)
        return carry

    lax.fori_loop(0, NZ, vertical, 0, unroll=2)

    def inside(k, carry):
        level = k.astype(jnp.float32)
        for o in range(OCTETS):
            here = [T[t, k, octet(o), :] for t in range(NT)]
            dz = [TZ[t, k, octet(o), :] for t in range(NT)]
            wet = be[octet(o), :] > level
            local = [jnp.where(wet, lanes_left(f) - f, 0.0) for f in here]
            before = [lanes_right(d) for d in local]
            after = [lanes_left(d) for d in local]
            speed = jnp.where(wet, U[k, pl.ds(8 * o, 8), :], 0.0)
            low, high, _, _ = face_fluxes(
                local, before, after, [z + lanes_left(z) for z in dz], speed
            )
            across_x = [lanes_right(high[t]) - low[t] for t in range(NT)]
            for t in range(NT):
                GX[t, k, octet(o), :] = local[t] + before[t]

            wet = bn[octet(o), :] > level
            wet_before = bn[shifted(o, -1), :] > level
            wet_after = bn[shifted(o, 1), :] > level
            nxt = [T[t, k, shifted(o, 1), :] for t in range(NT)]
            local = [jnp.where(wet, nxt[t] - here[t], 0.0) for t in range(NT)]
            before = [
                jnp.where(wet_before, here[t] - T[t, k, shifted(o, -1), :], 0.0) for t in range(NT)
            ]
            after = [
                jnp.where(wet_after, T[t, k, shifted(o, 2), :] - nxt[t], 0.0) for t in range(NT)
            ]
            speed = jnp.where(wet, V[k, pl.ds(8 * o, 8), :], 0.0)
            low, high, _, _ = face_fluxes(
                local, before, after, [dz[t] + TZ[t, k, shifted(o, 1), :] for t in range(NT)], speed
            )
            for t in range(NT):
                GY[t, k, octet(o), :] = local[t] + before[t]
                XY[t, k, octet(o), :] = across_x[t] - low[t]
                YB[t, k, octet(o), :] = high[t]
        return carry

    lax.fori_loop(0, NZ, inside, 0, unroll=2)

    @pl.when(late_entry)
    def _():
        pl.semaphore_wait(barrier, expected)
        start(northward)

        @pl.when(relays_up)
        def _():
            wait_recv(handed_up)
            start(forwarded_up)

        send_columns()
        start(southward)

    @pl.when(above_middle)
    def _():
        pl.semaphore_wait(go_north_sem, 1)
        start(northward)

    @pl.when(after_seam)
    def _():
        pl.semaphore_wait(go_sem, 1)
        westward.start()

    def prepare(octets):
        def body(k, carry):
            level = k.astype(jnp.float32)
            down = jnp.minimum(k + 1, NZ - 1)
            for o in octets:
                open_below = bf[octet(o), :] > level + 1.0
                here = [T[t, k, octet(o), :] for t in range(NT)]
                step = [T[t, down, octet(o), :] - here[t] for t in range(NT)]
                mean_y = [GY[t, k, octet(o), :] + GY[t, down, octet(o), :] for t in range(NT)]
                inverse = jnp.where(
                    open_below, reciprocal(jnp.maximum(4.0 * density(step), 1.0)), 0.0
                )
                slope = jnp.clip(density(mean_y) * inverse, -1.0, 1.0)
                square = 0.1 * (slope * slope)
                slope = 0.025 * slope
                Q[k, octet(o), :] = inverse
                for t in range(NT):
                    FY[t, k, octet(o), :] = square * step[t] - slope * mean_y[t]
                    XY[t, k, octet(o), :] += here[t] + YB[t, k, shifted(o, -1), :]
            return carry

        lax.fori_loop(0, NZ, body, 0, unroll=2)

    inner, outer = tuple(range(1, OCTETS - 1)), (0, OCTETS - 1)
    prepare(inner)

    def edge_rows_in():
        wait_recv(southward)
        pl.when(jnp.logical_not(base))(lambda: wait_recv(northward))

        @pl.when(top)
        def _():
            def gather(k, carry):
                for t in range(NT):
                    folded[pl.ds(2 * (NZ * t + k), 2), :] = strip[t, k, FROM_NORTH, :]
                return carry

            def scatter(k, carry):
                for t in range(NT):
                    strip[t, k, FROM_NORTH, :] = folded[pl.ds(2 * (NZ * t + k), 2), :]
                return carry

            lax.fori_loop(0, NZ, gather, 0, unroll=4)
            folded[pl.ds(64, 8), :] = strip_b[...].astype(jnp.float32)
            for i in range(FOLD_ROWS // 8):
                value = folded[pl.ds(8 * i, 8), :]
                for bit in (64, 32, 16, 8, 4, 2, 1):
                    value = jnp.where(
                        (lane & bit) != 0, pltpu.roll(value, bit, 1), pltpu.roll(value, CX - bit, 1)
                    )
                folded[pl.ds(8 * i, 8), :] = jnp.where(
                    (row & 1) != 0, rows_down(value), rows_up(value)
                )
            lax.fori_loop(0, NZ, scatter, 0, unroll=4)
            strip_b[FROM_NORTH, :] = folded[pl.ds(66, 2), :].astype(jnp.int32)

        def edge_rows(k, carry):
            level = k.astype(jnp.float32)
            above = jnp.where(k > 0, level, 99.0)
            down, up = jnp.minimum(k + 1, NZ - 1), jnp.maximum(k - 1, 0)
            depth = strip_b[...].astype(jnp.float32)
            here = [strip[t, k] for t in range(NT)]
            dz = [
                jnp.where(depth > level + 1.0, strip[t, down] - here[t], 0.0)
                + jnp.where(depth > above, here[t] - strip[t, up], 0.0)
                for t in range(NT)
            ]
            terms, grads = edge_terms(
                here, dz, depth, strip_v[k], level, rows_up, rows_down,
                row == 1, row == 5, row == 0, row == 6,
            )
            for t in range(NT):
                XY[t, k, octet(0), :] += jnp.where(row < 2, pltpu.roll(terms[t], 2, 0), 0.0)
                GY[t, k, octet(0), :] += jnp.where(row < 2, pltpu.roll(grads[t], 2, 0), 0.0)
                XY[t, k, octet(OCTETS - 1), :] += jnp.where(row > 5, pltpu.roll(terms[t], 6, 0), 0.0)
                GY[t, k, octet(OCTETS - 1), :] += jnp.where(row > 5, pltpu.roll(grads[t], 6, 0), 0.0)
            return carry

        lax.fori_loop(0, NZ, edge_rows, 0, unroll=16)

    rows_late = below_middle | above_middle | (gy == n_gy // 2 - 2) | top

    @pl.when(jnp.logical_not(rows_late))
    def _():
        edge_rows_in()
        prepare(outer)

    quarter = lax.rem(lane, 4)
    level_in_group = (lane // 32).astype(jnp.float32)
    def edge_columns_in(side, first):
        (eastward if side == 0 else westward).wait_recv()
        own = [[packed[4 * t + j] for j in range(4)] for t in range(NT)]
        if side == 0:
            depth = jnp.where(first_half, from_west[5], packed[12])
            fields = [
                [jnp.where(first_half, from_west[j], own[0][j]) for j in range(4)],
                [jnp.where(first_half, pltpu.roll(from_west[j], CX - 2, 1), own[1][j]) for j in range(4)],
            ]
        else:
            depth = jnp.where(first_half, packed[12], from_east[4])
            fields = [
                [jnp.where(first_half, own[0][j], from_east[j]) for j in range(4)],
                [jnp.where(first_half, own[1][j], pltpu.roll(from_east[j], 2, 1)) for j in range(4)],
            ]
        steps = []
        for t in range(NT):
            turned = [pltpu.roll(f, CX - 32, 1) for f in fields[t]]
            steps.append(
                [
                    jnp.where(
                        depth > level_in_group + (4 * j + 1.0),
                        jnp.where(lane < CX - 32, turned[j], turned[min(j + 1, 3)]) - fields[t][j],
                        0.0,
                    )
                    for j in range(4)
                ]
            )
        for j in range(4):
            dz = []
            for t in range(NT):
                before = pltpu.roll(steps[t][j - 1], 32, 1) if j > 0 else zeros
                dz.append(
                    steps[t][j] + jnp.where(lane < 32, before, pltpu.roll(steps[t][j], 32, 1))
                )
            speed = packed[8 + j]
            if side == 0:
                speed = jnp.where(first_half, pltpu.roll(from_west[4], (CX + 1 - j) % CX, 1), speed)
            terms, grads = edge_terms(
                [fields[t][j] for t in range(NT)], dz, depth, speed, level_in_group + 4.0 * j,
                lanes_left, lanes_right,
                None if side == 0 else quarter == 1, quarter == 1 if side == 0 else None,
                None if side == 0 else quarter == 0, quarter == 2 if side == 0 else None,
            )
            for t in range(NT):
                if first:
                    edge_c[t, j] = terms[t]
                    edge_g[t, j] = grads[t]
                else:
                    edge_c[t, j] += terms[t]
                    edge_g[t, j] += grads[t]

    @pl.when(even)
    def _():
        edge_columns_in(1, True)
        edge_columns_in(0, False)

    @pl.when(jnp.logical_not(even))
    def _():
        edge_columns_in(0, True)
        edge_columns_in(1, False)

    at_edge = (lane < 2) | (lane >= CX - 2)

    def finish(octets, prepared):
        def at(o, ref, t, group, b):
            rolled = pltpu.roll(ref[t, group], (CX - (4 * (b * 8 + o) + 2)) % CX, 1)
            return jnp.where(at_edge, rolled, 0.0)

        def body(group, carry):
            fluxes = [[carry[4 * i], carry[4 * i + 1]] for i in range(len(octets))]
            gx_here = [[carry[4 * i + 2], carry[4 * i + 3]] for i in range(len(octets))]
            after = jnp.minimum(group + 1, 3)
            for b in range(4):
                k = 4 * group + b
                level = k.astype(jnp.float32)
                down = jnp.minimum(k + 1, NZ - 1)
                for i, o in enumerate(octets):
                    depth = bf[octet(o), :]
                    here = [T[t, k, octet(o), :] for t in range(NT)]
                    step = [T[t, down, octet(o), :] - here[t] for t in range(NT)]
                    gx_down = [
                        GX[t, down, octet(o), :]
                        + (at(o, edge_g, t, group, b + 1) if b < 3 else at(o, edge_g, t, after, 0))
                        for t in range(NT)
                    ]
                    mean_x = [gx_here[i][t] + gx_down[t] for t in range(NT)]
                    wet = depth > level
                    if prepared:
                        inverse = Q[k, octet(o), :]
                        other = [FY[t, k, octet(o), :] for t in range(NT)]
                        rest = [XY[t, k, octet(o), :] for t in range(NT)]
                    else:
                        mean_y = [
                            GY[t, k, octet(o), :] + GY[t, down, octet(o), :] for t in range(NT)
                        ]
                        inverse = jnp.where(
                            depth > level + 1.0, reciprocal(jnp.maximum(4.0 * density(step), 1.0)), 0.0
                        )
                        slope = jnp.clip(density(mean_y) * inverse, -1.0, 1.0)
                        square = 0.1 * (slope * slope)
                        slope = 0.025 * slope
                        other = [square * step[t] - slope * mean_y[t] for t in range(NT)]
                        rest = [
                            here[t] + (XY[t, k, octet(o), :] + YB[t, k, shifted(o, -1), :])
                            for t in range(NT)
                        ]
                    slope = jnp.clip(density(mean_x) * inverse, -1.0, 1.0)
                    square = 0.1 * (slope * slope)
                    slope = 0.025 * slope
                    for t in range(NT):
                        flux = other[t] + (square * step[t] - slope * mean_x[t])
                        total = (rest[t] + at(o, edge_c, t, group, b)) + (flux - fluxes[i][t])
                        out[t, k, pl.ds(8 * o, 8), :] = jnp.where(wet, total, 0.0)
                        fluxes[i][t] = flux
                    gx_here[i] = gx_down
            return tuple(x for i in range(len(octets)) for x in (*fluxes[i], *gx_here[i]))

        start = []
        for o in octets:
            start += [zeros, zeros]
            start += [GX[t, 0, octet(o), :] + at(o, edge_g, t, 0, 0) for t in range(NT)]
        lax.fori_loop(0, 4, body, tuple(start), unroll=4)

    finish(inner, True)

    @pl.when(rows_late)
    def _():
        edge_rows_in()
        finish(outer, False)

    @pl.when(jnp.logical_not(rows_late))
    def _():
        finish(outer, True)

    eastward.wait_send()
    westward.wait_send()
    pl.when(southward_itself)(lambda: wait_send(southward))
    pl.when(northward_itself)(lambda: wait_send(northward))
    pl.when(relayed_up)(lambda: wait_send(handed_up))
    pl.when(relayed_down)(lambda: wait_send(handed_down))
    pl.when(top)(lambda: wait_send(across))
    pl.when(relays_up)(lambda: wait_send(forwarded_up))
    pl.when(relays_down)(lambda: wait_send(forwarded_down))


def solution(mesh):
    n_gx, n_gy = mesh.shape["gx"], mesh.shape["gy"]
    f32 = jnp.float32
    in_hbm = pl.BlockSpec(memory_space=pltpu.HBM)
    field = pltpu.VMEM((NT, NZ, TALL, CX), f32)
    levels = pltpu.VMEM((NZ, CY, CX), f32)
    plane = pltpu.VMEM((TALL, CX), f32)
    packed = pltpu.VMEM((PACKED, 8, CX), f32)
    eastward = pltpu.VMEM((EASTWARD, 8, CX), f32)
    westward = pltpu.VMEM((WESTWARD, 8, CX), f32)
    edge = pltpu.VMEM((NT, 4, 8, CX), f32)

    def on_device(tracers, east_speed, north_speed, bottom_level):
        return pl.pallas_call(
            functools.partial(kernel, n_gx, n_gy),
            out_shape=jax.ShapeDtypeStruct((NT, NZ, CY, CX), f32),
            in_specs=[in_hbm] * 4,
            out_specs=pl.BlockSpec(memory_space=pltpu.VMEM),
            scratch_shapes=[
                field, levels, levels, pltpu.VMEM((CY, CX), jnp.int32), plane, plane, plane,
                field, field, field, field, field, field, pltpu.VMEM((NZ, TALL, CX), f32),
                packed, eastward, westward, eastward, westward,
                pltpu.VMEM((NT, NZ, 2, CX), f32), pltpu.VMEM((2, CX), jnp.int32),
                pltpu.VMEM((NZ, 1, CX), f32), pltpu.VMEM((FOLD_ROWS, CX), f32),
                pltpu.VMEM((NT, NZ, 8, CX), f32), pltpu.VMEM((8, CX), jnp.int32),
                pltpu.VMEM((NZ, 8, CX), f32), edge, edge,
                pltpu.SemaphoreType.DMA((10,)), pltpu.SemaphoreType.DMA((10,)),
                pltpu.SemaphoreType.DMA((10,)), pltpu.SemaphoreType.REGULAR, pltpu.SemaphoreType.REGULAR,
            ],
            compiler_params=pltpu.CompilerParams(
                collective_id=0, has_side_effects=True, vmem_limit_bytes=24 * 1024 * 1024
            ),
        )(
            *[
                pltpu.with_memory_space_constraint(x, pltpu.HBM)
                for x in (tracers, east_speed, north_speed, bottom_level)
            ]
        )

    in_specs = (P(None, None, "gy", "gx"), P(None, "gy", "gx"), P(None, "gy", "gx"), P("gy", "gx"))
    return jax.shard_map(
        on_device, mesh=mesh, in_specs=in_specs, out_specs=P(None, None, "gy", "gx"), check_vma=False
    )
```

```python
import functools

import jax
import jax.numpy as jnp
from jax import lax
from jax.experimental import pallas as pl
from jax.experimental.pallas import tpu as pltpu
from jax.sharding import PartitionSpec as P

MESH = pl.DeviceIdType.MESH
NT, NZ, CY, CX = 2, 16, 48, 128
PAD = 8
TALL = CY + 2 * PAD
OCTETS = CY // 8
FOLD_ROWS = 72
OWN_LAST, FROM_NORTH, FROM_SOUTH, OWN_FIRST = (pl.ds(i, 2) for i in (0, 2, 4, 6))
PACKED = 13
EASTWARD = 6
WESTWARD = 5
BLOCK = 8
HEAT = 0.4
SALT = 0.6


def reciprocal(value):
    guess = pl.reciprocal(value, approx=True)
    return guess * (2.0 - value * guess)


def minmod(first, second):
    return jnp.maximum(jnp.minimum(first, second), 0.0) + jnp.minimum(
        jnp.maximum(first, second), 0.0
    )


def density(pair):
    return SALT * pair[1] - HEAT * pair[0]


def face_fluxes(local, before, after, dz_sum, speed):
    slope = jnp.clip(
        (0.1 * density(local)) * reciprocal(jnp.maximum(density(dz_sum), 1.0)), -0.025, 0.025
    )
    size = jnp.abs(speed)
    limited = 0.5 * size * (1.0 - size)
    forward = speed >= 0.0
    linear = jnp.minimum(speed, 0.0) - 0.1
    low, high, second = [], [], []
    for t in range(NT):
        correction = limited * minmod(local[t], jnp.where(forward, before[t], after[t]))
        taken = correction + (linear * local[t] + slope * dz_sum[t])
        low.append(taken)
        high.append(taken - speed * local[t])
        second.append(correction)
    return low, high, second, forward


def lanes_left(value):
    return pltpu.roll(value, CX - 1, 1)


def lanes_right(value):
    return pltpu.roll(value, 1, 1)


def rows_up(value):
    return pltpu.roll(value, 7, 0)


def rows_down(value):
    return pltpu.roll(value, 1, 0)


def edge_terms(field, dz, bottom, speed, level, nxt, prv, low_at, high_at, low_second, high_second):
    wet = jnp.minimum(bottom, nxt(bottom)) > level
    local = [jnp.where(wet, nxt(f) - f, 0.0) for f in field]
    dz_sum = [z + nxt(z) for z in dz]
    masked = jnp.where(wet, speed, 0.0)
    low, high, second, forward = face_fluxes(
        local, [prv(d) for d in local], [nxt(d) for d in local], dz_sum, masked
    )
    zero = jnp.zeros_like(masked)
    terms, steps = [], []
    for t in range(NT):
        late = zero
        if low_second is not None:
            late = late + jnp.where(low_second & ~forward, second[t], 0.0)
        if high_second is not None:
            late = late + jnp.where(high_second & forward, second[t], 0.0)
        arriving, term, step = late, -late, zero
        if high_at is not None:
            arriving = arriving + jnp.where(high_at, high[t], 0.0)
            step = step + prv(jnp.where(high_at, local[t], 0.0))
        if low_at is not None:
            term = term - jnp.where(low_at, low[t], 0.0)
            step = step + jnp.where(low_at, local[t], 0.0)
        terms.append(term + prv(arriving))
        steps.append(step)
    return terms, steps


def kernel(
    n_gx, n_gy,
    tracers, east, north, bottom, out,
    T, U, V, bottom_int, bf, be, bn, TZ, XY, YB, GX, GY, FY, Q,
    packed, to_east, to_west, from_west, from_east, relay, relay_b, relay_v, folded,
    strip, strip_b, strip_v, edge_c, edge_g,
    load_sem, send_sem, recv_sem, go_sem, go_north_sem,
):
    gx, gy = lax.axis_index("gx"), lax.axis_index("gy")
    east_id = (lax.rem(gx + 1, n_gx), gy)
    west_id = (lax.rem(gx + n_gx - 1, n_gx), gy)
    north_id = (gx, gy + 1)
    south_id = (gx, gy - 1)
    mirror_id = (n_gx - 1 - gx, gy)
    top = gy == n_gy - 1
    base = gy == 0
    below_middle = gy == n_gy // 2 - 1
    above_middle = gy == n_gy // 2
    place = lax.rem(gx, BLOCK)
    by_go = gy <= n_gy // 2
    after_seam = (place == 0) & by_go
    before_seam = (place == BLOCK - 1) & by_go
    crosses_down = place == BLOCK - 1
    crosses_up = crosses_down | (place == 2) | (place == 0)
    relayed_up = crosses_up & below_middle
    relayed_down = crosses_down & above_middle
    relays_up = ((place == BLOCK - 2) | (place == 3) | (place == 1)) & below_middle
    relays_down = (place == BLOCK - 2) & above_middle
    chip_mate = gx + 1 - 2 * lax.rem(gx, 2)

    barrier = pltpu.get_barrier_semaphore()

    def greet(device):
        pl.semaphore_signal(barrier, inc=1, device_id=device, device_id_type=MESH)

    pl.when(top)(lambda: greet(mirror_id))
    above_go = gy == n_gy // 2 + 1
    mate_sends_down = crosses_down & below_middle
    mate_sends_up = crosses_up & above_middle
    pl.when(mate_sends_down)(lambda: greet((chip_mate, gy + 1)))
    pl.when(mate_sends_up)(lambda: greet((chip_mate, gy - 1)))
    pl.when(jnp.logical_not(top | mate_sends_down))(lambda: greet(north_id))
    pl.when(jnp.logical_not(base | mate_sends_up | above_go))(lambda: greet(south_id))
    greet(west_id)
    pl.when(jnp.logical_not(before_seam))(lambda: greet(east_id))
    expected = (
        4 + (relays_up | relays_down).astype(jnp.int32) - (relayed_up | relayed_down).astype(jnp.int32)
        - after_seam.astype(jnp.int32) - base.astype(jnp.int32) - above_middle.astype(jnp.int32)
    )

    def load(source, target, index):
        copy = pltpu.make_async_copy(source, target, load_sem.at[index])
        copy.start()
        return copy

    last_rows, first_rows = pl.ds(CY - 2, 2), pl.ds(0, 2)
    early = [
        load(tracers.at[:, :, last_rows, :], strip.at[:, :, OWN_LAST, :], 0),
        load(tracers.at[:, :, first_rows, :], strip.at[:, :, OWN_FIRST, :], 1),
        load(bottom.at[last_rows, :], strip_b.at[OWN_LAST, :], 2),
        load(bottom.at[first_rows, :], strip_b.at[OWN_FIRST, :], 3),
        load(north.at[:, last_rows, :], strip_v.at[:, OWN_LAST, :], 4),
        load(north.at[:, first_rows, :], strip_v.at[:, OWN_FIRST, :], 5),
    ]
    late = [
        load(tracers, T.at[:, :, pl.ds(PAD, CY), :], 6),
        load(bottom, bottom_int, 7),
        load(east, U, 8),
        load(north, V, 9),
    ]

    lane = lax.broadcasted_iota(jnp.int32, (8, CX), 1)
    row = lax.broadcasted_iota(jnp.int32, (8, CX), 0)
    zeros = jnp.zeros((8, CX), jnp.float32)

    def octet(o):
        return pl.ds(PAD + 8 * o, 8)

    def shifted(o, by):
        return pl.ds(PAD + 8 * o + by, 8)

    for pad in (pl.ds(0, PAD), pl.ds(PAD + CY, PAD)):
        bf[pad, :] = zeros
        bn[pad, :] = zeros

    def clear(k, carry):
        for t in range(NT):
            YB[t, k, pl.ds(0, PAD), :] = zeros
            TZ[t, k, pl.ds(PAD + CY, PAD), :] = zeros
        return carry

    lax.fori_loop(0, NZ, clear, 0)

    @pl.when(base)
    def _():
        strip_b[FROM_SOUTH, :] = jnp.zeros((2, CX), jnp.int32)
        for t in range(NT):
            for k in range(NZ):
                strip[t, k, FROM_SOUTH, :] = jnp.zeros((2, CX), jnp.float32)

    for copy in early:
        copy.wait()

    def send(source, target, index, slot, device):
        return pltpu.make_async_remote_copy(
            src_ref=source, dst_ref=target, send_sem=send_sem.at[index], recv_sem=recv_sem.at[slot],
            device_id=device, device_id_type=MESH,
        )

    def bundle(sources, targets, index, slot, device):
        pairs = enumerate(zip(sources, targets, strict=True))
        return [send(source, target, index + i, slot + i, device) for i, (source, target) in pairs]

    def start(copies):
        for copy in copies:
            copy.start()

    def wait_recv(copies):
        for copy in copies:
            copy.wait_recv()

    def wait_send(copies):
        for copy in copies:
            copy.wait_send()

    eastward = send(to_east, from_west, 0, 0, east_id)
    westward = send(to_west, from_east, 1, 1, west_id)
    last = [strip.at[:, :, OWN_LAST, :], strip_b.at[OWN_LAST, :], strip_v.at[:, pl.ds(1, 1), :]]
    first = [strip.at[:, :, OWN_FIRST, :], strip_b.at[OWN_FIRST, :]]
    from_south = [strip.at[:, :, FROM_SOUTH, :], strip_b.at[FROM_SOUTH, :], strip_v.at[:, pl.ds(5, 1), :]]
    from_north = [strip.at[:, :, FROM_NORTH, :], strip_b.at[FROM_NORTH, :]]
    between = [relay, relay_b, relay_v]
    northward = bundle(last, from_south, 2, 2, north_id)
    southward = bundle(first, from_north, 5, 5, south_id)
    across = bundle(last[:2], from_north, 2, 5, mirror_id)
    handed_up = bundle(last, between, 2, 7, (chip_mate, gy))
    handed_down = bundle(first, between[:2], 5, 7, (chip_mate, gy))
    forwarded_up = bundle(between, from_south, 7, 2, (chip_mate, gy + 1))
    forwarded_down = bundle(between[:2], from_north, 7, 5, (chip_mate, gy - 1))
    northward_itself = jnp.logical_not(top | relayed_up)
    southward_itself = jnp.logical_not(base | relayed_down)
    even = lax.rem(gx, 2) == 0
    late_entry = below_middle & jnp.logical_not(relayed_up) & (place < BLOCK - 2)

    @pl.when(jnp.logical_not(late_entry))
    def _():
        pl.semaphore_wait(barrier, expected)

        @pl.when(before_seam)
        def _():
            pl.semaphore_signal(go_sem, inc=1, device_id=east_id, device_id_type=MESH)

        @pl.when(above_go)
        def _():
            pl.semaphore_signal(go_north_sem, inc=1, device_id=south_id, device_id_type=MESH)

        pl.when(relayed_up)(lambda: start(handed_up))

        @pl.when(relays_up)
        def _():
            wait_recv(handed_up)
            start(forwarded_up)

        pl.when(northward_itself & below_middle)(lambda: start(northward))
        pl.when(relayed_down)(lambda: start(handed_down))
        pl.when(southward_itself & jnp.logical_not(relays_down))(lambda: start(southward))
        pl.when(northward_itself & jnp.logical_not(below_middle | above_middle))(lambda: start(northward))
        pl.when(top)(lambda: start(across))

        @pl.when(relays_down)
        def _():
            wait_recv(handed_down)
            start(forwarded_down)
            start(southward)

    def send_columns():
        pl.when(jnp.logical_not(even))(eastward.start)
        pl.when(jnp.logical_not(after_seam))(westward.start)
        pl.when(even)(eastward.start)

    for copy in late[:3]:
        copy.wait()

    for o in range(OCTETS):
        bf[octet(o), :] = bottom_int[pl.ds(8 * o, 8), :].astype(jnp.float32)
    for o in range(OCTETS):
        here = bf[octet(o), :]
        be[octet(o), :] = jnp.where(lane == CX - 1, 0.0, jnp.minimum(here, lanes_left(here)))
        bn[octet(o), :] = jnp.minimum(here, bf[shifted(o, 1), :])

    slot_of = lane // 4

    def pack(group, carry):
        t0, t1, speed = zeros, zeros, zeros
        for b in range(4):
            for o in range(OCTETS):
                slot = b * 8 + o
                here = slot_of == slot
                shift = (4 * slot + 2) % CX
                k = 4 * group + b
                t0 = jnp.where(here, pltpu.roll(T[0, k, octet(o), :], shift, 1), t0)
                t1 = jnp.where(here, pltpu.roll(T[1, k, octet(o), :], shift, 1), t1)
                speed = jnp.where(here, pltpu.roll(U[k, pl.ds(8 * o, 8), :], shift, 1), speed)
        packed[group] = t0
        packed[4 + group] = t1
        packed[8 + group] = speed
        return carry

    lax.fori_loop(0, 4, pack, 0, unroll=4)
    packed_b = zeros
    for b in range(4):
        for o in range(OCTETS):
            slot = b * 8 + o
            packed_b = jnp.where(
                slot_of == slot, pltpu.roll(bf[octet(o), :], (4 * slot + 2) % CX, 1), packed_b
            )
    packed[12] = packed_b

    first_half = lax.rem(lane, 4) < 2
    east_speeds = zeros
    for j in range(4):
        to_east[j] = jnp.where(first_half, packed[j], pltpu.roll(packed[4 + j], 2, 1))
        to_west[j] = jnp.where(first_half, pltpu.roll(packed[4 + j], CX - 2, 1), packed[j])
        east_speeds = jnp.where(
            lax.rem(lane, 4) == j, pltpu.roll(packed[8 + j], (CX + j - 1) % CX, 1), east_speeds
        )
    to_east[4] = east_speeds
    to_east[5] = packed_b
    to_west[4] = packed_b

    pl.when(jnp.logical_not(late_entry))(send_columns)


    late[3].wait()

    def vertical(k, carry):
        level = k.astype(jnp.float32)
        above = jnp.where(k > 0, level, 99.0)
        down, up = jnp.minimum(k + 1, NZ - 1), jnp.maximum(k - 1, 0)
        for o in range(OCTETS):
            depth = bf[octet(o), :]
            for t in range(NT):
                here = T[t, k, octet(o), :]
                TZ[t, k, octet(o), :] = jnp.where(
                    depth > level + 1.0, T[t, down, octet(o), :] - here, 0.0
                ) + jnp.where(depth > above, here - T[t, up, octet(o), :], 0.0)
        return carry

    lax.fori_loop(0, NZ, vertical, 0, unroll=2)

    def inside(k, carry):
        level = k.astype(jnp.float32)
        for o in range(OCTETS):
            here = [T[t, k, octet(o), :] for t in range(NT)]
            dz = [TZ[t, k, octet(o), :] for t in range(NT)]
            wet = be[octet(o), :] > level
            local = [jnp.where(wet, lanes_left(f) - f, 0.0) for f in here]
            before = [lanes_right(d) for d in local]
            after = [lanes_left(d) for d in local]
            speed = jnp.where(wet, U[k, pl.ds(8 * o, 8), :], 0.0)
            low, high, _, _ = face_fluxes(
                local, before, after, [z + lanes_left(z) for z in dz], speed
            )
            across_x = [lanes_right(high[t]) - low[t] for t in range(NT)]
            for t in range(NT):
                GX[t, k, octet(o), :] = local[t] + before[t]

            wet = bn[octet(o), :] > level
            wet_before = bn[shifted(o, -1), :] > level
            wet_after = bn[shifted(o, 1), :] > level
            nxt = [T[t, k, shifted(o, 1), :] for t in range(NT)]
            local = [jnp.where(wet, nxt[t] - here[t], 0.0) for t in range(NT)]
            before = [
                jnp.where(wet_before, here[t] - T[t, k, shifted(o, -1), :], 0.0) for t in range(NT)
            ]
            after = [
                jnp.where(wet_after, T[t, k, shifted(o, 2), :] - nxt[t], 0.0) for t in range(NT)
            ]
            speed = jnp.where(wet, V[k, pl.ds(8 * o, 8), :], 0.0)
            low, high, _, _ = face_fluxes(
                local, before, after, [dz[t] + TZ[t, k, shifted(o, 1), :] for t in range(NT)], speed
            )
            for t in range(NT):
                GY[t, k, octet(o), :] = local[t] + before[t]
                XY[t, k, octet(o), :] = across_x[t] - low[t]
                YB[t, k, octet(o), :] = high[t]
        return carry

    lax.fori_loop(0, NZ, inside, 0, unroll=2)

    @pl.when(late_entry)
    def _():
        pl.semaphore_wait(barrier, expected)

        @pl.when(relays_up)
        def _():
            wait_recv(handed_up)
            start(forwarded_up)

        start(northward)
        send_columns()
        start(southward)

    @pl.when(above_middle)
    def _():
        pl.semaphore_wait(go_north_sem, 1)
        start(northward)

    @pl.when(after_seam)
    def _():
        pl.semaphore_wait(go_sem, 1)
        westward.start()

    def prepare(octets):
        def body(k, carry):
            level = k.astype(jnp.float32)
            down = jnp.minimum(k + 1, NZ - 1)
            for o in octets:
                open_below = bf[octet(o), :] > level + 1.0
                here = [T[t, k, octet(o), :] for t in range(NT)]
                step = [T[t, down, octet(o), :] - here[t] for t in range(NT)]
                mean_y = [GY[t, k, octet(o), :] + GY[t, down, octet(o), :] for t in range(NT)]
                inverse = jnp.where(
                    open_below, reciprocal(jnp.maximum(4.0 * density(step), 1.0)), 0.0
                )
                slope = jnp.clip(density(mean_y) * inverse, -1.0, 1.0)
                square = 0.1 * (slope * slope)
                slope = 0.025 * slope
                Q[k, octet(o), :] = inverse
                for t in range(NT):
                    FY[t, k, octet(o), :] = square * step[t] - slope * mean_y[t]
                    XY[t, k, octet(o), :] += here[t] + YB[t, k, shifted(o, -1), :]
            return carry

        lax.fori_loop(0, NZ, body, 0, unroll=2)

    inner, outer = tuple(range(1, OCTETS - 1)), (0, OCTETS - 1)
    prepare(inner)

    def edge_rows_in():
        wait_recv(southward)
        pl.when(jnp.logical_not(base))(lambda: wait_recv(northward))

        @pl.when(top)
        def _():
            def gather(k, carry):
                for t in range(NT):
                    folded[pl.ds(2 * (NZ * t + k), 2), :] = strip[t, k, FROM_NORTH, :]
                return carry

            def scatter(k, carry):
                for t in range(NT):
                    strip[t, k, FROM_NORTH, :] = folded[pl.ds(2 * (NZ * t + k), 2), :]
                return carry

            lax.fori_loop(0, NZ, gather, 0, unroll=4)
            folded[pl.ds(64, 8), :] = strip_b[...].astype(jnp.float32)
            for i in range(FOLD_ROWS // 8):
                value = folded[pl.ds(8 * i, 8), :]
                for bit in (64, 32, 16, 8, 4, 2, 1):
                    value = jnp.where(
                        (lane & bit) != 0, pltpu.roll(value, bit, 1), pltpu.roll(value, CX - bit, 1)
                    )
                folded[pl.ds(8 * i, 8), :] = jnp.where(
                    (row & 1) != 0, rows_down(value), rows_up(value)
                )
            lax.fori_loop(0, NZ, scatter, 0, unroll=4)
            strip_b[FROM_NORTH, :] = folded[pl.ds(66, 2), :].astype(jnp.int32)

        def edge_rows(k, carry):
            level = k.astype(jnp.float32)
            above = jnp.where(k > 0, level, 99.0)
            down, up = jnp.minimum(k + 1, NZ - 1), jnp.maximum(k - 1, 0)
            depth = strip_b[...].astype(jnp.float32)
            here = [strip[t, k] for t in range(NT)]
            dz = [
                jnp.where(depth > level + 1.0, strip[t, down] - here[t], 0.0)
                + jnp.where(depth > above, here[t] - strip[t, up], 0.0)
                for t in range(NT)
            ]
            terms, grads = edge_terms(
                here, dz, depth, strip_v[k], level, rows_up, rows_down,
                row == 1, row == 5, row == 0, row == 6,
            )
            for t in range(NT):
                XY[t, k, octet(0), :] += jnp.where(row < 2, pltpu.roll(terms[t], 2, 0), 0.0)
                GY[t, k, octet(0), :] += jnp.where(row < 2, pltpu.roll(grads[t], 2, 0), 0.0)
                XY[t, k, octet(OCTETS - 1), :] += jnp.where(row > 5, pltpu.roll(terms[t], 6, 0), 0.0)
                GY[t, k, octet(OCTETS - 1), :] += jnp.where(row > 5, pltpu.roll(grads[t], 6, 0), 0.0)
            return carry

        lax.fori_loop(0, NZ, edge_rows, 0, unroll=16)

    rows_late = ((gy >= n_gy // 2 - 2) & (gy <= n_gy // 2 + 1)) | top

    @pl.when(jnp.logical_not(rows_late))
    def _():
        edge_rows_in()
        prepare(outer)

    quarter = lax.rem(lane, 4)
    level_in_group = (lane // 32).astype(jnp.float32)
    def edge_columns_in(side, first):
        (eastward if side == 0 else westward).wait_recv()
        own = [[packed[4 * t + j] for j in range(4)] for t in range(NT)]
        if side == 0:
            depth = jnp.where(first_half, from_west[5], packed[12])
            fields = [
                [jnp.where(first_half, from_west[j], own[0][j]) for j in range(4)],
                [jnp.where(first_half, pltpu.roll(from_west[j], CX - 2, 1), own[1][j]) for j in range(4)],
            ]
        else:
            depth = jnp.where(first_half, packed[12], from_east[4])
            fields = [
                [jnp.where(first_half, own[0][j], from_east[j]) for j in range(4)],
                [jnp.where(first_half, own[1][j], pltpu.roll(from_east[j], 2, 1)) for j in range(4)],
            ]
        steps = []
        for t in range(NT):
            turned = [pltpu.roll(f, CX - 32, 1) for f in fields[t]]
            steps.append(
                [
                    jnp.where(
                        depth > level_in_group + (4 * j + 1.0),
                        jnp.where(lane < CX - 32, turned[j], turned[min(j + 1, 3)]) - fields[t][j],
                        0.0,
                    )
                    for j in range(4)
                ]
            )
        for j in range(4):
            dz = []
            for t in range(NT):
                before = pltpu.roll(steps[t][j - 1], 32, 1) if j > 0 else zeros
                dz.append(
                    steps[t][j] + jnp.where(lane < 32, before, pltpu.roll(steps[t][j], 32, 1))
                )
            speed = packed[8 + j]
            if side == 0:
                speed = jnp.where(first_half, pltpu.roll(from_west[4], (CX + 1 - j) % CX, 1), speed)
            terms, grads = edge_terms(
                [fields[t][j] for t in range(NT)], dz, depth, speed, level_in_group + 4.0 * j,
                lanes_left, lanes_right,
                None if side == 0 else quarter == 1, quarter == 1 if side == 0 else None,
                None if side == 0 else quarter == 0, quarter == 2 if side == 0 else None,
            )
            for t in range(NT):
                if first:
                    edge_c[t, j] = terms[t]
                    edge_g[t, j] = grads[t]
                else:
                    edge_c[t, j] += terms[t]
                    edge_g[t, j] += grads[t]

    @pl.when(even)
    def _():
        edge_columns_in(1, True)
        edge_columns_in(0, False)

    @pl.when(jnp.logical_not(even))
    def _():
        edge_columns_in(0, True)
        edge_columns_in(1, False)

    at_edge = (lane < 2) | (lane >= CX - 2)

    def finish(octets, prepared):
        def at(o, ref, t, group, b):
            rolled = pltpu.roll(ref[t, group], (CX - (4 * (b * 8 + o) + 2)) % CX, 1)
            return jnp.where(at_edge, rolled, 0.0)

        def body(group, carry):
            fluxes = [[carry[4 * i], carry[4 * i + 1]] for i in range(len(octets))]
            gx_here = [[carry[4 * i + 2], carry[4 * i + 3]] for i in range(len(octets))]
            after = jnp.minimum(group + 1, 3)
            for b in range(4):
                k = 4 * group + b
                level = k.astype(jnp.float32)
                down = jnp.minimum(k + 1, NZ - 1)
                for i, o in enumerate(octets):
                    depth = bf[octet(o), :]
                    here = [T[t, k, octet(o), :] for t in range(NT)]
                    step = [T[t, down, octet(o), :] - here[t] for t in range(NT)]
                    gx_down = [
                        GX[t, down, octet(o), :]
                        + (at(o, edge_g, t, group, b + 1) if b < 3 else at(o, edge_g, t, after, 0))
                        for t in range(NT)
                    ]
                    mean_x = [gx_here[i][t] + gx_down[t] for t in range(NT)]
                    wet = depth > level
                    if prepared:
                        inverse = Q[k, octet(o), :]
                        other = [FY[t, k, octet(o), :] for t in range(NT)]
                        rest = [XY[t, k, octet(o), :] for t in range(NT)]
                    else:
                        mean_y = [
                            GY[t, k, octet(o), :] + GY[t, down, octet(o), :] for t in range(NT)
                        ]
                        inverse = jnp.where(
                            depth > level + 1.0, reciprocal(jnp.maximum(4.0 * density(step), 1.0)), 0.0
                        )
                        slope = jnp.clip(density(mean_y) * inverse, -1.0, 1.0)
                        square = 0.1 * (slope * slope)
                        slope = 0.025 * slope
                        other = [square * step[t] - slope * mean_y[t] for t in range(NT)]
                        rest = [
                            here[t] + (XY[t, k, octet(o), :] + YB[t, k, shifted(o, -1), :])
                            for t in range(NT)
                        ]
                    slope = jnp.clip(density(mean_x) * inverse, -1.0, 1.0)
                    square = 0.1 * (slope * slope)
                    slope = 0.025 * slope
                    for t in range(NT):
                        flux = other[t] + (square * step[t] - slope * mean_x[t])
                        total = (rest[t] + at(o, edge_c, t, group, b)) + (flux - fluxes[i][t])
                        out[t, k, pl.ds(8 * o, 8), :] = jnp.where(wet, total, 0.0)
                        fluxes[i][t] = flux
                    gx_here[i] = gx_down
            return tuple(x for i in range(len(octets)) for x in (*fluxes[i], *gx_here[i]))

        start = []
        for o in octets:
            start += [zeros, zeros]
            start += [GX[t, 0, octet(o), :] + at(o, edge_g, t, 0, 0) for t in range(NT)]
        lax.fori_loop(0, 4, body, tuple(start), unroll=4)

    finish(inner, True)

    @pl.when(rows_late)
    def _():
        edge_rows_in()
        finish(outer, False)

    @pl.when(jnp.logical_not(rows_late))
    def _():
        finish(outer, True)

    eastward.wait_send()
    westward.wait_send()
    pl.when(southward_itself)(lambda: wait_send(southward))
    pl.when(northward_itself)(lambda: wait_send(northward))
    pl.when(relayed_up)(lambda: wait_send(handed_up))
    pl.when(relayed_down)(lambda: wait_send(handed_down))
    pl.when(top)(lambda: wait_send(across))
    pl.when(relays_up)(lambda: wait_send(forwarded_up))
    pl.when(relays_down)(lambda: wait_send(forwarded_down))


def solution(mesh):
    n_gx, n_gy = mesh.shape["gx"], mesh.shape["gy"]
    f32 = jnp.float32
    in_hbm = pl.BlockSpec(memory_space=pltpu.HBM)
    field = pltpu.VMEM((NT, NZ, TALL, CX), f32)
    levels = pltpu.VMEM((NZ, CY, CX), f32)
    plane = pltpu.VMEM((TALL, CX), f32)
    packed = pltpu.VMEM((PACKED, 8, CX), f32)
    eastward = pltpu.VMEM((EASTWARD, 8, CX), f32)
    westward = pltpu.VMEM((WESTWARD, 8, CX), f32)
    edge = pltpu.VMEM((NT, 4, 8, CX), f32)

    def on_device(tracers, east_speed, north_speed, bottom_level):
        return pl.pallas_call(
            functools.partial(kernel, n_gx, n_gy),
            out_shape=jax.ShapeDtypeStruct((NT, NZ, CY, CX), f32),
            in_specs=[in_hbm] * 4,
            out_specs=pl.BlockSpec(memory_space=pltpu.VMEM),
            scratch_shapes=[
                field, levels, levels, pltpu.VMEM((CY, CX), jnp.int32), plane, plane, plane,
                field, field, field, field, field, field, pltpu.VMEM((NZ, TALL, CX), f32),
                packed, eastward, westward, eastward, westward,
                pltpu.VMEM((NT, NZ, 2, CX), f32), pltpu.VMEM((2, CX), jnp.int32),
                pltpu.VMEM((NZ, 1, CX), f32), pltpu.VMEM((FOLD_ROWS, CX), f32),
                pltpu.VMEM((NT, NZ, 8, CX), f32), pltpu.VMEM((8, CX), jnp.int32),
                pltpu.VMEM((NZ, 8, CX), f32), edge, edge,
                pltpu.SemaphoreType.DMA((10,)), pltpu.SemaphoreType.DMA((10,)),
                pltpu.SemaphoreType.DMA((10,)), pltpu.SemaphoreType.REGULAR, pltpu.SemaphoreType.REGULAR,
            ],
            compiler_params=pltpu.CompilerParams(
                collective_id=0, has_side_effects=True, vmem_limit_bytes=24 * 1024 * 1024
            ),
        )(
            *[
                pltpu.with_memory_space_constraint(x, pltpu.HBM)
                for x in (tracers, east_speed, north_speed, bottom_level)
            ]
        )

    in_specs = (P(None, None, "gy", "gx"), P(None, "gy", "gx"), P(None, "gy", "gx"), P("gy", "gx"))
    return jax.shard_map(
        on_device, mesh=mesh, in_specs=in_specs, out_specs=P(None, None, "gy", "gx"), check_vma=False
    )
```

```python
import functools

import jax
import jax.numpy as jnp
from jax import lax
from jax.experimental import pallas as pl
from jax.experimental.pallas import tpu as pltpu
from jax.sharding import PartitionSpec as P

MESH = pl.DeviceIdType.MESH
NT, NZ, CY, CX = 2, 16, 48, 128
PAD = 8
TALL = CY + 2 * PAD
OCTETS = CY // 8
FOLD_ROWS = 72
OWN_LAST, FROM_NORTH, FROM_SOUTH, OWN_FIRST = (pl.ds(i, 2) for i in (0, 2, 4, 6))
PACKED = 13
EASTWARD = 6
WESTWARD = 5
BLOCK = 8
HEAT = 0.4
SALT = 0.6


def reciprocal(value):
    guess = pl.reciprocal(value, approx=True)
    return guess * (2.0 - value * guess)


def minmod(first, second):
    return jnp.maximum(jnp.minimum(first, second), 0.0) + jnp.minimum(
        jnp.maximum(first, second), 0.0
    )


def density(pair):
    return SALT * pair[1] - HEAT * pair[0]


def face_fluxes(local, before, after, dz_sum, speed):
    slope = jnp.clip(
        (0.1 * density(local)) * reciprocal(jnp.maximum(density(dz_sum), 1.0)), -0.025, 0.025
    )
    size = jnp.abs(speed)
    limited = 0.5 * size * (1.0 - size)
    forward = speed >= 0.0
    linear = jnp.minimum(speed, 0.0) - 0.1
    low, high, second = [], [], []
    for t in range(NT):
        correction = limited * minmod(local[t], jnp.where(forward, before[t], after[t]))
        taken = correction + (linear * local[t] + slope * dz_sum[t])
        low.append(taken)
        high.append(taken - speed * local[t])
        second.append(correction)
    return low, high, second, forward


def lanes_left(value):
    return pltpu.roll(value, CX - 1, 1)


def lanes_right(value):
    return pltpu.roll(value, 1, 1)


def rows_up(value):
    return pltpu.roll(value, 7, 0)


def rows_down(value):
    return pltpu.roll(value, 1, 0)


def edge_terms(field, dz, bottom, speed, level, nxt, prv, low_at, high_at, low_second, high_second):
    wet = jnp.minimum(bottom, nxt(bottom)) > level
    local = [jnp.where(wet, nxt(f) - f, 0.0) for f in field]
    dz_sum = [z + nxt(z) for z in dz]
    masked = jnp.where(wet, speed, 0.0)
    low, high, second, forward = face_fluxes(
        local, [prv(d) for d in local], [nxt(d) for d in local], dz_sum, masked
    )
    zero = jnp.zeros_like(masked)
    terms, steps = [], []
    for t in range(NT):
        late = zero
        if low_second is not None:
            late = late + jnp.where(low_second & ~forward, second[t], 0.0)
        if high_second is not None:
            late = late + jnp.where(high_second & forward, second[t], 0.0)
        arriving, term, step = late, -late, zero
        if high_at is not None:
            arriving = arriving + jnp.where(high_at, high[t], 0.0)
            step = step + prv(jnp.where(high_at, local[t], 0.0))
        if low_at is not None:
            term = term - jnp.where(low_at, low[t], 0.0)
            step = step + jnp.where(low_at, local[t], 0.0)
        terms.append(term + prv(arriving))
        steps.append(step)
    return terms, steps


def kernel(
    n_gx, n_gy,
    tracers, east, north, bottom, out,
    T, U, V, bottom_int, bf, be, bn, TZ, XY, YB, GX, GY, FY, Q,
    packed, to_east, to_west, from_west, from_east, relay, relay_b, relay_v, folded,
    strip, strip_b, strip_v, edge_c, edge_g,
    load_sem, send_sem, recv_sem, go_sem, go_north_sem,
):
    gx, gy = lax.axis_index("gx"), lax.axis_index("gy")
    east_id = (lax.rem(gx + 1, n_gx), gy)
    west_id = (lax.rem(gx + n_gx - 1, n_gx), gy)
    north_id = (gx, gy + 1)
    south_id = (gx, gy - 1)
    mirror_id = (n_gx - 1 - gx, gy)
    top = gy == n_gy - 1
    base = gy == 0
    below_middle = gy == n_gy // 2 - 1
    above_middle = gy == n_gy // 2
    place = lax.rem(gx, BLOCK)
    by_go = gy <= n_gy // 2
    after_seam = (place == 0) & by_go
    before_seam = (place == BLOCK - 1) & by_go
    crosses_down = place == BLOCK - 1
    crosses_up = crosses_down | ((lax.rem(place, 2) == 0) & (place != BLOCK - 2))
    relayed_up = crosses_up & below_middle
    relayed_down = crosses_down & above_middle
    relays_up = below_middle & jnp.logical_not(crosses_up)
    relays_down = (place == BLOCK - 2) & above_middle
    chip_mate = gx + 1 - 2 * lax.rem(gx, 2)

    barrier = pltpu.get_barrier_semaphore()

    def greet(device):
        pl.semaphore_signal(barrier, inc=1, device_id=device, device_id_type=MESH)

    pl.when(top)(lambda: greet(mirror_id))
    above_go = gy == n_gy // 2 + 1
    mate_sends_down = crosses_down & below_middle
    mate_sends_up = crosses_up & above_middle
    pl.when(mate_sends_down)(lambda: greet((chip_mate, gy + 1)))
    pl.when(mate_sends_up)(lambda: greet((chip_mate, gy - 1)))
    pl.when(jnp.logical_not(top | mate_sends_down))(lambda: greet(north_id))
    pl.when(jnp.logical_not(base | mate_sends_up | above_go))(lambda: greet(south_id))
    greet(west_id)
    pl.when(jnp.logical_not(before_seam))(lambda: greet(east_id))
    expected = (
        4 + (relays_up | relays_down).astype(jnp.int32) - (relayed_up | relayed_down).astype(jnp.int32)
        - after_seam.astype(jnp.int32) - base.astype(jnp.int32) - above_middle.astype(jnp.int32)
    )

    def load(source, target, index):
        copy = pltpu.make_async_copy(source, target, load_sem.at[index])
        copy.start()
        return copy

    last_rows, first_rows = pl.ds(CY - 2, 2), pl.ds(0, 2)
    early = [
        load(tracers.at[:, :, last_rows, :], strip.at[:, :, OWN_LAST, :], 0),
        load(tracers.at[:, :, first_rows, :], strip.at[:, :, OWN_FIRST, :], 1),
        load(bottom.at[last_rows, :], strip_b.at[OWN_LAST, :], 2),
        load(bottom.at[first_rows, :], strip_b.at[OWN_FIRST, :], 3),
        load(north.at[:, last_rows, :], strip_v.at[:, OWN_LAST, :], 4),
        load(north.at[:, first_rows, :], strip_v.at[:, OWN_FIRST, :], 5),
    ]
    late = [
        load(tracers, T.at[:, :, pl.ds(PAD, CY), :], 6),
        load(bottom, bottom_int, 7),
        load(east, U, 8),
        load(north, V, 9),
    ]

    lane = lax.broadcasted_iota(jnp.int32, (8, CX), 1)
    row = lax.broadcasted_iota(jnp.int32, (8, CX), 0)
    zeros = jnp.zeros((8, CX), jnp.float32)

    def octet(o):
        return pl.ds(PAD + 8 * o, 8)

    def shifted(o, by):
        return pl.ds(PAD + 8 * o + by, 8)

    for pad in (pl.ds(0, PAD), pl.ds(PAD + CY, PAD)):
        bf[pad, :] = zeros
        bn[pad, :] = zeros

    def clear(k, carry):
        for t in range(NT):
            YB[t, k, pl.ds(0, PAD), :] = zeros
            TZ[t, k, pl.ds(PAD + CY, PAD), :] = zeros
        return carry

    lax.fori_loop(0, NZ, clear, 0)

    @pl.when(base)
    def _():
        strip_b[FROM_SOUTH, :] = jnp.zeros((2, CX), jnp.int32)
        for t in range(NT):
            for k in range(NZ):
                strip[t, k, FROM_SOUTH, :] = jnp.zeros((2, CX), jnp.float32)

    for copy in early:
        copy.wait()

    def send(source, target, index, slot, device):
        return pltpu.make_async_remote_copy(
            src_ref=source, dst_ref=target, send_sem=send_sem.at[index], recv_sem=recv_sem.at[slot],
            device_id=device, device_id_type=MESH,
        )

    def bundle(sources, targets, index, slot, device):
        pairs = enumerate(zip(sources, targets, strict=True))
        return [send(source, target, index + i, slot + i, device) for i, (source, target) in pairs]

    def start(copies):
        for copy in copies:
            copy.start()

    def wait_recv(copies):
        for copy in copies:
            copy.wait_recv()

    def wait_send(copies):
        for copy in copies:
            copy.wait_send()

    eastward = send(to_east, from_west, 0, 0, east_id)
    westward = send(to_west, from_east, 1, 1, west_id)
    last = [strip.at[:, :, OWN_LAST, :], strip_b.at[OWN_LAST, :], strip_v.at[:, pl.ds(1, 1), :]]
    first = [strip.at[:, :, OWN_FIRST, :], strip_b.at[OWN_FIRST, :]]
    from_south = [strip.at[:, :, FROM_SOUTH, :], strip_b.at[FROM_SOUTH, :], strip_v.at[:, pl.ds(5, 1), :]]
    from_north = [strip.at[:, :, FROM_NORTH, :], strip_b.at[FROM_NORTH, :]]
    between = [relay, relay_b, relay_v]
    northward = bundle(last, from_south, 2, 2, north_id)
    southward = bundle(first, from_north, 5, 5, south_id)
    across = bundle(last[:2], from_north, 2, 5, mirror_id)
    handed_up = bundle(last, between, 2, 7, (chip_mate, gy))
    handed_down = bundle(first, between[:2], 5, 7, (chip_mate, gy))
    forwarded_up = bundle(between, from_south, 7, 2, (chip_mate, gy + 1))
    forwarded_down = bundle(between[:2], from_north, 7, 5, (chip_mate, gy - 1))
    northward_itself = jnp.logical_not(top | relayed_up)
    southward_itself = jnp.logical_not(base | relayed_down)
    even = lax.rem(gx, 2) == 0
    late_entry = below_middle & jnp.logical_not(relayed_up) & (place < BLOCK - 2)

    @pl.when(jnp.logical_not(late_entry))
    def _():
        pl.semaphore_wait(barrier, expected)

        @pl.when(before_seam)
        def _():
            pl.semaphore_signal(go_sem, inc=1, device_id=east_id, device_id_type=MESH)

        @pl.when(above_go)
        def _():
            pl.semaphore_signal(go_north_sem, inc=1, device_id=south_id, device_id_type=MESH)

        pl.when(relayed_up)(lambda: start(handed_up))

        @pl.when(relays_up)
        def _():
            wait_recv(handed_up)
            start(forwarded_up)

        pl.when(northward_itself & below_middle)(lambda: start(northward))
        pl.when(relayed_down)(lambda: start(handed_down))
        pl.when(southward_itself & jnp.logical_not(relays_down))(lambda: start(southward))
        pl.when(northward_itself & jnp.logical_not(below_middle | above_middle))(lambda: start(northward))
        pl.when(top)(lambda: start(across))

        @pl.when(relays_down)
        def _():
            wait_recv(handed_down)
            start(forwarded_down)
            start(southward)

    def send_columns():
        pl.when(jnp.logical_not(even))(eastward.start)
        pl.when(jnp.logical_not(after_seam))(westward.start)
        pl.when(even)(eastward.start)

    for copy in late[:3]:
        copy.wait()

    for o in range(OCTETS):
        bf[octet(o), :] = bottom_int[pl.ds(8 * o, 8), :].astype(jnp.float32)
    for o in range(OCTETS):
        here = bf[octet(o), :]
        be[octet(o), :] = jnp.where(lane == CX - 1, 0.0, jnp.minimum(here, lanes_left(here)))
        bn[octet(o), :] = jnp.minimum(here, bf[shifted(o, 1), :])

    slot_of = lane // 4

    def pack(group, carry):
        t0, t1, speed = zeros, zeros, zeros
        for b in range(4):
            for o in range(OCTETS):
                slot = b * 8 + o
                here = slot_of == slot
                shift = (4 * slot + 2) % CX
                k = 4 * group + b
                t0 = jnp.where(here, pltpu.roll(T[0, k, octet(o), :], shift, 1), t0)
                t1 = jnp.where(here, pltpu.roll(T[1, k, octet(o), :], shift, 1), t1)
                speed = jnp.where(here, pltpu.roll(U[k, pl.ds(8 * o, 8), :], shift, 1), speed)
        packed[group] = t0
        packed[4 + group] = t1
        packed[8 + group] = speed
        return carry

    lax.fori_loop(0, 4, pack, 0, unroll=4)
    packed_b = zeros
    for b in range(4):
        for o in range(OCTETS):
            slot = b * 8 + o
            packed_b = jnp.where(
                slot_of == slot, pltpu.roll(bf[octet(o), :], (4 * slot + 2) % CX, 1), packed_b
            )
    packed[12] = packed_b

    first_half = lax.rem(lane, 4) < 2
    east_speeds = zeros
    for j in range(4):
        to_east[j] = jnp.where(first_half, packed[j], pltpu.roll(packed[4 + j], 2, 1))
        to_west[j] = jnp.where(first_half, pltpu.roll(packed[4 + j], CX - 2, 1), packed[j])
        east_speeds = jnp.where(
            lax.rem(lane, 4) == j, pltpu.roll(packed[8 + j], (CX + j - 1) % CX, 1), east_speeds
        )
    to_east[4] = east_speeds
    to_east[5] = packed_b
    to_west[4] = packed_b

    pl.when(jnp.logical_not(late_entry))(send_columns)


    late[3].wait()

    def vertical(k, carry):
        level = k.astype(jnp.float32)
        above = jnp.where(k > 0, level, 99.0)
        down, up = jnp.minimum(k + 1, NZ - 1), jnp.maximum(k - 1, 0)
        for o in range(OCTETS):
            depth = bf[octet(o), :]
            for t in range(NT):
                here = T[t, k, octet(o), :]
                TZ[t, k, octet(o), :] = jnp.where(
                    depth > level + 1.0, T[t, down, octet(o), :] - here, 0.0
                ) + jnp.where(depth > above, here - T[t, up, octet(o), :], 0.0)
        return carry

    lax.fori_loop(0, NZ, vertical, 0, unroll=2)

    def inside(k, carry):
        level = k.astype(jnp.float32)
        for o in range(OCTETS):
            here = [T[t, k, octet(o), :] for t in range(NT)]
            dz = [TZ[t, k, octet(o), :] for t in range(NT)]
            wet = be[octet(o), :] > level
            local = [jnp.where(wet, lanes_left(f) - f, 0.0) for f in here]
            before = [lanes_right(d) for d in local]
            after = [lanes_left(d) for d in local]
            speed = jnp.where(wet, U[k, pl.ds(8 * o, 8), :], 0.0)
            low, high, _, _ = face_fluxes(
                local, before, after, [z + lanes_left(z) for z in dz], speed
            )
            across_x = [lanes_right(high[t]) - low[t] for t in range(NT)]
            for t in range(NT):
                GX[t, k, octet(o), :] = local[t] + before[t]

            wet = bn[octet(o), :] > level
            wet_before = bn[shifted(o, -1), :] > level
            wet_after = bn[shifted(o, 1), :] > level
            nxt = [T[t, k, shifted(o, 1), :] for t in range(NT)]
            local = [jnp.where(wet, nxt[t] - here[t], 0.0) for t in range(NT)]
            before = [
                jnp.where(wet_before, here[t] - T[t, k, shifted(o, -1), :], 0.0) for t in range(NT)
            ]
            after = [
                jnp.where(wet_after, T[t, k, shifted(o, 2), :] - nxt[t], 0.0) for t in range(NT)
            ]
            speed = jnp.where(wet, V[k, pl.ds(8 * o, 8), :], 0.0)
            low, high, _, _ = face_fluxes(
                local, before, after, [dz[t] + TZ[t, k, shifted(o, 1), :] for t in range(NT)], speed
            )
            for t in range(NT):
                GY[t, k, octet(o), :] = local[t] + before[t]
                XY[t, k, octet(o), :] = across_x[t] - low[t]
                YB[t, k, octet(o), :] = high[t]
        return carry

    lax.fori_loop(0, NZ, inside, 0, unroll=2)

    @pl.when(late_entry)
    def _():
        pl.semaphore_wait(barrier, expected)

        @pl.when(relays_up)
        def _():
            wait_recv(handed_up)
            start(forwarded_up)

        start(northward)
        send_columns()
        start(southward)

    @pl.when(above_middle)
    def _():
        pl.semaphore_wait(go_north_sem, 1)
        start(northward)

    @pl.when(after_seam)
    def _():
        pl.semaphore_wait(go_sem, 1)
        westward.start()

    def prepare(octets):
        def body(k, carry):
            level = k.astype(jnp.float32)
            down = jnp.minimum(k + 1, NZ - 1)
            for o in octets:
                open_below = bf[octet(o), :] > level + 1.0
                here = [T[t, k, octet(o), :] for t in range(NT)]
                step = [T[t, down, octet(o), :] - here[t] for t in range(NT)]
                mean_y = [GY[t, k, octet(o), :] + GY[t, down, octet(o), :] for t in range(NT)]
                inverse = jnp.where(
                    open_below, reciprocal(jnp.maximum(4.0 * density(step), 1.0)), 0.0
                )
                slope = jnp.clip(density(mean_y) * inverse, -1.0, 1.0)
                square = 0.1 * (slope * slope)
                slope = 0.025 * slope
                Q[k, octet(o), :] = inverse
                for t in range(NT):
                    FY[t, k, octet(o), :] = square * step[t] - slope * mean_y[t]
                    XY[t, k, octet(o), :] += here[t] + YB[t, k, shifted(o, -1), :]
            return carry

        lax.fori_loop(0, NZ, body, 0, unroll=2)

    inner, outer = tuple(range(1, OCTETS - 1)), (0, OCTETS - 1)
    prepare(inner)

    def edge_rows_in():
        wait_recv(southward)
        pl.when(jnp.logical_not(base))(lambda: wait_recv(northward))

        @pl.when(top)
        def _():
            def gather(k, carry):
                for t in range(NT):
                    folded[pl.ds(2 * (NZ * t + k), 2), :] = strip[t, k, FROM_NORTH, :]
                return carry

            def scatter(k, carry):
                for t in range(NT):
                    strip[t, k, FROM_NORTH, :] = folded[pl.ds(2 * (NZ * t + k), 2), :]
                return carry

            lax.fori_loop(0, NZ, gather, 0, unroll=4)
            folded[pl.ds(64, 8), :] = strip_b[...].astype(jnp.float32)
            for i in range(FOLD_ROWS // 8):
                value = folded[pl.ds(8 * i, 8), :]
                for bit in (64, 32, 16, 8, 4, 2, 1):
                    value = jnp.where(
                        (lane & bit) != 0, pltpu.roll(value, bit, 1), pltpu.roll(value, CX - bit, 1)
                    )
                folded[pl.ds(8 * i, 8), :] = jnp.where(
                    (row & 1) != 0, rows_down(value), rows_up(value)
                )
            lax.fori_loop(0, NZ, scatter, 0, unroll=4)
            strip_b[FROM_NORTH, :] = folded[pl.ds(66, 2), :].astype(jnp.int32)

        def edge_rows(k, carry):
            level = k.astype(jnp.float32)
            above = jnp.where(k > 0, level, 99.0)
            down, up = jnp.minimum(k + 1, NZ - 1), jnp.maximum(k - 1, 0)
            depth = strip_b[...].astype(jnp.float32)
            here = [strip[t, k] for t in range(NT)]
            dz = [
                jnp.where(depth > level + 1.0, strip[t, down] - here[t], 0.0)
                + jnp.where(depth > above, here[t] - strip[t, up], 0.0)
                for t in range(NT)
            ]
            terms, grads = edge_terms(
                here, dz, depth, strip_v[k], level, rows_up, rows_down,
                row == 1, row == 5, row == 0, row == 6,
            )
            for t in range(NT):
                XY[t, k, octet(0), :] += jnp.where(row < 2, pltpu.roll(terms[t], 2, 0), 0.0)
                GY[t, k, octet(0), :] += jnp.where(row < 2, pltpu.roll(grads[t], 2, 0), 0.0)
                XY[t, k, octet(OCTETS - 1), :] += jnp.where(row > 5, pltpu.roll(terms[t], 6, 0), 0.0)
                GY[t, k, octet(OCTETS - 1), :] += jnp.where(row > 5, pltpu.roll(grads[t], 6, 0), 0.0)
            return carry

        lax.fori_loop(0, NZ, edge_rows, 0, unroll=16)

    rows_late = ((gy >= n_gy // 2 - 2) & (gy <= n_gy // 2 + 1)) | top

    @pl.when(jnp.logical_not(rows_late))
    def _():
        edge_rows_in()
        prepare(outer)

    quarter = lax.rem(lane, 4)
    level_in_group = (lane // 32).astype(jnp.float32)
    def edge_columns_in(side, first):
        (eastward if side == 0 else westward).wait_recv()
        own = [[packed[4 * t + j] for j in range(4)] for t in range(NT)]
        if side == 0:
            depth = jnp.where(first_half, from_west[5], packed[12])
            fields = [
                [jnp.where(first_half, from_west[j], own[0][j]) for j in range(4)],
                [jnp.where(first_half, pltpu.roll(from_west[j], CX - 2, 1), own[1][j]) for j in range(4)],
            ]
        else:
            depth = jnp.where(first_half, packed[12], from_east[4])
            fields = [
                [jnp.where(first_half, own[0][j], from_east[j]) for j in range(4)],
                [jnp.where(first_half, own[1][j], pltpu.roll(from_east[j], 2, 1)) for j in range(4)],
            ]
        steps = []
        for t in range(NT):
            turned = [pltpu.roll(f, CX - 32, 1) for f in fields[t]]
            steps.append(
                [
                    jnp.where(
                        depth > level_in_group + (4 * j + 1.0),
                        jnp.where(lane < CX - 32, turned[j], turned[min(j + 1, 3)]) - fields[t][j],
                        0.0,
                    )
                    for j in range(4)
                ]
            )
        for j in range(4):
            dz = []
            for t in range(NT):
                before = pltpu.roll(steps[t][j - 1], 32, 1) if j > 0 else zeros
                dz.append(
                    steps[t][j] + jnp.where(lane < 32, before, pltpu.roll(steps[t][j], 32, 1))
                )
            speed = packed[8 + j]
            if side == 0:
                speed = jnp.where(first_half, pltpu.roll(from_west[4], (CX + 1 - j) % CX, 1), speed)
            terms, grads = edge_terms(
                [fields[t][j] for t in range(NT)], dz, depth, speed, level_in_group + 4.0 * j,
                lanes_left, lanes_right,
                None if side == 0 else quarter == 1, quarter == 1 if side == 0 else None,
                None if side == 0 else quarter == 0, quarter == 2 if side == 0 else None,
            )
            for t in range(NT):
                if first:
                    edge_c[t, j] = terms[t]
                    edge_g[t, j] = grads[t]
                else:
                    edge_c[t, j] += terms[t]
                    edge_g[t, j] += grads[t]

    @pl.when(even)
    def _():
        edge_columns_in(1, True)
        edge_columns_in(0, False)

    @pl.when(jnp.logical_not(even))
    def _():
        edge_columns_in(0, True)
        edge_columns_in(1, False)

    at_edge = (lane < 2) | (lane >= CX - 2)

    def finish(octets, prepared):
        def at(o, ref, t, group, b):
            rolled = pltpu.roll(ref[t, group], (CX - (4 * (b * 8 + o) + 2)) % CX, 1)
            return jnp.where(at_edge, rolled, 0.0)

        def body(group, carry):
            fluxes = [[carry[4 * i], carry[4 * i + 1]] for i in range(len(octets))]
            gx_here = [[carry[4 * i + 2], carry[4 * i + 3]] for i in range(len(octets))]
            after = jnp.minimum(group + 1, 3)
            for b in range(4):
                k = 4 * group + b
                level = k.astype(jnp.float32)
                down = jnp.minimum(k + 1, NZ - 1)
                for i, o in enumerate(octets):
                    depth = bf[octet(o), :]
                    here = [T[t, k, octet(o), :] for t in range(NT)]
                    step = [T[t, down, octet(o), :] - here[t] for t in range(NT)]
                    gx_down = [
                        GX[t, down, octet(o), :]
                        + (at(o, edge_g, t, group, b + 1) if b < 3 else at(o, edge_g, t, after, 0))
                        for t in range(NT)
                    ]
                    mean_x = [gx_here[i][t] + gx_down[t] for t in range(NT)]
                    wet = depth > level
                    if prepared:
                        inverse = Q[k, octet(o), :]
                        other = [FY[t, k, octet(o), :] for t in range(NT)]
                        rest = [XY[t, k, octet(o), :] for t in range(NT)]
                    else:
                        mean_y = [
                            GY[t, k, octet(o), :] + GY[t, down, octet(o), :] for t in range(NT)
                        ]
                        inverse = jnp.where(
                            depth > level + 1.0, reciprocal(jnp.maximum(4.0 * density(step), 1.0)), 0.0
                        )
                        slope = jnp.clip(density(mean_y) * inverse, -1.0, 1.0)
                        square = 0.1 * (slope * slope)
                        slope = 0.025 * slope
                        other = [square * step[t] - slope * mean_y[t] for t in range(NT)]
                        rest = [
                            here[t] + (XY[t, k, octet(o), :] + YB[t, k, shifted(o, -1), :])
                            for t in range(NT)
                        ]
                    slope = jnp.clip(density(mean_x) * inverse, -1.0, 1.0)
                    square = 0.1 * (slope * slope)
                    slope = 0.025 * slope
                    for t in range(NT):
                        flux = other[t] + (square * step[t] - slope * mean_x[t])
                        total = (rest[t] + at(o, edge_c, t, group, b)) + (flux - fluxes[i][t])
                        out[t, k, pl.ds(8 * o, 8), :] = jnp.where(wet, total, 0.0)
                        fluxes[i][t] = flux
                    gx_here[i] = gx_down
            return tuple(x for i in range(len(octets)) for x in (*fluxes[i], *gx_here[i]))

        start = []
        for o in octets:
            start += [zeros, zeros]
            start += [GX[t, 0, octet(o), :] + at(o, edge_g, t, 0, 0) for t in range(NT)]
        lax.fori_loop(0, 4, body, tuple(start), unroll=4)

    finish(inner, True)

    @pl.when(rows_late)
    def _():
        edge_rows_in()
        finish(outer, False)

    @pl.when(jnp.logical_not(rows_late))
    def _():
        finish(outer, True)

    eastward.wait_send()
    westward.wait_send()
    pl.when(southward_itself)(lambda: wait_send(southward))
    pl.when(northward_itself)(lambda: wait_send(northward))
    pl.when(relayed_up)(lambda: wait_send(handed_up))
    pl.when(relayed_down)(lambda: wait_send(handed_down))
    pl.when(top)(lambda: wait_send(across))
    pl.when(relays_up)(lambda: wait_send(forwarded_up))
    pl.when(relays_down)(lambda: wait_send(forwarded_down))


def solution(mesh):
    n_gx, n_gy = mesh.shape["gx"], mesh.shape["gy"]
    f32 = jnp.float32
    in_hbm = pl.BlockSpec(memory_space=pltpu.HBM)
    field = pltpu.VMEM((NT, NZ, TALL, CX), f32)
    levels = pltpu.VMEM((NZ, CY, CX), f32)
    plane = pltpu.VMEM((TALL, CX), f32)
    packed = pltpu.VMEM((PACKED, 8, CX), f32)
    eastward = pltpu.VMEM((EASTWARD, 8, CX), f32)
    westward = pltpu.VMEM((WESTWARD, 8, CX), f32)
    edge = pltpu.VMEM((NT, 4, 8, CX), f32)

    def on_device(tracers, east_speed, north_speed, bottom_level):
        return pl.pallas_call(
            functools.partial(kernel, n_gx, n_gy),
            out_shape=jax.ShapeDtypeStruct((NT, NZ, CY, CX), f32),
            in_specs=[in_hbm] * 4,
            out_specs=pl.BlockSpec(memory_space=pltpu.VMEM),
            scratch_shapes=[
                field, levels, levels, pltpu.VMEM((CY, CX), jnp.int32), plane, plane, plane,
                field, field, field, field, field, field, pltpu.VMEM((NZ, TALL, CX), f32),
                packed, eastward, westward, eastward, westward,
                pltpu.VMEM((NT, NZ, 2, CX), f32), pltpu.VMEM((2, CX), jnp.int32),
                pltpu.VMEM((NZ, 1, CX), f32), pltpu.VMEM((FOLD_ROWS, CX), f32),
                pltpu.VMEM((NT, NZ, 8, CX), f32), pltpu.VMEM((8, CX), jnp.int32),
                pltpu.VMEM((NZ, 8, CX), f32), edge, edge,
                pltpu.SemaphoreType.DMA((10,)), pltpu.SemaphoreType.DMA((10,)),
                pltpu.SemaphoreType.DMA((10,)), pltpu.SemaphoreType.REGULAR, pltpu.SemaphoreType.REGULAR,
            ],
            compiler_params=pltpu.CompilerParams(
                collective_id=0, has_side_effects=True, vmem_limit_bytes=24 * 1024 * 1024
            ),
        )(
            *[
                pltpu.with_memory_space_constraint(x, pltpu.HBM)
                for x in (tracers, east_speed, north_speed, bottom_level)
            ]
        )

    in_specs = (P(None, None, "gy", "gx"), P(None, "gy", "gx"), P(None, "gy", "gx"), P("gy", "gx"))
    return jax.shard_map(
        on_device, mesh=mesh, in_specs=in_specs, out_specs=P(None, None, "gy", "gx"), check_vma=False
    )
```

```python
import functools

import jax
import jax.numpy as jnp
from jax import lax
from jax.experimental import pallas as pl
from jax.experimental.pallas import tpu as pltpu
from jax.sharding import PartitionSpec as P

MESH = pl.DeviceIdType.MESH
NT, NZ, CY, CX = 2, 16, 48, 128
PAD = 8
TALL = CY + 2 * PAD
OCTETS = CY // 8
DEPTH = NT * NZ
SHORT = DEPTH + 1
PLANES = SHORT + NZ
FOLD_ROWS = 72
OWN_LAST, FROM_NORTH, FROM_SOUTH, OWN_FIRST = (pl.ds(i, 2) for i in (0, 2, 4, 6))
PACKED = 13
EASTWARD = 6
WESTWARD = 5
BLOCK = 8
HEAT = 0.4
SALT = 0.6


def reciprocal(value):
    guess = pl.reciprocal(value, approx=True)
    return guess * (2.0 - value * guess)


def minmod(first, second):
    return jnp.maximum(jnp.minimum(first, second), 0.0) + jnp.minimum(
        jnp.maximum(first, second), 0.0
    )


def density(pair):
    return SALT * pair[1] - HEAT * pair[0]


def face_fluxes(local, before, after, dz_sum, speed):
    slope = jnp.clip(
        (0.1 * density(local)) * reciprocal(jnp.maximum(density(dz_sum), 1.0)), -0.025, 0.025
    )
    size = jnp.abs(speed)
    limited = 0.5 * size * (1.0 - size)
    forward = speed >= 0.0
    linear = jnp.minimum(speed, 0.0) - 0.1
    low, high, second = [], [], []
    for t in range(NT):
        correction = limited * minmod(local[t], jnp.where(forward, before[t], after[t]))
        taken = correction + (linear * local[t] + slope * dz_sum[t])
        low.append(taken)
        high.append(taken - speed * local[t])
        second.append(correction)
    return low, high, second, forward


def lanes_left(value):
    return pltpu.roll(value, CX - 1, 1)


def lanes_right(value):
    return pltpu.roll(value, 1, 1)


def rows_up(value):
    return pltpu.roll(value, 7, 0)


def rows_down(value):
    return pltpu.roll(value, 1, 0)


def edge_terms(field, dz, bottom, speed, level, nxt, prv, low_at, high_at, low_second, high_second):
    wet = jnp.minimum(bottom, nxt(bottom)) > level
    local = [jnp.where(wet, nxt(f) - f, 0.0) for f in field]
    dz_sum = [z + nxt(z) for z in dz]
    masked = jnp.where(wet, speed, 0.0)
    low, high, second, forward = face_fluxes(
        local, [prv(d) for d in local], [nxt(d) for d in local], dz_sum, masked
    )
    zero = jnp.zeros_like(masked)
    terms, steps = [], []
    for t in range(NT):
        late = zero
        if low_second is not None:
            late = late + jnp.where(low_second & ~forward, second[t], 0.0)
        if high_second is not None:
            late = late + jnp.where(high_second & forward, second[t], 0.0)
        arriving, term, step = late, -late, zero
        if high_at is not None:
            arriving = arriving + jnp.where(high_at, high[t], 0.0)
            step = step + prv(jnp.where(high_at, local[t], 0.0))
        if low_at is not None:
            term = term - jnp.where(low_at, low[t], 0.0)
            step = step + jnp.where(low_at, local[t], 0.0)
        terms.append(term + prv(arriving))
        steps.append(step)
    return terms, steps


def kernel(
    n_gx, n_gy,
    tracers, east, north, bottom, out,
    T, U, V, bottom_int, bf, be, bn, TZ, XY, YB, GX, GY, FY, Q,
    packed, to_east, to_west, from_west, from_east, relay, folded,
    strip, strip_int, edge_c, edge_g,
    load_sem, send_sem, recv_sem, go_sem, go_north_sem,
):
    gx, gy = lax.axis_index("gx"), lax.axis_index("gy")
    east_id = (lax.rem(gx + 1, n_gx), gy)
    west_id = (lax.rem(gx + n_gx - 1, n_gx), gy)
    north_id = (gx, gy + 1)
    south_id = (gx, gy - 1)
    mirror_id = (n_gx - 1 - gx, gy)
    top = gy == n_gy - 1
    base = gy == 0
    below_middle = gy == n_gy // 2 - 1
    above_middle = gy == n_gy // 2
    place = lax.rem(gx, BLOCK)
    by_go = gy <= n_gy // 2
    after_seam = (place == 0) & by_go
    before_seam = (place == BLOCK - 1) & by_go
    crosses_down = place == BLOCK - 1
    crosses_up = crosses_down | ((lax.rem(place, 2) == 0) & (place != BLOCK - 2))
    relayed_up = crosses_up & below_middle
    relayed_down = crosses_down & above_middle
    relays_up = below_middle & jnp.logical_not(crosses_up)
    relays_down = (place == BLOCK - 2) & above_middle
    chip_mate = gx + 1 - 2 * lax.rem(gx, 2)

    barrier = pltpu.get_barrier_semaphore()

    def greet(device):
        pl.semaphore_signal(barrier, inc=1, device_id=device, device_id_type=MESH)

    pl.when(top)(lambda: greet(mirror_id))
    above_go = gy == n_gy // 2 + 1
    mate_sends_down = crosses_down & below_middle
    mate_sends_up = crosses_up & above_middle
    pl.when(mate_sends_down)(lambda: greet((chip_mate, gy + 1)))
    pl.when(mate_sends_up)(lambda: greet((chip_mate, gy - 1)))
    pl.when(jnp.logical_not(top | mate_sends_down))(lambda: greet(north_id))
    pl.when(jnp.logical_not(base | mate_sends_up | above_go))(lambda: greet(south_id))
    greet(west_id)
    pl.when(jnp.logical_not(before_seam))(lambda: greet(east_id))
    expected = (
        4 + (relays_up | relays_down).astype(jnp.int32) - (relayed_up | relayed_down).astype(jnp.int32)
        - after_seam.astype(jnp.int32) - base.astype(jnp.int32) - above_middle.astype(jnp.int32)
    )

    def load(source, target, index):
        copy = pltpu.make_async_copy(source, target, load_sem.at[index])
        copy.start()
        return copy

    last_rows, first_rows = pl.ds(CY - 2, 2), pl.ds(0, 2)
    speeds = pl.ds(SHORT, NZ)
    early = [
        load(bottom.at[last_rows, :], strip_int.at[OWN_LAST, :], 0),
        load(bottom.at[first_rows, :], strip_int.at[OWN_FIRST, :], 1),
    ]
    for t in range(NT):
        levels = pl.ds(NZ * t, NZ)
        early += [
            load(tracers.at[t, :, last_rows, :], strip.at[levels, OWN_LAST, :], 2 + 2 * t),
            load(tracers.at[t, :, first_rows, :], strip.at[levels, OWN_FIRST, :], 3 + 2 * t),
        ]
    early += [
        load(north.at[:, last_rows, :], strip.at[speeds, OWN_LAST, :], 6),
        load(north.at[:, first_rows, :], strip.at[speeds, OWN_FIRST, :], 7),
    ]
    late = [
        load(tracers, T.at[:, :, pl.ds(PAD, CY), :], 8),
        load(bottom, bottom_int, 9),
        load(east, U, 10),
        load(north, V, 11),
    ]

    lane = lax.broadcasted_iota(jnp.int32, (8, CX), 1)
    row = lax.broadcasted_iota(jnp.int32, (8, CX), 0)
    zeros = jnp.zeros((8, CX), jnp.float32)

    def octet(o):
        return pl.ds(PAD + 8 * o, 8)

    def shifted(o, by):
        return pl.ds(PAD + 8 * o + by, 8)

    for pad in (pl.ds(0, PAD), pl.ds(PAD + CY, PAD)):
        bf[pad, :] = zeros
        bn[pad, :] = zeros

    def clear(k, carry):
        for t in range(NT):
            YB[t, k, pl.ds(0, PAD), :] = zeros
            TZ[t, k, pl.ds(PAD + CY, PAD), :] = zeros
        return carry

    lax.fori_loop(0, NZ, clear, 0)

    @pl.when(base)
    def _():
        for plane in range(SHORT):
            strip[plane, FROM_SOUTH, :] = jnp.zeros((2, CX), jnp.float32)

    for copy in early:
        copy.wait()
    for rows in (OWN_LAST, OWN_FIRST):
        strip[DEPTH, rows, :] = strip_int[rows, :].astype(jnp.float32)

    @pl.when(top)
    def _():
        for plane in range(SHORT):
            folded[pl.ds(2 * plane, 2), :] = strip[plane, OWN_LAST, :]
        for i in range(FOLD_ROWS // 8):
            value = folded[pl.ds(8 * i, 8), :]
            for bit in (64, 32, 16, 8, 4, 2, 1):
                value = jnp.where(
                    (lane & bit) != 0, pltpu.roll(value, bit, 1), pltpu.roll(value, CX - bit, 1)
                )
            folded[pl.ds(8 * i, 8), :] = jnp.where((row & 1) != 0, rows_down(value), rows_up(value))
        for plane in range(SHORT):
            relay[plane] = folded[pl.ds(2 * plane, 2), :]

    def send(source, target, index, slot, device):
        return pltpu.make_async_remote_copy(
            src_ref=source, dst_ref=target, send_sem=send_sem.at[index], recv_sem=recv_sem.at[slot],
            device_id=device, device_id_type=MESH,
        )

    eastward = send(to_east, from_west, 0, 0, east_id)
    westward = send(to_west, from_east, 1, 1, west_id)
    short = pl.ds(0, SHORT)
    from_south, from_north = strip.at[:, FROM_SOUTH, :], strip.at[short, FROM_NORTH, :]
    last, first = strip.at[:, OWN_LAST, :], strip.at[short, OWN_FIRST, :]
    northward = send(last, from_south, 2, 2, north_id)
    southward = send(first, from_north, 3, 3, south_id)
    across = send(relay.at[short], from_north, 2, 3, mirror_id)
    handed_up = send(last, relay, 2, 4, (chip_mate, gy))
    handed_down = send(first, relay.at[short], 3, 4, (chip_mate, gy))
    forwarded_up = send(relay, from_south, 4, 2, (chip_mate, gy + 1))
    forwarded_down = send(relay.at[short], from_north, 4, 3, (chip_mate, gy - 1))
    northward_itself = jnp.logical_not(top | relayed_up)
    southward_itself = jnp.logical_not(base | relayed_down)
    even = lax.rem(gx, 2) == 0
    late_entry = below_middle & jnp.logical_not(relayed_up) & (place < BLOCK - 2)

    @pl.when(jnp.logical_not(late_entry))
    def _():
        pl.semaphore_wait(barrier, expected)

        @pl.when(before_seam)
        def _():
            pl.semaphore_signal(go_sem, inc=1, device_id=east_id, device_id_type=MESH)

        @pl.when(above_go)
        def _():
            pl.semaphore_signal(go_north_sem, inc=1, device_id=south_id, device_id_type=MESH)

        pl.when(relayed_up)(handed_up.start)

        @pl.when(relays_up)
        def _():
            handed_up.wait_recv()
            forwarded_up.start()

        pl.when(northward_itself & below_middle)(northward.start)
        pl.when(relayed_down)(handed_down.start)
        pl.when(southward_itself & jnp.logical_not(relays_down))(southward.start)
        pl.when(northward_itself & jnp.logical_not(below_middle | above_middle))(northward.start)
        pl.when(top)(across.start)

        @pl.when(relays_down)
        def _():
            handed_down.wait_recv()
            forwarded_down.start()
            southward.start()

    def send_columns():
        pl.when(jnp.logical_not(even))(eastward.start)
        pl.when(jnp.logical_not(after_seam))(westward.start)
        pl.when(even)(eastward.start)

    for copy in late[:3]:
        copy.wait()

    for o in range(OCTETS):
        bf[octet(o), :] = bottom_int[pl.ds(8 * o, 8), :].astype(jnp.float32)
    for o in range(OCTETS):
        here = bf[octet(o), :]
        be[octet(o), :] = jnp.where(lane == CX - 1, 0.0, jnp.minimum(here, lanes_left(here)))
        bn[octet(o), :] = jnp.minimum(here, bf[shifted(o, 1), :])

    slot_of = lane // 4

    def pack(group, carry):
        t0, t1, speed = zeros, zeros, zeros
        for b in range(4):
            for o in range(OCTETS):
                slot = b * 8 + o
                here = slot_of == slot
                shift = (4 * slot + 2) % CX
                k = 4 * group + b
                t0 = jnp.where(here, pltpu.roll(T[0, k, octet(o), :], shift, 1), t0)
                t1 = jnp.where(here, pltpu.roll(T[1, k, octet(o), :], shift, 1), t1)
                speed = jnp.where(here, pltpu.roll(U[k, pl.ds(8 * o, 8), :], shift, 1), speed)
        packed[group] = t0
        packed[4 + group] = t1
        packed[8 + group] = speed
        return carry

    lax.fori_loop(0, 4, pack, 0, unroll=4)
    packed_b = zeros
    for b in range(4):
        for o in range(OCTETS):
            slot = b * 8 + o
            packed_b = jnp.where(
                slot_of == slot, pltpu.roll(bf[octet(o), :], (4 * slot + 2) % CX, 1), packed_b
            )
    packed[12] = packed_b

    first_half = lax.rem(lane, 4) < 2
    east_speeds = zeros
    for j in range(4):
        to_east[j] = jnp.where(first_half, packed[j], pltpu.roll(packed[4 + j], 2, 1))
        to_west[j] = jnp.where(first_half, pltpu.roll(packed[4 + j], CX - 2, 1), packed[j])
        east_speeds = jnp.where(
            lax.rem(lane, 4) == j, pltpu.roll(packed[8 + j], (CX + j - 1) % CX, 1), east_speeds
        )
    to_east[4] = east_speeds
    to_east[5] = packed_b
    to_west[4] = packed_b

    pl.when(jnp.logical_not(late_entry))(send_columns)


    late[3].wait()

    def vertical(k, carry):
        level = k.astype(jnp.float32)
        above = jnp.where(k > 0, level, 99.0)
        down, up = jnp.minimum(k + 1, NZ - 1), jnp.maximum(k - 1, 0)
        for o in range(OCTETS):
            depth = bf[octet(o), :]
            for t in range(NT):
                here = T[t, k, octet(o), :]
                TZ[t, k, octet(o), :] = jnp.where(
                    depth > level + 1.0, T[t, down, octet(o), :] - here, 0.0
                ) + jnp.where(depth > above, here - T[t, up, octet(o), :], 0.0)
        return carry

    lax.fori_loop(0, NZ, vertical, 0, unroll=2)

    def inside(k, carry):
        level = k.astype(jnp.float32)
        for o in range(OCTETS):
            here = [T[t, k, octet(o), :] for t in range(NT)]
            dz = [TZ[t, k, octet(o), :] for t in range(NT)]
            wet = be[octet(o), :] > level
            local = [jnp.where(wet, lanes_left(f) - f, 0.0) for f in here]
            before = [lanes_right(d) for d in local]
            after = [lanes_left(d) for d in local]
            speed = jnp.where(wet, U[k, pl.ds(8 * o, 8), :], 0.0)
            low, high, _, _ = face_fluxes(
                local, before, after, [z + lanes_left(z) for z in dz], speed
            )
            across_x = [lanes_right(high[t]) - low[t] for t in range(NT)]
            for t in range(NT):
                GX[t, k, octet(o), :] = local[t] + before[t]

            wet = bn[octet(o), :] > level
            wet_before = bn[shifted(o, -1), :] > level
            wet_after = bn[shifted(o, 1), :] > level
            nxt = [T[t, k, shifted(o, 1), :] for t in range(NT)]
            local = [jnp.where(wet, nxt[t] - here[t], 0.0) for t in range(NT)]
            before = [
                jnp.where(wet_before, here[t] - T[t, k, shifted(o, -1), :], 0.0) for t in range(NT)
            ]
            after = [
                jnp.where(wet_after, T[t, k, shifted(o, 2), :] - nxt[t], 0.0) for t in range(NT)
            ]
            speed = jnp.where(wet, V[k, pl.ds(8 * o, 8), :], 0.0)
            low, high, _, _ = face_fluxes(
                local, before, after, [dz[t] + TZ[t, k, shifted(o, 1), :] for t in range(NT)], speed
            )
            for t in range(NT):
                GY[t, k, octet(o), :] = local[t] + before[t]
                XY[t, k, octet(o), :] = across_x[t] - low[t]
                YB[t, k, octet(o), :] = high[t]
        return carry

    lax.fori_loop(0, NZ, inside, 0, unroll=2)

    @pl.when(late_entry)
    def _():
        pl.semaphore_wait(barrier, expected)

        @pl.when(relays_up)
        def _():
            handed_up.wait_recv()
            forwarded_up.start()

        northward.start()
        send_columns()
        southward.start()

    @pl.when(above_middle)
    def _():
        pl.semaphore_wait(go_north_sem, 1)
        northward.start()

    @pl.when(after_seam)
    def _():
        pl.semaphore_wait(go_sem, 1)
        westward.start()

    def prepare(octets):
        def body(k, carry):
            level = k.astype(jnp.float32)
            down = jnp.minimum(k + 1, NZ - 1)
            for o in octets:
                open_below = bf[octet(o), :] > level + 1.0
                here = [T[t, k, octet(o), :] for t in range(NT)]
                step = [T[t, down, octet(o), :] - here[t] for t in range(NT)]
                mean_y = [GY[t, k, octet(o), :] + GY[t, down, octet(o), :] for t in range(NT)]
                inverse = jnp.where(
                    open_below, reciprocal(jnp.maximum(4.0 * density(step), 1.0)), 0.0
                )
                slope = jnp.clip(density(mean_y) * inverse, -1.0, 1.0)
                square = 0.1 * (slope * slope)
                slope = 0.025 * slope
                Q[k, octet(o), :] = inverse
                for t in range(NT):
                    FY[t, k, octet(o), :] = square * step[t] - slope * mean_y[t]
                    XY[t, k, octet(o), :] += here[t] + YB[t, k, shifted(o, -1), :]
            return carry

        lax.fori_loop(0, NZ, body, 0, unroll=2)

    inner, outer = tuple(range(1, OCTETS - 1)), (0, OCTETS - 1)
    prepare(inner)

    def edge_rows_in():
        southward.wait_recv()
        pl.when(jnp.logical_not(base))(northward.wait_recv)

        def edge_rows(k, carry):
            level = k.astype(jnp.float32)
            above = jnp.where(k > 0, level, 99.0)
            down, up = jnp.minimum(k + 1, NZ - 1), jnp.maximum(k - 1, 0)
            depth = strip[DEPTH]
            here = [strip[NZ * t + k] for t in range(NT)]
            dz = [
                jnp.where(depth > level + 1.0, strip[NZ * t + down] - here[t], 0.0)
                + jnp.where(depth > above, here[t] - strip[NZ * t + up], 0.0)
                for t in range(NT)
            ]
            terms, grads = edge_terms(
                here, dz, depth, strip[SHORT + k], level, rows_up, rows_down,
                row == 1, row == 5, row == 0, row == 6,
            )
            for t in range(NT):
                XY[t, k, octet(0), :] += jnp.where(row < 2, pltpu.roll(terms[t], 2, 0), 0.0)
                GY[t, k, octet(0), :] += jnp.where(row < 2, pltpu.roll(grads[t], 2, 0), 0.0)
                XY[t, k, octet(OCTETS - 1), :] += jnp.where(row > 5, pltpu.roll(terms[t], 6, 0), 0.0)
                GY[t, k, octet(OCTETS - 1), :] += jnp.where(row > 5, pltpu.roll(grads[t], 6, 0), 0.0)
            return carry

        lax.fori_loop(0, NZ, edge_rows, 0, unroll=16)

    rows_late = ((gy >= n_gy // 2 - 2) & (gy <= n_gy // 2 + 1)) | top

    @pl.when(jnp.logical_not(rows_late))
    def _():
        edge_rows_in()
        prepare(outer)

    quarter = lax.rem(lane, 4)
    level_in_group = (lane // 32).astype(jnp.float32)
    def edge_columns_in(side, first):
        (eastward if side == 0 else westward).wait_recv()
        own = [[packed[4 * t + j] for j in range(4)] for t in range(NT)]
        if side == 0:
            depth = jnp.where(first_half, from_west[5], packed[12])
            fields = [
                [jnp.where(first_half, from_west[j], own[0][j]) for j in range(4)],
                [jnp.where(first_half, pltpu.roll(from_west[j], CX - 2, 1), own[1][j]) for j in range(4)],
            ]
        else:
            depth = jnp.where(first_half, packed[12], from_east[4])
            fields = [
                [jnp.where(first_half, own[0][j], from_east[j]) for j in range(4)],
                [jnp.where(first_half, own[1][j], pltpu.roll(from_east[j], 2, 1)) for j in range(4)],
            ]
        steps = []
        for t in range(NT):
            turned = [pltpu.roll(f, CX - 32, 1) for f in fields[t]]
            steps.append(
                [
                    jnp.where(
                        depth > level_in_group + (4 * j + 1.0),
                        jnp.where(lane < CX - 32, turned[j], turned[min(j + 1, 3)]) - fields[t][j],
                        0.0,
                    )
                    for j in range(4)
                ]
            )
        for j in range(4):
            dz = []
            for t in range(NT):
                before = pltpu.roll(steps[t][j - 1], 32, 1) if j > 0 else zeros
                dz.append(
                    steps[t][j] + jnp.where(lane < 32, before, pltpu.roll(steps[t][j], 32, 1))
                )
            speed = packed[8 + j]
            if side == 0:
                speed = jnp.where(first_half, pltpu.roll(from_west[4], (CX + 1 - j) % CX, 1), speed)
            terms, grads = edge_terms(
                [fields[t][j] for t in range(NT)], dz, depth, speed, level_in_group + 4.0 * j,
                lanes_left, lanes_right,
                None if side == 0 else quarter == 1, quarter == 1 if side == 0 else None,
                None if side == 0 else quarter == 0, quarter == 2 if side == 0 else None,
            )
            for t in range(NT):
                if first:
                    edge_c[t, j] = terms[t]
                    edge_g[t, j] = grads[t]
                else:
                    edge_c[t, j] += terms[t]
                    edge_g[t, j] += grads[t]

    @pl.when(even)
    def _():
        edge_columns_in(1, True)
        edge_columns_in(0, False)

    @pl.when(jnp.logical_not(even))
    def _():
        edge_columns_in(0, True)
        edge_columns_in(1, False)

    at_edge = (lane < 2) | (lane >= CX - 2)

    def finish(octets, prepared):
        def at(o, ref, t, group, b):
            rolled = pltpu.roll(ref[t, group], (CX - (4 * (b * 8 + o) + 2)) % CX, 1)
            return jnp.where(at_edge, rolled, 0.0)

        def body(group, carry):
            fluxes = [[carry[4 * i], carry[4 * i + 1]] for i in range(len(octets))]
            gx_here = [[carry[4 * i + 2], carry[4 * i + 3]] for i in range(len(octets))]
            after = jnp.minimum(group + 1, 3)
            for b in range(4):
                k = 4 * group + b
                level = k.astype(jnp.float32)
                down = jnp.minimum(k + 1, NZ - 1)
                for i, o in enumerate(octets):
                    depth = bf[octet(o), :]
                    here = [T[t, k, octet(o), :] for t in range(NT)]
                    step = [T[t, down, octet(o), :] - here[t] for t in range(NT)]
                    gx_down = [
                        GX[t, down, octet(o), :]
                        + (at(o, edge_g, t, group, b + 1) if b < 3 else at(o, edge_g, t, after, 0))
                        for t in range(NT)
                    ]
                    mean_x = [gx_here[i][t] + gx_down[t] for t in range(NT)]
                    wet = depth > level
                    if prepared:
                        inverse = Q[k, octet(o), :]
                        other = [FY[t, k, octet(o), :] for t in range(NT)]
                        rest = [XY[t, k, octet(o), :] for t in range(NT)]
                    else:
                        mean_y = [
                            GY[t, k, octet(o), :] + GY[t, down, octet(o), :] for t in range(NT)
                        ]
                        inverse = jnp.where(
                            depth > level + 1.0, reciprocal(jnp.maximum(4.0 * density(step), 1.0)), 0.0
                        )
                        slope = jnp.clip(density(mean_y) * inverse, -1.0, 1.0)
                        square = 0.1 * (slope * slope)
                        slope = 0.025 * slope
                        other = [square * step[t] - slope * mean_y[t] for t in range(NT)]
                        rest = [
                            here[t] + (XY[t, k, octet(o), :] + YB[t, k, shifted(o, -1), :])
                            for t in range(NT)
                        ]
                    slope = jnp.clip(density(mean_x) * inverse, -1.0, 1.0)
                    square = 0.1 * (slope * slope)
                    slope = 0.025 * slope
                    for t in range(NT):
                        flux = other[t] + (square * step[t] - slope * mean_x[t])
                        total = (rest[t] + at(o, edge_c, t, group, b)) + (flux - fluxes[i][t])
                        out[t, k, pl.ds(8 * o, 8), :] = jnp.where(wet, total, 0.0)
                        fluxes[i][t] = flux
                    gx_here[i] = gx_down
            return tuple(x for i in range(len(octets)) for x in (*fluxes[i], *gx_here[i]))

        start = []
        for o in octets:
            start += [zeros, zeros]
            start += [GX[t, 0, octet(o), :] + at(o, edge_g, t, 0, 0) for t in range(NT)]
        lax.fori_loop(0, 4, body, tuple(start), unroll=4)

    finish(inner, True)

    @pl.when(rows_late)
    def _():
        edge_rows_in()
        finish(outer, False)

    @pl.when(jnp.logical_not(rows_late))
    def _():
        finish(outer, True)

    eastward.wait_send()
    westward.wait_send()
    pl.when(southward_itself)(southward.wait_send)
    pl.when(northward_itself)(northward.wait_send)
    pl.when(relayed_up)(handed_up.wait_send)
    pl.when(relayed_down)(handed_down.wait_send)
    pl.when(top)(across.wait_send)
    pl.when(relays_up)(forwarded_up.wait_send)
    pl.when(relays_down)(forwarded_down.wait_send)


def solution(mesh):
    n_gx, n_gy = mesh.shape["gx"], mesh.shape["gy"]
    f32 = jnp.float32
    in_hbm = pl.BlockSpec(memory_space=pltpu.HBM)
    field = pltpu.VMEM((NT, NZ, TALL, CX), f32)
    levels = pltpu.VMEM((NZ, CY, CX), f32)
    plane = pltpu.VMEM((TALL, CX), f32)
    packed = pltpu.VMEM((PACKED, 8, CX), f32)
    eastward = pltpu.VMEM((EASTWARD, 8, CX), f32)
    westward = pltpu.VMEM((WESTWARD, 8, CX), f32)
    edge = pltpu.VMEM((NT, 4, 8, CX), f32)

    def on_device(tracers, east_speed, north_speed, bottom_level):
        return pl.pallas_call(
            functools.partial(kernel, n_gx, n_gy),
            out_shape=jax.ShapeDtypeStruct((NT, NZ, CY, CX), f32),
            in_specs=[in_hbm] * 4,
            out_specs=pl.BlockSpec(memory_space=pltpu.VMEM),
            scratch_shapes=[
                field, levels, levels, pltpu.VMEM((CY, CX), jnp.int32), plane, plane, plane,
                field, field, field, field, field, field, pltpu.VMEM((NZ, TALL, CX), f32),
                packed, eastward, westward, eastward, westward,
                pltpu.VMEM((PLANES, 2, CX), f32), pltpu.VMEM((FOLD_ROWS, CX), f32),
                pltpu.VMEM((PLANES, 8, CX), f32), pltpu.VMEM((8, CX), jnp.int32), edge, edge,
                pltpu.SemaphoreType.DMA((12,)), pltpu.SemaphoreType.DMA((5,)),
                pltpu.SemaphoreType.DMA((5,)), pltpu.SemaphoreType.REGULAR, pltpu.SemaphoreType.REGULAR,
            ],
            compiler_params=pltpu.CompilerParams(
                collective_id=0, has_side_effects=True, vmem_limit_bytes=24 * 1024 * 1024
            ),
        )(
            *[
                pltpu.with_memory_space_constraint(x, pltpu.HBM)
                for x in (tracers, east_speed, north_speed, bottom_level)
            ]
        )

    in_specs = (P(None, None, "gy", "gx"), P(None, "gy", "gx"), P(None, "gy", "gx"), P("gy", "gx"))
    return jax.shard_map(
        on_device, mesh=mesh, in_specs=in_specs, out_specs=P(None, None, "gy", "gx"), check_vma=False
    )
```

```python
import functools

import jax
import jax.numpy as jnp
from jax import lax
from jax.experimental import pallas as pl
from jax.experimental.pallas import tpu as pltpu
from jax.sharding import PartitionSpec as P

MESH = pl.DeviceIdType.MESH
NT, NZ, CY, CX = 2, 16, 48, 128
PAD = 8
TALL = CY + 2 * PAD
OCTETS = CY // 8
FOLD_ROWS = 72
OWN_LAST, FROM_NORTH, FROM_SOUTH, OWN_FIRST = (pl.ds(i, 2) for i in (0, 2, 4, 6))
PACKED = 13
EASTWARD = 6
WESTWARD = 5
BLOCK = 8
HEAT = 0.4
SALT = 0.6


def reciprocal(value):
    guess = pl.reciprocal(value, approx=True)
    return guess * (2.0 - value * guess)


def minmod(first, second):
    return jnp.maximum(jnp.minimum(first, second), 0.0) + jnp.minimum(
        jnp.maximum(first, second), 0.0
    )


def density(pair):
    return SALT * pair[1] - HEAT * pair[0]


def face_fluxes(local, before, after, dz_sum, speed):
    slope = jnp.clip(
        (0.1 * density(local)) * reciprocal(jnp.maximum(density(dz_sum), 1.0)), -0.025, 0.025
    )
    size = jnp.abs(speed)
    limited = 0.5 * size * (1.0 - size)
    forward = speed >= 0.0
    linear = jnp.minimum(speed, 0.0) - 0.1
    low, high, second = [], [], []
    for t in range(NT):
        correction = limited * minmod(local[t], jnp.where(forward, before[t], after[t]))
        taken = correction + (linear * local[t] + slope * dz_sum[t])
        low.append(taken)
        high.append(taken - speed * local[t])
        second.append(correction)
    return low, high, second, forward


def lanes_left(value):
    return pltpu.roll(value, CX - 1, 1)


def lanes_right(value):
    return pltpu.roll(value, 1, 1)


def rows_up(value):
    return pltpu.roll(value, 7, 0)


def rows_down(value):
    return pltpu.roll(value, 1, 0)


def edge_terms(field, dz, bottom, speed, level, nxt, prv, low_at, high_at, low_second, high_second):
    wet = jnp.minimum(bottom, nxt(bottom)) > level
    local = [jnp.where(wet, nxt(f) - f, 0.0) for f in field]
    dz_sum = [z + nxt(z) for z in dz]
    masked = jnp.where(wet, speed, 0.0)
    low, high, second, forward = face_fluxes(
        local, [prv(d) for d in local], [nxt(d) for d in local], dz_sum, masked
    )
    zero = jnp.zeros_like(masked)
    terms, steps = [], []
    for t in range(NT):
        late = zero
        if low_second is not None:
            late = late + jnp.where(low_second & ~forward, second[t], 0.0)
        if high_second is not None:
            late = late + jnp.where(high_second & forward, second[t], 0.0)
        arriving, term, step = late, -late, zero
        if high_at is not None:
            arriving = arriving + jnp.where(high_at, high[t], 0.0)
            step = step + prv(jnp.where(high_at, local[t], 0.0))
        if low_at is not None:
            term = term - jnp.where(low_at, low[t], 0.0)
            step = step + jnp.where(low_at, local[t], 0.0)
        terms.append(term + prv(arriving))
        steps.append(step)
    return terms, steps


def kernel(
    n_gx, n_gy,
    tracers, east, north, bottom, out,
    T, U, V, bottom_int, bf, be, bn, TZ, XY, YB, GX, GY, FY, Q,
    packed, to_east, to_west, from_west, from_east, relay, relay_b, relay_v, folded,
    strip, strip_b, strip_v, edge_c, edge_g,
    load_sem, send_sem, recv_sem, go_sem, go_north_sem,
):
    gx, gy = lax.axis_index("gx"), lax.axis_index("gy")
    east_id = (lax.rem(gx + 1, n_gx), gy)
    west_id = (lax.rem(gx + n_gx - 1, n_gx), gy)
    north_id = (gx, gy + 1)
    south_id = (gx, gy - 1)
    mirror_id = (n_gx - 1 - gx, gy)
    top = gy == n_gy - 1
    base = gy == 0
    below_middle = gy == n_gy // 2 - 1
    above_middle = gy == n_gy // 2
    place = lax.rem(gx, BLOCK)
    by_go = gy <= n_gy // 2
    after_seam = (place == 0) & by_go
    before_seam = (place == BLOCK - 1) & by_go
    crosses_down = place == BLOCK - 1
    crosses_up = crosses_down | ((lax.rem(place, 2) == 0) & (place != BLOCK - 2))
    relayed_up = crosses_up & below_middle
    relayed_down = crosses_down & above_middle
    relays_up = below_middle & jnp.logical_not(crosses_up)
    relays_down = (place == BLOCK - 2) & above_middle
    chip_mate = gx + 1 - 2 * lax.rem(gx, 2)

    barrier = pltpu.get_barrier_semaphore()

    def greet(device):
        pl.semaphore_signal(barrier, inc=1, device_id=device, device_id_type=MESH)

    pl.when(top)(lambda: greet(mirror_id))
    above_go = gy == n_gy // 2 + 1
    mate_sends_down = crosses_down & below_middle
    mate_sends_up = crosses_up & above_middle
    pl.when(mate_sends_down)(lambda: greet((chip_mate, gy + 1)))
    pl.when(mate_sends_up)(lambda: greet((chip_mate, gy - 1)))
    pl.when(jnp.logical_not(top | mate_sends_down))(lambda: greet(north_id))
    pl.when(jnp.logical_not(base | mate_sends_up | above_go))(lambda: greet(south_id))
    greet(west_id)
    pl.when(jnp.logical_not(before_seam))(lambda: greet(east_id))
    expected = (
        4 + (relays_up | relays_down).astype(jnp.int32) - (relayed_up | relayed_down).astype(jnp.int32)
        - after_seam.astype(jnp.int32) - base.astype(jnp.int32) - above_middle.astype(jnp.int32)
    )

    def load(source, target, index):
        copy = pltpu.make_async_copy(source, target, load_sem.at[index])
        copy.start()
        return copy

    last_rows, first_rows = pl.ds(CY - 2, 2), pl.ds(0, 2)
    early = [
        load(tracers.at[:, :, last_rows, :], strip.at[:, :, OWN_LAST, :], 0),
        load(tracers.at[:, :, first_rows, :], strip.at[:, :, OWN_FIRST, :], 1),
        load(bottom.at[last_rows, :], strip_b.at[OWN_LAST, :], 2),
        load(bottom.at[first_rows, :], strip_b.at[OWN_FIRST, :], 3),
        load(north.at[:, last_rows, :], strip_v.at[:, OWN_LAST, :], 4),
        load(north.at[:, first_rows, :], strip_v.at[:, OWN_FIRST, :], 5),
    ]
    late = [
        load(tracers, T.at[:, :, pl.ds(PAD, CY), :], 6),
        load(bottom, bottom_int, 7),
        load(east, U, 8),
        load(north, V, 9),
    ]

    lane = lax.broadcasted_iota(jnp.int32, (8, CX), 1)
    row = lax.broadcasted_iota(jnp.int32, (8, CX), 0)
    zeros = jnp.zeros((8, CX), jnp.float32)

    def octet(o):
        return pl.ds(PAD + 8 * o, 8)

    def shifted(o, by):
        return pl.ds(PAD + 8 * o + by, 8)

    for pad in (pl.ds(0, PAD), pl.ds(PAD + CY, PAD)):
        bf[pad, :] = zeros
        bn[pad, :] = zeros

    def clear(k, carry):
        for t in range(NT):
            YB[t, k, pl.ds(0, PAD), :] = zeros
            TZ[t, k, pl.ds(PAD + CY, PAD), :] = zeros
        return carry

    lax.fori_loop(0, NZ, clear, 0)

    @pl.when(base)
    def _():
        strip_b[FROM_SOUTH, :] = jnp.zeros((2, CX), jnp.int32)
        for t in range(NT):
            for k in range(NZ):
                strip[t, k, FROM_SOUTH, :] = jnp.zeros((2, CX), jnp.float32)

    for copy in early:
        copy.wait()

    @pl.when(top)
    def _():
        spots = [(t, k, pl.ds(2 * (NZ * t + k), 2)) for t in range(NT) for k in range(NZ)]
        for t, k, spot in spots:
            folded[spot, :] = strip[t, k, OWN_LAST, :]
        folded[pl.ds(64, 2), :] = strip_b[OWN_LAST, :].astype(jnp.float32)
        for i in range(FOLD_ROWS // 8):
            value = folded[pl.ds(8 * i, 8), :]
            for bit in (64, 32, 16, 8, 4, 2, 1):
                value = jnp.where(
                    (lane & bit) != 0, pltpu.roll(value, bit, 1), pltpu.roll(value, CX - bit, 1)
                )
            folded[pl.ds(8 * i, 8), :] = jnp.where((row & 1) != 0, rows_down(value), rows_up(value))
        for t, k, spot in spots:
            relay[t, k] = folded[spot, :]
        relay_b[...] = folded[pl.ds(64, 2), :].astype(jnp.int32)

    def send(source, target, index, slot, device):
        return pltpu.make_async_remote_copy(
            src_ref=source, dst_ref=target, send_sem=send_sem.at[index], recv_sem=recv_sem.at[slot],
            device_id=device, device_id_type=MESH,
        )

    def bundle(sources, targets, index, slot, device):
        pairs = enumerate(zip(sources, targets, strict=True))
        return [send(source, target, index + i, slot + i, device) for i, (source, target) in pairs]

    def start(copies):
        for copy in copies:
            copy.start()

    def wait_recv(copies):
        for copy in copies:
            copy.wait_recv()

    def wait_send(copies):
        for copy in copies:
            copy.wait_send()

    eastward = send(to_east, from_west, 0, 0, east_id)
    westward = send(to_west, from_east, 1, 1, west_id)
    last = [strip.at[:, :, OWN_LAST, :], strip_b.at[OWN_LAST, :], strip_v.at[:, pl.ds(1, 1), :]]
    first = [strip.at[:, :, OWN_FIRST, :], strip_b.at[OWN_FIRST, :]]
    from_south = [strip.at[:, :, FROM_SOUTH, :], strip_b.at[FROM_SOUTH, :], strip_v.at[:, pl.ds(5, 1), :]]
    from_north = [strip.at[:, :, FROM_NORTH, :], strip_b.at[FROM_NORTH, :]]
    between = [relay, relay_b, relay_v]
    northward = bundle(last, from_south, 2, 2, north_id)
    southward = bundle(first, from_north, 5, 5, south_id)
    across = bundle(between[:2], from_north, 2, 5, mirror_id)
    handed_up = bundle(last, between, 2, 7, (chip_mate, gy))
    handed_down = bundle(first, between[:2], 5, 7, (chip_mate, gy))
    forwarded_up = bundle(between, from_south, 7, 2, (chip_mate, gy + 1))
    forwarded_down = bundle(between[:2], from_north, 7, 5, (chip_mate, gy - 1))
    northward_itself = jnp.logical_not(top | relayed_up)
    southward_itself = jnp.logical_not(base | relayed_down)
    even = lax.rem(gx, 2) == 0
    late_entry = below_middle & jnp.logical_not(relayed_up) & (place < BLOCK - 2)

    @pl.when(jnp.logical_not(late_entry))
    def _():
        pl.semaphore_wait(barrier, expected)

        @pl.when(before_seam)
        def _():
            pl.semaphore_signal(go_sem, inc=1, device_id=east_id, device_id_type=MESH)

        @pl.when(above_go)
        def _():
            pl.semaphore_signal(go_north_sem, inc=1, device_id=south_id, device_id_type=MESH)

        pl.when(relayed_up)(lambda: start(handed_up))

        pl.when(northward_itself & below_middle)(lambda: start(northward))

        @pl.when(relays_up)
        def _():
            wait_recv(handed_up)
            start(forwarded_up)

        pl.when(relayed_down)(lambda: start(handed_down))
        pl.when(southward_itself & jnp.logical_not(relays_down))(lambda: start(southward))
        pl.when(northward_itself & jnp.logical_not(below_middle | above_middle))(lambda: start(northward))
        pl.when(top)(lambda: start(across))

        @pl.when(relays_down)
        def _():
            wait_recv(handed_down)
            start(forwarded_down)
            start(southward)

    def send_columns():
        pl.when(jnp.logical_not(even))(eastward.start)
        pl.when(jnp.logical_not(after_seam))(westward.start)
        pl.when(even)(eastward.start)

    for copy in late[:3]:
        copy.wait()

    for o in range(OCTETS):
        bf[octet(o), :] = bottom_int[pl.ds(8 * o, 8), :].astype(jnp.float32)
    for o in range(OCTETS):
        here = bf[octet(o), :]
        be[octet(o), :] = jnp.where(lane == CX - 1, 0.0, jnp.minimum(here, lanes_left(here)))
        bn[octet(o), :] = jnp.minimum(here, bf[shifted(o, 1), :])

    slot_of = lane // 4

    def pack(group, carry):
        t0, t1, speed = zeros, zeros, zeros
        for b in range(4):
            for o in range(OCTETS):
                slot = b * 8 + o
                here = slot_of == slot
                shift = (4 * slot + 2) % CX
                k = 4 * group + b
                t0 = jnp.where(here, pltpu.roll(T[0, k, octet(o), :], shift, 1), t0)
                t1 = jnp.where(here, pltpu.roll(T[1, k, octet(o), :], shift, 1), t1)
                speed = jnp.where(here, pltpu.roll(U[k, pl.ds(8 * o, 8), :], shift, 1), speed)
        packed[group] = t0
        packed[4 + group] = t1
        packed[8 + group] = speed
        return carry

    lax.fori_loop(0, 4, pack, 0, unroll=4)
    packed_b = zeros
    for b in range(4):
        for o in range(OCTETS):
            slot = b * 8 + o
            packed_b = jnp.where(
                slot_of == slot, pltpu.roll(bf[octet(o), :], (4 * slot + 2) % CX, 1), packed_b
            )
    packed[12] = packed_b

    first_half = lax.rem(lane, 4) < 2
    east_speeds = zeros
    for j in range(4):
        to_east[j] = jnp.where(first_half, packed[j], pltpu.roll(packed[4 + j], 2, 1))
        to_west[j] = jnp.where(first_half, pltpu.roll(packed[4 + j], CX - 2, 1), packed[j])
        east_speeds = jnp.where(
            lax.rem(lane, 4) == j, pltpu.roll(packed[8 + j], (CX + j - 1) % CX, 1), east_speeds
        )
    to_east[4] = east_speeds
    to_east[5] = packed_b
    to_west[4] = packed_b

    pl.when(jnp.logical_not(late_entry))(send_columns)


    late[3].wait()

    def vertical(k, carry):
        level = k.astype(jnp.float32)
        above = jnp.where(k > 0, level, 99.0)
        down, up = jnp.minimum(k + 1, NZ - 1), jnp.maximum(k - 1, 0)
        for o in range(OCTETS):
            depth = bf[octet(o), :]
            for t in range(NT):
                here = T[t, k, octet(o), :]
                TZ[t, k, octet(o), :] = jnp.where(
                    depth > level + 1.0, T[t, down, octet(o), :] - here, 0.0
                ) + jnp.where(depth > above, here - T[t, up, octet(o), :], 0.0)
        return carry

    lax.fori_loop(0, NZ, vertical, 0, unroll=2)

    def inside(k, carry):
        level = k.astype(jnp.float32)
        for o in range(OCTETS):
            here = [T[t, k, octet(o), :] for t in range(NT)]
            dz = [TZ[t, k, octet(o), :] for t in range(NT)]
            wet = be[octet(o), :] > level
            local = [jnp.where(wet, lanes_left(f) - f, 0.0) for f in here]
            before = [lanes_right(d) for d in local]
            after = [lanes_left(d) for d in local]
            speed = jnp.where(wet, U[k, pl.ds(8 * o, 8), :], 0.0)
            low, high, _, _ = face_fluxes(
                local, before, after, [z + lanes_left(z) for z in dz], speed
            )
            across_x = [lanes_right(high[t]) - low[t] for t in range(NT)]
            for t in range(NT):
                GX[t, k, octet(o), :] = local[t] + before[t]

            wet = bn[octet(o), :] > level
            wet_before = bn[shifted(o, -1), :] > level
            wet_after = bn[shifted(o, 1), :] > level
            nxt = [T[t, k, shifted(o, 1), :] for t in range(NT)]
            local = [jnp.where(wet, nxt[t] - here[t], 0.0) for t in range(NT)]
            before = [
                jnp.where(wet_before, here[t] - T[t, k, shifted(o, -1), :], 0.0) for t in range(NT)
            ]
            after = [
                jnp.where(wet_after, T[t, k, shifted(o, 2), :] - nxt[t], 0.0) for t in range(NT)
            ]
            speed = jnp.where(wet, V[k, pl.ds(8 * o, 8), :], 0.0)
            low, high, _, _ = face_fluxes(
                local, before, after, [dz[t] + TZ[t, k, shifted(o, 1), :] for t in range(NT)], speed
            )
            for t in range(NT):
                GY[t, k, octet(o), :] = local[t] + before[t]
                XY[t, k, octet(o), :] = across_x[t] - low[t]
                YB[t, k, octet(o), :] = high[t]
        return carry

    lax.fori_loop(0, NZ, inside, 0, unroll=2)

    @pl.when(late_entry)
    def _():
        pl.semaphore_wait(barrier, expected)

        @pl.when(relays_up)
        def _():
            wait_recv(handed_up)
            start(forwarded_up)

        start(northward)
        send_columns()
        start(southward)

    @pl.when(above_middle)
    def _():
        pl.semaphore_wait(go_north_sem, 1)
        start(northward)

    @pl.when(after_seam)
    def _():
        pl.semaphore_wait(go_sem, 1)
        westward.start()

    def prepare(octets):
        def body(k, carry):
            level = k.astype(jnp.float32)
            down = jnp.minimum(k + 1, NZ - 1)
            for o in octets:
                open_below = bf[octet(o), :] > level + 1.0
                here = [T[t, k, octet(o), :] for t in range(NT)]
                step = [T[t, down, octet(o), :] - here[t] for t in range(NT)]
                mean_y = [GY[t, k, octet(o), :] + GY[t, down, octet(o), :] for t in range(NT)]
                inverse = jnp.where(
                    open_below, reciprocal(jnp.maximum(4.0 * density(step), 1.0)), 0.0
                )
                slope = jnp.clip(density(mean_y) * inverse, -1.0, 1.0)
                square = 0.1 * (slope * slope)
                slope = 0.025 * slope
                Q[k, octet(o), :] = inverse
                for t in range(NT):
                    FY[t, k, octet(o), :] = square * step[t] - slope * mean_y[t]
                    XY[t, k, octet(o), :] += here[t] + YB[t, k, shifted(o, -1), :]
            return carry

        lax.fori_loop(0, NZ, body, 0, unroll=2)

    inner, outer = tuple(range(1, OCTETS - 1)), (0, OCTETS - 1)
    prepare(inner)

    def edge_rows_in():
        wait_recv(southward)
        pl.when(jnp.logical_not(base))(lambda: wait_recv(northward))

        def edge_rows(k, carry):
            level = k.astype(jnp.float32)
            above = jnp.where(k > 0, level, 99.0)
            down, up = jnp.minimum(k + 1, NZ - 1), jnp.maximum(k - 1, 0)
            depth = strip_b[...].astype(jnp.float32)
            here = [strip[t, k] for t in range(NT)]
            dz = [
                jnp.where(depth > level + 1.0, strip[t, down] - here[t], 0.0)
                + jnp.where(depth > above, here[t] - strip[t, up], 0.0)
                for t in range(NT)
            ]
            terms, grads = edge_terms(
                here, dz, depth, strip_v[k], level, rows_up, rows_down,
                row == 1, row == 5, row == 0, row == 6,
            )
            for t in range(NT):
                XY[t, k, octet(0), :] += jnp.where(row < 2, pltpu.roll(terms[t], 2, 0), 0.0)
                GY[t, k, octet(0), :] += jnp.where(row < 2, pltpu.roll(grads[t], 2, 0), 0.0)
                XY[t, k, octet(OCTETS - 1), :] += jnp.where(row > 5, pltpu.roll(terms[t], 6, 0), 0.0)
                GY[t, k, octet(OCTETS - 1), :] += jnp.where(row > 5, pltpu.roll(grads[t], 6, 0), 0.0)
            return carry

        lax.fori_loop(0, NZ, edge_rows, 0, unroll=16)

    rows_late = ((gy >= n_gy // 2 - 2) & (gy <= n_gy // 2 + 1)) | top

    @pl.when(jnp.logical_not(rows_late))
    def _():
        edge_rows_in()
        prepare(outer)

    quarter = lax.rem(lane, 4)
    level_in_group = (lane // 32).astype(jnp.float32)
    def edge_columns_in(side, first):
        (eastward if side == 0 else westward).wait_recv()
        own = [[packed[4 * t + j] for j in range(4)] for t in range(NT)]
        if side == 0:
            depth = jnp.where(first_half, from_west[5], packed[12])
            fields = [
                [jnp.where(first_half, from_west[j], own[0][j]) for j in range(4)],
                [jnp.where(first_half, pltpu.roll(from_west[j], CX - 2, 1), own[1][j]) for j in range(4)],
            ]
        else:
            depth = jnp.where(first_half, packed[12], from_east[4])
            fields = [
                [jnp.where(first_half, own[0][j], from_east[j]) for j in range(4)],
                [jnp.where(first_half, own[1][j], pltpu.roll(from_east[j], 2, 1)) for j in range(4)],
            ]
        steps = []
        for t in range(NT):
            turned = [pltpu.roll(f, CX - 32, 1) for f in fields[t]]
            steps.append(
                [
                    jnp.where(
                        depth > level_in_group + (4 * j + 1.0),
                        jnp.where(lane < CX - 32, turned[j], turned[min(j + 1, 3)]) - fields[t][j],
                        0.0,
                    )
                    for j in range(4)
                ]
            )
        for j in range(4):
            dz = []
            for t in range(NT):
                before = pltpu.roll(steps[t][j - 1], 32, 1) if j > 0 else zeros
                dz.append(
                    steps[t][j] + jnp.where(lane < 32, before, pltpu.roll(steps[t][j], 32, 1))
                )
            speed = packed[8 + j]
            if side == 0:
                speed = jnp.where(first_half, pltpu.roll(from_west[4], (CX + 1 - j) % CX, 1), speed)
            terms, grads = edge_terms(
                [fields[t][j] for t in range(NT)], dz, depth, speed, level_in_group + 4.0 * j,
                lanes_left, lanes_right,
                None if side == 0 else quarter == 1, quarter == 1 if side == 0 else None,
                None if side == 0 else quarter == 0, quarter == 2 if side == 0 else None,
            )
            for t in range(NT):
                if first:
                    edge_c[t, j] = terms[t]
                    edge_g[t, j] = grads[t]
                else:
                    edge_c[t, j] += terms[t]
                    edge_g[t, j] += grads[t]

    @pl.when(even)
    def _():
        edge_columns_in(1, True)
        edge_columns_in(0, False)

    @pl.when(jnp.logical_not(even))
    def _():
        edge_columns_in(0, True)
        edge_columns_in(1, False)

    at_edge = (lane < 2) | (lane >= CX - 2)

    def finish(octets, prepared):
        def at(o, ref, t, group, b):
            rolled = pltpu.roll(ref[t, group], (CX - (4 * (b * 8 + o) + 2)) % CX, 1)
            return jnp.where(at_edge, rolled, 0.0)

        def body(group, carry):
            fluxes = [[carry[4 * i], carry[4 * i + 1]] for i in range(len(octets))]
            gx_here = [[carry[4 * i + 2], carry[4 * i + 3]] for i in range(len(octets))]
            after = jnp.minimum(group + 1, 3)
            for b in range(4):
                k = 4 * group + b
                level = k.astype(jnp.float32)
                down = jnp.minimum(k + 1, NZ - 1)
                for i, o in enumerate(octets):
                    depth = bf[octet(o), :]
                    here = [T[t, k, octet(o), :] for t in range(NT)]
                    step = [T[t, down, octet(o), :] - here[t] for t in range(NT)]
                    gx_down = [
                        GX[t, down, octet(o), :]
                        + (at(o, edge_g, t, group, b + 1) if b < 3 else at(o, edge_g, t, after, 0))
                        for t in range(NT)
                    ]
                    mean_x = [gx_here[i][t] + gx_down[t] for t in range(NT)]
                    wet = depth > level
                    if prepared:
                        inverse = Q[k, octet(o), :]
                        other = [FY[t, k, octet(o), :] for t in range(NT)]
                        rest = [XY[t, k, octet(o), :] for t in range(NT)]
                    else:
                        mean_y = [
                            GY[t, k, octet(o), :] + GY[t, down, octet(o), :] for t in range(NT)
                        ]
                        inverse = jnp.where(
                            depth > level + 1.0, reciprocal(jnp.maximum(4.0 * density(step), 1.0)), 0.0
                        )
                        slope = jnp.clip(density(mean_y) * inverse, -1.0, 1.0)
                        square = 0.1 * (slope * slope)
                        slope = 0.025 * slope
                        other = [square * step[t] - slope * mean_y[t] for t in range(NT)]
                        rest = [
                            here[t] + (XY[t, k, octet(o), :] + YB[t, k, shifted(o, -1), :])
                            for t in range(NT)
                        ]
                    slope = jnp.clip(density(mean_x) * inverse, -1.0, 1.0)
                    square = 0.1 * (slope * slope)
                    slope = 0.025 * slope
                    for t in range(NT):
                        flux = other[t] + (square * step[t] - slope * mean_x[t])
                        total = (rest[t] + at(o, edge_c, t, group, b)) + (flux - fluxes[i][t])
                        out[t, k, pl.ds(8 * o, 8), :] = jnp.where(wet, total, 0.0)
                        fluxes[i][t] = flux
                    gx_here[i] = gx_down
            return tuple(x for i in range(len(octets)) for x in (*fluxes[i], *gx_here[i]))

        start = []
        for o in octets:
            start += [zeros, zeros]
            start += [GX[t, 0, octet(o), :] + at(o, edge_g, t, 0, 0) for t in range(NT)]
        lax.fori_loop(0, 4, body, tuple(start), unroll=4)

    finish(inner, True)

    @pl.when(rows_late)
    def _():
        edge_rows_in()
        finish(outer, False)

    @pl.when(jnp.logical_not(rows_late))
    def _():
        finish(outer, True)

    eastward.wait_send()
    westward.wait_send()
    pl.when(southward_itself)(lambda: wait_send(southward))
    pl.when(northward_itself)(lambda: wait_send(northward))
    pl.when(relayed_up)(lambda: wait_send(handed_up))
    pl.when(relayed_down)(lambda: wait_send(handed_down))
    pl.when(top)(lambda: wait_send(across))
    pl.when(relays_up)(lambda: wait_send(forwarded_up))
    pl.when(relays_down)(lambda: wait_send(forwarded_down))


def solution(mesh):
    n_gx, n_gy = mesh.shape["gx"], mesh.shape["gy"]
    f32 = jnp.float32
    in_hbm = pl.BlockSpec(memory_space=pltpu.HBM)
    field = pltpu.VMEM((NT, NZ, TALL, CX), f32)
    levels = pltpu.VMEM((NZ, CY, CX), f32)
    plane = pltpu.VMEM((TALL, CX), f32)
    packed = pltpu.VMEM((PACKED, 8, CX), f32)
    eastward = pltpu.VMEM((EASTWARD, 8, CX), f32)
    westward = pltpu.VMEM((WESTWARD, 8, CX), f32)
    edge = pltpu.VMEM((NT, 4, 8, CX), f32)

    def on_device(tracers, east_speed, north_speed, bottom_level):
        return pl.pallas_call(
            functools.partial(kernel, n_gx, n_gy),
            out_shape=jax.ShapeDtypeStruct((NT, NZ, CY, CX), f32),
            in_specs=[in_hbm] * 4,
            out_specs=pl.BlockSpec(memory_space=pltpu.VMEM),
            scratch_shapes=[
                field, levels, levels, pltpu.VMEM((CY, CX), jnp.int32), plane, plane, plane,
                field, field, field, field, field, field, pltpu.VMEM((NZ, TALL, CX), f32),
                packed, eastward, westward, eastward, westward,
                pltpu.VMEM((NT, NZ, 2, CX), f32), pltpu.VMEM((2, CX), jnp.int32),
                pltpu.VMEM((NZ, 1, CX), f32), pltpu.VMEM((FOLD_ROWS, CX), f32),
                pltpu.VMEM((NT, NZ, 8, CX), f32), pltpu.VMEM((8, CX), jnp.int32),
                pltpu.VMEM((NZ, 8, CX), f32), edge, edge,
                pltpu.SemaphoreType.DMA((10,)), pltpu.SemaphoreType.DMA((10,)),
                pltpu.SemaphoreType.DMA((10,)), pltpu.SemaphoreType.REGULAR, pltpu.SemaphoreType.REGULAR,
            ],
            compiler_params=pltpu.CompilerParams(
                collective_id=0, has_side_effects=True, vmem_limit_bytes=24 * 1024 * 1024
            ),
        )(
            *[
                pltpu.with_memory_space_constraint(x, pltpu.HBM)
                for x in (tracers, east_speed, north_speed, bottom_level)
            ]
        )

    in_specs = (P(None, None, "gy", "gx"), P(None, "gy", "gx"), P(None, "gy", "gx"), P("gy", "gx"))
    return jax.shard_map(
        on_device, mesh=mesh, in_specs=in_specs, out_specs=P(None, None, "gy", "gx"), check_vma=False
    )
```

```python
import functools

import jax
import jax.numpy as jnp
from jax import lax
from jax.experimental import pallas as pl
from jax.experimental.pallas import tpu as pltpu
from jax.sharding import PartitionSpec as P

MESH = pl.DeviceIdType.MESH
NT, NZ, CY, CX = 2, 16, 48, 128
PAD = 8
TALL = CY + 2 * PAD
OCTETS = CY // 8
FOLD_ROWS = 72
OWN_LAST, FROM_NORTH, FROM_SOUTH, OWN_FIRST = (pl.ds(i, 2) for i in (0, 2, 4, 6))
PACKED = 13
EASTWARD = 6
WESTWARD = 5
BLOCK = 8
HEAT = 0.4
SALT = 0.6


def reciprocal(value):
    guess = pl.reciprocal(value, approx=True)
    return guess * (2.0 - value * guess)


def minmod(first, second):
    return jnp.maximum(jnp.minimum(first, second), 0.0) + jnp.minimum(
        jnp.maximum(first, second), 0.0
    )


def density(pair):
    return SALT * pair[1] - HEAT * pair[0]


def face_fluxes(local, before, after, dz_sum, speed):
    slope = jnp.clip(
        (0.1 * density(local)) * reciprocal(jnp.maximum(density(dz_sum), 1.0)), -0.025, 0.025
    )
    size = jnp.abs(speed)
    limited = 0.5 * size * (1.0 - size)
    forward = speed >= 0.0
    linear = jnp.minimum(speed, 0.0) - 0.1
    low, high, second = [], [], []
    for t in range(NT):
        correction = limited * minmod(local[t], jnp.where(forward, before[t], after[t]))
        taken = correction + (linear * local[t] + slope * dz_sum[t])
        low.append(taken)
        high.append(taken - speed * local[t])
        second.append(correction)
    return low, high, second, forward


def lanes_left(value):
    return pltpu.roll(value, CX - 1, 1)


def lanes_right(value):
    return pltpu.roll(value, 1, 1)


def rows_up(value):
    return pltpu.roll(value, 7, 0)


def rows_down(value):
    return pltpu.roll(value, 1, 0)


def edge_terms(field, dz, bottom, speed, level, nxt, prv, low_at, high_at, low_second, high_second):
    wet = jnp.minimum(bottom, nxt(bottom)) > level
    local = [jnp.where(wet, nxt(f) - f, 0.0) for f in field]
    dz_sum = [z + nxt(z) for z in dz]
    masked = jnp.where(wet, speed, 0.0)
    low, high, second, forward = face_fluxes(
        local, [prv(d) for d in local], [nxt(d) for d in local], dz_sum, masked
    )
    zero = jnp.zeros_like(masked)
    terms, steps = [], []
    for t in range(NT):
        late = zero
        if low_second is not None:
            late = late + jnp.where(low_second & ~forward, second[t], 0.0)
        if high_second is not None:
            late = late + jnp.where(high_second & forward, second[t], 0.0)
        arriving, term, step = late, -late, zero
        if high_at is not None:
            arriving = arriving + jnp.where(high_at, high[t], 0.0)
            step = step + prv(jnp.where(high_at, local[t], 0.0))
        if low_at is not None:
            term = term - jnp.where(low_at, low[t], 0.0)
            step = step + jnp.where(low_at, local[t], 0.0)
        terms.append(term + prv(arriving))
        steps.append(step)
    return terms, steps


def kernel(
    n_gx, n_gy,
    tracers, east, north, bottom, out,
    T, U, V, bottom_int, bf, be, bn, TZ, XY, YB, GX, GY, FY, Q,
    packed, to_east, to_west, from_west, from_east, relay, relay_b, relay_v, folded,
    strip, strip_b, strip_v, edge_c, edge_g,
    load_sem, send_sem, recv_sem, go_sem, go_north_sem,
):
    gx, gy = lax.axis_index("gx"), lax.axis_index("gy")
    east_id = (lax.rem(gx + 1, n_gx), gy)
    west_id = (lax.rem(gx + n_gx - 1, n_gx), gy)
    north_id = (gx, gy + 1)
    south_id = (gx, gy - 1)
    mirror_id = (n_gx - 1 - gx, gy)
    top = gy == n_gy - 1
    base = gy == 0
    below_middle = gy == n_gy // 2 - 1
    above_middle = gy == n_gy // 2
    place = lax.rem(gx, BLOCK)
    by_go = gy <= n_gy // 2
    after_seam = (place == 0) & by_go
    before_seam = (place == BLOCK - 1) & by_go
    crosses_down = place == BLOCK - 1
    crosses_up = crosses_down | ((lax.rem(place, 2) == 0) & (place != BLOCK - 2))
    relayed_up = crosses_up & below_middle
    relayed_down = crosses_down & above_middle
    relays_up = below_middle & jnp.logical_not(crosses_up)
    relays_down = (place == BLOCK - 2) & above_middle
    chip_mate = gx + 1 - 2 * lax.rem(gx, 2)

    barrier = pltpu.get_barrier_semaphore()

    def greet(device):
        pl.semaphore_signal(barrier, inc=1, device_id=device, device_id_type=MESH)

    pl.when(top)(lambda: greet(mirror_id))
    above_go = gy == n_gy // 2 + 1
    mate_sends_down = crosses_down & below_middle
    mate_sends_up = crosses_up & above_middle
    pl.when(mate_sends_down)(lambda: greet((chip_mate, gy + 1)))
    pl.when(mate_sends_up)(lambda: greet((chip_mate, gy - 1)))
    pl.when(jnp.logical_not(top | mate_sends_down))(lambda: greet(north_id))
    pl.when(jnp.logical_not(base | mate_sends_up | above_go))(lambda: greet(south_id))
    greet(west_id)
    pl.when(jnp.logical_not(before_seam))(lambda: greet(east_id))
    expected = (
        4 + (relays_up | relays_down).astype(jnp.int32) - (relayed_up | relayed_down).astype(jnp.int32)
        - after_seam.astype(jnp.int32) - base.astype(jnp.int32) - above_middle.astype(jnp.int32)
    )

    def load(source, target, index):
        copy = pltpu.make_async_copy(source, target, load_sem.at[index])
        copy.start()
        return copy

    last_rows, first_rows = pl.ds(CY - 2, 2), pl.ds(0, 2)
    early = [
        load(tracers.at[:, :, last_rows, :], strip.at[:, :, OWN_LAST, :], 0),
        load(tracers.at[:, :, first_rows, :], strip.at[:, :, OWN_FIRST, :], 1),
        load(bottom.at[last_rows, :], strip_b.at[OWN_LAST, :], 2),
        load(bottom.at[first_rows, :], strip_b.at[OWN_FIRST, :], 3),
        load(north.at[:, last_rows, :], strip_v.at[:, OWN_LAST, :], 4),
        load(north.at[:, first_rows, :], strip_v.at[:, OWN_FIRST, :], 5),
    ]
    late = [
        load(tracers, T.at[:, :, pl.ds(PAD, CY), :], 6),
        load(bottom, bottom_int, 7),
        load(east, U, 8),
        load(north, V, 9),
    ]

    lane = lax.broadcasted_iota(jnp.int32, (8, CX), 1)
    row = lax.broadcasted_iota(jnp.int32, (8, CX), 0)
    zeros = jnp.zeros((8, CX), jnp.float32)

    def octet(o):
        return pl.ds(PAD + 8 * o, 8)

    def shifted(o, by):
        return pl.ds(PAD + 8 * o + by, 8)

    for pad in (pl.ds(0, PAD), pl.ds(PAD + CY, PAD)):
        bf[pad, :] = zeros
        bn[pad, :] = zeros

    def clear(k, carry):
        for t in range(NT):
            YB[t, k, pl.ds(0, PAD), :] = zeros
            TZ[t, k, pl.ds(PAD + CY, PAD), :] = zeros
        return carry

    lax.fori_loop(0, NZ, clear, 0)

    @pl.when(base)
    def _():
        strip_b[FROM_SOUTH, :] = jnp.zeros((2, CX), jnp.int32)
        for t in range(NT):
            for k in range(NZ):
                strip[t, k, FROM_SOUTH, :] = jnp.zeros((2, CX), jnp.float32)

    for copy in early:
        copy.wait()

    @pl.when(top)
    def _():
        spots = [(t, k, pl.ds(2 * (NZ * t + k), 2)) for t in range(NT) for k in range(NZ)]
        for t, k, spot in spots:
            folded[spot, :] = strip[t, k, OWN_LAST, :]
        folded[pl.ds(64, 2), :] = strip_b[OWN_LAST, :].astype(jnp.float32)
        for i in range(FOLD_ROWS // 8):
            value = folded[pl.ds(8 * i, 8), :]
            for bit in (64, 32, 16, 8, 4, 2, 1):
                value = jnp.where(
                    (lane & bit) != 0, pltpu.roll(value, bit, 1), pltpu.roll(value, CX - bit, 1)
                )
            folded[pl.ds(8 * i, 8), :] = jnp.where((row & 1) != 0, rows_down(value), rows_up(value))
        for t, k, spot in spots:
            relay[t, k] = folded[spot, :]
        relay_b[...] = folded[pl.ds(64, 2), :].astype(jnp.int32)

    def send(source, target, index, slot, device):
        return pltpu.make_async_remote_copy(
            src_ref=source, dst_ref=target, send_sem=send_sem.at[index], recv_sem=recv_sem.at[slot],
            device_id=device, device_id_type=MESH,
        )

    def bundle(sources, targets, index, slot, device):
        pairs = enumerate(zip(sources, targets, strict=True))
        return [send(source, target, index + i, slot + i, device) for i, (source, target) in pairs]

    def start(copies):
        for copy in copies:
            copy.start()

    def wait_recv(copies):
        for copy in copies:
            copy.wait_recv()

    def wait_send(copies):
        for copy in copies:
            copy.wait_send()

    eastward = send(to_east, from_west, 0, 0, east_id)
    westward = send(to_west, from_east, 1, 1, west_id)
    last = [strip.at[:, :, OWN_LAST, :], strip_b.at[OWN_LAST, :], strip_v.at[:, pl.ds(1, 1), :]]
    first = [strip.at[:, :, OWN_FIRST, :], strip_b.at[OWN_FIRST, :]]
    from_south = [strip.at[:, :, FROM_SOUTH, :], strip_b.at[FROM_SOUTH, :], strip_v.at[:, pl.ds(5, 1), :]]
    from_north = [strip.at[:, :, FROM_NORTH, :], strip_b.at[FROM_NORTH, :]]
    between = [relay, relay_b, relay_v]
    northward = bundle(last, from_south, 2, 2, north_id)
    southward = bundle(first, from_north, 5, 5, south_id)
    across = bundle(between[:2], from_north, 2, 5, mirror_id)
    handed_up = bundle(last, between, 2, 7, (chip_mate, gy))
    handed_down = bundle(first, between[:2], 5, 7, (chip_mate, gy))
    forwarded_up = bundle(between, from_south, 7, 2, (chip_mate, gy + 1))
    forwarded_down = bundle(between[:2], from_north, 7, 5, (chip_mate, gy - 1))
    northward_itself = jnp.logical_not(top | relayed_up)
    southward_itself = jnp.logical_not(base | relayed_down)
    even = lax.rem(gx, 2) == 0
    late_entry = below_middle & jnp.logical_not(relayed_up) & (place < BLOCK - 2)

    @pl.when(jnp.logical_not(late_entry))
    def _():
        pl.semaphore_wait(barrier, expected)

        @pl.when(before_seam)
        def _():
            pl.semaphore_signal(go_sem, inc=1, device_id=east_id, device_id_type=MESH)

        @pl.when(above_go)
        def _():
            pl.semaphore_signal(go_north_sem, inc=1, device_id=south_id, device_id_type=MESH)

        pl.when(relayed_up)(lambda: start(handed_up))

        @pl.when(relays_up)
        def _():
            wait_recv(handed_up)
            start(forwarded_up)

        pl.when(northward_itself & below_middle)(lambda: start(northward))
        pl.when(relayed_down)(lambda: start(handed_down))
        pl.when(southward_itself & jnp.logical_not(relays_down))(lambda: start(southward))
        pl.when(northward_itself & jnp.logical_not(below_middle | above_middle))(lambda: start(northward))
        pl.when(top)(lambda: start(across))

        @pl.when(relays_down)
        def _():
            wait_recv(handed_down)
            start(forwarded_down)
            start(southward)

    def send_columns():
        pl.when(jnp.logical_not(even))(eastward.start)
        pl.when(jnp.logical_not(after_seam))(westward.start)
        pl.when(even)(eastward.start)

    for copy in late[:3]:
        copy.wait()

    for o in range(OCTETS):
        bf[octet(o), :] = bottom_int[pl.ds(8 * o, 8), :].astype(jnp.float32)
    for o in range(OCTETS):
        here = bf[octet(o), :]
        be[octet(o), :] = jnp.where(lane == CX - 1, 0.0, jnp.minimum(here, lanes_left(here)))
        bn[octet(o), :] = jnp.minimum(here, bf[shifted(o, 1), :])

    slot_of = lane // 4

    def pack(group, carry):
        t0, t1, speed = zeros, zeros, zeros
        for b in range(4):
            for o in range(OCTETS):
                slot = b * 8 + o
                here = slot_of == slot
                shift = (4 * slot + 2) % CX
                k = 4 * group + b
                t0 = jnp.where(here, pltpu.roll(T[0, k, octet(o), :], shift, 1), t0)
                t1 = jnp.where(here, pltpu.roll(T[1, k, octet(o), :], shift, 1), t1)
                speed = jnp.where(here, pltpu.roll(U[k, pl.ds(8 * o, 8), :], shift, 1), speed)
        packed[group] = t0
        packed[4 + group] = t1
        packed[8 + group] = speed
        return carry

    lax.fori_loop(0, 4, pack, 0, unroll=4)
    packed_b = zeros
    for b in range(4):
        for o in range(OCTETS):
            slot = b * 8 + o
            packed_b = jnp.where(
                slot_of == slot, pltpu.roll(bf[octet(o), :], (4 * slot + 2) % CX, 1), packed_b
            )
    packed[12] = packed_b

    first_half = lax.rem(lane, 4) < 2
    east_speeds = zeros
    for j in range(4):
        to_east[j] = jnp.where(first_half, packed[j], pltpu.roll(packed[4 + j], 2, 1))
        to_west[j] = jnp.where(first_half, pltpu.roll(packed[4 + j], CX - 2, 1), packed[j])
        east_speeds = jnp.where(
            lax.rem(lane, 4) == j, pltpu.roll(packed[8 + j], (CX + j - 1) % CX, 1), east_speeds
        )
    to_east[4] = east_speeds
    to_east[5] = packed_b
    to_west[4] = packed_b

    pl.when(jnp.logical_not(late_entry))(send_columns)


    late[3].wait()

    def vertical(k, carry):
        level = k.astype(jnp.float32)
        above = jnp.where(k > 0, level, 99.0)
        down, up = jnp.minimum(k + 1, NZ - 1), jnp.maximum(k - 1, 0)
        for o in range(OCTETS):
            depth = bf[octet(o), :]
            for t in range(NT):
                here = T[t, k, octet(o), :]
                TZ[t, k, octet(o), :] = jnp.where(
                    depth > level + 1.0, T[t, down, octet(o), :] - here, 0.0
                ) + jnp.where(depth > above, here - T[t, up, octet(o), :], 0.0)
        return carry

    lax.fori_loop(0, NZ, vertical, 0, unroll=2)

    def inside(k, carry):
        level = k.astype(jnp.float32)
        for o in range(OCTETS):
            here = [T[t, k, octet(o), :] for t in range(NT)]
            dz = [TZ[t, k, octet(o), :] for t in range(NT)]
            wet = be[octet(o), :] > level
            local = [jnp.where(wet, lanes_left(f) - f, 0.0) for f in here]
            before = [lanes_right(d) for d in local]
            after = [lanes_left(d) for d in local]
            speed = jnp.where(wet, U[k, pl.ds(8 * o, 8), :], 0.0)
            low, high, _, _ = face_fluxes(
                local, before, after, [z + lanes_left(z) for z in dz], speed
            )
            across_x = [lanes_right(high[t]) - low[t] for t in range(NT)]
            for t in range(NT):
                GX[t, k, octet(o), :] = local[t] + before[t]

            wet = bn[octet(o), :] > level
            wet_before = bn[shifted(o, -1), :] > level
            wet_after = bn[shifted(o, 1), :] > level
            nxt = [T[t, k, shifted(o, 1), :] for t in range(NT)]
            local = [jnp.where(wet, nxt[t] - here[t], 0.0) for t in range(NT)]
            before = [
                jnp.where(wet_before, here[t] - T[t, k, shifted(o, -1), :], 0.0) for t in range(NT)
            ]
            after = [
                jnp.where(wet_after, T[t, k, shifted(o, 2), :] - nxt[t], 0.0) for t in range(NT)
            ]
            speed = jnp.where(wet, V[k, pl.ds(8 * o, 8), :], 0.0)
            low, high, _, _ = face_fluxes(
                local, before, after, [dz[t] + TZ[t, k, shifted(o, 1), :] for t in range(NT)], speed
            )
            for t in range(NT):
                GY[t, k, octet(o), :] = local[t] + before[t]
                XY[t, k, octet(o), :] = across_x[t] - low[t]
                YB[t, k, octet(o), :] = high[t]
        return carry

    lax.fori_loop(0, NZ, inside, 0, unroll=2)

    @pl.when(late_entry)
    def _():
        pl.semaphore_wait(barrier, expected)

        @pl.when(relays_up)
        def _():
            wait_recv(handed_up)
            start(forwarded_up)

        start(northward)
        send_columns()
        start(southward)

    @pl.when(above_middle)
    def _():
        pl.semaphore_wait(go_north_sem, 1)
        start(northward)

    @pl.when(after_seam)
    def _():
        pl.semaphore_wait(go_sem, 1)
        westward.start()

    def prepare(octets):
        def body(k, carry):
            level = k.astype(jnp.float32)
            down = jnp.minimum(k + 1, NZ - 1)
            for o in octets:
                open_below = bf[octet(o), :] > level + 1.0
                here = [T[t, k, octet(o), :] for t in range(NT)]
                step = [T[t, down, octet(o), :] - here[t] for t in range(NT)]
                mean_y = [GY[t, k, octet(o), :] + GY[t, down, octet(o), :] for t in range(NT)]
                inverse = jnp.where(
                    open_below, reciprocal(jnp.maximum(4.0 * density(step), 1.0)), 0.0
                )
                slope = jnp.clip(density(mean_y) * inverse, -1.0, 1.0)
                square = 0.1 * (slope * slope)
                slope = 0.025 * slope
                Q[k, octet(o), :] = inverse
                for t in range(NT):
                    FY[t, k, octet(o), :] = square * step[t] - slope * mean_y[t]
                    XY[t, k, octet(o), :] += here[t] + YB[t, k, shifted(o, -1), :]
            return carry

        lax.fori_loop(0, NZ, body, 0, unroll=2)

    inner, outer = tuple(range(1, OCTETS - 1)), (0, OCTETS - 1)
    prepare(inner)

    def edge_rows_in():
        wait_recv(southward)
        pl.when(jnp.logical_not(base))(lambda: wait_recv(northward))

        def edge_rows(k, carry):
            level = k.astype(jnp.float32)
            above = jnp.where(k > 0, level, 99.0)
            down, up = jnp.minimum(k + 1, NZ - 1), jnp.maximum(k - 1, 0)
            depth = strip_b[...].astype(jnp.float32)
            here = [strip[t, k] for t in range(NT)]
            dz = [
                jnp.where(depth > level + 1.0, strip[t, down] - here[t], 0.0)
                + jnp.where(depth > above, here[t] - strip[t, up], 0.0)
                for t in range(NT)
            ]
            terms, grads = edge_terms(
                here, dz, depth, strip_v[k], level, rows_up, rows_down,
                row == 1, row == 5, row == 0, row == 6,
            )
            for t in range(NT):
                XY[t, k, octet(0), :] += jnp.where(row < 2, pltpu.roll(terms[t], 2, 0), 0.0)
                GY[t, k, octet(0), :] += jnp.where(row < 2, pltpu.roll(grads[t], 2, 0), 0.0)
                XY[t, k, octet(OCTETS - 1), :] += jnp.where(row > 5, pltpu.roll(terms[t], 6, 0), 0.0)
                GY[t, k, octet(OCTETS - 1), :] += jnp.where(row > 5, pltpu.roll(grads[t], 6, 0), 0.0)
            return carry

        lax.fori_loop(0, NZ, edge_rows, 0, unroll=16)

    rows_late = ((gy >= n_gy // 2 - 2) & (gy <= n_gy // 2 + 1)) | top

    @pl.when(jnp.logical_not(rows_late))
    def _():
        edge_rows_in()
        prepare(outer)

    quarter = lax.rem(lane, 4)
    level_in_group = (lane // 32).astype(jnp.float32)
    def edge_columns_in(side, first):
        (eastward if side == 0 else westward).wait_recv()
        own = [[packed[4 * t + j] for j in range(4)] for t in range(NT)]
        if side == 0:
            depth = jnp.where(first_half, from_west[5], packed[12])
            fields = [
                [jnp.where(first_half, from_west[j], own[0][j]) for j in range(4)],
                [jnp.where(first_half, pltpu.roll(from_west[j], CX - 2, 1), own[1][j]) for j in range(4)],
            ]
        else:
            depth = jnp.where(first_half, packed[12], from_east[4])
            fields = [
                [jnp.where(first_half, own[0][j], from_east[j]) for j in range(4)],
                [jnp.where(first_half, own[1][j], pltpu.roll(from_east[j], 2, 1)) for j in range(4)],
            ]
        steps = []
        for t in range(NT):
            turned = [pltpu.roll(f, CX - 32, 1) for f in fields[t]]
            steps.append(
                [
                    jnp.where(
                        depth > level_in_group + (4 * j + 1.0),
                        jnp.where(lane < CX - 32, turned[j], turned[min(j + 1, 3)]) - fields[t][j],
                        0.0,
                    )
                    for j in range(4)
                ]
            )
        for j in range(4):
            dz = []
            for t in range(NT):
                before = pltpu.roll(steps[t][j - 1], 32, 1) if j > 0 else zeros
                dz.append(
                    steps[t][j] + jnp.where(lane < 32, before, pltpu.roll(steps[t][j], 32, 1))
                )
            speed = packed[8 + j]
            if side == 0:
                speed = jnp.where(first_half, pltpu.roll(from_west[4], (CX + 1 - j) % CX, 1), speed)
            terms, grads = edge_terms(
                [fields[t][j] for t in range(NT)], dz, depth, speed, level_in_group + 4.0 * j,
                lanes_left, lanes_right,
                None if side == 0 else quarter == 1, quarter == 1 if side == 0 else None,
                None if side == 0 else quarter == 0, quarter == 2 if side == 0 else None,
            )
            for t in range(NT):
                if first:
                    edge_c[t, j] = terms[t]
                    edge_g[t, j] = grads[t]
                else:
                    edge_c[t, j] += terms[t]
                    edge_g[t, j] += grads[t]

    @pl.when(even)
    def _():
        edge_columns_in(1, True)
        edge_columns_in(0, False)

    @pl.when(jnp.logical_not(even))
    def _():
        edge_columns_in(0, True)
        edge_columns_in(1, False)

    at_edge = (lane < 2) | (lane >= CX - 2)

    def finish(octets, prepared):
        def at(o, ref, t, group, b):
            rolled = pltpu.roll(ref[t, group], (CX - (4 * (b * 8 + o) + 2)) % CX, 1)
            return jnp.where(at_edge, rolled, 0.0)

        def body(group, carry):
            fluxes = [[carry[4 * i], carry[4 * i + 1]] for i in range(len(octets))]
            gx_here = [[carry[4 * i + 2], carry[4 * i + 3]] for i in range(len(octets))]
            after = jnp.minimum(group + 1, 3)
            for b in range(4):
                k = 4 * group + b
                level = k.astype(jnp.float32)
                down = jnp.minimum(k + 1, NZ - 1)
                for i, o in enumerate(octets):
                    depth = bf[octet(o), :]
                    here = [T[t, k, octet(o), :] for t in range(NT)]
                    step = [T[t, down, octet(o), :] - here[t] for t in range(NT)]
                    gx_down = [
                        GX[t, down, octet(o), :]
                        + (at(o, edge_g, t, group, b + 1) if b < 3 else at(o, edge_g, t, after, 0))
                        for t in range(NT)
                    ]
                    mean_x = [gx_here[i][t] + gx_down[t] for t in range(NT)]
                    wet = depth > level
                    if prepared:
                        inverse = Q[k, octet(o), :]
                        other = [FY[t, k, octet(o), :] for t in range(NT)]
                        rest = [XY[t, k, octet(o), :] for t in range(NT)]
                    else:
                        inverse = jnp.where(
                            depth > level + 1.0, reciprocal(jnp.maximum(4.0 * density(step), 1.0)), 0.0
                        )
                        Q[k, octet(o), :] = inverse
                    slope = jnp.clip(density(mean_x) * inverse, -1.0, 1.0)
                    square = 0.1 * (slope * slope)
                    slope = 0.025 * slope
                    for t in range(NT):
                        flux = square * step[t] - slope * mean_x[t]
                        term = at(o, edge_c, t, group, b)
                        if prepared:
                            flux = other[t] + flux
                            total = (rest[t] + term) + (flux - fluxes[i][t])
                            out[t, k, pl.ds(8 * o, 8), :] = jnp.where(wet, total, 0.0)
                            fluxes[i][t] = flux
                        else:
                            FY[t, k, octet(o), :] = flux
                            XY[t, k, octet(o), :] += term + (here[t] + YB[t, k, shifted(o, -1), :])
                    gx_here[i] = gx_down
            return tuple(x for i in range(len(octets)) for x in (*fluxes[i], *gx_here[i]))

        start = []
        for o in octets:
            start += [zeros, zeros]
            start += [GX[t, 0, octet(o), :] + at(o, edge_g, t, 0, 0) for t in range(NT)]
        lax.fori_loop(0, 4, body, tuple(start), unroll=4)

    finish(inner, True)

    def finish_rows(octets):
        def body(k, carry):
            level = k.astype(jnp.float32)
            down = jnp.minimum(k + 1, NZ - 1)
            fluxes, gy_down = [], []
            for i, o in enumerate(octets):
                inverse = Q[k, octet(o), :]
                wet = bf[octet(o), :] > level
                below = [GY[t, down, octet(o), :] for t in range(NT)]
                mean_y = [carry[1][NT * i + t] + below[t] for t in range(NT)]
                slope = jnp.clip(density(mean_y) * inverse, -1.0, 1.0)
                square = 0.1 * (slope * slope)
                slope = 0.025 * slope
                for t in range(NT):
                    step = T[t, down, octet(o), :] - T[t, k, octet(o), :]
                    flux = FY[t, k, octet(o), :] + (square * step - slope * mean_y[t])
                    total = XY[t, k, octet(o), :] + (flux - carry[0][NT * i + t])
                    out[t, k, pl.ds(8 * o, 8), :] = jnp.where(wet, total, 0.0)
                    fluxes.append(flux)
                gy_down += below
            return tuple(fluxes), tuple(gy_down)

        top_gy = tuple(GY[t, 0, octet(o), :] for o in octets for t in range(NT))
        lax.fori_loop(0, NZ, body, (tuple(zeros for _ in top_gy), top_gy), unroll=16)

    @pl.when(rows_late)
    def _():
        finish(outer, False)
        edge_rows_in()
        finish_rows(outer)

    @pl.when(jnp.logical_not(rows_late))
    def _():
        finish(outer, True)

    eastward.wait_send()
    westward.wait_send()
    pl.when(southward_itself)(lambda: wait_send(southward))
    pl.when(northward_itself)(lambda: wait_send(northward))
    pl.when(relayed_up)(lambda: wait_send(handed_up))
    pl.when(relayed_down)(lambda: wait_send(handed_down))
    pl.when(top)(lambda: wait_send(across))
    pl.when(relays_up)(lambda: wait_send(forwarded_up))
    pl.when(relays_down)(lambda: wait_send(forwarded_down))


def solution(mesh):
    n_gx, n_gy = mesh.shape["gx"], mesh.shape["gy"]
    f32 = jnp.float32
    in_hbm = pl.BlockSpec(memory_space=pltpu.HBM)
    field = pltpu.VMEM((NT, NZ, TALL, CX), f32)
    levels = pltpu.VMEM((NZ, CY, CX), f32)
    plane = pltpu.VMEM((TALL, CX), f32)
    packed = pltpu.VMEM((PACKED, 8, CX), f32)
    eastward = pltpu.VMEM((EASTWARD, 8, CX), f32)
    westward = pltpu.VMEM((WESTWARD, 8, CX), f32)
    edge = pltpu.VMEM((NT, 4, 8, CX), f32)

    def on_device(tracers, east_speed, north_speed, bottom_level):
        return pl.pallas_call(
            functools.partial(kernel, n_gx, n_gy),
            out_shape=jax.ShapeDtypeStruct((NT, NZ, CY, CX), f32),
            in_specs=[in_hbm] * 4,
            out_specs=pl.BlockSpec(memory_space=pltpu.VMEM),
            scratch_shapes=[
                field, levels, levels, pltpu.VMEM((CY, CX), jnp.int32), plane, plane, plane,
                field, field, field, field, field, field, pltpu.VMEM((NZ, TALL, CX), f32),
                packed, eastward, westward, eastward, westward,
                pltpu.VMEM((NT, NZ, 2, CX), f32), pltpu.VMEM((2, CX), jnp.int32),
                pltpu.VMEM((NZ, 1, CX), f32), pltpu.VMEM((FOLD_ROWS, CX), f32),
                pltpu.VMEM((NT, NZ, 8, CX), f32), pltpu.VMEM((8, CX), jnp.int32),
                pltpu.VMEM((NZ, 8, CX), f32), edge, edge,
                pltpu.SemaphoreType.DMA((10,)), pltpu.SemaphoreType.DMA((10,)),
                pltpu.SemaphoreType.DMA((10,)), pltpu.SemaphoreType.REGULAR, pltpu.SemaphoreType.REGULAR,
            ],
            compiler_params=pltpu.CompilerParams(
                collective_id=0, has_side_effects=True, vmem_limit_bytes=24 * 1024 * 1024
            ),
        )(
            *[
                pltpu.with_memory_space_constraint(x, pltpu.HBM)
                for x in (tracers, east_speed, north_speed, bottom_level)
            ]
        )

    in_specs = (P(None, None, "gy", "gx"), P(None, "gy", "gx"), P(None, "gy", "gx"), P("gy", "gx"))
    return jax.shard_map(
        on_device, mesh=mesh, in_specs=in_specs, out_specs=P(None, None, "gy", "gx"), check_vma=False
    )
```

```python
import functools

import jax
import jax.numpy as jnp
from jax import lax
from jax.experimental import pallas as pl
from jax.experimental.pallas import tpu as pltpu
from jax.sharding import PartitionSpec as P

MESH = pl.DeviceIdType.MESH
NT, NZ, CY, CX = 2, 16, 48, 128
PAD = 8
TALL = CY + 2 * PAD
OCTETS = CY // 8
FOLD_ROWS = 72
OWN_LAST, FROM_NORTH, FROM_SOUTH, OWN_FIRST = (pl.ds(i, 2) for i in (0, 2, 4, 6))
PACKED = 13
EASTWARD = 6
WESTWARD = 5
BLOCK = 8
HEAT = 0.4
SALT = 0.6


def reciprocal(value):
    guess = pl.reciprocal(value, approx=True)
    return guess * (2.0 - value * guess)


def minmod(first, second):
    return jnp.maximum(jnp.minimum(first, second), 0.0) + jnp.minimum(
        jnp.maximum(first, second), 0.0
    )


def density(pair):
    return SALT * pair[1] - HEAT * pair[0]


def face_fluxes(local, before, after, dz_sum, speed):
    slope = jnp.clip(
        (0.1 * density(local)) * reciprocal(jnp.maximum(density(dz_sum), 1.0)), -0.025, 0.025
    )
    size = jnp.abs(speed)
    limited = 0.5 * size * (1.0 - size)
    forward = speed >= 0.0
    linear = jnp.minimum(speed, 0.0) - 0.1
    low, high, second = [], [], []
    for t in range(NT):
        correction = limited * minmod(local[t], jnp.where(forward, before[t], after[t]))
        taken = correction + (linear * local[t] + slope * dz_sum[t])
        low.append(taken)
        high.append(taken - speed * local[t])
        second.append(correction)
    return low, high, second, forward


def lanes_left(value):
    return pltpu.roll(value, CX - 1, 1)


def lanes_right(value):
    return pltpu.roll(value, 1, 1)


def rows_up(value):
    return pltpu.roll(value, 7, 0)


def rows_down(value):
    return pltpu.roll(value, 1, 0)


def edge_terms(field, dz, bottom, speed, level, nxt, prv, low_at, high_at, low_second, high_second):
    wet = jnp.minimum(bottom, nxt(bottom)) > level
    local = [jnp.where(wet, nxt(f) - f, 0.0) for f in field]
    dz_sum = [z + nxt(z) for z in dz]
    masked = jnp.where(wet, speed, 0.0)
    low, high, second, forward = face_fluxes(
        local, [prv(d) for d in local], [nxt(d) for d in local], dz_sum, masked
    )
    zero = jnp.zeros_like(masked)
    terms, steps = [], []
    for t in range(NT):
        late = zero
        if low_second is not None:
            late = late + jnp.where(low_second & ~forward, second[t], 0.0)
        if high_second is not None:
            late = late + jnp.where(high_second & forward, second[t], 0.0)
        arriving, term, step = late, -late, zero
        if high_at is not None:
            arriving = arriving + jnp.where(high_at, high[t], 0.0)
            step = step + prv(jnp.where(high_at, local[t], 0.0))
        if low_at is not None:
            term = term - jnp.where(low_at, low[t], 0.0)
            step = step + jnp.where(low_at, local[t], 0.0)
        terms.append(term + prv(arriving))
        steps.append(step)
    return terms, steps


def kernel(
    n_gx, n_gy,
    tracers, east, north, bottom, out,
    T, U, V, bottom_int, bf, be, bn, TZ, XY, YB, GX, GY, FY, Q,
    packed, to_east, to_west, from_west, from_east, relay, relay_b, relay_v, folded,
    strip, strip_b, strip_v, edge_c, edge_g,
    load_sem, send_sem, recv_sem, go_sem, go_north_sem,
):
    gx, gy = lax.axis_index("gx"), lax.axis_index("gy")
    east_id = (lax.rem(gx + 1, n_gx), gy)
    west_id = (lax.rem(gx + n_gx - 1, n_gx), gy)
    north_id = (gx, gy + 1)
    south_id = (gx, gy - 1)
    mirror_id = (n_gx - 1 - gx, gy)
    top = gy == n_gy - 1
    base = gy == 0
    below_middle = gy == n_gy // 2 - 1
    above_middle = gy == n_gy // 2
    place = lax.rem(gx, BLOCK)
    by_go = gy <= n_gy // 2
    after_seam = (place == 0) & by_go
    before_seam = (place == BLOCK - 1) & by_go
    crosses_down = place == BLOCK - 1
    crosses_up = crosses_down | ((lax.rem(place, 2) == 0) & (place != BLOCK - 2))
    relayed_up = crosses_up & below_middle
    relayed_down = crosses_down & above_middle
    relays_up = below_middle & jnp.logical_not(crosses_up)
    relays_down = (place == BLOCK - 2) & above_middle
    chip_mate = gx + 1 - 2 * lax.rem(gx, 2)

    barrier = pltpu.get_barrier_semaphore()

    def greet(device):
        pl.semaphore_signal(barrier, inc=1, device_id=device, device_id_type=MESH)

    pl.when(top)(lambda: greet(mirror_id))
    above_go = gy == n_gy // 2 + 1
    mate_sends_down = crosses_down & below_middle
    mate_sends_up = crosses_up & above_middle
    pl.when(mate_sends_down)(lambda: greet((chip_mate, gy + 1)))
    pl.when(mate_sends_up)(lambda: greet((chip_mate, gy - 1)))
    pl.when(jnp.logical_not(top | mate_sends_down))(lambda: greet(north_id))
    pl.when(jnp.logical_not(base | mate_sends_up | above_go))(lambda: greet(south_id))
    greet(west_id)
    pl.when(jnp.logical_not(before_seam))(lambda: greet(east_id))
    expected = (
        4 + (relays_up | relays_down).astype(jnp.int32) - (relayed_up | relayed_down).astype(jnp.int32)
        - after_seam.astype(jnp.int32) - base.astype(jnp.int32) - above_middle.astype(jnp.int32)
    )

    def load(source, target, index):
        return pltpu.make_async_copy(source, target, load_sem.at[index])

    last_rows, first_rows = pl.ds(CY - 2, 2), pl.ds(0, 2)
    early = [
        load(tracers.at[:, :, last_rows, :], strip.at[:, :, OWN_LAST, :], 0),
        load(tracers.at[:, :, first_rows, :], strip.at[:, :, OWN_FIRST, :], 1),
        load(bottom.at[last_rows, :], strip_b.at[OWN_LAST, :], 2),
        load(bottom.at[first_rows, :], strip_b.at[OWN_FIRST, :], 3),
        load(north.at[:, last_rows, :], strip_v.at[:, OWN_LAST, :], 4),
        load(north.at[:, first_rows, :], strip_v.at[:, OWN_FIRST, :], 5),
    ]
    late = [
        load(tracers, T.at[:, :, pl.ds(PAD, CY), :], 6),
        load(bottom, bottom_int, 7),
        load(east, U, 8),
        load(north, V, 9),
    ]

    bulk_first = before_seam & (gy < n_gy // 2 - 1)

    @pl.when(bulk_first)
    def _():
        for copy in late[:3] + early + late[3:]:
            copy.start()

    @pl.when(jnp.logical_not(bulk_first))
    def _():
        for copy in early + late:
            copy.start()

    lane = lax.broadcasted_iota(jnp.int32, (8, CX), 1)
    row = lax.broadcasted_iota(jnp.int32, (8, CX), 0)
    zeros = jnp.zeros((8, CX), jnp.float32)

    def octet(o):
        return pl.ds(PAD + 8 * o, 8)

    def shifted(o, by):
        return pl.ds(PAD + 8 * o + by, 8)

    for pad in (pl.ds(0, PAD), pl.ds(PAD + CY, PAD)):
        bf[pad, :] = zeros
        bn[pad, :] = zeros

    def clear(k, carry):
        for t in range(NT):
            YB[t, k, pl.ds(0, PAD), :] = zeros
            TZ[t, k, pl.ds(PAD + CY, PAD), :] = zeros
        return carry

    lax.fori_loop(0, NZ, clear, 0)

    @pl.when(base)
    def _():
        strip_b[FROM_SOUTH, :] = jnp.zeros((2, CX), jnp.int32)
        for t in range(NT):
            for k in range(NZ):
                strip[t, k, FROM_SOUTH, :] = jnp.zeros((2, CX), jnp.float32)

    for copy in early:
        copy.wait()

    @pl.when(top)
    def _():
        spots = [(t, k, pl.ds(2 * (NZ * t + k), 2)) for t in range(NT) for k in range(NZ)]
        for t, k, spot in spots:
            folded[spot, :] = strip[t, k, OWN_LAST, :]
        folded[pl.ds(64, 2), :] = strip_b[OWN_LAST, :].astype(jnp.float32)
        for i in range(FOLD_ROWS // 8):
            value = folded[pl.ds(8 * i, 8), :]
            for bit in (64, 32, 16, 8, 4, 2, 1):
                value = jnp.where(
                    (lane & bit) != 0, pltpu.roll(value, bit, 1), pltpu.roll(value, CX - bit, 1)
                )
            folded[pl.ds(8 * i, 8), :] = jnp.where((row & 1) != 0, rows_down(value), rows_up(value))
        for t, k, spot in spots:
            relay[t, k] = folded[spot, :]
        relay_b[...] = folded[pl.ds(64, 2), :].astype(jnp.int32)

    def send(source, target, index, slot, device):
        return pltpu.make_async_remote_copy(
            src_ref=source, dst_ref=target, send_sem=send_sem.at[index], recv_sem=recv_sem.at[slot],
            device_id=device, device_id_type=MESH,
        )

    def bundle(sources, targets, index, slot, device):
        pairs = enumerate(zip(sources, targets, strict=True))
        return [send(source, target, index + i, slot + i, device) for i, (source, target) in pairs]

    def start(copies):
        for copy in copies:
            copy.start()

    def wait_recv(copies):
        for copy in copies:
            copy.wait_recv()

    def wait_send(copies):
        for copy in copies:
            copy.wait_send()

    eastward = send(to_east, from_west, 0, 0, east_id)
    westward = send(to_west, from_east, 1, 1, west_id)
    last = [strip.at[:, :, OWN_LAST, :], strip_b.at[OWN_LAST, :], strip_v.at[:, pl.ds(1, 1), :]]
    first = [strip.at[:, :, OWN_FIRST, :], strip_b.at[OWN_FIRST, :]]
    from_south = [strip.at[:, :, FROM_SOUTH, :], strip_b.at[FROM_SOUTH, :], strip_v.at[:, pl.ds(5, 1), :]]
    from_north = [strip.at[:, :, FROM_NORTH, :], strip_b.at[FROM_NORTH, :]]
    between = [relay, relay_b, relay_v]
    northward = bundle(last, from_south, 2, 2, north_id)
    southward = bundle(first, from_north, 5, 5, south_id)
    across = bundle(between[:2], from_north, 2, 5, mirror_id)
    handed_up = bundle(last, between, 2, 7, (chip_mate, gy))
    handed_down = bundle(first, between[:2], 5, 7, (chip_mate, gy))
    forwarded_up = bundle(between, from_south, 7, 2, (chip_mate, gy + 1))
    forwarded_down = bundle(between[:2], from_north, 7, 5, (chip_mate, gy - 1))
    northward_itself = jnp.logical_not(top | relayed_up)
    southward_itself = jnp.logical_not(base | relayed_down)
    even = lax.rem(gx, 2) == 0
    late_entry = below_middle & jnp.logical_not(relayed_up) & (place < BLOCK - 2)

    @pl.when(jnp.logical_not(late_entry))
    def _():
        pl.semaphore_wait(barrier, expected)

        @pl.when(before_seam)
        def _():
            pl.semaphore_signal(go_sem, inc=1, device_id=east_id, device_id_type=MESH)

        @pl.when(above_go)
        def _():
            pl.semaphore_signal(go_north_sem, inc=1, device_id=south_id, device_id_type=MESH)

        pl.when(relayed_up)(lambda: start(handed_up))

        @pl.when(relays_up)
        def _():
            wait_recv(handed_up)
            start(forwarded_up)

        pl.when(northward_itself & below_middle)(lambda: start(northward))
        pl.when(relayed_down)(lambda: start(handed_down))
        pl.when(southward_itself & jnp.logical_not(relays_down))(lambda: start(southward))
        pl.when(northward_itself & jnp.logical_not(below_middle | above_middle))(lambda: start(northward))
        pl.when(top)(lambda: start(across))

        @pl.when(relays_down)
        def _():
            wait_recv(handed_down)
            start(forwarded_down)
            start(southward)

    def send_columns():
        pl.when(jnp.logical_not(even))(eastward.start)
        pl.when(jnp.logical_not(after_seam))(westward.start)
        pl.when(even)(eastward.start)

    for copy in late[:3]:
        copy.wait()

    for o in range(OCTETS):
        bf[octet(o), :] = bottom_int[pl.ds(8 * o, 8), :].astype(jnp.float32)
    for o in range(OCTETS):
        here = bf[octet(o), :]
        be[octet(o), :] = jnp.where(lane == CX - 1, 0.0, jnp.minimum(here, lanes_left(here)))
        bn[octet(o), :] = jnp.minimum(here, bf[shifted(o, 1), :])

    slot_of = lane // 4

    def pack(group, carry):
        t0, t1, speed = zeros, zeros, zeros
        for b in range(4):
            for o in range(OCTETS):
                slot = b * 8 + o
                here = slot_of == slot
                shift = (4 * slot + 2) % CX
                k = 4 * group + b
                t0 = jnp.where(here, pltpu.roll(T[0, k, octet(o), :], shift, 1), t0)
                t1 = jnp.where(here, pltpu.roll(T[1, k, octet(o), :], shift, 1), t1)
                speed = jnp.where(here, pltpu.roll(U[k, pl.ds(8 * o, 8), :], shift, 1), speed)
        packed[group] = t0
        packed[4 + group] = t1
        packed[8 + group] = speed
        return carry

    lax.fori_loop(0, 4, pack, 0, unroll=4)
    packed_b = zeros
    for b in range(4):
        for o in range(OCTETS):
            slot = b * 8 + o
            packed_b = jnp.where(
                slot_of == slot, pltpu.roll(bf[octet(o), :], (4 * slot + 2) % CX, 1), packed_b
            )
    packed[12] = packed_b

    first_half = lax.rem(lane, 4) < 2
    east_speeds = zeros
    for j in range(4):
        to_east[j] = jnp.where(first_half, packed[j], pltpu.roll(packed[4 + j], 2, 1))
        to_west[j] = jnp.where(first_half, pltpu.roll(packed[4 + j], CX - 2, 1), packed[j])
        east_speeds = jnp.where(
            lax.rem(lane, 4) == j, pltpu.roll(packed[8 + j], (CX + j - 1) % CX, 1), east_speeds
        )
    to_east[4] = east_speeds
    to_east[5] = packed_b
    to_west[4] = packed_b

    pl.when(jnp.logical_not(late_entry))(send_columns)


    late[3].wait()

    def vertical(k, carry):
        level = k.astype(jnp.float32)
        above = jnp.where(k > 0, level, 99.0)
        down, up = jnp.minimum(k + 1, NZ - 1), jnp.maximum(k - 1, 0)
        for o in range(OCTETS):
            depth = bf[octet(o), :]
            for t in range(NT):
                here = T[t, k, octet(o), :]
                TZ[t, k, octet(o), :] = jnp.where(
                    depth > level + 1.0, T[t, down, octet(o), :] - here, 0.0
                ) + jnp.where(depth > above, here - T[t, up, octet(o), :], 0.0)
        return carry

    lax.fori_loop(0, NZ, vertical, 0, unroll=2)

    def inside(k, carry):
        level = k.astype(jnp.float32)
        for o in range(OCTETS):
            here = [T[t, k, octet(o), :] for t in range(NT)]
            dz = [TZ[t, k, octet(o), :] for t in range(NT)]
            wet = be[octet(o), :] > level
            local = [jnp.where(wet, lanes_left(f) - f, 0.0) for f in here]
            before = [lanes_right(d) for d in local]
            after = [lanes_left(d) for d in local]
            speed = jnp.where(wet, U[k, pl.ds(8 * o, 8), :], 0.0)
            low, high, _, _ = face_fluxes(
                local, before, after, [z + lanes_left(z) for z in dz], speed
            )
            across_x = [lanes_right(high[t]) - low[t] for t in range(NT)]
            for t in range(NT):
                GX[t, k, octet(o), :] = local[t] + before[t]

            wet = bn[octet(o), :] > level
            wet_before = bn[shifted(o, -1), :] > level
            wet_after = bn[shifted(o, 1), :] > level
            nxt = [T[t, k, shifted(o, 1), :] for t in range(NT)]
            local = [jnp.where(wet, nxt[t] - here[t], 0.0) for t in range(NT)]
            before = [
                jnp.where(wet_before, here[t] - T[t, k, shifted(o, -1), :], 0.0) for t in range(NT)
            ]
            after = [
                jnp.where(wet_after, T[t, k, shifted(o, 2), :] - nxt[t], 0.0) for t in range(NT)
            ]
            speed = jnp.where(wet, V[k, pl.ds(8 * o, 8), :], 0.0)
            low, high, _, _ = face_fluxes(
                local, before, after, [dz[t] + TZ[t, k, shifted(o, 1), :] for t in range(NT)], speed
            )
            for t in range(NT):
                GY[t, k, octet(o), :] = local[t] + before[t]
                XY[t, k, octet(o), :] = across_x[t] - low[t]
                YB[t, k, octet(o), :] = high[t]
        return carry

    lax.fori_loop(0, NZ, inside, 0, unroll=2)

    @pl.when(late_entry)
    def _():
        pl.semaphore_wait(barrier, expected)

        @pl.when(relays_up)
        def _():
            wait_recv(handed_up)
            start(forwarded_up)

        start(northward)
        send_columns()
        start(southward)

    @pl.when(above_middle)
    def _():
        pl.semaphore_wait(go_north_sem, 1)
        start(northward)

    @pl.when(after_seam)
    def _():
        pl.semaphore_wait(go_sem, 1)
        westward.start()

    def prepare(octets):
        def body(k, carry):
            level = k.astype(jnp.float32)
            down = jnp.minimum(k + 1, NZ - 1)
            for o in octets:
                open_below = bf[octet(o), :] > level + 1.0
                here = [T[t, k, octet(o), :] for t in range(NT)]
                step = [T[t, down, octet(o), :] - here[t] for t in range(NT)]
                mean_y = [GY[t, k, octet(o), :] + GY[t, down, octet(o), :] for t in range(NT)]
                inverse = jnp.where(
                    open_below, reciprocal(jnp.maximum(4.0 * density(step), 1.0)), 0.0
                )
                slope = jnp.clip(density(mean_y) * inverse, -1.0, 1.0)
                square = 0.1 * (slope * slope)
                slope = 0.025 * slope
                Q[k, octet(o), :] = inverse
                for t in range(NT):
                    FY[t, k, octet(o), :] = square * step[t] - slope * mean_y[t]
                    XY[t, k, octet(o), :] += here[t] + YB[t, k, shifted(o, -1), :]
            return carry

        lax.fori_loop(0, NZ, body, 0, unroll=2)

    inner, outer = tuple(range(1, OCTETS - 1)), (0, OCTETS - 1)
    prepare(inner)

    def edge_rows_in():
        wait_recv(southward)
        pl.when(jnp.logical_not(base))(lambda: wait_recv(northward))

        def edge_rows(k, carry):
            level = k.astype(jnp.float32)
            above = jnp.where(k > 0, level, 99.0)
            down, up = jnp.minimum(k + 1, NZ - 1), jnp.maximum(k - 1, 0)
            depth = strip_b[...].astype(jnp.float32)
            here = [strip[t, k] for t in range(NT)]
            dz = [
                jnp.where(depth > level + 1.0, strip[t, down] - here[t], 0.0)
                + jnp.where(depth > above, here[t] - strip[t, up], 0.0)
                for t in range(NT)
            ]
            terms, grads = edge_terms(
                here, dz, depth, strip_v[k], level, rows_up, rows_down,
                row == 1, row == 5, row == 0, row == 6,
            )
            for t in range(NT):
                XY[t, k, octet(0), :] += jnp.where(row < 2, pltpu.roll(terms[t], 2, 0), 0.0)
                GY[t, k, octet(0), :] += jnp.where(row < 2, pltpu.roll(grads[t], 2, 0), 0.0)
                XY[t, k, octet(OCTETS - 1), :] += jnp.where(row > 5, pltpu.roll(terms[t], 6, 0), 0.0)
                GY[t, k, octet(OCTETS - 1), :] += jnp.where(row > 5, pltpu.roll(grads[t], 6, 0), 0.0)
            return carry

        lax.fori_loop(0, NZ, edge_rows, 0, unroll=16)

    rows_late = ((gy >= n_gy // 2 - 1) & (gy <= n_gy // 2 + 1)) | top | (
        (gy == n_gy // 2 - 2) & jnp.logical_not(crosses_up)
    )

    @pl.when(jnp.logical_not(rows_late))
    def _():
        edge_rows_in()
        prepare(outer)

    quarter = lax.rem(lane, 4)
    level_in_group = (lane // 32).astype(jnp.float32)
    def edge_columns_in(side, first):
        (eastward if side == 0 else westward).wait_recv()
        own = [[packed[4 * t + j] for j in range(4)] for t in range(NT)]
        if side == 0:
            depth = jnp.where(first_half, from_west[5], packed[12])
            fields = [
                [jnp.where(first_half, from_west[j], own[0][j]) for j in range(4)],
                [jnp.where(first_half, pltpu.roll(from_west[j], CX - 2, 1), own[1][j]) for j in range(4)],
            ]
        else:
            depth = jnp.where(first_half, packed[12], from_east[4])
            fields = [
                [jnp.where(first_half, own[0][j], from_east[j]) for j in range(4)],
                [jnp.where(first_half, own[1][j], pltpu.roll(from_east[j], 2, 1)) for j in range(4)],
            ]
        steps = []
        for t in range(NT):
            turned = [pltpu.roll(f, CX - 32, 1) for f in fields[t]]
            steps.append(
                [
                    jnp.where(
                        depth > level_in_group + (4 * j + 1.0),
                        jnp.where(lane < CX - 32, turned[j], turned[min(j + 1, 3)]) - fields[t][j],
                        0.0,
                    )
                    for j in range(4)
                ]
            )
        for j in range(4):
            dz = []
            for t in range(NT):
                before = pltpu.roll(steps[t][j - 1], 32, 1) if j > 0 else zeros
                dz.append(
                    steps[t][j] + jnp.where(lane < 32, before, pltpu.roll(steps[t][j], 32, 1))
                )
            speed = packed[8 + j]
            if side == 0:
                speed = jnp.where(first_half, pltpu.roll(from_west[4], (CX + 1 - j) % CX, 1), speed)
            terms, grads = edge_terms(
                [fields[t][j] for t in range(NT)], dz, depth, speed, level_in_group + 4.0 * j,
                lanes_left, lanes_right,
                None if side == 0 else quarter == 1, quarter == 1 if side == 0 else None,
                None if side == 0 else quarter == 0, quarter == 2 if side == 0 else None,
            )
            for t in range(NT):
                if first:
                    edge_c[t, j] = terms[t]
                    edge_g[t, j] = grads[t]
                else:
                    edge_c[t, j] += terms[t]
                    edge_g[t, j] += grads[t]

    @pl.when(even)
    def _():
        edge_columns_in(1, True)
        edge_columns_in(0, False)

    @pl.when(jnp.logical_not(even))
    def _():
        edge_columns_in(0, True)
        edge_columns_in(1, False)

    at_edge = (lane < 2) | (lane >= CX - 2)

    def finish(octets, prepared):
        def at(o, ref, t, group, b):
            rolled = pltpu.roll(ref[t, group], (CX - (4 * (b * 8 + o) + 2)) % CX, 1)
            return jnp.where(at_edge, rolled, 0.0)

        def body(group, carry):
            fluxes = [[carry[4 * i], carry[4 * i + 1]] for i in range(len(octets))]
            gx_here = [[carry[4 * i + 2], carry[4 * i + 3]] for i in range(len(octets))]
            after = jnp.minimum(group + 1, 3)
            for b in range(4):
                k = 4 * group + b
                level = k.astype(jnp.float32)
                down = jnp.minimum(k + 1, NZ - 1)
                for i, o in enumerate(octets):
                    depth = bf[octet(o), :]
                    here = [T[t, k, octet(o), :] for t in range(NT)]
                    step = [T[t, down, octet(o), :] - here[t] for t in range(NT)]
                    gx_down = [
                        GX[t, down, octet(o), :]
                        + (at(o, edge_g, t, group, b + 1) if b < 3 else at(o, edge_g, t, after, 0))
                        for t in range(NT)
                    ]
                    mean_x = [gx_here[i][t] + gx_down[t] for t in range(NT)]
                    wet = depth > level
                    if prepared:
                        inverse = Q[k, octet(o), :]
                        other = [FY[t, k, octet(o), :] for t in range(NT)]
                        rest = [XY[t, k, octet(o), :] for t in range(NT)]
                    else:
                        inverse = jnp.where(
                            depth > level + 1.0, reciprocal(jnp.maximum(4.0 * density(step), 1.0)), 0.0
                        )
                        Q[k, octet(o), :] = inverse
                    slope = jnp.clip(density(mean_x) * inverse, -1.0, 1.0)
                    square = 0.1 * (slope * slope)
                    slope = 0.025 * slope
                    for t in range(NT):
                        flux = square * step[t] - slope * mean_x[t]
                        term = at(o, edge_c, t, group, b)
                        if prepared:
                            flux = other[t] + flux
                            total = (rest[t] + term) + (flux - fluxes[i][t])
                            out[t, k, pl.ds(8 * o, 8), :] = jnp.where(wet, total, 0.0)
                            fluxes[i][t] = flux
                        else:
                            FY[t, k, octet(o), :] = flux
                            XY[t, k, octet(o), :] += term + (here[t] + YB[t, k, shifted(o, -1), :])
                    gx_here[i] = gx_down
            return tuple(x for i in range(len(octets)) for x in (*fluxes[i], *gx_here[i]))

        start = []
        for o in octets:
            start += [zeros, zeros]
            start += [GX[t, 0, octet(o), :] + at(o, edge_g, t, 0, 0) for t in range(NT)]
        lax.fori_loop(0, 4, body, tuple(start), unroll=4)

    finish(inner, True)

    def finish_rows(octets):
        def body(k, carry):
            level = k.astype(jnp.float32)
            down = jnp.minimum(k + 1, NZ - 1)
            fluxes, gy_down = [], []
            for i, o in enumerate(octets):
                inverse = Q[k, octet(o), :]
                wet = bf[octet(o), :] > level
                below = [GY[t, down, octet(o), :] for t in range(NT)]
                mean_y = [carry[1][NT * i + t] + below[t] for t in range(NT)]
                slope = jnp.clip(density(mean_y) * inverse, -1.0, 1.0)
                square = 0.1 * (slope * slope)
                slope = 0.025 * slope
                for t in range(NT):
                    step = T[t, down, octet(o), :] - T[t, k, octet(o), :]
                    flux = FY[t, k, octet(o), :] + (square * step - slope * mean_y[t])
                    total = XY[t, k, octet(o), :] + (flux - carry[0][NT * i + t])
                    out[t, k, pl.ds(8 * o, 8), :] = jnp.where(wet, total, 0.0)
                    fluxes.append(flux)
                gy_down += below
            return tuple(fluxes), tuple(gy_down)

        top_gy = tuple(GY[t, 0, octet(o), :] for o in octets for t in range(NT))
        lax.fori_loop(0, NZ, body, (tuple(zeros for _ in top_gy), top_gy), unroll=16)

    @pl.when(rows_late)
    def _():
        finish(outer, False)
        edge_rows_in()
        finish_rows(outer)

    @pl.when(jnp.logical_not(rows_late))
    def _():
        finish(outer, True)

    eastward.wait_send()
    westward.wait_send()
    pl.when(southward_itself)(lambda: wait_send(southward))
    pl.when(northward_itself)(lambda: wait_send(northward))
    pl.when(relayed_up)(lambda: wait_send(handed_up))
    pl.when(relayed_down)(lambda: wait_send(handed_down))
    pl.when(top)(lambda: wait_send(across))
    pl.when(relays_up)(lambda: wait_send(forwarded_up))
    pl.when(relays_down)(lambda: wait_send(forwarded_down))


def solution(mesh):
    n_gx, n_gy = mesh.shape["gx"], mesh.shape["gy"]
    f32 = jnp.float32
    in_hbm = pl.BlockSpec(memory_space=pltpu.HBM)
    field = pltpu.VMEM((NT, NZ, TALL, CX), f32)
    levels = pltpu.VMEM((NZ, CY, CX), f32)
    plane = pltpu.VMEM((TALL, CX), f32)
    packed = pltpu.VMEM((PACKED, 8, CX), f32)
    eastward = pltpu.VMEM((EASTWARD, 8, CX), f32)
    westward = pltpu.VMEM((WESTWARD, 8, CX), f32)
    edge = pltpu.VMEM((NT, 4, 8, CX), f32)

    def on_device(tracers, east_speed, north_speed, bottom_level):
        return pl.pallas_call(
            functools.partial(kernel, n_gx, n_gy),
            out_shape=jax.ShapeDtypeStruct((NT, NZ, CY, CX), f32),
            in_specs=[in_hbm] * 4,
            out_specs=pl.BlockSpec(memory_space=pltpu.VMEM),
            scratch_shapes=[
                field, levels, levels, pltpu.VMEM((CY, CX), jnp.int32), plane, plane, plane,
                field, field, field, field, field, field, pltpu.VMEM((NZ, TALL, CX), f32),
                packed, eastward, westward, eastward, westward,
                pltpu.VMEM((NT, NZ, 2, CX), f32), pltpu.VMEM((2, CX), jnp.int32),
                pltpu.VMEM((NZ, 1, CX), f32), pltpu.VMEM((FOLD_ROWS, CX), f32),
                pltpu.VMEM((NT, NZ, 8, CX), f32), pltpu.VMEM((8, CX), jnp.int32),
                pltpu.VMEM((NZ, 8, CX), f32), edge, edge,
                pltpu.SemaphoreType.DMA((10,)), pltpu.SemaphoreType.DMA((10,)),
                pltpu.SemaphoreType.DMA((10,)), pltpu.SemaphoreType.REGULAR, pltpu.SemaphoreType.REGULAR,
            ],
            compiler_params=pltpu.CompilerParams(
                collective_id=0, has_side_effects=True, vmem_limit_bytes=24 * 1024 * 1024
            ),
        )(
            *[
                pltpu.with_memory_space_constraint(x, pltpu.HBM)
                for x in (tracers, east_speed, north_speed, bottom_level)
            ]
        )

    in_specs = (P(None, None, "gy", "gx"), P(None, "gy", "gx"), P(None, "gy", "gx"), P("gy", "gx"))
    return jax.shard_map(
        on_device, mesh=mesh, in_specs=in_specs, out_specs=P(None, None, "gy", "gx"), check_vma=False
    )
```
